32 devices in a mesh: dp: 8 (over z, x), mp: 4 (over y, core).
Axes of the slice: x: 2, y: 2, z: 4, core: 2. Of those that a mesh axis runs over, the one named last changes fastest.
Arguments:
- tokens: bfloat16 [8, 1536, 768], P('dp', 'mp'), may hold values from -6 to 6
- cotangent: bfloat16 [8, 1536, 768], P('dp', 'mp'), may hold values from -6 to 6
- w_qkv: bfloat16 [2, 768, 2304], replicated, may hold values from -0.21875 to 0.21875
- w_attn: bfloat16 [2, 768, 768], replicated, may hold values from -3.5 to 3.5
- attn_gain: float32 [2, 768], replicated, may hold values from 0.5 to 1.5
- rel_bias: float32 [2, 12, 32], replicated, may hold values from -4 to 4
- ffn_gain: float32 [2, 768], replicated, may hold values from 0.5 to 1.5
- router: bfloat16 [2, 768, 16], replicated, may hold values from -0.21875 to 0.21875
- w_in: bfloat16 [2, 16, 768, 3072], P(None, 'dp', None, 'mp'), may hold values from -0.21875 to 0.21875
- w_out: bfloat16 [2, 16, 3072, 768], P(None, 'dp', 'mp'), may hold values from -0.109375 to 0.109375
- cont_lengths: int32 [8, 8], P('dp'), may hold values from 1 to 128, 512 in all within a row
- routes: int32 [2, 8, 1536, 2], P(None, 'dp', 'mp'), may hold values from 0 to 15, as said below
- slots: int32 [2, 8, 1536, 2], P(None, 'dp', 'mp'), may hold values from 0 to 53, as said below
- drops: int32 [2, 8, 1536, 2], P(None, 'dp', 'mp'), may hold values from 0 to 1, as said below
Outputs:
- output: bfloat16 [8, 1536, 768], P('dp', 'mp')
- input_grad: float32 [8, 1536, 768], P('dp', 'mp')
- grad_w_qkv: float32 [2, 768, 2304], replicated
- grad_w_attn: float32 [2, 768, 768], replicated
- grad_attn_gain: float32 [2, 768], replicated
- grad_rel_bias: float32 [2, 12, 32], replicated
- grad_ffn_gain: float32 [2, 768], replicated
- grad_router: float32 [2, 768, 16], replicated
- grad_w_in: float32 [2, 16, 768, 3072], P(None, 'dp', None, 'mp')
- grad_w_out: float32 [2, 16, 3072, 768], P(None, 'dp', 'mp')
The draws below stay inside these ranges and needn't reach their ends.
Inputs may be any that keep to these rules, and one draw needn't show every extreme that they name: `cont_lengths`: each row sums to 512; its largest entry is 128. `routes`: a token's two experts differ; in every layer one expert is named by 54 or more tokens of every device. Among the kept pairs of one device that name one expert the slots are distinct; dropped pairs have slot 0; in every layer one expert receives exactly 54 kept pairs from every device. `drops`: a pair is dropped only where its expert already holds 54 kept pairs of the same device.
All inputs are finite; a program needn't handle non-finite values.
Results may differ from the reference program's by a relative error of at most 0.022.
Values may be sent and summed in bfloat16 or wider, within the bound.
A program may use at most 384 MiB of HBM per device.

```python
import math
import jax
import jax.numpy as jnp
import numpy as np
from jax import lax

D = 768
HEADS = 12
FF = 3072
BUCKETS = 32
LAYERS = 2
PROMPT = 1024
CONTS = 8
CONT_TOK = 512
GROUP_DEV = 1
HEAD_DIM = 64
EXPERTS = 16
CONT_MOST = 128
GLEN = 1536
MP_ROWS = 384
GROUPS = 8
SOURCES = 32
TOK_DEV = 384
CAP = 54
N_DP = 8
N_MP = 4


def shuffled(key, number, length):
    key_list = jax.random.split(key, number)

    def one_perm(single_key):
        return jax.random.permutation(single_key, length)
    return jax.vmap(one_perm)(key_list)


def layout(values):
    shaped = values.reshape(LAYERS, N_DP, N_MP, GROUP_DEV, MP_ROWS, 2)
    return jnp.transpose(shaped, (0, 1, 3, 2, 4, 5)).reshape(LAYERS, GROUPS, GLEN, 2).astype(jnp.int32)


def expert_plan(key):
    blocks = N_DP * N_MP
    key_list = jax.random.split(key, 7)
    draw_shape = (LAYERS, blocks, TOK_DEV)
    order = shuffled(key_list[0], LAYERS, EXPERTS)
    hot_count = max(EXPERTS // 8, 1)
    picked = jax.random.randint(key_list[1], (LAYERS, blocks * TOK_DEV), 0, hot_count)
    hot_pick = jnp.take_along_axis(order, picked, axis=1).reshape(draw_shape)
    spread = jax.random.randint(key_list[2], draw_shape, 0, EXPERTS)
    coin_flip = jax.random.randint(key_list[3], draw_shape, 0, 4)
    first = jnp.where(coin_flip == 0, hot_pick, spread)
    forced = shuffled(key_list[4], LAYERS * blocks, TOK_DEV).reshape(draw_shape) < CAP
    first = jnp.where(forced, order[:, 0][:, None, None], first)
    second = (first + jax.random.randint(key_list[5], draw_shape, 1, EXPERTS)) % EXPERTS
    pairs = jnp.stack([first, second], axis=-1).reshape(LAYERS, blocks, 2 * TOK_DEV)
    priority = shuffled(key_list[6], LAYERS * blocks, 2 * TOK_DEV).reshape(LAYERS, blocks, 2 * TOK_DEV)
    inverse = jnp.argsort(priority, axis=-1)
    ranked = jnp.take_along_axis(pairs, inverse, axis=-1)
    hits = (ranked[..., None] == jnp.arange(EXPERTS, dtype=jnp.int32)).astype(jnp.int32)
    before = (jnp.cumsum(hits, axis=2) - hits).astype(jnp.int32)
    rank_sorted = jnp.sum(before * hits, axis=-1).astype(jnp.int32)
    rank_pair = jnp.take_along_axis(rank_sorted, priority, axis=-1)
    dropped = (rank_pair >= CAP).astype(jnp.int32)
    slot_pair = jnp.where(rank_pair >= CAP, 0, rank_pair)
    return (layout(pairs), layout(slot_pair), layout(dropped))


def draw_routes(key, part):
    plan = expert_plan(key)
    return plan[0]


def draw_slots(key, part):
    plan = expert_plan(key)
    return plan[1]


def draw_drops(key, part):
    plan = expert_plan(key)
    return plan[2]


def steps_of(stream_key, shape, cuts, smallest, high):
    gain, own = 1.0, jax.random.fold_in(stream_key, 6)
    for dim, shards_of in cuts:
        draws = jnp.exp(jax.random.uniform(jax.random.fold_in(own, dim), (shards_of,), jnp.float32, smallest / len(cuts), high / len(cuts)))
        gain = gain * jnp.repeat(draws, shape[dim] // shards_of).reshape([-1 if axis == dim else 1 for axis in range(len(shape))])
    return gain


def profile(count, total, limit, slope):
    loads = [(1 << 20) // math.isqrt(grade ** slope) + 1 for grade in range(2, count + 1)]
    surplus, given = total - limit - (count - 1), [1] * (count - 1)
    while surplus > 0:
        movable = [i for i in range(count - 1) if given[i] < limit]
        whole, remaining = sum([loads[i] for i in movable]), surplus
        for i in movable:
            extra = min(limit - given[i], max(1, remaining * loads[i] // whole), surplus)
            given[i] = given[i] + extra
            surplus = surplus - extra
    return np.array([limit] + given)


def ragged(key, number_of, total, limit, skew):
    if number_of == 2:
        one = jax.random.randint(key, (), max(1, total - limit), min(limit, total - 1) + 1)
        return jnp.stack([one, total - one])
    tallies = jnp.asarray(profile(number_of, total, limit, skew), jnp.int32)
    couples = (number_of - 1) // 2
    giver, receiver = tallies[1:1 + 2 * couples:2], tallies[2:2 + 2 * couples:2]
    margin = jnp.minimum(giver - 1, limit - receiver)
    moved = jax.random.randint(jax.random.fold_in(key, 1), (couples,), 0, 1 << 20) % (margin + 1)
    tallies = tallies.at[1:1 + 2 * couples:2].set(giver - moved).at[2:2 + 2 * couples:2].set(receiver + moved)
    return tallies[jax.random.permutation(jax.random.fold_in(key, 2), number_of)]


def centred(rng, extent, scale, bound, shards=(), kind=jnp.bfloat16):
    values = jax.random.normal(rng, extent, jnp.float32) * scale
    if len(shards) > 0:
        values = steps_of(rng, extent, shards, -0.22, 0.18) * values
    return jnp.clip(values, min=-bound, max=bound).astype(kind)


def setup_inputs(seed: int = 0) -> dict:
    key_of = jax.random.split(jax.random.key(seed), 15)
    tokens = centred(key_of[0], (GROUPS, GLEN, D), 1.0, 6.0, ((0, 8), (1, 4)))
    cotangent = centred(key_of[1], (GROUPS, GLEN, D), 1.0, 6.0, ((0, 8), (1, 4)))
    w_qkv = centred(key_of[2], (LAYERS, D, 3 * D), D ** -0.5, 0.21875)
    w_attn = centred(key_of[3], (LAYERS, D, D), (max(D // 256, 2)) ** -0.5, 3.5)
    attn_gain = jnp.clip(1.0 + 0.1 * jax.random.normal(key_of[4], (LAYERS, D), jnp.float32), 0.5, 1.5)
    rel_bias = centred(key_of[5], (LAYERS, HEADS, BUCKETS), 1.0, 4.0, (), jnp.float32)
    ffn_gain = jnp.clip(1.0 + 0.1 * jax.random.normal(key_of[6], (LAYERS, D), jnp.float32), 0.5, 1.5)
    router = centred(key_of[7], (LAYERS, D, EXPERTS), D ** -0.5, 0.21875)
    w_in = centred(key_of[8], (LAYERS, EXPERTS, D, FF), D ** -0.5, 0.21875, ((1, 8), (3, 4)))
    w_out = centred(key_of[9], (LAYERS, EXPERTS, FF, D), FF ** -0.5, 0.109375, ((1, 8), (2, 4)))
    cont_lengths = jax.vmap(lambda own: ragged(own, CONTS, CONT_TOK, CONT_MOST, 2))(jax.random.split(key_of[10], GROUPS)).reshape((GROUPS, CONTS)).astype(jnp.int32)
    routes = draw_routes(jax.random.fold_in(key_of[14], 71), 0)
    slots = draw_slots(jax.random.fold_in(key_of[14], 71), 0)
    drops = draw_drops(jax.random.fold_in(key_of[14], 71), 0)
    return {"tokens": tokens, "cotangent": cotangent, "w_qkv": w_qkv, "w_attn": w_attn, "attn_gain": attn_gain, "rel_bias": rel_bias, "ffn_gain": ffn_gain, "router": router, "w_in": w_in, "w_out": w_out, "cont_lengths": cont_lengths, "routes": routes, "slots": slots, "drops": drops}


EPSILON = 1e-06
SQRT_TWO_PI = 0.7978845608028654
THRESHOLDS = (16, 20, 24, 32, 40, 48, 64, 80, 96, 128, 160, 192, 256, 384, 512, 768)
HIGHEST = lax.Precision.HIGHEST

@jax.custom_vjp
def low(v):
    return lax.optimization_barrier(v.astype(jnp.bfloat16)).astype(jnp.float32)

@jax.custom_vjp
def low_back(v):
    return v

def low_keep(v):
    return (low(v), None)

def low_pass(kept, grad):
    return (grad,)

def back_keep(v):
    return (v, None)

def back_low(kept, grad):
    return (low(grad),)
low.defvjp(low_keep, low_pass)
low_back.defvjp(back_keep, back_low)

def rms_scale(values, gain_row):
    return values * lax.rsqrt(lax.optimization_barrier(jnp.mean(values * values, axis=-1, keepdims=True)) + EPSILON) * gain_row

def gelu_tanh(values):
    return 0.5 * values * (1.0 + jnp.tanh(SQRT_TWO_PI * (values + 0.044715 * values * values * values)))

def bucket_of(distance):
    counted = jnp.minimum(distance, 15)
    for threshold in THRESHOLDS:
        counted = counted + (distance >= threshold).astype(jnp.int32)
    return counted

def geometry(lengths, row_ids):
    starts = PROMPT + jnp.cumsum(lengths, axis=-1) - lengths
    inside = row_ids[None, :, None] >= starts[:, None, :]
    segment = lax.optimization_barrier(jnp.sum(inside.astype(jnp.int32), axis=-1)) - 1
    begin_at = lax.optimization_barrier(jnp.max(jnp.where(inside, starts[:, None, :], 0), axis=-1))
    position = jnp.where(row_ids[None, :] < PROMPT, row_ids[None, :], PROMPT + row_ids[None, :] - begin_at)
    return (position.astype(jnp.int32), segment.astype(jnp.int32))

def visibility(query_pos, query_seg, key_pos, key_seg):
    query_at = query_pos[:, :, None]
    query_in = query_seg[:, :, None]
    key_at = key_pos[:, None, :]
    key_in = key_seg[:, None, :]
    earlier = key_at <= query_at
    allowed = (key_in < 0) & ((query_in >= 0) | earlier) | (key_in >= 0) & (key_in == query_in) & earlier
    bucket = bucket_of(jnp.maximum(query_at - key_at, 0)).astype(jnp.int32)
    return (allowed, bucket)

def attend(group_items, bias_row):
    query_f, keys_f, values_f, lengths = group_items
    row_ids = jnp.arange(GLEN, dtype=jnp.int32)
    position, segment = geometry(lengths[None, :], row_ids)
    allowed, bucket = visibility(position, segment, position, segment)
    raw = jnp.einsum('qhd,khd->hqk', query_f, keys_f, precision=HIGHEST) * HEAD_DIM ** (-0.5) + bias_row[:, bucket[0]]
    raw = jnp.where(allowed[0][None], low_back(raw), -1e+30)
    probs = low(jax.nn.softmax(raw, axis=-1))
    return jnp.einsum('hqk,khd->qhd', probs, values_f, precision=HIGHEST)

def expert_apply(expert_items):
    rows_in, up_weight, down_weight = expert_items
    inner_act = low_back(jnp.einsum('scd,df->scf', rows_in, up_weight, precision=HIGHEST))
    hidden = low(gelu_tanh(inner_act))
    return low_back(low(jnp.einsum('scf,fd->scd', hidden, down_weight, precision=HIGHEST)))

def reference(tokens, cotangent, w_qkv, w_attn, attn_gain, rel_bias, ffn_gain, router, w_in, w_out, cont_lengths, routes, slots, drops):
    group_ids = jnp.arange(GROUPS, dtype=jnp.int32)[:, None]
    row_ids = jnp.arange(GLEN, dtype=jnp.int32)[None, :]
    source = group_ids // GROUP_DEV * (GLEN // MP_ROWS) + row_ids // MP_ROWS
    source_pair = jnp.broadcast_to(source[:, :, None], (GROUPS, GLEN, 2)).astype(jnp.int32)

    def forward(stream, qkv_weight, attn_weight, gain_attn, bias_table, gain_ffn, router_weight, up_weight, down_weight):
        for layer_now in range(LAYERS):
            normed = low(rms_scale(stream, gain_attn[layer_now]))
            qkv_all = low_back(low(jnp.einsum('gtd,de->gte', normed, qkv_weight[layer_now], precision=HIGHEST)))
            split_shape = (GROUPS, GLEN, HEADS, HEAD_DIM)
            query_all = qkv_all[:, :, :D].reshape(split_shape)
            keys_all = qkv_all[:, :, D:2 * D].reshape(split_shape)
            values_all = qkv_all[:, :, 2 * D:].reshape(split_shape)
            bias_row = bias_table[layer_now]

            def one_group(group_items):
                return attend(group_items, bias_row)
            mixed_out = lax.map(jax.checkpoint(one_group), (query_all, keys_all, values_all, cont_lengths))
            mixed_out = low_back(low(mixed_out.reshape(GROUPS, GLEN, D)))
            stream = stream + low_back(jnp.einsum('gtd,de->gte', mixed_out, attn_weight[layer_now], precision=HIGHEST))
            ffn_in = low(rms_scale(stream, gain_ffn[layer_now]))
            logits = jnp.einsum('gtd,de->gte', ffn_in, router_weight[layer_now], precision=HIGHEST)
            chosen = routes[layer_now]
            gate_pair = jax.nn.softmax(jnp.take_along_axis(logits, chosen, axis=-1), axis=-1)
            keep_pair = (1 - drops[layer_now]).astype(jnp.float32)
            slot_now = slots[layer_now]
            buffer = jnp.zeros((EXPERTS, SOURCES, CAP, D), jnp.float32)
            buffer = buffer.at[chosen, source_pair, slot_now].add(ffn_in[:, :, None, :] * keep_pair[:, :, :, None])
            buffer = low_back(buffer)
            results = lax.map(jax.checkpoint(expert_apply), (buffer, up_weight[layer_now], down_weight[layer_now]))
            pair_out = results[chosen, source_pair, slot_now]
            stream = stream + lax.optimization_barrier(jnp.sum((gate_pair * keep_pair)[:, :, :, None] * pair_out, axis=2))
        return stream
    floats = (tokens.astype(jnp.float32), w_qkv.astype(jnp.float32), w_attn.astype(jnp.float32), attn_gain.astype(jnp.float32), rel_bias.astype(jnp.float32), ffn_gain.astype(jnp.float32), router.astype(jnp.float32), w_in.astype(jnp.float32), w_out.astype(jnp.float32))
    result, pull = jax.vjp(forward, *floats)
    grads = pull(cotangent.astype(jnp.float32))
    return (result.astype(jnp.bfloat16), grads[0], grads[1], grads[2], grads[3], grads[4], grads[5], grads[6], grads[7], grads[8])
```

```python
import functools

import jax
import jax.numpy as jnp
from jax import lax
from jax.experimental import pallas as pl
from jax.experimental.pallas import tpu as pltpu
from jax.sharding import PartitionSpec as P

PROMPT = 1024


EPSILON = 1e-06
SQRT_TWO_PI = 0.7978845608028654
THRESHOLDS = (16, 20, 24, 32, 40, 48, 64, 80, 96, 128, 160, 192, 256, 384, 512, 768)
HIGHEST = lax.Precision.HIGHEST


def rms_scale(values, gain_row):
    return (
        values * lax.rsqrt(jnp.mean(values * values, axis=-1, keepdims=True) + EPSILON) * gain_row
    )


def gelu_tanh(values):
    return (
        0.5
        * values
        * (1.0 + jnp.tanh(SQRT_TWO_PI * (values + 0.044715 * values * values * values)))
    )


def bucket_of(distance):
    counted = jnp.minimum(distance, 15)
    for threshold in THRESHOLDS:
        counted = counted + (distance >= threshold).astype(jnp.int32)
    return counted


def geometry(lengths, row_ids):
    starts = PROMPT + jnp.cumsum(lengths, axis=-1) - lengths
    inside = row_ids[None, :, None] >= starts[:, None, :]
    segment = jnp.sum(inside.astype(jnp.int32), axis=-1) - 1
    begin_at = jnp.max(jnp.where(inside, starts[:, None, :], 0), axis=-1)
    position = jnp.where(
        row_ids[None, :] < PROMPT, row_ids[None, :], PROMPT + row_ids[None, :] - begin_at
    )
    return (position, segment)


def visibility(query_pos, query_seg, key_pos, key_seg):
    query_at = query_pos[:, :, None]
    query_in = query_seg[:, :, None]
    key_at = key_pos[:, None, :]
    key_in = key_seg[:, None, :]
    earlier = key_at <= query_at
    allowed = (key_in < 0) & ((query_in >= 0) | earlier) | (key_in >= 0) & (
        key_in == query_in
    ) & earlier
    bucket = bucket_of(jnp.maximum(query_at - key_at, 0))
    return (allowed, bucket)


def bias_table(bias_row, bucket):
    full_bias = jnp.zeros((bias_row.shape[0],) + bucket.shape, jnp.float32)
    for number in range(bias_row.shape[1]):
        full_bias = full_bias + jnp.where(
            bucket[None] == number, bias_row[:, number][:, None, None, None], 0.0
        )
    return full_bias


def score_block(query_b, key_every, full_bias, allowed, factor):
    raw = (
        jnp.einsum("grhd,gkhd->hgrk", query_b, key_every, preferred_element_type=jnp.float32)
        * factor
    )
    raw = raw + full_bias
    return jnp.where(allowed[None], raw, -1e30)


def body(
    tokens,
    cotangent,
    w_qkv,
    w_attn,
    attn_gain,
    rel_bias,
    ffn_gain,
    router,
    w_in,
    w_out,
    cont_lengths,
    routes,
    slots,
    drops,
):
    groups, local_rows, model_width = tokens.shape
    head_count = rel_bias.shape[1]
    bucket_count = rel_bias.shape[2]
    head_size = model_width // head_count
    factor = head_size ** (-0.5)
    layer_count = w_qkv.shape[0]
    dp_count = lax.axis_size("dp")
    mp_count = lax.axis_size("mp")
    seq_len = local_rows * mp_count
    local_experts = w_in.shape[1]
    expert_total = local_experts * dp_count
    tok_count = groups * local_rows
    capacity = max(2, 9 * 2 * tok_count // (8 * expert_total))
    slot_total = expert_total * capacity
    rows_here = lax.axis_index("mp") * local_rows + jnp.arange(local_rows, dtype=jnp.int32)
    rows_every = jnp.arange(seq_len, dtype=jnp.int32)
    query_pos, query_seg = geometry(cont_lengths, rows_here)
    key_pos, key_seg = geometry(cont_lengths, rows_every)
    allowed, bucket = visibility(query_pos, query_seg, key_pos, key_seg)
    route_all = routes.reshape(layer_count, tok_count, 2)
    slot_all = slots.reshape(layer_count, tok_count, 2)
    keep_all = (1 - drops.reshape(layer_count, tok_count, 2)).astype(jnp.float32)
    head_shape = (groups, seq_len, head_count, head_size)
    stream = tokens.reshape(tok_count, model_width).astype(jnp.float32)
    stored = []
    for layer_now in range(layer_count):
        normed_b = rms_scale(stream, attn_gain[layer_now]).astype(jnp.bfloat16)
        qkv_all = jnp.dot(normed_b, w_qkv[layer_now], preferred_element_type=jnp.float32).astype(
            jnp.bfloat16
        )
        query_b = qkv_all[:, :model_width].reshape(groups, local_rows, head_count, head_size)
        key_own = qkv_all[:, model_width : 2 * model_width].reshape(groups, local_rows, model_width)
        value_own = qkv_all[:, 2 * model_width :].reshape(groups, local_rows, model_width)
        key_every, value_every = (
            lax.all_gather(key_own, "mp", axis=1, tiled=True),
            lax.all_gather(value_own, "mp", axis=1, tiled=True),
        )
        key_every = key_every.reshape(head_shape)
        value_every = value_every.reshape(head_shape)
        full_bias = bias_table(rel_bias[layer_now], bucket)
        scores = score_block(query_b, key_every, full_bias, allowed, factor)
        top_score = jnp.max(scores, axis=-1, keepdims=True)
        weights = jnp.exp(scores - top_score)
        weight_sum = jnp.sum(weights, axis=-1, keepdims=True)
        log_total = top_score + jnp.log(weight_sum)
        probs_b = (weights / weight_sum).astype(jnp.bfloat16)
        mixed_b = jnp.einsum(
            "hgrk,gkhd->grhd", probs_b, value_every, preferred_element_type=jnp.float32
        )
        mixed_b = mixed_b.reshape(tok_count, model_width).astype(jnp.bfloat16)
        middle = stream + jnp.dot(mixed_b, w_attn[layer_now], preferred_element_type=jnp.float32)
        kept_keys = (key_every, value_every)
        ffn_b = rms_scale(middle, ffn_gain[layer_now]).astype(jnp.bfloat16)
        logits = jnp.dot(ffn_b, router[layer_now], preferred_element_type=jnp.float32)
        chosen = route_all[layer_now]
        keep_pair = keep_all[layer_now]
        gate_pair = jax.nn.softmax(jnp.take_along_axis(logits, chosen, axis=1), axis=-1)
        target = chosen * capacity + slot_all[layer_now]
        sending = jnp.where(
            keep_pair[:, :, None] > 0, ffn_b[:, None, :], jnp.zeros((), jnp.bfloat16)
        )
        send_rows = (
            jnp.zeros((slot_total, model_width), jnp.bfloat16)
            .at[target.reshape(-1)]
            .add(sending.reshape(-1, model_width))
        )
        arrived = lax.all_to_all(
            send_rows.reshape(dp_count, local_experts, capacity, model_width),
            "dp",
            split_axis=0,
            concat_axis=0,
            tiled=True,
        )
        rows_in = lax.all_gather(arrived, "mp", axis=0, tiled=True)
        up_block = w_in[layer_now]
        down_block = w_out[layer_now]
        inner_act = jnp.einsum(
            "secd,edf->secf", rows_in, up_block, preferred_element_type=jnp.float32
        )
        hidden_b = gelu_tanh(inner_act).astype(jnp.bfloat16)
        summed = lax.psum_scatter(
            jnp.einsum(
                "secf,efd->secd", hidden_b, down_block, preferred_element_type=jnp.float32
            ).astype(jnp.bfloat16),
            "mp",
            scatter_dimension=0,
            tiled=True,
        )
        kept_rows = (rows_in, inner_act, hidden_b)
        returned = lax.all_to_all(summed, "dp", split_axis=0, concat_axis=0, tiled=True).reshape(
            slot_total, model_width
        )
        pair_out = returned[target].astype(jnp.float32)
        stored.append(
            (
                stream,
                normed_b,
                query_b,
                key_own,
                value_own,
                kept_keys,
                log_total,
                mixed_b,
                middle,
                ffn_b,
                chosen,
                keep_pair,
                gate_pair,
                target,
                pair_out,
                kept_rows,
                full_bias,
            )
        )
        stream = middle + jnp.sum((gate_pair * keep_pair)[:, :, None] * pair_out, axis=1)
    output = stream.astype(jnp.bfloat16).reshape(groups, local_rows, model_width)
    one_hot = (
        bucket[None] == jnp.arange(bucket_count, dtype=jnp.int32)[:, None, None, None]
    ).astype(jnp.bfloat16)
    expert_ids = jnp.arange(expert_total, dtype=jnp.int32)
    qkv_grads = [None] * layer_count
    attn_grads = [None] * layer_count
    attn_gain_grads = [None] * layer_count
    bias_grads = [None] * layer_count
    ffn_gain_grads = [None] * layer_count
    router_grads = [None] * layer_count
    up_grads = [None] * layer_count
    down_grads = [None] * layer_count
    flowing = cotangent.reshape(tok_count, model_width).astype(jnp.float32)
    for layer_now in reversed(range(layer_count)):
        (
            stream_in,
            normed_b,
            query_b,
            key_own,
            value_own,
            kept_keys,
            log_total,
            mixed_b,
            middle,
            ffn_b,
            chosen,
            keep_pair,
            gate_pair,
            target,
            pair_out,
            kept_rows,
            full_bias,
        ) = stored[layer_now]
        weighted = gate_pair * keep_pair
        pair_grad = weighted[:, :, None] * flowing[:, None, :]
        gate_grad = keep_pair * jnp.sum(flowing[:, None, :] * pair_out, axis=-1)
        picked_grad = gate_pair * (
            gate_grad - jnp.sum(gate_pair * gate_grad, axis=-1, keepdims=True)
        )
        logit_grad = jnp.sum(
            picked_grad[:, :, None] * (chosen[:, :, None] == expert_ids).astype(jnp.float32), axis=1
        )
        back_rows = (
            jnp.zeros((slot_total, model_width), jnp.float32)
            .at[target.reshape(-1)]
            .add(pair_grad.reshape(-1, model_width))
        )
        back_rows = back_rows.astype(jnp.bfloat16).reshape(
            dp_count, local_experts, capacity, model_width
        )
        grad_arrived = lax.all_to_all(back_rows, "dp", split_axis=0, concat_axis=0, tiled=True)
        grad_rows = lax.all_gather(grad_arrived, "mp", axis=0, tiled=True)
        up_block = w_in[layer_now]
        down_block = w_out[layer_now]
        rows_in, inner_act, hidden_b = kept_rows
        down_grad = jnp.einsum(
            "secf,secd->efd", hidden_b, grad_rows, preferred_element_type=jnp.float32
        )
        hidden_grad = jnp.einsum(
            "secd,efd->secf", grad_rows, down_block, preferred_element_type=jnp.float32
        )
        inner_grad = jax.vjp(gelu_tanh, inner_act)[1](hidden_grad)[0].astype(jnp.bfloat16)
        up_grad = jnp.einsum(
            "secd,secf->edf", rows_in, inner_grad, preferred_element_type=jnp.float32
        )
        rows_grad = lax.psum_scatter(
            jnp.einsum(
                "secf,edf->secd", inner_grad, up_block, preferred_element_type=jnp.float32
            ).astype(jnp.bfloat16),
            "mp",
            scatter_dimension=0,
            tiled=True,
        )
        up_grads[layer_now] = up_grad
        down_grads[layer_now] = down_grad
        grad_back = lax.all_to_all(
            rows_grad, "dp", split_axis=0, concat_axis=0, tiled=True
        ).reshape(slot_total, model_width)
        ffn_grad = jnp.sum(keep_pair[:, :, None] * grad_back[target].astype(jnp.float32), axis=1)
        ffn_grad = ffn_grad + jnp.einsum(
            "te,de->td", logit_grad, router[layer_now].astype(jnp.float32), precision=HIGHEST
        )
        router_grads[layer_now] = jnp.einsum(
            "td,te->de", ffn_b.astype(jnp.float32), logit_grad, precision=HIGHEST
        )
        middle_grad, ffn_gain_grads[layer_now] = jax.vjp(rms_scale, middle, ffn_gain[layer_now])[1](
            ffn_grad
        )
        middle_grad = middle_grad + flowing
        branch_grad = middle_grad.astype(jnp.bfloat16)
        attn_grads[layer_now] = jnp.einsum(
            "td,te->de", mixed_b, branch_grad, preferred_element_type=jnp.float32
        )
        mixed_grad = jnp.einsum(
            "te,de->td", branch_grad, w_attn[layer_now], preferred_element_type=jnp.float32
        )
        mixed_grad = mixed_grad.astype(jnp.bfloat16).reshape(
            groups, local_rows, head_count, head_size
        )
        key_every, value_every = kept_keys
        scores = score_block(query_b, key_every, full_bias, allowed, factor)
        probs = jnp.exp(scores - log_total)
        prob_grad = jnp.einsum(
            "grhd,gkhd->hgrk", mixed_grad, value_every, preferred_element_type=jnp.float32
        )
        score_grad = (
            probs * (prob_grad - jnp.sum(probs * prob_grad, axis=-1, keepdims=True))
        ).astype(jnp.bfloat16)
        query_grad = (
            jnp.einsum("hgrk,gkhd->grhd", score_grad, key_every, preferred_element_type=jnp.float32)
            * factor
        )
        key_part = (
            jnp.einsum("hgrk,grhd->gkhd", score_grad, query_b, preferred_element_type=jnp.float32)
            * factor
        )
        value_part = jnp.einsum(
            "hgrk,grhd->gkhd",
            probs.astype(jnp.bfloat16),
            mixed_grad,
            preferred_element_type=jnp.float32,
        )
        key_grad, value_grad = (
            lax.psum_scatter(
                key_part.reshape(groups, seq_len, model_width).astype(jnp.bfloat16),
                "mp",
                scatter_dimension=1,
                tiled=True,
            ).astype(jnp.float32),
            lax.psum_scatter(
                value_part.reshape(groups, seq_len, model_width).astype(jnp.bfloat16),
                "mp",
                scatter_dimension=1,
                tiled=True,
            ).astype(jnp.float32),
        )
        bias_grads[layer_now] = jnp.einsum(
            "hgrk,bgrk->hb", score_grad, one_hot, preferred_element_type=jnp.float32
        )
        qkv_grad = jnp.concatenate(
            [
                query_grad.reshape(tok_count, model_width),
                key_grad.reshape(tok_count, model_width),
                value_grad.reshape(tok_count, model_width),
            ],
            axis=1,
        ).astype(jnp.bfloat16)
        qkv_grads[layer_now] = jnp.einsum(
            "td,te->de", normed_b, qkv_grad, preferred_element_type=jnp.float32
        )
        normed_grad = jnp.einsum(
            "te,de->td", qkv_grad, w_qkv[layer_now], preferred_element_type=jnp.float32
        )
        stream_grad, attn_gain_grads[layer_now] = jax.vjp(
            rms_scale, stream_in, attn_gain[layer_now]
        )[1](normed_grad)
        flowing = middle_grad + stream_grad
    totals = lax.psum(
        (
            jnp.stack(qkv_grads),
            jnp.stack(attn_grads),
            jnp.stack(attn_gain_grads),
            jnp.stack(bias_grads),
            jnp.stack(ffn_gain_grads),
            jnp.stack(router_grads),
        ),
        ("dp", "mp"),
    )
    input_grad = flowing.reshape(groups, local_rows, model_width)
    return (
        output,
        input_grad,
        totals[0],
        totals[1],
        totals[2],
        totals[3],
        totals[4],
        totals[5],
        jnp.stack(up_grads),
        jnp.stack(down_grads),
    )


BF = jnp.bfloat16
F32 = jnp.float32
VMEM = pl.BlockSpec(memory_space=pltpu.VMEM)
SMEM = pl.BlockSpec(memory_space=pltpu.SMEM)
ANY = pl.BlockSpec(memory_space=pl.ANY)
VMEM_BYTES = 60 << 20
MESH = pl.DeviceIdType.MESH
LANES = 128
QB = 256


def nn(a, b):
    return lax.dot_general(a, b, (((1,), (0,)), ((), ())), preferred_element_type=F32)


def nt(a, b):
    return lax.dot_general(a, b, (((1,), (1,)), ((), ())), preferred_element_type=F32)


def tn(a, b):
    return lax.dot_general(a, b, (((0,), (0,)), ((), ())), preferred_element_type=F32)


def segments(lens, shape, dim):
    at = lax.broadcasted_iota(jnp.int32, shape, dim)
    segment = jnp.full(shape, -1, jnp.int32)
    begin = jnp.zeros(shape, jnp.int32)
    start = jnp.int32(0)
    for number in range(lens.shape[1]):
        inside = at >= start
        segment = segment + inside.astype(jnp.int32)
        begin = jnp.where(inside, start, begin)
        start = start + lens[0, number]
    return segment, at - begin


def bias_stage(vec, lens, table, cont_bias):
    width = vec.shape[1]
    rows = lax.broadcasted_iota(jnp.int32, (LANES, width), 0)
    skewed = jnp.broadcast_to(vec, (LANES, width))
    for bit in range(7):
        skewed = jnp.where((rows >> bit) % 2 == 1, pltpu.roll(skewed, 1 << bit, 1), skewed)
    table[...] = skewed[:, : width - LANES].T
    cont = cont_bias.shape[1]
    _, offset = segments(lens, (LANES, cont), 1)
    place = (lax.broadcasted_iota(jnp.int32, (LANES, cont), 0) == offset).astype(BF)
    full = table[0:PROMPT, :]
    high = full.astype(BF)
    low = (full - high.astype(F32)).astype(BF)
    cont_bias[...] = nn(jnp.concatenate([high, low], 1), jnp.concatenate([place, place], 0))


def blocks_of(seq):
    out = []
    for start in range(0, PROMPT, QB):
        out.append((start, start + QB, None))
    for start in range(0, seq - PROMPT, QB):
        out.append((PROMPT + start, PROMPT, max(0, start - LANES)))
    return out


def scores_of(keys, query, table, cont_bias, seg_col, seg_row, block, h):
    q0, prompt_keys, cont_from = block
    if cont_from is None:
        left = PROMPT - q0
        bias = jnp.concatenate(
            [table[left : left + prompt_keys, :], table[left - LANES : left - LANES + prompt_keys, :]], 1
        )
        return [(0, prompt_keys, nt(keys[h, 0:prompt_keys, :], query) + bias)]
    at = q0 - PROMPT
    first = nt(keys[h, 0:PROMPT, :], query) + cont_bias[:, at : at + QB]
    k0, k1 = PROMPT + cont_from, q0 + QB
    left = PROMPT + cont_from - at
    bias = jnp.concatenate(
        [table[left : left + k1 - k0, :], table[left - LANES : left - LANES + k1 - k0, :]], 1
    )
    same = seg_col[cont_from : at + QB, :][:, 0:1] == seg_row[:, at : at + QB]
    second = jnp.where(same, nt(keys[h, k0:k1, :], query) + bias, -1e30)
    return [(0, PROMPT, first), (k0, k1, second)]


def attn_fwd_kernel(heads, size, lens, normed, weight, vecs, qkv_o, mixed_o, lse_o, q_s, k_s, vt_s, table, cont_bias, mixt, segc):
    seq = normed.shape[0]
    own = heads * size
    for i in range(seq // QB):
        rows = pl.ds(i * QB, QB)
        part = nn(normed[rows, :], weight[...]).astype(BF)
        qkv_o[rows, :] = part
        for h in range(heads):
            q_s[h, rows, :] = part[:, h * size : (h + 1) * size] * BF(0.125)
            k_s[h, rows, :] = part[:, own + h * size : own + (h + 1) * size]
            vt_s[h, :, rows] = part[:, 2 * own + h * size : 2 * own + (h + 1) * size].astype(F32).T.astype(BF)
    seg_row, _ = segments(lens, (1, seq - PROMPT), 1)
    segc[...] = segments(lens, (seq - PROMPT, LANES), 0)[0]

    def head(h, carry):
        bias_stage(vecs[pl.ds(h, 1), :], lens, table, cont_bias)
        for block in blocks_of(seq):
            q0 = block[0]
            parts = scores_of(k_s, q_s[h, q0 : q0 + QB, :], table, cont_bias, segc, seg_row, block, h)
            top = functools.reduce(jnp.maximum, [jnp.max(s, axis=0, keepdims=True) for _, _, s in parts])
            total, mixed = 0.0, 0.0
            for k0, k1, s in parts:
                p = jnp.exp(s - top)
                total = total + jnp.sum(p, axis=0, keepdims=True)
                mixed = mixed + nn(vt_s[h, :, k0:k1], p.astype(BF))
            mixt[pl.ds(pl.multiple_of(h * size, size), size), q0 : q0 + QB] = mixed / total
            lse_o[pl.ds(h, 1), q0 : q0 + QB] = top + jnp.log(total)
        return carry

    lax.fori_loop(0, heads, head, 0)
    for i in range(seq // QB):
        mixed_o[i * QB : (i + 1) * QB, :] = mixt[:, i * QB : (i + 1) * QB].T.astype(BF)


def attn_fwd(lens, normed, weight, vecs, heads, size):
    seq = normed.shape[0]
    own = heads * size
    width = vecs.shape[1]
    return pl.pallas_call(
        functools.partial(attn_fwd_kernel, heads, size),
        out_shape=(
            jax.ShapeDtypeStruct((seq, 3 * own), BF),
            jax.ShapeDtypeStruct((seq, own), BF),
            jax.ShapeDtypeStruct((heads, seq), F32),
        ),
        in_specs=[SMEM, VMEM, VMEM, VMEM],
        out_specs=(VMEM, VMEM, VMEM),
        scratch_shapes=[
            pltpu.VMEM((heads, seq, size), BF),
            pltpu.VMEM((heads, seq, size), BF),
            pltpu.VMEM((heads, size, seq), BF),
            pltpu.VMEM((width - LANES, LANES), F32),
            pltpu.VMEM((PROMPT, seq - PROMPT), F32),
            pltpu.VMEM((own, seq), F32),
            pltpu.VMEM((seq - PROMPT, LANES), jnp.int32),
        ],
        compiler_params=pltpu.CompilerParams(vmem_limit_bytes=VMEM_BYTES),
    )(lens, normed, weight, vecs)


def attn_bwd_kernel(
    heads, size, lens, qkv, normed, branch, w_attn, mixed, lse, vecs,
    dqkv_o, gw_o, dvec_o,
    q_s, k_s, v_s, kt_s, do_s, table, cont_bias, fold, dtable, dk_s, dv_s, dqt, dk_all, dv_all, segc,
):
    seq = normed.shape[0]
    own = heads * size
    cont = seq - PROMPT
    for i in range(seq // QB):
        rows = pl.ds(i * QB, QB)
        part = qkv[rows, :]
        dmix = nt(branch[rows, :], w_attn[...]).astype(BF)
        for h in range(heads):
            q_s[h, rows, :] = part[:, h * size : (h + 1) * size] * BF(0.125)
            key = part[:, own + h * size : own + (h + 1) * size]
            k_s[h, rows, :] = key
            kt_s[h, :, rows] = (key.astype(F32) * 0.125).T.astype(BF)
            v_s[h, rows, :] = part[:, 2 * own + h * size : 2 * own + (h + 1) * size]
            do_s[h, rows, :] = dmix[:, h * size : (h + 1) * size]
    seg_row, _ = segments(lens, (1, cont), 1)
    segc[...] = segments(lens, (cont, LANES), 0)[0]
    _, offset = segments(lens, (cont, LANES), 0)
    unplace = (lax.broadcasted_iota(jnp.int32, (cont, LANES), 1) == offset).astype(BF)
    width = vecs.shape[1]

    def head(h, carry):
        bias_stage(vecs[pl.ds(h, 1), :], lens, table, cont_bias)
        dtable[...] = jnp.zeros_like(dtable)
        dk_s[...] = jnp.zeros_like(dk_s)
        dv_s[...] = jnp.zeros_like(dv_s)
        for block in blocks_of(seq):
            q0, prompt_keys, cont_from = block
            query = q_s[h, q0 : q0 + QB, :]
            dout = do_s[h, q0 : q0 + QB, :]
            parts = scores_of(k_s, query, table, cont_bias, segc, seg_row, block, h)
            lse_row = lse[pl.ds(h, 1), q0 : q0 + QB]
            kept, delta = [], 0.0
            for k0, k1, s in parts:
                p = jnp.exp(s - lse_row)
                dp = nt(v_s[h, k0:k1, :], dout)
                delta = delta + jnp.sum(p * dp, axis=0, keepdims=True)
                dv_s[k0:k1, :] += nn(p.astype(BF), dout)
                kept.append((k0, k1, p, dp))
            dq = 0.0
            for k0, k1, p, dp in kept:
                ds = p * (dp - delta)
                dsb = ds.astype(BF)
                dk_s[k0:k1, :] += nn(dsb, query)
                dq = dq + nn(kt_s[h, :, k0:k1], dsb)
                if cont_from is not None and k0 == 0:
                    fold[:, q0 - PROMPT : q0 - PROMPT + QB] = dsb
                else:
                    left = PROMPT - q0 if cont_from is None else PROMPT + cont_from - (q0 - PROMPT)
                    dtable[left : left + k1 - k0, :] += ds[:, 0:LANES]
                    dtable[left - LANES : left - LANES + k1 - k0, :] += ds[:, LANES:]
            dqt[pl.ds(pl.multiple_of(h * size, size), size), q0 : q0 + QB] = dq
        dk_all[h] = dk_s[...].astype(BF)
        dv_all[h] = dv_s[...].astype(BF)
        dtable[0:PROMPT, :] += nn(fold[...], unplace)
        flat = dtable[...].T
        flat = jnp.concatenate([flat, jnp.zeros((LANES, LANES), F32)], 1)
        rows = lax.broadcasted_iota(jnp.int32, (LANES, width), 0)
        for bit in range(7):
            flat = jnp.where((rows >> bit) % 2 == 1, pltpu.roll(flat, width - (1 << bit), 1), flat)
        dvec_o[pl.ds(h, 1), :] = jnp.sum(flat, axis=0, keepdims=True)
        return carry

    lax.fori_loop(0, heads, head, 0)
    for i in range(seq // QB):
        rows = pl.ds(i * QB, QB)
        pieces = [dqt[:, i * QB : (i + 1) * QB].T.astype(BF)]
        pieces += [dk_all[h, rows, :] for h in range(heads)] + [dv_all[h, rows, :] for h in range(heads)]
        dqkv_o[rows, :] = jnp.concatenate(pieces, 1)
    half = normed.shape[1] // 2
    for i in range(2):
        cols = slice(i * half, (i + 1) * half)
        gw_o[cols, 0 : 3 * own] = tn(normed[:, cols], dqkv_o[...])
        gw_o[cols, 3 * own :] = tn(branch[:, cols], mixed[...])


def attn_bwd(lens, qkv, normed, branch, w_attn, mixed, lse, vecs, heads, size):
    seq, model = normed.shape
    own = heads * size
    width = vecs.shape[1]
    cont = seq - PROMPT
    return pl.pallas_call(
        functools.partial(attn_bwd_kernel, heads, size),
        out_shape=(
            jax.ShapeDtypeStruct((seq, 3 * own), BF),
            jax.ShapeDtypeStruct((model, 4 * own), F32),
            jax.ShapeDtypeStruct((heads, width), F32),
        ),
        in_specs=[SMEM] + [VMEM] * 7,
        out_specs=(VMEM, VMEM, VMEM),
        scratch_shapes=[
            pltpu.VMEM((heads, seq, size), BF),
            pltpu.VMEM((heads, seq, size), BF),
            pltpu.VMEM((heads, seq, size), BF),
            pltpu.VMEM((heads, size, seq), BF),
            pltpu.VMEM((heads, seq, size), BF),
            pltpu.VMEM((width - LANES, LANES), F32),
            pltpu.VMEM((PROMPT, cont), F32),
            pltpu.VMEM((PROMPT, cont), BF),
            pltpu.VMEM((width - LANES, LANES), F32),
            pltpu.VMEM((seq, size), F32),
            pltpu.VMEM((seq, size), F32),
            pltpu.VMEM((own, seq), F32),
            pltpu.VMEM((heads, seq, size), BF),
            pltpu.VMEM((heads, seq, size), BF),
            pltpu.VMEM((cont, LANES), jnp.int32),
        ],
        compiler_params=pltpu.CompilerParams(vmem_limit_bytes=VMEM_BYTES),
    )(lens, qkv, normed, branch, w_attn, mixed, lse, vecs)


def diagonals():
    width = PROMPT + 3 * LANES
    at = jnp.arange(width, dtype=jnp.int32)
    distance = jnp.where(at <= PROMPT, PROMPT - at, PROMPT + width - at)
    valid = (at <= PROMPT) | (at > width - LANES)
    return width, distance, valid


def bias_vectors(bias):
    _, distance, valid = diagonals()
    hot = bucket_of(distance)[None, :] == jnp.arange(bias.shape[-1], dtype=jnp.int32)[:, None]
    picked = jnp.sum(jnp.where(hot, bias[..., :, None], 0.0), axis=-2)
    return jnp.where(valid, picked, -1e30)


def bias_grads(dvecs, buckets):
    _, distance, valid = diagonals()
    hot = (bucket_of(distance)[None, :] == jnp.arange(buckets, dtype=jnp.int32)[:, None]) & valid[None, :]
    return jnp.sum(jnp.where(hot, dvecs[..., None, :], 0.0), axis=-1)


def scatter_rows(rows, values, send):
    experts, tile, _ = send.shape
    tokens, model = values[0].shape
    half = model // 2
    at = lax.broadcasted_iota(jnp.int32, (experts * tile, tokens), 0)
    place, piece = [], []
    for j in range(2):
        slot = rows[2 + j : 3 + j, :]
        piece.append(jnp.where(rows[4 + j : 5 + j, :] > 0, slot // tile, -1))
        place.append(rows[j : j + 1, :] * tile + slot % tile)

    def pick(number, shift, columns):
        hots = [
            (jnp.where(piece[j] == number, place[j] + shift, -1) == at) for j in range(2)
        ]
        if len(values) == 1:
            return nn((hots[0] | hots[1]).astype(BF), values[0][:, columns])
        return nn(hots[0].astype(BF), values[0][:, columns]) + nn(hots[1].astype(BF), values[1][:, columns])

    for i in range(3):
        send[:, :, i * model : (i + 1) * model] = pick(i, 0, slice(0, model)).astype(BF).reshape(experts, tile, model)
    tail = pick(3, 0, slice(0, half)) + pick(3, 8, slice(half, model))
    send[:, :, 3 * model :] = tail.astype(BF).reshape(experts, tile, half)


def gather_rows(cols, j, back):
    experts, tile, wide = back.shape
    half = wide // 7
    model = 2 * half
    tokens = cols.shape[0]
    at = lax.broadcasted_iota(jnp.int32, (tokens, experts * tile), 1)
    slot = cols[:, 2 + j : 3 + j]
    piece = jnp.where(cols[:, 4 + j : 5 + j] > 0, slot // tile, -1)
    place = cols[:, j : j + 1] * tile + slot % tile
    total = 0.0
    for i in range(3):
        hot = (jnp.where(piece == i, place, -1) == at).astype(BF)
        total = total + nn(hot, back[:, :, i * model : (i + 1) * model].reshape(experts * tile, model))
    tail = back[:, :, 3 * model :].reshape(experts * tile, half)
    left = nn((jnp.where(piece == 3, place, -1) == at).astype(BF), tail)
    right = nn((jnp.where(piece == 3, place + 8, -1) == at).astype(BF), tail)
    return total + jnp.concatenate([left, right], 1)


def unfold_tail(block, half):
    wide = block.astype(F32)
    return jnp.concatenate([wide[0:8, :], wide[8:16, :]], 1)


def mp_places():
    me = lax.axis_index("mp")
    core, row = lax.rem(me, 2), me // 2
    return me, core, row * 2 + 1 - core, (1 - row) * 2 + core, (1 - row) * 2 + 1 - core


def signal_to(barrier, **place):
    pl.semaphore_signal(barrier, inc=1, device_id=place, device_id_type=MESH)


def remote(src, dst, send_sem, recv_sem, **place):
    return pltpu.make_async_remote_copy(
        src_ref=src, dst_ref=dst, send_sem=send_sem, recv_sem=recv_sem, device_id=place, device_id_type=MESH
    )


def gather_mp(held, ssem, rsem):
    me, core, mate, across, diagonal = mp_places()
    to_mate = remote(held.at[me], held.at[me], ssem.at[0], rsem.at[0], mp=mate)
    over = remote(held.at[me], held.at[me], ssem.at[1], rsem.at[1], mp=across)
    over.start()
    to_mate.start()
    over.wait_recv()
    passed = remote(held.at[across], held.at[across], ssem.at[2], rsem.at[2], mp=mate)
    passed.start()
    to_mate.wait_recv()
    passed.wait_recv()
    for copy in (to_mate, over, passed):
        copy.wait_send()


def swap_mp(out, held, ssem, rsem, lsem):
    me, core, mate, across, diagonal = mp_places()
    copies = [
        remote(out.at[to], held.at[me], ssem.at[n], rsem.at[n], mp=to) for n, to in enumerate((diagonal, across, mate))
    ]
    for copy in copies:
        copy.start()
    own = pltpu.make_async_copy(out.at[me], held.at[me], lsem)
    own.start()
    own.wait()
    for copy in copies:
        copy.wait()


def greet_mp(count):
    me, core, mate, across, diagonal = mp_places()
    barrier = pltpu.get_barrier_semaphore()
    for to in (mate, across, diagonal)[:count]:
        signal_to(barrier, mp=to)
    pl.semaphore_wait(barrier, count)


def mean_square_scale(values):
    return lax.rsqrt(jnp.mean(values * values, axis=-1, keepdims=True) + EPSILON)


def norm_grads(values, gain, upstream):
    scale = mean_square_scale(values)
    scaled = upstream * gain
    drift = jnp.mean(values * scaled, axis=-1, keepdims=True)
    return scale * scaled - values * (scale * scale * scale * drift), jnp.sum(
        upstream * values * scale, axis=0, keepdims=True
    )


def first_kernel(tokens, gain, all_o, held, ssem, rsem):
    greet_mp(2)
    me = lax.axis_index("mp")
    stream = tokens[...].astype(F32)
    held[me] = (stream * mean_square_scale(stream) * gain[...]).astype(BF)
    gather_mp(held, ssem, rsem)
    all_o[...] = held[...]


def next_kernel(middle, back, cols, gates, gain, stream_o, all_o, held, ssem, rsem):
    greet_mp(2)
    me = lax.axis_index("mp")
    stream = middle[...]
    for j in range(2):
        stream = stream + gates[:, j : j + 1] * gather_rows(cols, j, back)
    stream_o[...] = stream
    held[me] = (stream * mean_square_scale(stream) * gain[...]).astype(BF)
    gather_mp(held, ssem, rsem)
    all_o[...] = held[...]


def middle_kernel(with_grad, *refs):
    if with_grad:
        (mixed, stream, w_attn, gain, router, rows, cols, cotangent, middle_o, ffn_o, gates_o, send_o, back_o, held, ssem, rsem, lsem) = refs
    else:
        (mixed, stream, w_attn, gain, router, rows, cols, middle_o, ffn_o, gates_o, send_o, held, ssem, rsem, lsem) = refs
    greet_mp(3)
    swap_mp(mixed, held, ssem, rsem, lsem)
    part = held.shape[2]
    middle = stream[...].astype(F32)
    for m in range(held.shape[0]):
        middle = middle + nn(held[m], w_attn[m * part : (m + 1) * part, :])
    middle_o[...] = middle
    ffn = (middle * mean_square_scale(middle) * gain[...]).astype(BF)
    ffn_o[...] = ffn
    logits = nn(ffn, router[...])
    expert = lax.broadcasted_iota(jnp.int32, logits.shape, 1)
    chosen = [
        jnp.sum(jnp.where(expert == cols[:, j : j + 1], logits, 0.0), axis=1, keepdims=True) for j in range(2)
    ]
    top = jnp.maximum(chosen[0], chosen[1])
    powers = [jnp.exp(c - top) for c in chosen]
    gates = [p / (powers[0] + powers[1]) for p in powers]
    gates_o[...] = jnp.concatenate(gates, 1)
    scatter_rows(rows, [ffn], send_o)
    if with_grad:
        flow = cotangent[...].astype(F32)
        scatter_rows(rows, [(gates[j] * cols[:, 4 + j : 5 + j].astype(F32) * flow).astype(BF) for j in range(2)], back_o)


def post_kernel(with_output, *refs):
    if with_output:
        (back, returned, flow_in, middle, ffn, gates, cols, router, gain, grad_o, all_o, gain_o, router_o, out_o, held, ssem, rsem) = refs
    else:
        (back, returned, flow_in, middle, ffn, gates, cols, router, gain, grad_o, all_o, gain_o, router_o, held, ssem, rsem) = refs
    greet_mp(2)
    me = lax.axis_index("mp")
    flow = flow_in[...].astype(F32)
    outs = [gather_rows(cols, j, returned) for j in range(2)]
    gate = [gates[:, j : j + 1] for j in range(2)]
    keep = [cols[:, 4 + j : 5 + j].astype(F32) for j in range(2)]
    if with_output:
        out_o[...] = (middle[...] + gate[0] * keep[0] * outs[0] + gate[1] * keep[1] * outs[1]).astype(BF)
    gate_grad = [keep[j] * jnp.sum(flow * outs[j], axis=1, keepdims=True) for j in range(2)]
    shared = gate[0] * gate_grad[0] + gate[1] * gate_grad[1]
    expert = lax.broadcasted_iota(jnp.int32, (flow.shape[0], router.shape[1]), 1)
    logit_grad = 0.0
    for j in range(2):
        logit_grad = logit_grad + jnp.where(expert == cols[:, j : j + 1], gate[j] * (gate_grad[j] - shared), 0.0)
    high = logit_grad.astype(BF)
    low = (logit_grad - high.astype(F32)).astype(BF)
    upstream = gather_rows(cols, 0, back) + gather_rows(cols, 1, back)
    upstream = upstream + nt(high, router[...]) + nt(low, router[...])
    router_o[...] = tn(high, ffn[...]) + tn(low, ffn[...])
    grad, gain_o[...] = norm_grads(middle[...], gain[...], upstream)
    grad = grad + flow
    grad_o[...] = grad
    held[me] = grad.astype(BF)
    gather_mp(held, ssem, rsem)
    all_o[...] = held[...]


def close_kernel(with_send, *refs):
    if with_send:
        (dqkv, weight, stream, gain, grad, rows, cols, gates, flow_o, gain_o, send_o, held, ssem, rsem, lsem) = refs
    else:
        (dqkv, weight, stream, gain, grad, flow_o, gain_o, held, ssem, rsem, lsem) = refs
    greet_mp(3)
    swap_mp(dqkv, held, ssem, rsem, lsem)
    upstream = 0.0
    for m in range(held.shape[0]):
        upstream = upstream + nt(held[m], weight[m])
    inner, gain_o[...] = norm_grads(stream[...].astype(F32), gain[...], upstream)
    flow = grad[...] + inner
    flow_o[...] = flow
    if with_send:
        scatter_rows(
            rows,
            [(gates[:, j : j + 1] * cols[:, 4 + j : 5 + j].astype(F32) * flow).astype(BF) for j in range(2)],
            send_o,
        )


def mp_call(kernel, number, outs, scratch, swap, *args):
    sems = [pltpu.SemaphoreType.DMA((3,)), pltpu.SemaphoreType.DMA((3,))] + ([pltpu.SemaphoreType.DMA] if swap else [])
    return pl.pallas_call(
        kernel,
        out_shape=tuple(jax.ShapeDtypeStruct(shape, kind) for shape, kind in outs),
        in_specs=[VMEM] * len(args),
        out_specs=tuple([VMEM] * len(outs)),
        scratch_shapes=[pltpu.VMEM(scratch, BF)] + sems,
        compiler_params=pltpu.CompilerParams(
            collective_id=number, has_side_effects=True, vmem_limit_bytes=VMEM_BYTES
        ),
    )(*args)


def gelu_grad(values):
    inner = jnp.tanh(SQRT_TWO_PI * (values + 0.044715 * values * values * values))
    slope = SQRT_TWO_PI * (1.0 + 3.0 * 0.044715 * values * values)
    return 0.5 * values * (1.0 + inner), 0.5 * (1.0 + inner) + 0.5 * values * (1.0 - inner * inner) * slope


def expert_kernel(mode, layer, dp_count, *refs):
    forward, backward = mode in ("fwd", "both"), mode in ("both", "bwd")
    refs = list(refs)

    def take(count):
        taken = refs[:count]
        del refs[:count]
        return taken

    (send_x,) = take(1) if forward else (None,)
    (send_g,) = take(1) if backward else (None,)
    (x_in,) = take(1) if mode == "bwd" else (None,)
    w_in, w_out = take(2)
    (out_o,) = take(1) if forward else (None,)
    (x_o,) = take(1) if mode == "fwd" else (None,)
    grad_o, gw_in_o, gw_out_o = take(3) if backward else (None, None, None)
    w1, w2, wsem, wssem, wrsem = take(5)
    kept_part, x_all, xsem = take(3)
    paths = []
    for sending in ([send_x] if forward else []) + ([send_g] if backward else []):
        paths.append((sending, take(14)))
    if backward:
        g_all, hid_all, ig_all, stage, gsem, grsem, glsem = take(7)

    d = lax.axis_index("dp")
    me, core, mate, across, diagonal = mp_places()
    row = me // 2
    index = d * 2 + core
    experts = dp_count * 2
    groups = dp_count // 2
    model = w1.shape[1]
    half = model // 2
    rows_a = x_all.shape[1] // 2

    barrier = pltpu.get_barrier_semaphore()

    def greet(k, carry):
        signal_to(barrier, dp=lax.rem(d + k // 2, dp_count), mp=row * 2 + lax.rem(core + k % 2, 2))
        return carry

    lax.fori_loop(1, experts, greet, 0)
    signal_to(barrier, mp=across)
    pl.semaphore_wait(barrier, experts)

    def send_all(path):
        sending, (recv_a, recv_b, ssem, asem, fsem, bsem, part, pssem, prsem, ret_s, ret, rssem, rrsem, psend) = path

        def one(k, carry):
            dd, cc = lax.rem(d + k // 2, dp_count), lax.rem(core + k % 2, 2)
            to = dd * 2 + cc
            remote(sending.at[to], recv_a.at[index], ssem.at[to], asem.at[index], dp=dd, mp=row * 2 + cc).start()
            return carry

        lax.fori_loop(1, experts, one, 0)
        pltpu.make_async_copy(sending.at[index], recv_a.at[index], asem.at[index]).start()

    send_all(paths[0])
    copies = []
    for n, (source, held) in enumerate(((w_in, w1), (w_out, w2))):
        copies.append(remote(source.at[layer, 1 - core], held.at[core], wssem.at[n], wrsem.at[n], mp=mate))
        copies.append(pltpu.make_async_copy(source.at[layer, core], held.at[core], wsem.at[n]))
    for copy in copies:
        copy.start()
    if mode == "bwd":
        saved = pltpu.make_async_copy(x_in, x_all, xsem)
        saved.start()
    for path in paths[1:]:
        send_all(path)
    for copy in copies:
        copy.wait()
    if mode == "bwd":
        saved.wait()

    def source_of(g, kk):
        return lax.rem(d + dp_count - (g * 2 + kk), dp_count)

    def unpack(held, g, side, into):
        base = side * rows_a
        for kk in range(2):
            s0 = source_of(g, kk)
            tails = []
            for cc in range(2):
                block = held[s0 * 2 + cc]
                for i in range(3):
                    into[g, base + i * 64 + kk * 32 + cc * 16 : base + i * 64 + kk * 32 + cc * 16 + 16, :] = block[
                        :, i * model : (i + 1) * model
                    ]
                tails.append(unfold_tail(block[:, 3 * model :], half))
            into[g, base + 192 + kk * 16 : base + 208 + kk * 16, :] = jnp.concatenate(tails, 0).astype(BF)

    def run_path(path, into, compute):
        sending, (recv_a, recv_b, ssem, asem, fsem, bsem, part, pssem, prsem, ret_s, ret, rssem, rrsem, psend) = path

        def forward_copy(s0):
            two = pl.ds(s0 * 2, 2)
            return remote(recv_a.at[two], recv_b.at[two], fsem.at[s0], bsem.at[s0], mp=across)

        def partial_copy(g):
            return remote(psend.at[g], part.at[g], pssem.at[g], prsem.at[g], mp=across)

        def step(i, carry):
            @pl.when(i < groups)
            def _():
                for kk in range(2):
                    s0 = source_of(i, kk)
                    for cc in range(2):
                        src = s0 * 2 + cc
                        pltpu.make_async_copy(recv_a.at[src], recv_a.at[src], asem.at[src]).wait()
                    forward_copy(s0).start()

            @pl.when((i >= 1) & (i <= groups))
            def _():
                g = i - 1
                for kk in range(2):
                    forward_copy(source_of(g, kk)).wait_recv()
                unpack(recv_a, g, 0, into)
                unpack(recv_b, g, 1, into)
                total = compute(g)
                kept_part[lax.rem(g, 2)] = total[0:rows_a, :]
                psend[g] = total[rows_a:, :].astype(BF)
                partial_copy(g).start()

            @pl.when(i >= 2)
            def _():
                g = i - 2
                partial_copy(g).wait_recv()
                total = kept_part[lax.rem(g, 2)] + part[g].astype(F32)
                for kk in range(2):
                    s0 = source_of(g, kk)
                    for cc in range(2):
                        src = s0 * 2 + cc
                        for n in range(3):
                            at = n * 64 + kk * 32 + cc * 16
                            ret_s[src, :, n * model : (n + 1) * model] = total[at : at + 16, :].astype(BF)
                        at = 192 + kk * 16 + cc * 8
                        ret_s[src, :, 3 * model :] = jnp.concatenate(
                            [total[at : at + 8, 0:half], total[at : at + 8, half:]], 0
                        ).astype(BF)

                        @pl.when(src == index)
                        def _():
                            pltpu.make_async_copy(ret_s.at[src], ret.at[index], rrsem.at[index]).start()

                        @pl.when(src != index)
                        def _():
                            remote(
                                ret_s.at[src], ret.at[index], rssem.at[src], rrsem.at[index], dp=s0, mp=row * 2 + cc
                            ).start()

            return carry

        lax.fori_loop(0, groups + 2, step, 0)

    def finish_path(path, result):
        sending, (recv_a, recv_b, ssem, asem, fsem, bsem, part, pssem, prsem, ret_s, ret, rssem, rrsem, psend) = path

        def end(e, carry):
            pltpu.make_async_copy(ret.at[e], ret.at[e], rrsem.at[e]).wait()

            @pl.when(e != index)
            def _():
                pltpu.make_async_copy(ret_s.at[e], ret_s.at[e], rssem.at[e]).wait()
                pltpu.make_async_copy(sending.at[e], sending.at[e], ssem.at[e]).wait()

            return carry

        lax.fori_loop(0, experts, end, 0)

        def end_pair(s0, carry):
            two = pl.ds(s0 * 2, 2)
            pltpu.make_async_copy(recv_a.at[two], recv_a.at[two], fsem.at[s0]).wait()
            return carry

        lax.fori_loop(0, dp_count, end_pair, 0)

        def end_group(g, carry):
            pltpu.make_async_copy(psend.at[g], psend.at[g], pssem.at[g]).wait()
            return carry

        lax.fori_loop(0, groups, end_group, 0)
        result[...] = ret[...]

    def compute_forward(g):
        x = x_all[g]
        total = 0.0
        for q in range(2):
            hidden = gelu_tanh(nn(x, w1[q])).astype(BF)
            if backward:
                hid_all[q, g] = hidden
            total = total + nn(hidden, w2[q])
        return total

    def compute_backward(g):
        x, gr = x_all[g], g_all[g]
        total = 0.0
        for q in range(2):
            value, slope = gelu_grad(nn(x, w1[q]))
            if not forward:
                hid_all[q, g] = value.astype(BF)
            inner = (nt(gr, w2[q]) * slope).astype(BF)
            ig_all[q, g] = inner
            total = total + nt(inner, w1[q])
        return total

    if forward:
        run_path(paths[0], x_all, compute_forward)
        if mode == "fwd":
            saved = pltpu.make_async_copy(x_all, x_o, xsem)
            saved.start()
    if backward:
        run_path(paths[-1], g_all, compute_backward)
        count = groups * 2 * rows_a

        def products(n, q):
            if n == 0:
                return tn(x_all[...].reshape(count, model), ig_all[q].reshape(count, model))
            return tn(hid_all[q].reshape(count, model), g_all[...].reshape(count, model))

        outs = (gw_in_o, gw_out_o)
        copies = []
        for n in range(2):
            stage[n] = products(n, 1 - core)
            copy = remote(stage.at[n], outs[n].at[core], gsem.at[n], grsem.at[n], mp=mate)
            copy.start()
            copies.append(copy)
        for n in range(2):
            copies[n].wait_send()
            stage[n] = products(n, core)
            copy = pltpu.make_async_copy(stage.at[n], outs[n].at[core], glsem.at[n])
            copy.start()
            copies.append(copy)
        for n in range(2):
            copies[n].wait_recv()
            copies[2 + n].wait()
    if forward:
        finish_path(paths[0], out_o)
        if mode == "fwd":
            saved.wait()
    if backward:
        finish_path(paths[-1], grad_o)


def expert_call(mode, layer, number, dp_count, sends, x_in, w_in, w_out):
    forward, backward = mode in ("fwd", "both"), mode in ("both", "bwd")
    shape = sends[0].shape
    experts, tile, wide = shape
    model = w_in.shape[2]
    groups = dp_count // 2
    rows = 2 * 4 * 56
    dma = pltpu.SemaphoreType.DMA
    args = list(sends)
    specs = [VMEM] * len(sends)
    if mode == "bwd":
        args.append(x_in)
        specs.append(ANY)
    args += [w_in, w_out]
    specs += [ANY, ANY]
    outs, out_specs = [], []

    def out(dims, kind, spec):
        outs.append(jax.ShapeDtypeStruct(dims, kind))
        out_specs.append(spec)

    if forward:
        out(shape, BF, VMEM)
    if mode == "fwd":
        out((groups, rows, model), BF, ANY)
    if backward:
        out(shape, BF, VMEM)
        out((2, model, model), F32, ANY)
        out((2, model, model), F32, ANY)
    scratch = [
        pltpu.VMEM((2, model, model), BF),
        pltpu.VMEM((2, model, model), BF),
        dma((2,)),
        dma((2,)),
        dma((2,)),
        pltpu.VMEM((2, rows // 2, model), F32),
        pltpu.VMEM((groups, rows, model), BF),
        dma,
    ]
    for _ in sends:
        scratch += [
            pltpu.VMEM(shape, BF),
            pltpu.VMEM(shape, BF),
            dma((experts,)),
            dma((experts,)),
            dma((dp_count,)),
            dma((dp_count,)),
            pltpu.VMEM((groups, rows // 2, model), BF),
            dma((groups,)),
            dma((groups,)),
            pltpu.VMEM(shape, BF),
            pltpu.VMEM(shape, BF),
            dma((experts,)),
            dma((experts,)),
            pltpu.VMEM((groups, rows // 2, model), BF),
        ]
    if backward:
        scratch += [
            pltpu.VMEM((groups, rows, model), BF),
            pltpu.VMEM((2, groups, rows, model), BF),
            pltpu.VMEM((2, groups, rows, model), BF),
            pltpu.VMEM((2, model, model), F32),
            dma((2,)),
            dma((2,)),
            dma((2,)),
        ]
    return pl.pallas_call(
        functools.partial(expert_kernel, mode, layer, dp_count),
        out_shape=tuple(outs),
        in_specs=specs,
        out_specs=tuple(out_specs),
        scratch_shapes=scratch,
        compiler_params=pltpu.CompilerParams(
            collective_id=number, has_side_effects=True, vmem_limit_bytes=VMEM_BYTES
        ),
    )(*args)


def reduce_kernel(layers, dp_count, *refs):
    grads = refs[:layers]
    small, all_o, small_o, part, come, small_come, small_mp, small_all, ssem, rsem, tsem, usem, vsem, zsem, csem, dsem, esem, fsem, hsem, isem = refs[layers:]
    d = lax.axis_index("dp")
    me, core, mate, across, diagonal = mp_places()
    rows = come.shape[2]
    barrier = pltpu.get_barrier_semaphore()

    def peer(k):
        return lax.rem(d + k, dp_count)

    for k in range(1, dp_count):
        signal_to(barrier, dp=peer(k), mp=me)
    for to in (mate, across, diagonal):
        signal_to(barrier, mp=to)
    for j in range(dp_count):
        for n in range(layers):
            part[j, n] = grads[n][j * rows : (j + 1) * rows, :].astype(BF)
    pl.semaphore_wait(barrier, dp_count + 2)

    def small_copy(k):
        to = peer(k)
        return remote(small.at[to], small_come.at[d], tsem.at[k], usem.at[k], dp=to, mp=me)

    def big_copy(k):
        to = peer(k)
        return remote(part.at[to], come.at[d], ssem.at[k], rsem.at[k], dp=to, mp=me)

    for k in range(1, dp_count):
        small_copy(k).start()
    for k in range(1, dp_count):
        big_copy(k).start()
    total = small[d]
    for k in range(1, dp_count):
        small_copy(k).wait_recv()
        total = total + small_come[lax.rem(d + dp_count - k, dp_count)]
    small_mp[me] = total
    swaps = [remote(small_mp.at[me], small_mp.at[me], csem.at[n], dsem.at[n], mp=to) for n, to in enumerate((mate, across, diagonal))]
    for copy in swaps:
        copy.start()
    sums = [part[d, n].astype(F32) for n in range(layers)]
    for copy in swaps:
        copy.wait_recv()
    small_all[d] = small_mp[0] + small_mp[1] + small_mp[2] + small_mp[3]

    def small_share(k):
        return remote(small_all.at[d], small_all.at[d], vsem.at[k], zsem.at[k], dp=peer(k), mp=me)

    for k in range(1, dp_count):
        small_share(k).start()
    for k in range(1, dp_count):
        big_copy(k).wait_recv()
        src = lax.rem(d + dp_count - k, dp_count)
        for n in range(layers):
            sums[n] = sums[n] + come[src, n].astype(F32)
    for n in range(layers):
        all_o[me, d, n] = sums[n].astype(BF)

    def share(k):
        return remote(all_o.at[me, d], all_o.at[me, d], esem.at[k], fsem.at[k], dp=peer(k), mp=me)

    def over(n, j):
        whose = across if n == 2 else me
        return remote(all_o.at[whose, j], all_o.at[whose, j], hsem.at[n, j], isem.at[n, j], mp=across if n == 1 else mate)

    for k in range(1, dp_count):
        share(k).start()
    for k in range(dp_count):
        j = lax.rem(d + dp_count - k, dp_count)
        if k > 0:
            share(k).wait_recv()
        over(1, j).start()
        over(0, j).start()
        if k > 0:
            last = lax.rem(d + dp_count - k + 1, dp_count)
            over(1, last).wait_recv()
            over(2, last).start()
    last = lax.rem(d + 1, dp_count)
    over(1, last).wait_recv()
    over(2, last).start()
    for k in range(1, dp_count):
        small_share(k).wait_recv()
    small_o[...] = small_all[...]
    for j in range(dp_count):
        over(0, j).wait_recv()
        over(2, j).wait_recv()
        for n in range(3):
            over(n, j).wait_send()
    for copy in swaps:
        copy.wait_send()
    for k in range(1, dp_count):
        small_copy(k).wait_send()
        big_copy(k).wait_send()
        small_share(k).wait_send()
        share(k).wait_send()


def reduce_call(number, dp_count, grads, small):
    model, width = grads[0].shape
    layers = len(grads)
    rows = model // dp_count
    dma = pltpu.SemaphoreType.DMA
    return pl.pallas_call(
        functools.partial(reduce_kernel, layers, dp_count),
        out_shape=(
            jax.ShapeDtypeStruct((4, dp_count, layers, rows, width), BF),
            jax.ShapeDtypeStruct(small.shape, F32),
        ),
        in_specs=[VMEM] * (layers + 1),
        out_specs=(VMEM, VMEM),
        scratch_shapes=[
            pltpu.VMEM((dp_count, layers, rows, width), BF),
            pltpu.VMEM((dp_count, layers, rows, width), BF),
            pltpu.VMEM(small.shape, F32),
            pltpu.VMEM((4,) + small.shape[1:], F32),
            pltpu.VMEM(small.shape, F32),
        ]
        + [dma((dp_count,))] * 6
        + [dma((3,))] * 2
        + [dma((dp_count,))] * 2
        + [dma((3, dp_count))] * 2,
        compiler_params=pltpu.CompilerParams(
            collective_id=number, has_side_effects=True, vmem_limit_bytes=VMEM_BYTES
        ),
    )(*grads, small)


def spread_kernel(own, parts, qkv_o, attn_o):
    for n in range(parts.shape[2]):
        pieces = [parts[m, 0, n].astype(F32) for m in range(parts.shape[0])]
        qkv_o[n] = jnp.concatenate([p[:, t * own : (t + 1) * own] for t in range(3) for p in pieces], 1)
        attn_o[n, 0] = jnp.concatenate([p[:, 3 * own :] for p in pieces], 1)


def spread_call(parts, own):
    count, blocks, layers, rows, width = parts.shape
    return pl.pallas_call(
        functools.partial(spread_kernel, own),
        grid=(blocks,),
        out_shape=(
            jax.ShapeDtypeStruct((layers, blocks * rows, 3 * count * own), F32),
            jax.ShapeDtypeStruct((layers, blocks, rows, count * own), F32),
        ),
        in_specs=[pl.BlockSpec((count, 1, layers, rows, width), lambda i: (0, i, 0, 0, 0))],
        out_specs=(
            pl.BlockSpec((layers, rows, 3 * count * own), lambda i: (0, i, 0)),
            pl.BlockSpec((layers, 1, rows, count * own), lambda i: (0, i, 0, 0)),
        ),
        compiler_params=pltpu.CompilerParams(vmem_limit_bytes=VMEM_BYTES),
    )(parts)


def fast_body(
    tokens, cotangent, w_qkv, w_attn, attn_gain, rel_bias, ffn_gain, router, w_in, w_out, cont_lengths, routes, slots, drops
):
    _, local, model = tokens.shape
    heads, buckets = rel_bias.shape[1:]
    size = model // heads
    layers = w_qkv.shape[0]
    dp_count, mp_count = lax.axis_size("dp"), lax.axis_size("mp")
    seq = local * mp_count
    own_heads = heads // mp_count
    own = own_heads * size
    experts = dp_count * 2
    me = lax.axis_index("mp")
    half = model // 2
    block = (experts, 16, 7 * half)
    pairs = jnp.concatenate(
        [routes.reshape(layers, local, 2), slots.reshape(layers, local, 2), 1 - drops.reshape(layers, local, 2)], 2
    )
    cols = jnp.pad(pairs, ((0, 0), (0, 0), (0, 2)))
    rows = cols.transpose(0, 2, 1)
    vecs = bias_vectors(lax.dynamic_slice_in_dim(rel_bias, me * own_heads, own_heads, 1))
    weights = w_qkv.reshape(layers, model, 3, mp_count, own).transpose(0, 3, 1, 2, 4)
    weights = weights.reshape(layers, mp_count, model, 3 * own)
    mine = lax.dynamic_index_in_dim(weights, me, 1, keepdims=False)
    mine_attn = lax.dynamic_slice_in_dim(w_attn, me * own, own, 1)
    held = (mp_count, local, model)

    kept = [None] * layers
    stream = tokens[0]
    sends, back, x_rows = None, None, None
    for l in range(layers):
        gain = attn_gain[l][None]
        if l == 0:
            (normed,) = mp_call(first_kernel, 0, [(held, BF)], held, False, stream, gain)
        else:
            before = kept[l - 1]
            stream, normed = mp_call(
                next_kernel, 1, [((local, model), F32), (held, BF)], held, False,
                before["middle"], before["out"], cols[l - 1], before["gates"], gain,
            )
        normed = normed.reshape(seq, model)
        qkv, mixed, lse = attn_fwd(cont_lengths, normed, mine[l], vecs[l], own_heads, size)
        last = l == layers - 1
        outs = [((local, model), F32), ((local, model), BF), ((local, 2), F32), (block, BF)] + ([(block, BF)] if last else [])
        args = [mixed.reshape(mp_count, local, own), stream, w_attn[l], ffn_gain[l][None], router[l], rows[l], cols[l]]
        got = mp_call(
            functools.partial(middle_kernel, last), 2 + last, outs, (mp_count, local, own), True,
            *args, *([cotangent[0]] if last else []),
        )
        middle, ffn, gates = got[:3]
        kept[l] = dict(stream=stream, normed=normed, qkv=qkv, mixed=mixed, lse=lse, middle=middle, ffn=ffn, gates=gates)
        if last:
            out, back, gw_in, gw_out = expert_call("both", l, 5, dp_count, got[3:5], None, w_in, w_out)
            kept[l].update(gw_in=gw_in, gw_out=gw_out)
        else:
            out, x_rows = expert_call("fwd", l, 4, dp_count, got[3:4], None, w_in, w_out)
            kept[l].update(x_rows=x_rows)
        kept[l].update(out=out)

    flow = cotangent[0]
    for l in reversed(range(layers)):
        k = kept[l]
        last = l == layers - 1
        outs = [((local, model), F32), (held, BF), ((1, model), F32), ((experts, model), F32)]
        got = mp_call(
            functools.partial(post_kernel, last), 6 + last, outs + ([((local, model), BF)] if last else []), held, False,
            back, k["out"], flow, k["middle"], k["ffn"], k["gates"], cols[l], router[l], ffn_gain[l][None],
        )
        grad, branch, k["ffn_gain"], k["router"] = got[:4]
        if last:
            output = got[4]
        dqkv, k["heads"], dvecs = attn_bwd(
            cont_lengths, k["qkv"], k["normed"], branch.reshape(seq, model), mine_attn[l], k["mixed"], k["lse"], vecs[l],
            own_heads, size,
        )
        k["bias"] = bias_grads(dvecs, buckets)
        outs = [((local, model), F32), ((1, model), F32)]
        args = [dqkv.reshape(mp_count, local, 3 * own), weights[l], k["stream"], attn_gain[l][None], grad]
        if l > 0:
            outs.append((block, BF))
            args += [rows[l - 1], cols[l - 1], kept[l - 1]["gates"]]
        got = mp_call(functools.partial(close_kernel, l > 0), 8 + (l > 0), outs, (mp_count, local, 3 * own), True, *args)
        flow, k["attn_gain"] = got[:2]
        if l > 0:
            b = kept[l - 1]
            back, b["gw_in"], b["gw_out"] = expert_call("bwd", l - 1, 10, dp_count, [got[2]], b["x_rows"], w_in, w_out)

    small = []
    for l in range(layers):
        k = kept[l]
        bias = lax.dynamic_update_slice_in_dim(jnp.zeros((heads, buckets), F32), k["bias"], me * own_heads, 0)
        small += [k["attn_gain"], k["ffn_gain"], jnp.pad(bias.reshape(1, -1), ((0, 5), (0, model - heads * buckets)))]
        small += [k["router"]]
    lines = 8 + experts
    total_lines = -(-layers * lines // (8 * dp_count)) * 8
    small = jnp.pad(jnp.concatenate(small, 0), ((0, total_lines * dp_count - layers * lines), (0, 0)))
    parts, small = reduce_call(11, dp_count, [kept[l]["heads"] for l in range(layers)], small.reshape(dp_count, total_lines, model))
    small = small.reshape(-1, model)[: layers * lines].reshape(layers, lines, model)
    grad_qkv, grad_attn = spread_call(parts, own)
    grad_attn = grad_attn.reshape(layers, model, model).transpose(0, 2, 1)
    return (
        output[None],
        flow[None],
        grad_qkv,
        grad_attn,
        small[:, 0],
        small[:, 2, : heads * buckets].reshape(layers, heads, buckets),
        small[:, 1],
        small[:, 8:].transpose(0, 2, 1),
        jnp.stack([k["gw_in"] for k in kept]),
        jnp.stack([k["gw_out"] for k in kept]),
    )


def chosen_body(
    tokens, cotangent, w_qkv, w_attn, attn_gain, rel_bias, ffn_gain, router, w_in, w_out, cont_lengths, routes, slots, drops
):
    groups, local, model = tokens.shape
    heads = rel_bias.shape[1]
    dp_count, mp_count = lax.axis_size("dp"), lax.axis_size("mp")
    capacity = max(2, 9 * 2 * groups * local // (8 * w_in.shape[1] * dp_count))
    seq = local * mp_count
    fits = (
        groups == 1
        and mp_count == 4
        and dp_count % 8 == 0
        and heads % mp_count == 0
        and model // heads == 64
        and model % 256 == 0
        and local % 128 == 0
        and w_in.shape[1:] == (2, model, model)
        and w_out.shape[1:] == (2, model, model)
        and 48 < capacity <= 56
        and seq > PROMPT
        and (seq - PROMPT) % QB == 0
    )
    plan = fast_body if fits else body
    return plan(
        tokens, cotangent, w_qkv, w_attn, attn_gain, rel_bias, ffn_gain, router, w_in, w_out, cont_lengths, routes, slots, drops
    )


def solution(mesh):
    return jax.shard_map(
        chosen_body,
        mesh=mesh,
        in_specs=(
            P("dp", "mp", None),
            P("dp", "mp", None),
            P(),
            P(),
            P(),
            P(),
            P(),
            P(),
            P(None, "dp", None, "mp"),
            P(None, "dp", "mp", None),
            P("dp", None),
            P(None, "dp", "mp", None),
            P(None, "dp", "mp", None),
            P(None, "dp", "mp", None),
        ),
        out_specs=(
            P("dp", "mp", None),
            P("dp", "mp", None),
            P(),
            P(),
            P(),
            P(),
            P(),
            P(),
            P(None, "dp", None, "mp"),
            P(None, "dp", "mp", None),
        ),
        check_vma=False,
    )
```

```python
import functools

import jax
import jax.numpy as jnp
from jax import lax
from jax.experimental import pallas as pl
from jax.experimental.pallas import tpu as pltpu
from jax.sharding import PartitionSpec as P

PROMPT = 1024


EPSILON = 1e-06
SQRT_TWO_PI = 0.7978845608028654
THRESHOLDS = (16, 20, 24, 32, 40, 48, 64, 80, 96, 128, 160, 192, 256, 384, 512, 768)
HIGHEST = lax.Precision.HIGHEST


def rms_scale(values, gain_row):
    return (
        values * lax.rsqrt(jnp.mean(values * values, axis=-1, keepdims=True) + EPSILON) * gain_row
    )


def gelu_tanh(values):
    return (
        0.5
        * values
        * (1.0 + jnp.tanh(SQRT_TWO_PI * (values + 0.044715 * values * values * values)))
    )


def bucket_of(distance):
    counted = jnp.minimum(distance, 15)
    for threshold in THRESHOLDS:
        counted = counted + (distance >= threshold).astype(jnp.int32)
    return counted


def geometry(lengths, row_ids):
    starts = PROMPT + jnp.cumsum(lengths, axis=-1) - lengths
    inside = row_ids[None, :, None] >= starts[:, None, :]
    segment = jnp.sum(inside.astype(jnp.int32), axis=-1) - 1
    begin_at = jnp.max(jnp.where(inside, starts[:, None, :], 0), axis=-1)
    position = jnp.where(
        row_ids[None, :] < PROMPT, row_ids[None, :], PROMPT + row_ids[None, :] - begin_at
    )
    return (position, segment)


def visibility(query_pos, query_seg, key_pos, key_seg):
    query_at = query_pos[:, :, None]
    query_in = query_seg[:, :, None]
    key_at = key_pos[:, None, :]
    key_in = key_seg[:, None, :]
    earlier = key_at <= query_at
    allowed = (key_in < 0) & ((query_in >= 0) | earlier) | (key_in >= 0) & (
        key_in == query_in
    ) & earlier
    bucket = bucket_of(jnp.maximum(query_at - key_at, 0))
    return (allowed, bucket)


def bias_table(bias_row, bucket):
    full_bias = jnp.zeros((bias_row.shape[0],) + bucket.shape, jnp.float32)
    for number in range(bias_row.shape[1]):
        full_bias = full_bias + jnp.where(
            bucket[None] == number, bias_row[:, number][:, None, None, None], 0.0
        )
    return full_bias


def score_block(query_b, key_every, full_bias, allowed, factor):
    raw = (
        jnp.einsum("grhd,gkhd->hgrk", query_b, key_every, preferred_element_type=jnp.float32)
        * factor
    )
    raw = raw + full_bias
    return jnp.where(allowed[None], raw, -1e30)


def body(
    tokens,
    cotangent,
    w_qkv,
    w_attn,
    attn_gain,
    rel_bias,
    ffn_gain,
    router,
    w_in,
    w_out,
    cont_lengths,
    routes,
    slots,
    drops,
):
    groups, local_rows, model_width = tokens.shape
    head_count = rel_bias.shape[1]
    bucket_count = rel_bias.shape[2]
    head_size = model_width // head_count
    factor = head_size ** (-0.5)
    layer_count = w_qkv.shape[0]
    dp_count = lax.axis_size("dp")
    mp_count = lax.axis_size("mp")
    seq_len = local_rows * mp_count
    local_experts = w_in.shape[1]
    expert_total = local_experts * dp_count
    tok_count = groups * local_rows
    capacity = max(2, 9 * 2 * tok_count // (8 * expert_total))
    slot_total = expert_total * capacity
    rows_here = lax.axis_index("mp") * local_rows + jnp.arange(local_rows, dtype=jnp.int32)
    rows_every = jnp.arange(seq_len, dtype=jnp.int32)
    query_pos, query_seg = geometry(cont_lengths, rows_here)
    key_pos, key_seg = geometry(cont_lengths, rows_every)
    allowed, bucket = visibility(query_pos, query_seg, key_pos, key_seg)
    route_all = routes.reshape(layer_count, tok_count, 2)
    slot_all = slots.reshape(layer_count, tok_count, 2)
    keep_all = (1 - drops.reshape(layer_count, tok_count, 2)).astype(jnp.float32)
    head_shape = (groups, seq_len, head_count, head_size)
    stream = tokens.reshape(tok_count, model_width).astype(jnp.float32)
    stored = []
    for layer_now in range(layer_count):
        normed_b = rms_scale(stream, attn_gain[layer_now]).astype(jnp.bfloat16)
        qkv_all = jnp.dot(normed_b, w_qkv[layer_now], preferred_element_type=jnp.float32).astype(
            jnp.bfloat16
        )
        query_b = qkv_all[:, :model_width].reshape(groups, local_rows, head_count, head_size)
        key_own = qkv_all[:, model_width : 2 * model_width].reshape(groups, local_rows, model_width)
        value_own = qkv_all[:, 2 * model_width :].reshape(groups, local_rows, model_width)
        key_every, value_every = (
            lax.all_gather(key_own, "mp", axis=1, tiled=True),
            lax.all_gather(value_own, "mp", axis=1, tiled=True),
        )
        key_every = key_every.reshape(head_shape)
        value_every = value_every.reshape(head_shape)
        full_bias = bias_table(rel_bias[layer_now], bucket)
        scores = score_block(query_b, key_every, full_bias, allowed, factor)
        top_score = jnp.max(scores, axis=-1, keepdims=True)
        weights = jnp.exp(scores - top_score)
        weight_sum = jnp.sum(weights, axis=-1, keepdims=True)
        log_total = top_score + jnp.log(weight_sum)
        probs_b = (weights / weight_sum).astype(jnp.bfloat16)
        mixed_b = jnp.einsum(
            "hgrk,gkhd->grhd", probs_b, value_every, preferred_element_type=jnp.float32
        )
        mixed_b = mixed_b.reshape(tok_count, model_width).astype(jnp.bfloat16)
        middle = stream + jnp.dot(mixed_b, w_attn[layer_now], preferred_element_type=jnp.float32)
        kept_keys = (key_every, value_every)
        ffn_b = rms_scale(middle, ffn_gain[layer_now]).astype(jnp.bfloat16)
        logits = jnp.dot(ffn_b, router[layer_now], preferred_element_type=jnp.float32)
        chosen = route_all[layer_now]
        keep_pair = keep_all[layer_now]
        gate_pair = jax.nn.softmax(jnp.take_along_axis(logits, chosen, axis=1), axis=-1)
        target = chosen * capacity + slot_all[layer_now]
        sending = jnp.where(
            keep_pair[:, :, None] > 0, ffn_b[:, None, :], jnp.zeros((), jnp.bfloat16)
        )
        send_rows = (
            jnp.zeros((slot_total, model_width), jnp.bfloat16)
            .at[target.reshape(-1)]
            .add(sending.reshape(-1, model_width))
        )
        arrived = lax.all_to_all(
            send_rows.reshape(dp_count, local_experts, capacity, model_width),
            "dp",
            split_axis=0,
            concat_axis=0,
            tiled=True,
        )
        rows_in = lax.all_gather(arrived, "mp", axis=0, tiled=True)
        up_block = w_in[layer_now]
        down_block = w_out[layer_now]
        inner_act = jnp.einsum(
            "secd,edf->secf", rows_in, up_block, preferred_element_type=jnp.float32
        )
        hidden_b = gelu_tanh(inner_act).astype(jnp.bfloat16)
        summed = lax.psum_scatter(
            jnp.einsum(
                "secf,efd->secd", hidden_b, down_block, preferred_element_type=jnp.float32
            ).astype(jnp.bfloat16),
            "mp",
            scatter_dimension=0,
            tiled=True,
        )
        kept_rows = (rows_in, inner_act, hidden_b)
        returned = lax.all_to_all(summed, "dp", split_axis=0, concat_axis=0, tiled=True).reshape(
            slot_total, model_width
        )
        pair_out = returned[target].astype(jnp.float32)
        stored.append(
            (
                stream,
                normed_b,
                query_b,
                key_own,
                value_own,
                kept_keys,
                log_total,
                mixed_b,
                middle,
                ffn_b,
                chosen,
                keep_pair,
                gate_pair,
                target,
                pair_out,
                kept_rows,
                full_bias,
            )
        )
        stream = middle + jnp.sum((gate_pair * keep_pair)[:, :, None] * pair_out, axis=1)
    output = stream.astype(jnp.bfloat16).reshape(groups, local_rows, model_width)
    one_hot = (
        bucket[None] == jnp.arange(bucket_count, dtype=jnp.int32)[:, None, None, None]
    ).astype(jnp.bfloat16)
    expert_ids = jnp.arange(expert_total, dtype=jnp.int32)
    qkv_grads = [None] * layer_count
    attn_grads = [None] * layer_count
    attn_gain_grads = [None] * layer_count
    bias_grads = [None] * layer_count
    ffn_gain_grads = [None] * layer_count
    router_grads = [None] * layer_count
    up_grads = [None] * layer_count
    down_grads = [None] * layer_count
    flowing = cotangent.reshape(tok_count, model_width).astype(jnp.float32)
    for layer_now in reversed(range(layer_count)):
        (
            stream_in,
            normed_b,
            query_b,
            key_own,
            value_own,
            kept_keys,
            log_total,
            mixed_b,
            middle,
            ffn_b,
            chosen,
            keep_pair,
            gate_pair,
            target,
            pair_out,
            kept_rows,
            full_bias,
        ) = stored[layer_now]
        weighted = gate_pair * keep_pair
        pair_grad = weighted[:, :, None] * flowing[:, None, :]
        gate_grad = keep_pair * jnp.sum(flowing[:, None, :] * pair_out, axis=-1)
        picked_grad = gate_pair * (
            gate_grad - jnp.sum(gate_pair * gate_grad, axis=-1, keepdims=True)
        )
        logit_grad = jnp.sum(
            picked_grad[:, :, None] * (chosen[:, :, None] == expert_ids).astype(jnp.float32), axis=1
        )
        back_rows = (
            jnp.zeros((slot_total, model_width), jnp.float32)
            .at[target.reshape(-1)]
            .add(pair_grad.reshape(-1, model_width))
        )
        back_rows = back_rows.astype(jnp.bfloat16).reshape(
            dp_count, local_experts, capacity, model_width
        )
        grad_arrived = lax.all_to_all(back_rows, "dp", split_axis=0, concat_axis=0, tiled=True)
        grad_rows = lax.all_gather(grad_arrived, "mp", axis=0, tiled=True)
        up_block = w_in[layer_now]
        down_block = w_out[layer_now]
        rows_in, inner_act, hidden_b = kept_rows
        down_grad = jnp.einsum(
            "secf,secd->efd", hidden_b, grad_rows, preferred_element_type=jnp.float32
        )
        hidden_grad = jnp.einsum(
            "secd,efd->secf", grad_rows, down_block, preferred_element_type=jnp.float32
        )
        inner_grad = jax.vjp(gelu_tanh, inner_act)[1](hidden_grad)[0].astype(jnp.bfloat16)
        up_grad = jnp.einsum(
            "secd,secf->edf", rows_in, inner_grad, preferred_element_type=jnp.float32
        )
        rows_grad = lax.psum_scatter(
            jnp.einsum(
                "secf,edf->secd", inner_grad, up_block, preferred_element_type=jnp.float32
            ).astype(jnp.bfloat16),
            "mp",
            scatter_dimension=0,
            tiled=True,
        )
        up_grads[layer_now] = up_grad
        down_grads[layer_now] = down_grad
        grad_back = lax.all_to_all(
            rows_grad, "dp", split_axis=0, concat_axis=0, tiled=True
        ).reshape(slot_total, model_width)
        ffn_grad = jnp.sum(keep_pair[:, :, None] * grad_back[target].astype(jnp.float32), axis=1)
        ffn_grad = ffn_grad + jnp.einsum(
            "te,de->td", logit_grad, router[layer_now].astype(jnp.float32), precision=HIGHEST
        )
        router_grads[layer_now] = jnp.einsum(
            "td,te->de", ffn_b.astype(jnp.float32), logit_grad, precision=HIGHEST
        )
        middle_grad, ffn_gain_grads[layer_now] = jax.vjp(rms_scale, middle, ffn_gain[layer_now])[1](
            ffn_grad
        )
        middle_grad = middle_grad + flowing
        branch_grad = middle_grad.astype(jnp.bfloat16)
        attn_grads[layer_now] = jnp.einsum(
            "td,te->de", mixed_b, branch_grad, preferred_element_type=jnp.float32
        )
        mixed_grad = jnp.einsum(
            "te,de->td", branch_grad, w_attn[layer_now], preferred_element_type=jnp.float32
        )
        mixed_grad = mixed_grad.astype(jnp.bfloat16).reshape(
            groups, local_rows, head_count, head_size
        )
        key_every, value_every = kept_keys
        scores = score_block(query_b, key_every, full_bias, allowed, factor)
        probs = jnp.exp(scores - log_total)
        prob_grad = jnp.einsum(
            "grhd,gkhd->hgrk", mixed_grad, value_every, preferred_element_type=jnp.float32
        )
        score_grad = (
            probs * (prob_grad - jnp.sum(probs * prob_grad, axis=-1, keepdims=True))
        ).astype(jnp.bfloat16)
        query_grad = (
            jnp.einsum("hgrk,gkhd->grhd", score_grad, key_every, preferred_element_type=jnp.float32)
            * factor
        )
        key_part = (
            jnp.einsum("hgrk,grhd->gkhd", score_grad, query_b, preferred_element_type=jnp.float32)
            * factor
        )
        value_part = jnp.einsum(
            "hgrk,grhd->gkhd",
            probs.astype(jnp.bfloat16),
            mixed_grad,
            preferred_element_type=jnp.float32,
        )
        key_grad, value_grad = (
            lax.psum_scatter(
                key_part.reshape(groups, seq_len, model_width).astype(jnp.bfloat16),
                "mp",
                scatter_dimension=1,
                tiled=True,
            ).astype(jnp.float32),
            lax.psum_scatter(
                value_part.reshape(groups, seq_len, model_width).astype(jnp.bfloat16),
                "mp",
                scatter_dimension=1,
                tiled=True,
            ).astype(jnp.float32),
        )
        bias_grads[layer_now] = jnp.einsum(
            "hgrk,bgrk->hb", score_grad, one_hot, preferred_element_type=jnp.float32
        )
        qkv_grad = jnp.concatenate(
            [
                query_grad.reshape(tok_count, model_width),
                key_grad.reshape(tok_count, model_width),
                value_grad.reshape(tok_count, model_width),
            ],
            axis=1,
        ).astype(jnp.bfloat16)
        qkv_grads[layer_now] = jnp.einsum(
            "td,te->de", normed_b, qkv_grad, preferred_element_type=jnp.float32
        )
        normed_grad = jnp.einsum(
            "te,de->td", qkv_grad, w_qkv[layer_now], preferred_element_type=jnp.float32
        )
        stream_grad, attn_gain_grads[layer_now] = jax.vjp(
            rms_scale, stream_in, attn_gain[layer_now]
        )[1](normed_grad)
        flowing = middle_grad + stream_grad
    totals = lax.psum(
        (
            jnp.stack(qkv_grads),
            jnp.stack(attn_grads),
            jnp.stack(attn_gain_grads),
            jnp.stack(bias_grads),
            jnp.stack(ffn_gain_grads),
            jnp.stack(router_grads),
        ),
        ("dp", "mp"),
    )
    input_grad = flowing.reshape(groups, local_rows, model_width)
    return (
        output,
        input_grad,
        totals[0],
        totals[1],
        totals[2],
        totals[3],
        totals[4],
        totals[5],
        jnp.stack(up_grads),
        jnp.stack(down_grads),
    )


BF = jnp.bfloat16
F32 = jnp.float32
VMEM = pl.BlockSpec(memory_space=pltpu.VMEM)
SMEM = pl.BlockSpec(memory_space=pltpu.SMEM)
ANY = pl.BlockSpec(memory_space=pl.ANY)
VMEM_BYTES = 60 << 20
MESH = pl.DeviceIdType.MESH
LANES = 128
QB = 256


def nn(a, b):
    return lax.dot_general(a, b, (((1,), (0,)), ((), ())), preferred_element_type=F32)


def nt(a, b):
    return lax.dot_general(a, b, (((1,), (1,)), ((), ())), preferred_element_type=F32)


def tn(a, b):
    return lax.dot_general(a, b, (((0,), (0,)), ((), ())), preferred_element_type=F32)


def layer_spec(array, layer):
    zeros = (0,) * (array.ndim - 1)
    return pl.BlockSpec((None,) + array.shape[1:], lambda i: (layer,) + zeros)


def segments(lens, shape, dim):
    at = lax.broadcasted_iota(jnp.int32, shape, dim)
    segment = jnp.full(shape, -1, jnp.int32)
    begin = jnp.zeros(shape, jnp.int32)
    start = jnp.int32(0)
    for number in range(lens.shape[1]):
        inside = at >= start
        segment = segment + inside.astype(jnp.int32)
        begin = jnp.where(inside, start, begin)
        start = start + lens[0, number]
    return segment, at - begin


def bias_stage(vec, lens, table, cont_bias):
    width = vec.shape[1]
    rows = lax.broadcasted_iota(jnp.int32, (LANES, width), 0)
    skewed = jnp.broadcast_to(vec, (LANES, width))
    for bit in range(7):
        skewed = jnp.where((rows >> bit) % 2 == 1, pltpu.roll(skewed, 1 << bit, 1), skewed)
    table[...] = skewed[:, : width - LANES].T
    cont = cont_bias.shape[1]
    _, offset = segments(lens, (LANES, cont), 1)
    place = (lax.broadcasted_iota(jnp.int32, (LANES, cont), 0) == offset).astype(BF)
    full = table[0:PROMPT, :]
    high = full.astype(BF)
    low = (full - high.astype(F32)).astype(BF)
    cont_bias[...] = nn(jnp.concatenate([high, low], 1), jnp.concatenate([place, place], 0))


def blocks_of(seq):
    out = []
    for start in range(0, PROMPT, QB):
        out.append((start, start + QB, None))
    for start in range(0, seq - PROMPT, QB):
        out.append((PROMPT + start, PROMPT, max(0, start - LANES)))
    return out


def scores_of(keys, query, table, cont_bias, seg_col, seg_row, block, h):
    q0, prompt_keys, cont_from = block
    if cont_from is None:
        left = PROMPT - q0
        bias = jnp.concatenate(
            [table[left : left + prompt_keys, :], table[left - LANES : left - LANES + prompt_keys, :]], 1
        )
        return [(0, prompt_keys, nt(keys[h, 0:prompt_keys, :], query) + bias)]
    at = q0 - PROMPT
    first = nt(keys[h, 0:PROMPT, :], query) + cont_bias[:, at : at + QB]
    k0, k1 = PROMPT + cont_from, q0 + QB
    left = PROMPT + cont_from - at
    bias = jnp.concatenate(
        [table[left : left + k1 - k0, :], table[left - LANES : left - LANES + k1 - k0, :]], 1
    )
    same = seg_col[cont_from : at + QB, :][:, 0:1] == seg_row[:, at : at + QB]
    second = jnp.where(same, nt(keys[h, k0:k1, :], query) + bias, -1e30)
    return [(0, PROMPT, first), (k0, k1, second)]


def attn_fwd_kernel(heads, size, lens, normed, w_qkv, vecs, qkv_o, mixed_o, lse_o, weight, q_s, k_s, vt_s, table, cont_bias, mixt, segc):
    seq, model = normed.shape
    own = heads * size
    me = lax.axis_index("mp")
    for m in range(model // own):

        @pl.when(me == m)
        def _():
            for t in range(3):
                weight[:, t * own : (t + 1) * own] = w_qkv[:, t * model + m * own : t * model + (m + 1) * own]

    for i in range(seq // QB):
        rows = pl.ds(i * QB, QB)
        part = nn(normed[rows, :], weight[...]).astype(BF)
        qkv_o[rows, :] = part
        for h in range(heads):
            q_s[h, rows, :] = part[:, h * size : (h + 1) * size] * BF(0.125)
            k_s[h, rows, :] = part[:, own + h * size : own + (h + 1) * size]
            vt_s[h, :, rows] = part[:, 2 * own + h * size : 2 * own + (h + 1) * size].astype(F32).T.astype(BF)
    seg_row, _ = segments(lens, (1, seq - PROMPT), 1)
    segc[...] = segments(lens, (seq - PROMPT, LANES), 0)[0]

    def head(h, carry):
        bias_stage(vecs[pl.ds(h, 1), :], lens, table, cont_bias)
        for block in blocks_of(seq):
            q0 = block[0]
            parts = scores_of(k_s, q_s[h, q0 : q0 + QB, :], table, cont_bias, segc, seg_row, block, h)
            top = functools.reduce(jnp.maximum, [jnp.max(s, axis=0, keepdims=True) for _, _, s in parts])
            total, mixed = 0.0, 0.0
            for k0, k1, s in parts:
                p = jnp.exp(s - top)
                total = total + jnp.sum(p, axis=0, keepdims=True)
                mixed = mixed + nn(vt_s[h, :, k0:k1], p.astype(BF))
            mixt[pl.ds(pl.multiple_of(h * size, size), size), q0 : q0 + QB] = mixed / total
            lse_o[pl.ds(h, 1), q0 : q0 + QB] = top + jnp.log(total)
        return carry

    lax.fori_loop(0, heads, head, 0)
    for i in range(seq // QB):
        mixed_o[i * QB : (i + 1) * QB, :] = mixt[:, i * QB : (i + 1) * QB].T.astype(BF)


def attn_fwd(lens, normed, w_qkv, layer, vecs, heads, size):
    seq, model = normed.shape
    own = heads * size
    width = vecs.shape[1]
    return pl.pallas_call(
        functools.partial(attn_fwd_kernel, heads, size),
        grid=(1,),
        out_shape=(
            jax.ShapeDtypeStruct((seq, 3 * own), BF),
            jax.ShapeDtypeStruct((seq, own), BF),
            jax.ShapeDtypeStruct((heads, seq), F32),
        ),
        in_specs=[SMEM, VMEM, layer_spec(w_qkv, layer), VMEM],
        out_specs=(VMEM, VMEM, VMEM),
        scratch_shapes=[
            pltpu.VMEM((model, 3 * own), BF),
            pltpu.VMEM((heads, seq, size), BF),
            pltpu.VMEM((heads, seq, size), BF),
            pltpu.VMEM((heads, size, seq), BF),
            pltpu.VMEM((width - LANES, LANES), F32),
            pltpu.VMEM((PROMPT, seq - PROMPT), F32),
            pltpu.VMEM((own, seq), F32),
            pltpu.VMEM((seq - PROMPT, LANES), jnp.int32),
        ],
        compiler_params=pltpu.CompilerParams(vmem_limit_bytes=VMEM_BYTES),
    )(lens, normed, w_qkv, vecs)


def attn_bwd_kernel(heads, size, extra, lens, qkv, normed, branch, w_attn, mixed, lse, vecs, *refs):
    refs = list(refs)
    if extra == "copy":
        sources, refs = refs[:2], refs[2:]
    elif extra == "share":
        shared, refs = refs[0], refs[1:]
    dqkv_o, gw_o, dvec_o = refs[:3]
    refs = refs[3:]
    if extra == "copy":
        targets, refs = refs[:2], refs[2:]
    elif extra == "share":
        all_o, refs = refs[0], refs[1:]
    q_s, k_s, v_s, kt_s, do_s, table, cont_bias, fold, dtable, dk_s, dv_s, dqt, dk_all, dv_all, segc = refs[:15]
    refs = refs[15:]
    me, core, mate, across, diagonal = mp_places()
    if extra == "copy":
        spaces, sems = refs[:2], refs[2]
        takes = [pltpu.make_async_copy(sources[n], spaces[n], sems.at[n]) for n in range(2)]
        puts = [pltpu.make_async_copy(spaces[n], targets[n].at[targets[n].shape[0] - 1], sems.at[2 + n]) for n in range(2)]
        for copy in takes:
            copy.start()
    elif extra == "share":
        held, ssem, rsem = refs
        greet_mp(2)
        held[me] = shared[...]
        to_mate = remote(held.at[me], held.at[me], ssem.at[0], rsem.at[0], mp=mate)
        over = remote(held.at[me], held.at[me], ssem.at[1], rsem.at[1], mp=across)
        passed = remote(held.at[across], held.at[across], ssem.at[2], rsem.at[2], mp=mate)
        over.start()
        to_mate.start()

    seq, model = normed.shape
    own = heads * size
    cont = seq - PROMPT
    own_rows = pl.ds(pl.multiple_of(me * own, size), own)
    for i in range(seq // QB):
        rows = pl.ds(i * QB, QB)
        part = qkv[rows, :]
        dmix = nt(branch[rows, :], w_attn[own_rows, :]).astype(BF)
        for h in range(heads):
            q_s[h, rows, :] = part[:, h * size : (h + 1) * size] * BF(0.125)
            key = part[:, own + h * size : own + (h + 1) * size]
            k_s[h, rows, :] = key
            kt_s[h, :, rows] = (key.astype(F32) * 0.125).T.astype(BF)
            v_s[h, rows, :] = part[:, 2 * own + h * size : 2 * own + (h + 1) * size]
            do_s[h, rows, :] = dmix[:, h * size : (h + 1) * size]
    seg_row, _ = segments(lens, (1, cont), 1)
    segc[...] = segments(lens, (cont, LANES), 0)[0]
    _, offset = segments(lens, (cont, LANES), 0)
    unplace = (lax.broadcasted_iota(jnp.int32, (cont, LANES), 1) == offset).astype(BF)
    width = vecs.shape[1]

    def head(h, carry):
        bias_stage(vecs[pl.ds(h, 1), :], lens, table, cont_bias)
        dtable[...] = jnp.zeros_like(dtable)
        dk_s[...] = jnp.zeros_like(dk_s)
        dv_s[...] = jnp.zeros_like(dv_s)
        for block in blocks_of(seq):
            q0, prompt_keys, cont_from = block
            query = q_s[h, q0 : q0 + QB, :]
            dout = do_s[h, q0 : q0 + QB, :]
            parts = scores_of(k_s, query, table, cont_bias, segc, seg_row, block, h)
            lse_row = lse[pl.ds(h, 1), q0 : q0 + QB]
            kept, delta = [], 0.0
            for k0, k1, s in parts:
                p = jnp.exp(s - lse_row)
                dp = nt(v_s[h, k0:k1, :], dout)
                delta = delta + jnp.sum(p * dp, axis=0, keepdims=True)
                dv_s[k0:k1, :] += nn(p.astype(BF), dout)
                kept.append((k0, k1, p, dp))
            dq = 0.0
            for k0, k1, p, dp in kept:
                ds = p * (dp - delta)
                dsb = ds.astype(BF)
                dk_s[k0:k1, :] += nn(dsb, query)
                dq = dq + nn(kt_s[h, :, k0:k1], dsb)
                if cont_from is not None and k0 == 0:
                    fold[:, q0 - PROMPT : q0 - PROMPT + QB] = dsb
                else:
                    left = PROMPT - q0 if cont_from is None else PROMPT + cont_from - (q0 - PROMPT)
                    dtable[left : left + k1 - k0, :] += ds[:, 0:LANES]
                    dtable[left - LANES : left - LANES + k1 - k0, :] += ds[:, LANES:]
            dqt[pl.ds(pl.multiple_of(h * size, size), size), q0 : q0 + QB] = dq
        dk_all[h] = dk_s[...].astype(BF)
        dv_all[h] = dv_s[...].astype(BF)
        dtable[0:PROMPT, :] += nn(fold[...], unplace)
        flat = dtable[...].T
        flat = jnp.concatenate([flat, jnp.zeros((LANES, LANES), F32)], 1)
        rows = lax.broadcasted_iota(jnp.int32, (LANES, width), 0)
        for bit in range(7):
            flat = jnp.where((rows >> bit) % 2 == 1, pltpu.roll(flat, width - (1 << bit), 1), flat)
        dvec_o[pl.ds(h, 1), :] = jnp.sum(flat, axis=0, keepdims=True)
        return carry

    lax.fori_loop(0, heads, head, 0)
    if extra == "copy":
        for n in range(2):
            takes[n].wait()
            puts[n].start()
    elif extra == "share":
        over.wait_recv()
        passed.start()
    for i in range(seq // QB):
        rows = pl.ds(i * QB, QB)
        pieces = [dqt[:, i * QB : (i + 1) * QB].T.astype(BF)]
        pieces += [dk_all[h, rows, :] for h in range(heads)] + [dv_all[h, rows, :] for h in range(heads)]
        dqkv_o[rows, :] = jnp.concatenate(pieces, 1)
    half = normed.shape[1] // 2
    for i in range(2):
        cols = slice(i * half, (i + 1) * half)
        gw_o[cols, 0 : 3 * own] = tn(normed[:, cols], dqkv_o[...])
        gw_o[cols, 3 * own :] = tn(branch[:, cols], mixed[...])
    if extra == "copy":
        for copy in puts:
            copy.wait()
    elif extra == "share":
        to_mate.wait()
        over.wait_send()
        passed.wait()
        all_o[...] = held[...]


def attn_bwd(lens, qkv, normed, branch, w_attn, layer, mixed, lse, vecs, heads, size, extra=None, more=(), number=None):
    seq, model = normed.shape
    own = heads * size
    width = vecs.shape[1]
    cont = seq - PROMPT
    params = pltpu.CompilerParams(vmem_limit_bytes=VMEM_BYTES)
    outs, scratch, in_spec = (), [], VMEM
    if extra == "copy":
        outs = tuple(jax.ShapeDtypeStruct((w_attn.shape[0],) + g.shape, F32) for g in more)
        scratch, in_spec = [pltpu.VMEM(g.shape, F32) for g in more] + [pltpu.SemaphoreType.DMA((4,))], ANY
    elif extra == "share":
        shape = (4,) + more[0].shape
        outs = (jax.ShapeDtypeStruct(shape, BF),)
        scratch = [pltpu.VMEM(shape, BF), pltpu.SemaphoreType.DMA((3,)), pltpu.SemaphoreType.DMA((3,))]
        params = pltpu.CompilerParams(collective_id=number, has_side_effects=True, vmem_limit_bytes=VMEM_BYTES)
    return pl.pallas_call(
        functools.partial(attn_bwd_kernel, heads, size, extra),
        grid=(1,),
        out_shape=(
            jax.ShapeDtypeStruct((seq, 3 * own), BF),
            jax.ShapeDtypeStruct((model, 4 * own), F32),
            jax.ShapeDtypeStruct((heads, width), F32),
        )
        + outs,
        in_specs=[SMEM] + [VMEM] * 3 + [layer_spec(w_attn, layer)] + [VMEM] * 3 + [in_spec] * len(more),
        out_specs=(VMEM, VMEM, VMEM) + (in_spec,) * len(outs),
        scratch_shapes=[
            pltpu.VMEM((heads, seq, size), BF),
            pltpu.VMEM((heads, seq, size), BF),
            pltpu.VMEM((heads, seq, size), BF),
            pltpu.VMEM((heads, size, seq), BF),
            pltpu.VMEM((heads, seq, size), BF),
            pltpu.VMEM((width - LANES, LANES), F32),
            pltpu.VMEM((PROMPT, cont), F32),
            pltpu.VMEM((PROMPT, cont), BF),
            pltpu.VMEM((width - LANES, LANES), F32),
            pltpu.VMEM((seq, size), F32),
            pltpu.VMEM((seq, size), F32),
            pltpu.VMEM((own, seq), F32),
            pltpu.VMEM((heads, seq, size), BF),
            pltpu.VMEM((heads, seq, size), BF),
            pltpu.VMEM((cont, LANES), jnp.int32),
        ]
        + scratch,
        compiler_params=params,
    )(lens, qkv, normed, branch, w_attn, mixed, lse, vecs, *more)


def diagonals():
    width = PROMPT + 3 * LANES
    at = jnp.arange(width, dtype=jnp.int32)
    distance = jnp.where(at <= PROMPT, PROMPT - at, PROMPT + width - at)
    valid = (at <= PROMPT) | (at > width - LANES)
    return width, distance, valid


def bias_vectors(bias):
    _, distance, valid = diagonals()
    hot = bucket_of(distance)[None, :] == jnp.arange(bias.shape[-1], dtype=jnp.int32)[:, None]
    picked = jnp.sum(jnp.where(hot, bias[..., :, None], 0.0), axis=-2)
    return jnp.where(valid, picked, -1e30)


def bias_grads(dvecs, buckets):
    _, distance, valid = diagonals()
    hot = (bucket_of(distance)[None, :] == jnp.arange(buckets, dtype=jnp.int32)[:, None]) & valid[None, :]
    return jnp.sum(jnp.where(hot, dvecs[..., None, :], 0.0), axis=-1)


def scatter_rows(rows, values, send):
    experts, tile, _ = send.shape
    tokens, model = values[0].shape
    half = model // 2
    at = lax.broadcasted_iota(jnp.int32, (experts * tile, tokens), 0)
    place, piece = [], []
    for j in range(2):
        slot = rows[2 + j : 3 + j, :]
        piece.append(jnp.where(rows[4 + j : 5 + j, :] > 0, slot // tile, -1))
        place.append(rows[j : j + 1, :] * tile + slot % tile)

    def pick(number, shift, columns):
        hots = [
            (jnp.where(piece[j] == number, place[j] + shift, -1) == at) for j in range(2)
        ]
        if len(values) == 1:
            return nn((hots[0] | hots[1]).astype(BF), values[0][:, columns])
        return nn(hots[0].astype(BF), values[0][:, columns]) + nn(hots[1].astype(BF), values[1][:, columns])

    for i in range(3):
        send[:, :, i * model : (i + 1) * model] = pick(i, 0, slice(0, model)).astype(BF).reshape(experts, tile, model)
    tail = pick(3, 0, slice(0, half)) + pick(3, 8, slice(half, model))
    send[:, :, 3 * model :] = tail.astype(BF).reshape(experts, tile, half)


def gather_rows(cols, j, back):
    experts, tile, wide = back.shape
    half = wide // 7
    model = 2 * half
    tokens = cols.shape[0]
    at = lax.broadcasted_iota(jnp.int32, (tokens, experts * tile), 1)
    slot = cols[:, 2 + j : 3 + j]
    piece = jnp.where(cols[:, 4 + j : 5 + j] > 0, slot // tile, -1)
    place = cols[:, j : j + 1] * tile + slot % tile
    total = 0.0
    for i in range(3):
        hot = (jnp.where(piece == i, place, -1) == at).astype(BF)
        total = total + nn(hot, back[:, :, i * model : (i + 1) * model].reshape(experts * tile, model))
    tail = back[:, :, 3 * model :].reshape(experts * tile, half)
    left = nn((jnp.where(piece == 3, place, -1) == at).astype(BF), tail)
    right = nn((jnp.where(piece == 3, place + 8, -1) == at).astype(BF), tail)
    return total + jnp.concatenate([left, right], 1)


def unfold_tail(block, half):
    wide = block.astype(F32)
    return jnp.concatenate([wide[0:8, :], wide[8:16, :]], 1)


def mp_places():
    me = lax.axis_index("mp")
    core, row = lax.rem(me, 2), me // 2
    return me, core, row * 2 + 1 - core, (1 - row) * 2 + core, (1 - row) * 2 + 1 - core


def signal_to(barrier, **place):
    pl.semaphore_signal(barrier, inc=1, device_id=place, device_id_type=MESH)


def remote(src, dst, send_sem, recv_sem, **place):
    return pltpu.make_async_remote_copy(
        src_ref=src, dst_ref=dst, send_sem=send_sem, recv_sem=recv_sem, device_id=place, device_id_type=MESH
    )


def gather_mp(held, ssem, rsem):
    me, core, mate, across, diagonal = mp_places()
    to_mate = remote(held.at[me], held.at[me], ssem.at[0], rsem.at[0], mp=mate)
    over = remote(held.at[me], held.at[me], ssem.at[1], rsem.at[1], mp=across)
    over.start()
    to_mate.start()
    over.wait_recv()
    passed = remote(held.at[across], held.at[across], ssem.at[2], rsem.at[2], mp=mate)
    passed.start()
    to_mate.wait_recv()
    passed.wait_recv()
    for copy in (to_mate, over, passed):
        copy.wait_send()


def swap_mp(out, held, ssem, rsem, lsem):
    me, core, mate, across, diagonal = mp_places()
    copies = [
        remote(out.at[to], held.at[me], ssem.at[n], rsem.at[n], mp=to) for n, to in enumerate((diagonal, across, mate))
    ]
    copies.append(pltpu.make_async_copy(out.at[me], held.at[me], lsem))
    for copy in copies:
        copy.start()
    return copies


def greet_mp(count, dp_count=1):
    me, core, mate, across, diagonal = mp_places()
    d = lax.axis_index("dp")
    barrier = pltpu.get_barrier_semaphore()
    for to in (mate, across, diagonal)[:count]:
        signal_to(barrier, mp=to)
    for k in range(1, dp_count):
        signal_to(barrier, dp=lax.rem(d + k, dp_count), mp=me)
    pl.semaphore_wait(barrier, count + dp_count - 1)


def share_dp(held, ssem, rsem):
    d, me, count = lax.axis_index("dp"), lax.axis_index("mp"), held.shape[0]
    return [
        remote(held.at[d], held.at[d], ssem.at[k], rsem.at[k], dp=lax.rem(d + k, count), mp=me) for k in range(1, count)
    ]


def scatter_dp(part, come, ssem, rsem):
    d, me, count = lax.axis_index("dp"), lax.axis_index("mp"), part.shape[0]
    copies = []
    for k in range(1, count):
        to = lax.rem(d + k, count)
        copies.append(remote(part.at[to], come.at[d], ssem.at[k], rsem.at[k], dp=to, mp=me))
    return copies


def sum_dp(copies, part, come):
    d, count = lax.axis_index("dp"), part.shape[0]
    total = part[d].astype(F32)
    for k in range(1, count):
        copies[k - 1].wait_recv()
        total = total + come[lax.rem(d + count - k, count)].astype(F32)
    return total


def mean_square_scale(values):
    return lax.rsqrt(jnp.mean(values * values, axis=-1, keepdims=True) + EPSILON)


def norm_grads(values, gain, upstream):
    scale = mean_square_scale(values)
    scaled = upstream * gain
    drift = jnp.mean(values * scaled, axis=-1, keepdims=True)
    return scale * scaled - values * (scale * scale * scale * drift), jnp.sum(
        upstream * values * scale, axis=0, keepdims=True
    )


def first_kernel(tokens, gain, all_o, held, ssem, rsem):
    greet_mp(2)
    me = lax.axis_index("mp")
    stream = tokens[...].astype(F32)
    held[me] = (stream * mean_square_scale(stream) * gain[...]).astype(BF)
    gather_mp(held, ssem, rsem)
    all_o[...] = held[...]


def next_kernel(middle, back, cols, gates, gain, stream_o, all_o, held, ssem, rsem):
    greet_mp(2)
    me = lax.axis_index("mp")
    stream = middle[...]
    for j in range(2):
        stream = stream + gates[:, j : j + 1] * gather_rows(cols, j, back)
    stream_o[...] = stream
    held[me] = (stream * mean_square_scale(stream) * gain[...]).astype(BF)
    gather_mp(held, ssem, rsem)
    all_o[...] = held[...]


def middle_kernel(with_grad, *refs):
    if with_grad:
        (mixed, stream, w_attn, gain, router, rows, cols, cotangent, middle_o, ffn_o, gates_o, send_o, back_o, held, ssem, rsem, lsem) = refs
    else:
        (mixed, stream, w_attn, gain, router, rows, cols, middle_o, ffn_o, gates_o, send_o, held, ssem, rsem, lsem) = refs
    greet_mp(3)
    for copy in swap_mp(mixed, held, ssem, rsem, lsem):
        copy.wait()
    part = held.shape[2]
    middle = stream[...].astype(F32)
    for m in range(held.shape[0]):
        middle = middle + nn(held[m], w_attn[m * part : (m + 1) * part, :])
    middle_o[...] = middle
    ffn = (middle * mean_square_scale(middle) * gain[...]).astype(BF)
    ffn_o[...] = ffn
    logits = nn(ffn, router[...])
    expert = lax.broadcasted_iota(jnp.int32, logits.shape, 1)
    chosen = [
        jnp.sum(jnp.where(expert == cols[:, j : j + 1], logits, 0.0), axis=1, keepdims=True) for j in range(2)
    ]
    top = jnp.maximum(chosen[0], chosen[1])
    powers = [jnp.exp(c - top) for c in chosen]
    gates = [p / (powers[0] + powers[1]) for p in powers]
    gates_o[...] = jnp.concatenate(gates, 1)
    scatter_rows(rows, [ffn], send_o)
    if with_grad:
        flow = cotangent[...].astype(F32)
        scatter_rows(rows, [(gates[j] * cols[:, 4 + j : 5 + j].astype(F32) * flow).astype(BF) for j in range(2)], back_o)


def post_kernel(with_output, *refs):
    if with_output:
        (back, returned, flow_in, middle, ffn, gates, cols, router, gain, grad_o, all_o, gain_o, router_o, out_o, held, ssem, rsem) = refs
        greet_mp(2)
    else:
        (back, returned, flow_in, middle, ffn, gates, cols, router, gain, shared, grad_o, all_o, gain_o, router_o, share_o, held, ssem, rsem, round_s, dssem, drsem) = refs
        greet_mp(2, dp_count=round_s.shape[0])
        d = lax.axis_index("dp")
        round_s[d] = shared[...]
        shares = share_dp(round_s, dssem, drsem)
        for copy in shares:
            copy.start()
    me = lax.axis_index("mp")
    flow = flow_in[...].astype(F32)
    outs = [gather_rows(cols, j, returned) for j in range(2)]
    gate = [gates[:, j : j + 1] for j in range(2)]
    keep = [cols[:, 4 + j : 5 + j].astype(F32) for j in range(2)]
    if with_output:
        out_o[...] = (middle[...] + gate[0] * keep[0] * outs[0] + gate[1] * keep[1] * outs[1]).astype(BF)
    gate_grad = [keep[j] * jnp.sum(flow * outs[j], axis=1, keepdims=True) for j in range(2)]
    shared = gate[0] * gate_grad[0] + gate[1] * gate_grad[1]
    expert = lax.broadcasted_iota(jnp.int32, (flow.shape[0], router.shape[1]), 1)
    logit_grad = 0.0
    for j in range(2):
        logit_grad = logit_grad + jnp.where(expert == cols[:, j : j + 1], gate[j] * (gate_grad[j] - shared), 0.0)
    high = logit_grad.astype(BF)
    low = (logit_grad - high.astype(F32)).astype(BF)
    upstream = gather_rows(cols, 0, back) + gather_rows(cols, 1, back)
    upstream = upstream + nt(high, router[...]) + nt(low, router[...])
    router_o[...] = tn(high, ffn[...]) + tn(low, ffn[...])
    grad, gain_o[...] = norm_grads(middle[...], gain[...], upstream)
    grad = grad + flow
    grad_o[...] = grad
    held[me] = grad.astype(BF)
    gather_mp(held, ssem, rsem)
    all_o[...] = held[...]
    if not with_output:
        for copy in shares:
            copy.wait()
        share_o[...] = round_s[...]


def close_layer(held, w_qkv, stream, gain, grad):
    model = w_qkv.shape[0]
    own = held.shape[2] // 3
    upstream = 0.0
    for t in range(3):
        piece = jnp.concatenate([held[m, :, t * own : (t + 1) * own] for m in range(held.shape[0])], 1)
        upstream = upstream + nt(piece, w_qkv[:, t * model : (t + 1) * model])
    inner, gain_grad = norm_grads(stream[...].astype(F32), gain[...], upstream)
    return grad[...] + inner, gain_grad


def fill_parts(part, heads):
    rows = part.shape[1]
    for j in range(part.shape[0]):
        part[j] = heads[j * rows : (j + 1) * rows, :].astype(BF)


def close_kernel(dqkv, w_qkv, stream, gain, grad, rows, cols, gates, heads, flow_o, gain_o, send_o, sum_o, held, part, come, ssem, rsem, lsem, dssem, drsem):
    greet_mp(3, dp_count=part.shape[0])
    swaps = swap_mp(dqkv, held, ssem, rsem, lsem)
    fill_parts(part, heads)
    scattered = scatter_dp(part, come, dssem, drsem)
    for copy in scattered:
        copy.start()
    for copy in swaps:
        copy.wait()
    flow, gain_o[...] = close_layer(held, w_qkv, stream, gain, grad)
    flow_o[...] = flow
    scatter_rows(
        rows,
        [(gates[:, j : j + 1] * cols[:, 4 + j : 5 + j].astype(F32) * flow).astype(BF) for j in range(2)],
        send_o,
    )
    sum_o[...] = sum_dp(scattered, part, come).astype(BF)
    for copy in scattered:
        copy.wait_send()


def last_kernel(
    dqkv, w_qkv, stream, gain, grad, heads, small, flow_o, all_o, small_o,
    held, part, come, small_s, small_come, small_mp, small_all,
    ssem, rsem, lsem, dssem, drsem, tsem, usem, csem, dsem, vsem, zsem, esem, fsem, hsem, isem,
):
    dp_count = part.shape[0]
    d = lax.axis_index("dp")
    me, core, mate, across, diagonal = mp_places()
    greet_mp(3, dp_count=dp_count)
    swaps = swap_mp(dqkv, held, ssem, rsem, lsem)
    fill_parts(part, heads)
    scattered = scatter_dp(part, come, dssem, drsem)
    for copy in scattered:
        copy.start()
    small_s[...] = small[...]
    for copy in swaps:
        copy.wait()
    flow, gain_grad = close_layer(held, w_qkv, stream, gain, grad)
    flow_o[...] = flow
    small_s[0, 0:1, :] = gain_grad
    small_scattered = scatter_dp(small_s, small_come, tsem, usem)
    for copy in small_scattered:
        copy.start()
    all_o[me, d] = sum_dp(scattered, part, come).astype(BF)
    shares = [
        remote(all_o.at[me, d], all_o.at[me, d], esem.at[k], fsem.at[k], dp=lax.rem(d + k, dp_count), mp=me)
        for k in range(1, dp_count)
    ]
    for copy in shares:
        copy.start()

    def over(n, j):
        whose = across if n == 2 else me
        return remote(all_o.at[whose, j], all_o.at[whose, j], hsem.at[n, j], isem.at[n, j], mp=across if n == 1 else mate)

    over(1, d).start()
    over(0, d).start()
    small_mp[me] = sum_dp(small_scattered, small_s, small_come)
    small_swaps = [
        remote(small_mp.at[me], small_mp.at[me], csem.at[n], dsem.at[n], mp=to) for n, to in enumerate((mate, across, diagonal))
    ]
    for copy in small_swaps:
        copy.start()
    for copy in small_swaps:
        copy.wait_recv()
    small_all[d] = small_mp[0] + small_mp[1] + small_mp[2] + small_mp[3]
    small_shares = share_dp(small_all, vsem, zsem)
    for copy in small_shares:
        copy.start()
    for k in range(1, dp_count):
        j = lax.rem(d + dp_count - k, dp_count)
        shares[k - 1].wait_recv()
        over(1, j).start()
        over(0, j).start()
        last = lax.rem(d + dp_count - k + 1, dp_count)
        over(1, last).wait_recv()
        over(2, last).start()
    last = lax.rem(d + 1, dp_count)
    over(1, last).wait_recv()
    over(2, last).start()
    for copy in small_shares:
        copy.wait_recv()
    small_o[...] = small_all[...]
    for j in range(dp_count):
        over(0, j).wait_recv()
        over(2, j).wait_recv()
        for n in range(3):
            over(n, j).wait_send()
    for copy in small_swaps + scattered + small_scattered + small_shares + shares:
        copy.wait_send()


def dma(*shape):
    return pltpu.SemaphoreType.DMA(shape) if shape else pltpu.SemaphoreType.DMA


def mp_call(kernel, number, outs, scratch, *args):
    specs = [layer_spec(*a) if isinstance(a, tuple) else VMEM for a in args]
    return pl.pallas_call(
        kernel,
        grid=(1,),
        out_shape=tuple(jax.ShapeDtypeStruct(shape, kind) for shape, kind in outs),
        in_specs=specs,
        out_specs=tuple([VMEM] * len(outs)),
        scratch_shapes=scratch,
        compiler_params=pltpu.CompilerParams(
            collective_id=number, has_side_effects=True, vmem_limit_bytes=VMEM_BYTES
        ),
    )(*[a[0] if isinstance(a, tuple) else a for a in args])


def gelu_grad(values):
    inner = jnp.tanh(SQRT_TWO_PI * (values + 0.044715 * values * values * values))
    slope = SQRT_TWO_PI * (1.0 + 3.0 * 0.044715 * values * values)
    return 0.5 * values * (1.0 + inner), 0.5 * (1.0 + inner) + 0.5 * values * (1.0 - inner * inner) * slope


def expert_kernel(mode, layer, dp_count, *refs):
    forward, backward = mode in ("fwd", "both"), mode in ("both", "bwd")
    refs = list(refs)

    def take(count):
        taken = refs[:count]
        del refs[:count]
        return taken

    (send_x,) = take(1) if forward else (None,)
    (send_g,) = take(1) if backward else (None,)
    (x_in,) = take(1) if mode == "bwd" else (None,)
    w_in, w_out = take(2)
    (out_o,) = take(1) if forward else (None,)
    (x_o,) = take(1) if mode == "fwd" else (None,)
    grad_o, gw_in_o, gw_out_o = take(3) if backward else (None, None, None)
    w1, w2, wsem, wssem, wrsem = take(5)
    kept_part, x_all, xsem = take(3)
    paths = []
    for sending in ([send_x] if forward else []) + ([send_g] if backward else []):
        paths.append((sending, take(14)))
    if backward:
        g_all, hid_all, ig_all, stage, gsem, grsem, glsem = take(7)

    d = lax.axis_index("dp")
    me, core, mate, across, diagonal = mp_places()
    row = me // 2
    index = d * 2 + core
    experts = dp_count * 2
    groups = dp_count // 2
    model = w1.shape[1]
    half = model // 2
    rows_a = x_all.shape[1] // 2

    barrier = pltpu.get_barrier_semaphore()

    def greet(k, carry):
        signal_to(barrier, dp=lax.rem(d + k // 2, dp_count), mp=row * 2 + lax.rem(core + k % 2, 2))
        return carry

    lax.fori_loop(1, experts, greet, 0)
    signal_to(barrier, mp=across)
    pl.semaphore_wait(barrier, experts)

    def send_all(path):
        sending, (recv_a, recv_b, ssem, asem, fsem, bsem, part, pssem, prsem, ret_s, ret, rssem, rrsem, psend) = path

        def one(k, carry):
            dd, cc = lax.rem(d + k // 2, dp_count), lax.rem(core + k % 2, 2)
            to = dd * 2 + cc
            remote(sending.at[to], recv_a.at[index], ssem.at[to], asem.at[index], dp=dd, mp=row * 2 + cc).start()
            return carry

        lax.fori_loop(1, experts, one, 0)
        pltpu.make_async_copy(sending.at[index], recv_a.at[index], asem.at[index]).start()

    send_all(paths[0])
    copies = []
    for n, (source, held) in enumerate(((w_in, w1), (w_out, w2))):
        copies.append(remote(source.at[layer, 1 - core], held.at[core], wssem.at[n], wrsem.at[n], mp=mate))
        copies.append(pltpu.make_async_copy(source.at[layer, core], held.at[core], wsem.at[n]))
    for copy in copies:
        copy.start()
    if mode == "bwd":
        saved = pltpu.make_async_copy(x_in, x_all, xsem)
        saved.start()
    for path in paths[1:]:
        send_all(path)
    for copy in copies:
        copy.wait()
    if mode == "bwd":
        saved.wait()

    def source_of(g, kk):
        return lax.rem(d + dp_count - (g * 2 + kk), dp_count)

    def unpack(held, g, side, into):
        base = side * rows_a
        for kk in range(2):
            s0 = source_of(g, kk)
            tails = []
            for cc in range(2):
                block = held[s0 * 2 + cc]
                for i in range(3):
                    into[g, base + i * 64 + kk * 32 + cc * 16 : base + i * 64 + kk * 32 + cc * 16 + 16, :] = block[
                        :, i * model : (i + 1) * model
                    ]
                tails.append(unfold_tail(block[:, 3 * model :], half))
            into[g, base + 192 + kk * 16 : base + 208 + kk * 16, :] = jnp.concatenate(tails, 0).astype(BF)

    def run_path(path, into, compute):
        sending, (recv_a, recv_b, ssem, asem, fsem, bsem, part, pssem, prsem, ret_s, ret, rssem, rrsem, psend) = path

        def forward_copy(s0):
            two = pl.ds(s0 * 2, 2)
            return remote(recv_a.at[two], recv_b.at[two], fsem.at[s0], bsem.at[s0], mp=across)

        def partial_copy(g):
            return remote(psend.at[g], part.at[g], pssem.at[g], prsem.at[g], mp=across)

        def step(i, carry):
            @pl.when(i < groups)
            def _():
                for kk in range(2):
                    s0 = source_of(i, kk)
                    for cc in range(2):
                        src = s0 * 2 + cc
                        pltpu.make_async_copy(recv_a.at[src], recv_a.at[src], asem.at[src]).wait()
                    forward_copy(s0).start()

            @pl.when((i >= 1) & (i <= groups))
            def _():
                g = i - 1
                for kk in range(2):
                    forward_copy(source_of(g, kk)).wait_recv()
                unpack(recv_a, g, 0, into)
                unpack(recv_b, g, 1, into)
                total = compute(g)
                kept_part[lax.rem(g, 2)] = total[0:rows_a, :]
                psend[g] = total[rows_a:, :].astype(BF)
                partial_copy(g).start()

            @pl.when(i >= 2)
            def _():
                g = i - 2
                partial_copy(g).wait_recv()
                total = kept_part[lax.rem(g, 2)] + part[g].astype(F32)
                for kk in range(2):
                    s0 = source_of(g, kk)
                    for cc in range(2):
                        src = s0 * 2 + cc
                        for n in range(3):
                            at = n * 64 + kk * 32 + cc * 16
                            ret_s[src, :, n * model : (n + 1) * model] = total[at : at + 16, :].astype(BF)
                        at = 192 + kk * 16 + cc * 8
                        ret_s[src, :, 3 * model :] = jnp.concatenate(
                            [total[at : at + 8, 0:half], total[at : at + 8, half:]], 0
                        ).astype(BF)

                        @pl.when(src == index)
                        def _():
                            pltpu.make_async_copy(ret_s.at[src], ret.at[index], rrsem.at[index]).start()

                        @pl.when(src != index)
                        def _():
                            remote(
                                ret_s.at[src], ret.at[index], rssem.at[src], rrsem.at[index], dp=s0, mp=row * 2 + cc
                            ).start()

            return carry

        lax.fori_loop(0, groups + 2, step, 0)

    def finish_path(path, result):
        sending, (recv_a, recv_b, ssem, asem, fsem, bsem, part, pssem, prsem, ret_s, ret, rssem, rrsem, psend) = path

        def end(e, carry):
            pltpu.make_async_copy(ret.at[e], ret.at[e], rrsem.at[e]).wait()

            @pl.when(e != index)
            def _():
                pltpu.make_async_copy(ret_s.at[e], ret_s.at[e], rssem.at[e]).wait()
                pltpu.make_async_copy(sending.at[e], sending.at[e], ssem.at[e]).wait()

            return carry

        lax.fori_loop(0, experts, end, 0)

        def end_pair(s0, carry):
            two = pl.ds(s0 * 2, 2)
            pltpu.make_async_copy(recv_a.at[two], recv_a.at[two], fsem.at[s0]).wait()
            return carry

        lax.fori_loop(0, dp_count, end_pair, 0)

        def end_group(g, carry):
            pltpu.make_async_copy(psend.at[g], psend.at[g], pssem.at[g]).wait()
            return carry

        lax.fori_loop(0, groups, end_group, 0)
        result[...] = ret[...]

    def compute_forward(g):
        x = x_all[g]
        total = 0.0
        for q in range(2):
            hidden = gelu_tanh(nn(x, w1[q])).astype(BF)
            if backward:
                hid_all[q, g] = hidden
            total = total + nn(hidden, w2[q])
        return total

    def compute_backward(g):
        x, gr = x_all[g], g_all[g]
        total = 0.0
        for q in range(2):
            value, slope = gelu_grad(nn(x, w1[q]))
            if not forward:
                hid_all[q, g] = value.astype(BF)
            inner = (nt(gr, w2[q]) * slope).astype(BF)
            ig_all[q, g] = inner
            total = total + nt(inner, w1[q])
        return total

    if forward:
        run_path(paths[0], x_all, compute_forward)
        if mode == "fwd":
            saved = pltpu.make_async_copy(x_all, x_o, xsem)
            saved.start()
    if backward:
        run_path(paths[-1], g_all, compute_backward)
        count = groups * 2 * rows_a

        def products(n, q):
            if n == 0:
                return tn(x_all[...].reshape(count, model), ig_all[q].reshape(count, model))
            return tn(hid_all[q].reshape(count, model), g_all[...].reshape(count, model))

        outs = (gw_in_o, gw_out_o)
        copies = []
        for n in range(2):
            stage[n] = products(n, 1 - core)
            copy = remote(stage.at[n], outs[n].at[core], gsem.at[n], grsem.at[n], mp=mate)
            copy.start()
            copies.append(copy)
        for n in range(2):
            copies[n].wait_send()
            stage[n] = products(n, core)
            copy = pltpu.make_async_copy(stage.at[n], outs[n].at[core], glsem.at[n])
            copy.start()
            copies.append(copy)
        for n in range(2):
            copies[n].wait_recv()
            copies[2 + n].wait()
    if forward:
        finish_path(paths[0], out_o)
        if mode == "fwd":
            saved.wait()
    if backward:
        finish_path(paths[-1], grad_o)


def expert_call(mode, layer, number, dp_count, sends, x_in, w_in, w_out):
    forward, backward = mode in ("fwd", "both"), mode in ("both", "bwd")
    shape = sends[0].shape
    experts, tile, wide = shape
    model = w_in.shape[2]
    groups = dp_count // 2
    rows = 2 * 4 * 56
    args = list(sends)
    specs = [VMEM] * len(sends)
    if mode == "bwd":
        args.append(x_in)
        specs.append(ANY)
    args += [w_in, w_out]
    specs += [ANY, ANY]
    outs, out_specs = [], []

    def out(dims, kind, spec):
        outs.append(jax.ShapeDtypeStruct(dims, kind))
        out_specs.append(spec)

    if forward:
        out(shape, BF, VMEM)
    if mode == "fwd":
        out((groups, rows, model), BF, ANY)
    if backward:
        out(shape, BF, VMEM)
        out((2, model, model), F32, ANY)
        out((2, model, model), F32, ANY)
    scratch = [
        pltpu.VMEM((2, model, model), BF),
        pltpu.VMEM((2, model, model), BF),
        dma(2),
        dma(2),
        dma(2),
        pltpu.VMEM((2, rows // 2, model), F32),
        pltpu.VMEM((groups, rows, model), BF),
        dma(),
    ]
    for _ in sends:
        scratch += [
            pltpu.VMEM(shape, BF),
            pltpu.VMEM(shape, BF),
            dma(experts),
            dma(experts),
            dma(dp_count),
            dma(dp_count),
            pltpu.VMEM((groups, rows // 2, model), BF),
            dma(groups),
            dma(groups),
            pltpu.VMEM(shape, BF),
            pltpu.VMEM(shape, BF),
            dma(experts),
            dma(experts),
            pltpu.VMEM((groups, rows // 2, model), BF),
        ]
    if backward:
        scratch += [
            pltpu.VMEM((groups, rows, model), BF),
            pltpu.VMEM((2, groups, rows, model), BF),
            pltpu.VMEM((2, groups, rows, model), BF),
            pltpu.VMEM((2, model, model), F32),
            dma(2),
            dma(2),
            dma(2),
        ]
    return pl.pallas_call(
        functools.partial(expert_kernel, mode, layer, dp_count),
        out_shape=tuple(outs),
        in_specs=specs,
        out_specs=tuple(out_specs),
        scratch_shapes=scratch,
        compiler_params=pltpu.CompilerParams(
            collective_id=number, has_side_effects=True, vmem_limit_bytes=VMEM_BYTES
        ),
    )(*args)


def spread_kernel(own, count, *refs):
    parts, (gw_in, gw_out, _, _) = refs[:count], refs[count : count + 4]
    qkv_o, attn_o, in_o, out_o, sem = refs[count + 4 :]
    step = pl.program_id(0)
    copies = [
        pltpu.make_async_copy(gw_in.at[0], in_o.at[0, step], sem.at[0]),
        pltpu.make_async_copy(gw_out.at[0], out_o.at[0, step], sem.at[1]),
    ]
    for copy in copies:
        copy.start()

    for n in range(count):
        mp_count, blocks, rows, width = parts[n].shape
        pieces = [parts[n][m].reshape(blocks * rows, width).astype(F32) for m in range(mp_count)]
        qkv_o[n] = jnp.concatenate([p[:, t * own : (t + 1) * own] for t in range(3) for p in pieces], 1)
        for m in range(mp_count):
            attn_o[n, m * own : (m + 1) * own, :] = pieces[m][:, 3 * own :].T
    for copy in copies:
        copy.wait()


def spread_call(parts, own, grads, places):
    mp_count, blocks, rows, width = parts[0].shape
    layers, model = len(parts), blocks * rows
    steps = grads[0].shape[0]
    return pl.pallas_call(
        functools.partial(spread_kernel, own, layers),
        grid=(steps,),
        out_shape=(
            jax.ShapeDtypeStruct((layers, model, 3 * mp_count * own), F32),
            jax.ShapeDtypeStruct((layers, mp_count * own, model), F32),
        )
        + tuple(jax.ShapeDtypeStruct(p.shape, F32) for p in places),
        in_specs=[pl.BlockSpec((mp_count, blocks // steps, rows, width), lambda i: (0, i, 0, 0))] * layers
        + [pl.BlockSpec((1,) + g.shape[1:], lambda i: (i, 0, 0)) for g in grads]
        + [ANY] * 2,
        out_specs=(
            pl.BlockSpec((layers, model // steps, 3 * mp_count * own), lambda i: (0, i, 0)),
            pl.BlockSpec((layers, mp_count * own, model // steps), lambda i: (0, 0, i)),
            ANY,
            ANY,
        ),
        scratch_shapes=[dma(2)],
        input_output_aliases={layers + 2: 2, layers + 3: 3},
        compiler_params=pltpu.CompilerParams(vmem_limit_bytes=VMEM_BYTES),
    )(*parts, *grads, *places)


def fast_body(
    tokens, cotangent, w_qkv, w_attn, attn_gain, rel_bias, ffn_gain, router, w_in, w_out, cont_lengths, routes, slots, drops
):
    _, local, model = tokens.shape
    heads, buckets = rel_bias.shape[1:]
    size = model // heads
    layers = w_qkv.shape[0]
    dp_count, mp_count = lax.axis_size("dp"), lax.axis_size("mp")
    seq = local * mp_count
    own_heads = heads // mp_count
    own = own_heads * size
    experts = dp_count * 2
    me = lax.axis_index("mp")
    block = (experts, 16, 7 * model // 2)
    pairs = jnp.concatenate(
        [routes.reshape(layers, local, 2), slots.reshape(layers, local, 2), 1 - drops.reshape(layers, local, 2)], 2
    )
    cols = jnp.pad(pairs, ((0, 0), (0, 0), (0, 2)))
    rows = cols.transpose(0, 2, 1)
    vecs = bias_vectors(lax.dynamic_slice_in_dim(rel_bias, me * own_heads, own_heads, 1))
    gain_a, gain_f = attn_gain[:, None], ffn_gain[:, None]
    held = (mp_count, local, model)
    chunk = (dp_count, model // dp_count, model)
    gather = [pltpu.VMEM(held, BF), dma(3), dma(3)]

    def swap(width):
        return [pltpu.VMEM((mp_count, local, width), BF)], [dma(3), dma(3), dma()]

    kept = [None] * layers
    stream = tokens[0]
    sends, back, x_rows = None, None, None
    for l in range(layers):
        if l == 0:
            (normed,) = mp_call(first_kernel, 0, [(held, BF)], gather, stream, (gain_a, l))
        else:
            before = kept[l - 1]
            stream, normed = mp_call(
                next_kernel, 1, [((local, model), F32), (held, BF)], gather,
                before["middle"], before["out"], (cols, l - 1), before["gates"], (gain_a, l),
            )
        normed = normed.reshape(seq, model)
        qkv, mixed, lse = attn_fwd(cont_lengths, normed, w_qkv, l, vecs[l], own_heads, size)
        last = l == layers - 1
        outs = [((local, model), F32), ((local, model), BF), ((local, 2), F32), (block, BF)] + ([(block, BF)] if last else [])
        args = [mixed.reshape(mp_count, local, own), stream, (w_attn, l), (gain_f, l), (router, l), (rows, l), (cols, l)]
        space, sems = swap(own)
        got = mp_call(
            functools.partial(middle_kernel, last), 2 + last, outs, space + sems,
            *args, *([cotangent[0]] if last else []),
        )
        middle, ffn, gates = got[:3]
        kept[l] = dict(stream=stream, normed=normed, qkv=qkv, mixed=mixed, lse=lse, middle=middle, ffn=ffn, gates=gates)
        if last:
            out, back, gw_in, gw_out = expert_call("both", l, 5, dp_count, got[3:5], None, w_in, w_out)
            kept[l].update(gw_in=gw_in, gw_out=gw_out)
        else:
            out, x_rows = expert_call("fwd", l, 4, dp_count, got[3:4], None, w_in, w_out)
            kept[l].update(x_rows=x_rows)
        kept[l].update(out=out)

    flow = cotangent[0]
    for l in reversed(range(layers)):
        k = kept[l]
        last = l == layers - 1
        outs = [((local, model), F32), (held, BF), ((1, model), F32), ((experts, model), F32)]
        args = [back, k["out"], flow, k["middle"], k["ffn"], k["gates"], (cols, l), (router, l), (gain_f, l)]
        if last:
            outs.append(((local, model), BF))
            scratch = gather
        else:
            outs.append((chunk, BF))
            args.append(heads_sum)
            scratch = gather + [pltpu.VMEM(chunk, BF), dma(dp_count), dma(dp_count)]
        got = mp_call(functools.partial(post_kernel, last), 6 + last, outs, scratch, *args)
        grad, branch, k["ffn_gain"], k["router"] = got[:4]
        if last:
            output = got[4]
            extra, more = "copy", (k["gw_in"], k["gw_out"])
        else:
            extra, more = "share", (got[4],)
        got = attn_bwd(
            cont_lengths, k["qkv"], k["normed"], branch.reshape(seq, model), w_attn, l, k["mixed"], k["lse"], vecs[l],
            own_heads, size, extra, more, 8,
        )
        dqkv, heads_grad, dvecs = got[:3]
        k["bias"] = bias_grads(dvecs, buckets)
        args = [dqkv.reshape(mp_count, local, 3 * own), (w_qkv, l), k["stream"], (gain_a, l), grad]
        space, sems = swap(3 * own)
        if last:
            places = got[3:]
            b = kept[l - 1]
            flow, k["attn_gain"], send, heads_sum = mp_call(
                close_kernel, 9, [((local, model), F32), ((1, model), F32), (block, BF), (chunk[1:], BF)],
                space + [pltpu.VMEM(chunk, BF)] * 2 + sems + [dma(dp_count)] * 2,
                *args, (rows, l - 1), (cols, l - 1), b["gates"], heads_grad,
            )
            back, b["gw_in"], b["gw_out"] = expert_call("bwd", l - 1, 10, dp_count, [send], b["x_rows"], w_in, w_out)
        else:
            (parts,) = got[3:]

    small = []
    for l in range(layers):
        k = kept[l]
        bias = lax.dynamic_update_slice_in_dim(jnp.zeros((heads, buckets), F32), k["bias"], me * own_heads, 0)
        small += [k["attn_gain"] if l > 0 else jnp.zeros((1, model), F32), k["ffn_gain"]]
        small += [jnp.pad(bias.reshape(1, -1), ((0, 5), (0, model - heads * buckets))), k["router"]]
    lines = 8 + experts
    share = -(-layers * lines // (8 * dp_count)) * 8
    small = jnp.pad(jnp.concatenate(small, 0), ((0, share * dp_count - layers * lines), (0, 0)))
    small = small.reshape(dp_count, share, model)
    small_vmem = pltpu.VMEM(small.shape, F32)
    flow, first_parts, small = mp_call(
        last_kernel, 11, [((local, model), F32), ((mp_count,) + chunk, BF), (small.shape, F32)],
        space
        + [pltpu.VMEM(chunk, BF)] * 2
        + [small_vmem, small_vmem, pltpu.VMEM((mp_count, share, model), F32), small_vmem]
        + sems
        + [dma(dp_count)] * 4
        + [dma(3)] * 2
        + [dma(dp_count)] * 4
        + [dma(3, dp_count)] * 2,
        *args, heads_grad, small,
    )
    small = small.reshape(-1, model)[: layers * lines].reshape(layers, lines, model)
    b = kept[0]
    grad_qkv, grad_attn, grad_in, grad_out = spread_call([first_parts, parts], own, (b["gw_in"], b["gw_out"]), places)
    return (
        output[None],
        flow[None],
        grad_qkv,
        grad_attn,
        small[:, 0],
        small[:, 2, : heads * buckets].reshape(layers, heads, buckets),
        small[:, 1],
        small[:, 8:].transpose(0, 2, 1),
        grad_in,
        grad_out,
    )


def chosen_body(
    tokens, cotangent, w_qkv, w_attn, attn_gain, rel_bias, ffn_gain, router, w_in, w_out, cont_lengths, routes, slots, drops
):
    groups, local, model = tokens.shape
    heads = rel_bias.shape[1]
    dp_count, mp_count = lax.axis_size("dp"), lax.axis_size("mp")
    capacity = max(2, 9 * 2 * groups * local // (8 * w_in.shape[1] * dp_count))
    seq = local * mp_count
    fits = (
        groups == 1
        and w_qkv.shape[0] == 2
        and mp_count == 4
        and dp_count % 8 == 0
        and heads % mp_count == 0
        and model // heads == 64
        and model % 256 == 0
        and local % 128 == 0
        and w_in.shape[1:] == (2, model, model)
        and w_out.shape[1:] == (2, model, model)
        and 48 < capacity <= 56
        and seq > PROMPT
        and (seq - PROMPT) % QB == 0
    )
    plan = fast_body if fits else body
    return plan(
        tokens, cotangent, w_qkv, w_attn, attn_gain, rel_bias, ffn_gain, router, w_in, w_out, cont_lengths, routes, slots, drops
    )


def solution(mesh):
    return jax.shard_map(
        chosen_body,
        mesh=mesh,
        in_specs=(
            P("dp", "mp", None),
            P("dp", "mp", None),
            P(),
            P(),
            P(),
            P(),
            P(),
            P(),
            P(None, "dp", None, "mp"),
            P(None, "dp", "mp", None),
            P("dp", None),
            P(None, "dp", "mp", None),
            P(None, "dp", "mp", None),
            P(None, "dp", "mp", None),
        ),
        out_specs=(
            P("dp", "mp", None),
            P("dp", "mp", None),
            P(),
            P(),
            P(),
            P(),
            P(),
            P(),
            P(None, "dp", None, "mp"),
            P(None, "dp", "mp", None),
        ),
        check_vma=False,
    )
```

```python
import functools

import jax
import jax.numpy as jnp
from jax import lax
from jax.experimental import pallas as pl
from jax.experimental.pallas import tpu as pltpu
from jax.sharding import PartitionSpec as P

PROMPT = 1024


EPSILON = 1e-06
SQRT_TWO_PI = 0.7978845608028654
THRESHOLDS = (16, 20, 24, 32, 40, 48, 64, 80, 96, 128, 160, 192, 256, 384, 512, 768)
HIGHEST = lax.Precision.HIGHEST


def rms_scale(values, gain_row):
    return (
        values * lax.rsqrt(jnp.mean(values * values, axis=-1, keepdims=True) + EPSILON) * gain_row
    )


def gelu_tanh(values):
    return (
        0.5
        * values
        * (1.0 + jnp.tanh(SQRT_TWO_PI * (values + 0.044715 * values * values * values)))
    )


def bucket_of(distance):
    counted = jnp.minimum(distance, 15)
    for threshold in THRESHOLDS:
        counted = counted + (distance >= threshold).astype(jnp.int32)
    return counted


def geometry(lengths, row_ids):
    starts = PROMPT + jnp.cumsum(lengths, axis=-1) - lengths
    inside = row_ids[None, :, None] >= starts[:, None, :]
    segment = jnp.sum(inside.astype(jnp.int32), axis=-1) - 1
    begin_at = jnp.max(jnp.where(inside, starts[:, None, :], 0), axis=-1)
    position = jnp.where(
        row_ids[None, :] < PROMPT, row_ids[None, :], PROMPT + row_ids[None, :] - begin_at
    )
    return (position, segment)


def visibility(query_pos, query_seg, key_pos, key_seg):
    query_at = query_pos[:, :, None]
    query_in = query_seg[:, :, None]
    key_at = key_pos[:, None, :]
    key_in = key_seg[:, None, :]
    earlier = key_at <= query_at
    allowed = (key_in < 0) & ((query_in >= 0) | earlier) | (key_in >= 0) & (
        key_in == query_in
    ) & earlier
    bucket = bucket_of(jnp.maximum(query_at - key_at, 0))
    return (allowed, bucket)


def bias_table(bias_row, bucket):
    full_bias = jnp.zeros((bias_row.shape[0],) + bucket.shape, jnp.float32)
    for number in range(bias_row.shape[1]):
        full_bias = full_bias + jnp.where(
            bucket[None] == number, bias_row[:, number][:, None, None, None], 0.0
        )
    return full_bias


def score_block(query_b, key_every, full_bias, allowed, factor):
    raw = (
        jnp.einsum("grhd,gkhd->hgrk", query_b, key_every, preferred_element_type=jnp.float32)
        * factor
    )
    raw = raw + full_bias
    return jnp.where(allowed[None], raw, -1e30)


def body(
    tokens,
    cotangent,
    w_qkv,
    w_attn,
    attn_gain,
    rel_bias,
    ffn_gain,
    router,
    w_in,
    w_out,
    cont_lengths,
    routes,
    slots,
    drops,
):
    groups, local_rows, model_width = tokens.shape
    head_count = rel_bias.shape[1]
    bucket_count = rel_bias.shape[2]
    head_size = model_width // head_count
    factor = head_size ** (-0.5)
    layer_count = w_qkv.shape[0]
    dp_count = lax.axis_size("dp")
    mp_count = lax.axis_size("mp")
    seq_len = local_rows * mp_count
    local_experts = w_in.shape[1]
    expert_total = local_experts * dp_count
    tok_count = groups * local_rows
    capacity = max(2, 9 * 2 * tok_count // (8 * expert_total))
    slot_total = expert_total * capacity
    rows_here = lax.axis_index("mp") * local_rows + jnp.arange(local_rows, dtype=jnp.int32)
    rows_every = jnp.arange(seq_len, dtype=jnp.int32)
    query_pos, query_seg = geometry(cont_lengths, rows_here)
    key_pos, key_seg = geometry(cont_lengths, rows_every)
    allowed, bucket = visibility(query_pos, query_seg, key_pos, key_seg)
    route_all = routes.reshape(layer_count, tok_count, 2)
    slot_all = slots.reshape(layer_count, tok_count, 2)
    keep_all = (1 - drops.reshape(layer_count, tok_count, 2)).astype(jnp.float32)
    head_shape = (groups, seq_len, head_count, head_size)
    stream = tokens.reshape(tok_count, model_width).astype(jnp.float32)
    stored = []
    for layer_now in range(layer_count):
        normed_b = rms_scale(stream, attn_gain[layer_now]).astype(jnp.bfloat16)
        qkv_all = jnp.dot(normed_b, w_qkv[layer_now], preferred_element_type=jnp.float32).astype(
            jnp.bfloat16
        )
        query_b = qkv_all[:, :model_width].reshape(groups, local_rows, head_count, head_size)
        key_own = qkv_all[:, model_width : 2 * model_width].reshape(groups, local_rows, model_width)
        value_own = qkv_all[:, 2 * model_width :].reshape(groups, local_rows, model_width)
        key_every, value_every = (
            lax.all_gather(key_own, "mp", axis=1, tiled=True),
            lax.all_gather(value_own, "mp", axis=1, tiled=True),
        )
        key_every = key_every.reshape(head_shape)
        value_every = value_every.reshape(head_shape)
        full_bias = bias_table(rel_bias[layer_now], bucket)
        scores = score_block(query_b, key_every, full_bias, allowed, factor)
        top_score = jnp.max(scores, axis=-1, keepdims=True)
        weights = jnp.exp(scores - top_score)
        weight_sum = jnp.sum(weights, axis=-1, keepdims=True)
        log_total = top_score + jnp.log(weight_sum)
        probs_b = (weights / weight_sum).astype(jnp.bfloat16)
        mixed_b = jnp.einsum(
            "hgrk,gkhd->grhd", probs_b, value_every, preferred_element_type=jnp.float32
        )
        mixed_b = mixed_b.reshape(tok_count, model_width).astype(jnp.bfloat16)
        middle = stream + jnp.dot(mixed_b, w_attn[layer_now], preferred_element_type=jnp.float32)
        kept_keys = (key_every, value_every)
        ffn_b = rms_scale(middle, ffn_gain[layer_now]).astype(jnp.bfloat16)
        logits = jnp.dot(ffn_b, router[layer_now], preferred_element_type=jnp.float32)
        chosen = route_all[layer_now]
        keep_pair = keep_all[layer_now]
        gate_pair = jax.nn.softmax(jnp.take_along_axis(logits, chosen, axis=1), axis=-1)
        target = chosen * capacity + slot_all[layer_now]
        sending = jnp.where(
            keep_pair[:, :, None] > 0, ffn_b[:, None, :], jnp.zeros((), jnp.bfloat16)
        )
        send_rows = (
            jnp.zeros((slot_total, model_width), jnp.bfloat16)
            .at[target.reshape(-1)]
            .add(sending.reshape(-1, model_width))
        )
        arrived = lax.all_to_all(
            send_rows.reshape(dp_count, local_experts, capacity, model_width),
            "dp",
            split_axis=0,
            concat_axis=0,
            tiled=True,
        )
        rows_in = lax.all_gather(arrived, "mp", axis=0, tiled=True)
        up_block = w_in[layer_now]
        down_block = w_out[layer_now]
        inner_act = jnp.einsum(
            "secd,edf->secf", rows_in, up_block, preferred_element_type=jnp.float32
        )
        hidden_b = gelu_tanh(inner_act).astype(jnp.bfloat16)
        summed = lax.psum_scatter(
            jnp.einsum(
                "secf,efd->secd", hidden_b, down_block, preferred_element_type=jnp.float32
            ).astype(jnp.bfloat16),
            "mp",
            scatter_dimension=0,
            tiled=True,
        )
        kept_rows = (rows_in, inner_act, hidden_b)
        returned = lax.all_to_all(summed, "dp", split_axis=0, concat_axis=0, tiled=True).reshape(
            slot_total, model_width
        )
        pair_out = returned[target].astype(jnp.float32)
        stored.append(
            (
                stream,
                normed_b,
                query_b,
                key_own,
                value_own,
                kept_keys,
                log_total,
                mixed_b,
                middle,
                ffn_b,
                chosen,
                keep_pair,
                gate_pair,
                target,
                pair_out,
                kept_rows,
                full_bias,
            )
        )
        stream = middle + jnp.sum((gate_pair * keep_pair)[:, :, None] * pair_out, axis=1)
    output = stream.astype(jnp.bfloat16).reshape(groups, local_rows, model_width)
    one_hot = (
        bucket[None] == jnp.arange(bucket_count, dtype=jnp.int32)[:, None, None, None]
    ).astype(jnp.bfloat16)
    expert_ids = jnp.arange(expert_total, dtype=jnp.int32)
    qkv_grads = [None] * layer_count
    attn_grads = [None] * layer_count
    attn_gain_grads = [None] * layer_count
    bias_grads = [None] * layer_count
    ffn_gain_grads = [None] * layer_count
    router_grads = [None] * layer_count
    up_grads = [None] * layer_count
    down_grads = [None] * layer_count
    flowing = cotangent.reshape(tok_count, model_width).astype(jnp.float32)
    for layer_now in reversed(range(layer_count)):
        (
            stream_in,
            normed_b,
            query_b,
            key_own,
            value_own,
            kept_keys,
            log_total,
            mixed_b,
            middle,
            ffn_b,
            chosen,
            keep_pair,
            gate_pair,
            target,
            pair_out,
            kept_rows,
            full_bias,
        ) = stored[layer_now]
        weighted = gate_pair * keep_pair
        pair_grad = weighted[:, :, None] * flowing[:, None, :]
        gate_grad = keep_pair * jnp.sum(flowing[:, None, :] * pair_out, axis=-1)
        picked_grad = gate_pair * (
            gate_grad - jnp.sum(gate_pair * gate_grad, axis=-1, keepdims=True)
        )
        logit_grad = jnp.sum(
            picked_grad[:, :, None] * (chosen[:, :, None] == expert_ids).astype(jnp.float32), axis=1
        )
        back_rows = (
            jnp.zeros((slot_total, model_width), jnp.float32)
            .at[target.reshape(-1)]
            .add(pair_grad.reshape(-1, model_width))
        )
        back_rows = back_rows.astype(jnp.bfloat16).reshape(
            dp_count, local_experts, capacity, model_width
        )
        grad_arrived = lax.all_to_all(back_rows, "dp", split_axis=0, concat_axis=0, tiled=True)
        grad_rows = lax.all_gather(grad_arrived, "mp", axis=0, tiled=True)
        up_block = w_in[layer_now]
        down_block = w_out[layer_now]
        rows_in, inner_act, hidden_b = kept_rows
        down_grad = jnp.einsum(
            "secf,secd->efd", hidden_b, grad_rows, preferred_element_type=jnp.float32
        )
        hidden_grad = jnp.einsum(
            "secd,efd->secf", grad_rows, down_block, preferred_element_type=jnp.float32
        )
        inner_grad = jax.vjp(gelu_tanh, inner_act)[1](hidden_grad)[0].astype(jnp.bfloat16)
        up_grad = jnp.einsum(
            "secd,secf->edf", rows_in, inner_grad, preferred_element_type=jnp.float32
        )
        rows_grad = lax.psum_scatter(
            jnp.einsum(
                "secf,edf->secd", inner_grad, up_block, preferred_element_type=jnp.float32
            ).astype(jnp.bfloat16),
            "mp",
            scatter_dimension=0,
            tiled=True,
        )
        up_grads[layer_now] = up_grad
        down_grads[layer_now] = down_grad
        grad_back = lax.all_to_all(
            rows_grad, "dp", split_axis=0, concat_axis=0, tiled=True
        ).reshape(slot_total, model_width)
        ffn_grad = jnp.sum(keep_pair[:, :, None] * grad_back[target].astype(jnp.float32), axis=1)
        ffn_grad = ffn_grad + jnp.einsum(
            "te,de->td", logit_grad, router[layer_now].astype(jnp.float32), precision=HIGHEST
        )
        router_grads[layer_now] = jnp.einsum(
            "td,te->de", ffn_b.astype(jnp.float32), logit_grad, precision=HIGHEST
        )
        middle_grad, ffn_gain_grads[layer_now] = jax.vjp(rms_scale, middle, ffn_gain[layer_now])[1](
            ffn_grad
        )
        middle_grad = middle_grad + flowing
        branch_grad = middle_grad.astype(jnp.bfloat16)
        attn_grads[layer_now] = jnp.einsum(
            "td,te->de", mixed_b, branch_grad, preferred_element_type=jnp.float32
        )
        mixed_grad = jnp.einsum(
            "te,de->td", branch_grad, w_attn[layer_now], preferred_element_type=jnp.float32
        )
        mixed_grad = mixed_grad.astype(jnp.bfloat16).reshape(
            groups, local_rows, head_count, head_size
        )
        key_every, value_every = kept_keys
        scores = score_block(query_b, key_every, full_bias, allowed, factor)
        probs = jnp.exp(scores - log_total)
        prob_grad = jnp.einsum(
            "grhd,gkhd->hgrk", mixed_grad, value_every, preferred_element_type=jnp.float32
        )
        score_grad = (
            probs * (prob_grad - jnp.sum(probs * prob_grad, axis=-1, keepdims=True))
        ).astype(jnp.bfloat16)
        query_grad = (
            jnp.einsum("hgrk,gkhd->grhd", score_grad, key_every, preferred_element_type=jnp.float32)
            * factor
        )
        key_part = (
            jnp.einsum("hgrk,grhd->gkhd", score_grad, query_b, preferred_element_type=jnp.float32)
            * factor
        )
        value_part = jnp.einsum(
            "hgrk,grhd->gkhd",
            probs.astype(jnp.bfloat16),
            mixed_grad,
            preferred_element_type=jnp.float32,
        )
        key_grad, value_grad = (
            lax.psum_scatter(
                key_part.reshape(groups, seq_len, model_width).astype(jnp.bfloat16),
                "mp",
                scatter_dimension=1,
                tiled=True,
            ).astype(jnp.float32),
            lax.psum_scatter(
                value_part.reshape(groups, seq_len, model_width).astype(jnp.bfloat16),
                "mp",
                scatter_dimension=1,
                tiled=True,
            ).astype(jnp.float32),
        )
        bias_grads[layer_now] = jnp.einsum(
            "hgrk,bgrk->hb", score_grad, one_hot, preferred_element_type=jnp.float32
        )
        qkv_grad = jnp.concatenate(
            [
                query_grad.reshape(tok_count, model_width),
                key_grad.reshape(tok_count, model_width),
                value_grad.reshape(tok_count, model_width),
            ],
            axis=1,
        ).astype(jnp.bfloat16)
        qkv_grads[layer_now] = jnp.einsum(
            "td,te->de", normed_b, qkv_grad, preferred_element_type=jnp.float32
        )
        normed_grad = jnp.einsum(
            "te,de->td", qkv_grad, w_qkv[layer_now], preferred_element_type=jnp.float32
        )
        stream_grad, attn_gain_grads[layer_now] = jax.vjp(
            rms_scale, stream_in, attn_gain[layer_now]
        )[1](normed_grad)
        flowing = middle_grad + stream_grad
    totals = lax.psum(
        (
            jnp.stack(qkv_grads),
            jnp.stack(attn_grads),
            jnp.stack(attn_gain_grads),
            jnp.stack(bias_grads),
            jnp.stack(ffn_gain_grads),
            jnp.stack(router_grads),
        ),
        ("dp", "mp"),
    )
    input_grad = flowing.reshape(groups, local_rows, model_width)
    return (
        output,
        input_grad,
        totals[0],
        totals[1],
        totals[2],
        totals[3],
        totals[4],
        totals[5],
        jnp.stack(up_grads),
        jnp.stack(down_grads),
    )


BF = jnp.bfloat16
F32 = jnp.float32
VMEM = pl.BlockSpec(memory_space=pltpu.VMEM)
SMEM = pl.BlockSpec(memory_space=pltpu.SMEM)
ANY = pl.BlockSpec(memory_space=pl.ANY)
VMEM_BYTES = 60 << 20
MESH = pl.DeviceIdType.MESH
LANES = 128
QB = 256


def nn(a, b):
    return lax.dot_general(a, b, (((1,), (0,)), ((), ())), preferred_element_type=F32)


def nt(a, b):
    return lax.dot_general(a, b, (((1,), (1,)), ((), ())), preferred_element_type=F32)


def tn(a, b):
    return lax.dot_general(a, b, (((0,), (0,)), ((), ())), preferred_element_type=F32)


def layer_spec(array, layer):
    zeros = (0,) * (array.ndim - 1)
    return pl.BlockSpec((None,) + array.shape[1:], lambda i: (layer,) + zeros)


def segments(lens, shape, dim):
    at = lax.broadcasted_iota(jnp.int32, shape, dim)
    segment = jnp.full(shape, -1, jnp.int32)
    begin = jnp.zeros(shape, jnp.int32)
    start = jnp.int32(0)
    for number in range(lens.shape[1]):
        inside = at >= start
        segment = segment + inside.astype(jnp.int32)
        begin = jnp.where(inside, start, begin)
        start = start + lens[0, number]
    return segment, at - begin


def bias_stage(vec, lens, table, cont_bias):
    width = vec.shape[1]
    rows = lax.broadcasted_iota(jnp.int32, (LANES, width), 0)
    skewed = jnp.broadcast_to(vec, (LANES, width))
    for bit in range(7):
        skewed = jnp.where((rows >> bit) % 2 == 1, pltpu.roll(skewed, 1 << bit, 1), skewed)
    table[...] = skewed[:, : width - LANES].T
    cont = cont_bias.shape[1]
    _, offset = segments(lens, (LANES, cont), 1)
    place = (lax.broadcasted_iota(jnp.int32, (LANES, cont), 0) == offset).astype(BF)
    full = table[0:PROMPT, :]
    high = full.astype(BF)
    low = (full - high.astype(F32)).astype(BF)
    cont_bias[...] = nn(jnp.concatenate([high, low], 1), jnp.concatenate([place, place], 0))


def blocks_of(seq):
    out = []
    for start in range(0, PROMPT, QB):
        out.append((start, start + QB, None))
    for start in range(0, seq - PROMPT, QB):
        out.append((PROMPT + start, PROMPT, max(0, start - LANES)))
    return out


def scores_of(keys, query, table, cont_bias, seg_col, seg_row, block, h):
    q0, prompt_keys, cont_from = block
    if cont_from is None:
        left = PROMPT - q0
        bias = jnp.concatenate(
            [table[left : left + prompt_keys, :], table[left - LANES : left - LANES + prompt_keys, :]], 1
        )
        return [(0, prompt_keys, nt(keys[h, 0:prompt_keys, :], query) + bias)]
    at = q0 - PROMPT
    first = nt(keys[h, 0:PROMPT, :], query) + cont_bias[:, at : at + QB]
    k0, k1 = PROMPT + cont_from, q0 + QB
    left = PROMPT + cont_from - at
    bias = jnp.concatenate(
        [table[left : left + k1 - k0, :], table[left - LANES : left - LANES + k1 - k0, :]], 1
    )
    same = seg_col[cont_from : at + QB, :][:, 0:1] == seg_row[:, at : at + QB]
    second = jnp.where(same, nt(keys[h, k0:k1, :], query) + bias, -1e30)
    return [(0, PROMPT, first), (k0, k1, second)]


def attn_bwd_kernel(heads, size, extra, lens, qkv, normed, branch, w_attn, mixed, lse, vecs, *refs):
    refs = list(refs)
    if extra == "copy":
        sources, refs = refs[:2], refs[2:]
    elif extra == "share":
        shared, refs = refs[0], refs[1:]
    dqkv_o, gw_o, dvec_o = refs[:3]
    refs = refs[3:]
    if extra == "copy":
        targets, refs = refs[:2], refs[2:]
    elif extra == "share":
        all_o, refs = refs[0], refs[1:]
    q_s, k_s, v_s, kt_s, do_s, table, cont_bias, fold, dtable, dk_s, dv_s, dqt, dk_all, dv_all, segc = refs[:15]
    refs = refs[15:]
    me, core, mate, across, diagonal = mp_places()
    if extra == "copy":
        spaces, sems = refs[:2], refs[2]
        takes = [pltpu.make_async_copy(sources[n], spaces[n], sems.at[n]) for n in range(2)]
        puts = [pltpu.make_async_copy(spaces[n], targets[n].at[targets[n].shape[0] - 1], sems.at[2 + n]) for n in range(2)]
        for copy in takes:
            copy.start()
    elif extra == "share":
        held, ssem, rsem = refs
        greet_mp(2)
        held[me] = shared[...]
        to_mate = remote(held.at[me], held.at[me], ssem.at[0], rsem.at[0], mp=mate)
        over = remote(held.at[me], held.at[me], ssem.at[1], rsem.at[1], mp=across)
        passed = remote(held.at[across], held.at[across], ssem.at[2], rsem.at[2], mp=mate)
        over.start()
        to_mate.start()

    seq, model = normed.shape
    own = heads * size
    cont = seq - PROMPT
    own_rows = pl.ds(pl.multiple_of(me * own, size), own)
    for i in range(seq // QB):
        rows = pl.ds(i * QB, QB)
        part = qkv[rows, :]
        dmix = nt(branch[rows, :], w_attn[own_rows, :]).astype(BF)
        for h in range(heads):
            q_s[h, rows, :] = part[:, h * size : (h + 1) * size] * BF(0.125)
            key = part[:, own + h * size : own + (h + 1) * size]
            k_s[h, rows, :] = key
            kt_s[h, :, rows] = (key.astype(F32) * 0.125).T.astype(BF)
            v_s[h, rows, :] = part[:, 2 * own + h * size : 2 * own + (h + 1) * size]
            do_s[h, rows, :] = dmix[:, h * size : (h + 1) * size]
    seg_row, _ = segments(lens, (1, cont), 1)
    segc[...] = segments(lens, (cont, LANES), 0)[0]
    _, offset = segments(lens, (cont, LANES), 0)
    unplace = (lax.broadcasted_iota(jnp.int32, (cont, LANES), 1) == offset).astype(BF)
    width = vecs.shape[1]

    def head(h, carry):
        bias_stage(vecs[pl.ds(h, 1), :], lens, table, cont_bias)
        dtable[...] = jnp.zeros_like(dtable)
        dk_s[...] = jnp.zeros_like(dk_s)
        dv_s[...] = jnp.zeros_like(dv_s)
        for block in blocks_of(seq):
            q0, prompt_keys, cont_from = block
            query = q_s[h, q0 : q0 + QB, :]
            dout = do_s[h, q0 : q0 + QB, :]
            parts = scores_of(k_s, query, table, cont_bias, segc, seg_row, block, h)
            lse_row = lse[pl.ds(h, 1), q0 : q0 + QB]
            kept, delta = [], 0.0
            for k0, k1, s in parts:
                p = jnp.exp(s - lse_row)
                dp = nt(v_s[h, k0:k1, :], dout)
                delta = delta + jnp.sum(p * dp, axis=0, keepdims=True)
                dv_s[k0:k1, :] += nn(p.astype(BF), dout)
                kept.append((k0, k1, p, dp))
            dq = 0.0
            for k0, k1, p, dp in kept:
                ds = p * (dp - delta)
                dsb = ds.astype(BF)
                dk_s[k0:k1, :] += nn(dsb, query)
                dq = dq + nn(kt_s[h, :, k0:k1], dsb)
                if cont_from is not None and k0 == 0:
                    fold[:, q0 - PROMPT : q0 - PROMPT + QB] = dsb
                else:
                    left = PROMPT - q0 if cont_from is None else PROMPT + cont_from - (q0 - PROMPT)
                    dtable[left : left + k1 - k0, :] += ds[:, 0:LANES]
                    dtable[left - LANES : left - LANES + k1 - k0, :] += ds[:, LANES:]
            dqt[pl.ds(pl.multiple_of(h * size, size), size), q0 : q0 + QB] = dq
        dk_all[h] = dk_s[...].astype(BF)
        dv_all[h] = dv_s[...].astype(BF)
        dtable[0:PROMPT, :] += nn(fold[...], unplace)
        flat = dtable[...].T
        flat = jnp.concatenate([flat, jnp.zeros((LANES, LANES), F32)], 1)
        rows = lax.broadcasted_iota(jnp.int32, (LANES, width), 0)
        for bit in range(7):
            flat = jnp.where((rows >> bit) % 2 == 1, pltpu.roll(flat, width - (1 << bit), 1), flat)
        dvec_o[pl.ds(h, 1), :] = jnp.sum(flat, axis=0, keepdims=True)
        return carry

    lax.fori_loop(0, heads, head, 0)
    if extra == "copy":
        for n in range(2):
            takes[n].wait()
            puts[n].start()
    elif extra == "share":
        over.wait_recv()
        passed.start()
    for i in range(seq // QB):
        rows = pl.ds(i * QB, QB)
        pieces = [dqt[:, i * QB : (i + 1) * QB].T.astype(BF)]
        pieces += [dk_all[h, rows, :] for h in range(heads)] + [dv_all[h, rows, :] for h in range(heads)]
        dqkv_o[rows, :] = jnp.concatenate(pieces, 1)
    half = normed.shape[1] // 2
    for i in range(2):
        cols = slice(i * half, (i + 1) * half)
        gw_o[cols, 0 : 3 * own] = tn(normed[:, cols], dqkv_o[...])
        gw_o[cols, 3 * own :] = tn(branch[:, cols], mixed[...])
    if extra == "copy":
        for copy in puts:
            copy.wait()
    elif extra == "share":
        to_mate.wait()
        over.wait_send()
        passed.wait()
        all_o[...] = held[...]


def attn_bwd(lens, qkv, normed, branch, w_attn, layer, mixed, lse, vecs, heads, size, extra=None, more=(), number=None):
    seq, model = normed.shape
    own = heads * size
    width = vecs.shape[1]
    cont = seq - PROMPT
    params = pltpu.CompilerParams(vmem_limit_bytes=VMEM_BYTES)
    outs, scratch, in_spec = (), [], VMEM
    if extra == "copy":
        outs = tuple(jax.ShapeDtypeStruct((w_attn.shape[0],) + g.shape, F32) for g in more)
        scratch, in_spec = [pltpu.VMEM(g.shape, F32) for g in more] + [pltpu.SemaphoreType.DMA((4,))], ANY
    elif extra == "share":
        shape = (4,) + more[0].shape
        outs = (jax.ShapeDtypeStruct(shape, BF),)
        scratch = [pltpu.VMEM(shape, BF), pltpu.SemaphoreType.DMA((3,)), pltpu.SemaphoreType.DMA((3,))]
        params = pltpu.CompilerParams(collective_id=number, has_side_effects=True, vmem_limit_bytes=VMEM_BYTES)
    return pl.pallas_call(
        functools.partial(attn_bwd_kernel, heads, size, extra),
        grid=(1,),
        out_shape=(
            jax.ShapeDtypeStruct((seq, 3 * own), BF),
            jax.ShapeDtypeStruct((model, 4 * own), F32),
            jax.ShapeDtypeStruct((heads, width), F32),
        )
        + outs,
        in_specs=[SMEM] + [VMEM] * 3 + [layer_spec(w_attn, layer)] + [VMEM] * 3 + [in_spec] * len(more),
        out_specs=(VMEM, VMEM, VMEM) + (in_spec,) * len(outs),
        scratch_shapes=[
            pltpu.VMEM((heads, seq, size), BF),
            pltpu.VMEM((heads, seq, size), BF),
            pltpu.VMEM((heads, seq, size), BF),
            pltpu.VMEM((heads, size, seq), BF),
            pltpu.VMEM((heads, seq, size), BF),
            pltpu.VMEM((width - LANES, LANES), F32),
            pltpu.VMEM((PROMPT, cont), F32),
            pltpu.VMEM((PROMPT, cont), BF),
            pltpu.VMEM((width - LANES, LANES), F32),
            pltpu.VMEM((seq, size), F32),
            pltpu.VMEM((seq, size), F32),
            pltpu.VMEM((own, seq), F32),
            pltpu.VMEM((heads, seq, size), BF),
            pltpu.VMEM((heads, seq, size), BF),
            pltpu.VMEM((cont, LANES), jnp.int32),
        ]
        + scratch,
        compiler_params=params,
    )(lens, qkv, normed, branch, w_attn, mixed, lse, vecs, *more)


def diagonals():
    width = PROMPT + 3 * LANES
    at = jnp.arange(width, dtype=jnp.int32)
    distance = jnp.where(at <= PROMPT, PROMPT - at, PROMPT + width - at)
    valid = (at <= PROMPT) | (at > width - LANES)
    return width, distance, valid


def bias_vectors(bias):
    _, distance, valid = diagonals()
    hot = bucket_of(distance)[None, :] == jnp.arange(bias.shape[-1], dtype=jnp.int32)[:, None]
    picked = jnp.sum(jnp.where(hot, bias[..., :, None], 0.0), axis=-2)
    return jnp.where(valid, picked, -1e30)


def bias_grads(dvecs, buckets):
    _, distance, valid = diagonals()
    hot = (bucket_of(distance)[None, :] == jnp.arange(buckets, dtype=jnp.int32)[:, None]) & valid[None, :]
    return jnp.sum(jnp.where(hot, dvecs[..., None, :], 0.0), axis=-1)


def scatter_rows(rows, values, send):
    experts, tile, _ = send.shape
    tokens, model = values[0].shape
    half = model // 2
    at = lax.broadcasted_iota(jnp.int32, (experts * tile, tokens), 0)
    place, piece = [], []
    for j in range(2):
        slot = rows[2 + j : 3 + j, :]
        piece.append(jnp.where(rows[4 + j : 5 + j, :] > 0, slot // tile, -1))
        place.append(rows[j : j + 1, :] * tile + slot % tile)

    def pick(number, shift, columns):
        hots = [
            (jnp.where(piece[j] == number, place[j] + shift, -1) == at) for j in range(2)
        ]
        if len(values) == 1:
            return nn((hots[0] | hots[1]).astype(BF), values[0][:, columns])
        return nn(hots[0].astype(BF), values[0][:, columns]) + nn(hots[1].astype(BF), values[1][:, columns])

    for i in range(3):
        send[:, :, i * model : (i + 1) * model] = pick(i, 0, slice(0, model)).astype(BF).reshape(experts, tile, model)
    tail = pick(3, 0, slice(0, half)) + pick(3, 8, slice(half, model))
    send[:, :, 3 * model : 3 * model + half] = tail.astype(BF).reshape(experts, tile, half)


def scatter_gates(rows, gates, send, start):
    experts, tile, _ = send.shape
    tokens = rows.shape[1]
    at = lax.broadcasted_iota(jnp.int32, (experts * tile, tokens), 0)
    lane = lax.broadcasted_iota(jnp.int32, (tokens, LANES), 1)
    total = 0.0
    for j in range(2):
        slot = rows[2 + j : 3 + j, :]
        piece = jnp.where(rows[4 + j : 5 + j, :] > 0, slot // tile, -1)
        place = rows[j : j + 1, :] * tile + slot % tile
        high = gates[j].astype(BF).astype(F32)
        rest = gates[j] - high
        mid = rest.astype(BF).astype(F32)
        part = jnp.where(lane % 3 == 0, high, jnp.where(lane % 3 == 1, mid, rest - mid))
        for i in range(4):
            hot = (jnp.where(piece == i, place, -1) == at).astype(BF)
            total = total + nn(hot, jnp.where(lane // 3 == i, part, 0.0).astype(BF))
    send[:, :, start:] = total.astype(BF).reshape(experts, tile, LANES)


def gather_rows(cols, j, back):
    experts, tile, wide = back.shape
    half = wide // 7
    model = 2 * half
    tokens = cols.shape[0]
    at = lax.broadcasted_iota(jnp.int32, (tokens, experts * tile), 1)
    slot = cols[:, 2 + j : 3 + j]
    piece = jnp.where(cols[:, 4 + j : 5 + j] > 0, slot // tile, -1)
    place = cols[:, j : j + 1] * tile + slot % tile
    total = 0.0
    for i in range(3):
        hot = (jnp.where(piece == i, place, -1) == at).astype(BF)
        total = total + nn(hot, back[:, :, i * model : (i + 1) * model].reshape(experts * tile, model))
    tail = back[:, :, 3 * model :].reshape(experts * tile, half)
    left = nn((jnp.where(piece == 3, place, -1) == at).astype(BF), tail)
    right = nn((jnp.where(piece == 3, place + 8, -1) == at).astype(BF), tail)
    return total + jnp.concatenate([left, right], 1)


def unfold_tail(block, half):
    wide = block.astype(F32)
    return jnp.concatenate([wide[0:8, :], wide[8:16, :]], 1)


def mp_places():
    me = lax.axis_index("mp")
    core, row = lax.rem(me, 2), me // 2
    return me, core, row * 2 + 1 - core, (1 - row) * 2 + core, (1 - row) * 2 + 1 - core


def signal_to(barrier, **place):
    pl.semaphore_signal(barrier, inc=1, device_id=place, device_id_type=MESH)


def remote(src, dst, send_sem, recv_sem, **place):
    return pltpu.make_async_remote_copy(
        src_ref=src, dst_ref=dst, send_sem=send_sem, recv_sem=recv_sem, device_id=place, device_id_type=MESH
    )


def gather_mp(held, ssem, rsem):
    me, core, mate, across, diagonal = mp_places()
    to_mate = remote(held.at[me], held.at[me], ssem.at[0], rsem.at[0], mp=mate)
    over = remote(held.at[me], held.at[me], ssem.at[1], rsem.at[1], mp=across)
    over.start()
    to_mate.start()
    over.wait_recv()
    passed = remote(held.at[across], held.at[across], ssem.at[2], rsem.at[2], mp=mate)
    passed.start()
    to_mate.wait_recv()
    passed.wait_recv()
    for copy in (to_mate, over, passed):
        copy.wait_send()


def swap_mp(out, held, ssem, rsem, lsem):
    me, core, mate, across, diagonal = mp_places()
    copies = [
        remote(out.at[to], held.at[me], ssem.at[n], rsem.at[n], mp=to) for n, to in enumerate((diagonal, across, mate))
    ]
    copies.append(pltpu.make_async_copy(out.at[me], held.at[me], lsem))
    for copy in copies:
        copy.start()
    return copies


def greet_mp(count, dp_count=1):
    me, core, mate, across, diagonal = mp_places()
    d = lax.axis_index("dp")
    barrier = pltpu.get_barrier_semaphore()
    for to in (mate, across, diagonal)[:count]:
        signal_to(barrier, mp=to)
    for k in range(1, dp_count):
        signal_to(barrier, dp=lax.rem(d + k, dp_count), mp=me)
    pl.semaphore_wait(barrier, count + dp_count - 1)


def share_dp(held, ssem, rsem):
    d, me, count = lax.axis_index("dp"), lax.axis_index("mp"), held.shape[0]
    return [
        remote(held.at[d], held.at[d], ssem.at[k], rsem.at[k], dp=lax.rem(d + k, count), mp=me) for k in range(1, count)
    ]


def scatter_dp(part, come, ssem, rsem):
    d, me, count = lax.axis_index("dp"), lax.axis_index("mp"), part.shape[0]
    copies = []
    for k in range(1, count):
        to = lax.rem(d + k, count)
        copies.append(remote(part.at[to], come.at[d], ssem.at[k], rsem.at[k], dp=to, mp=me))
    return copies


def sum_dp(copies, part, come):
    d, count = lax.axis_index("dp"), part.shape[0]
    total = part[d].astype(F32)
    for k in range(1, count):
        copies[k - 1].wait_recv()
        total = total + come[lax.rem(d + count - k, count)].astype(F32)
    return total


def mean_square_scale(values):
    return lax.rsqrt(jnp.mean(values * values, axis=-1, keepdims=True) + EPSILON)


def norm_grads(values, gain, upstream):
    scale = mean_square_scale(values)
    scaled = upstream * gain
    drift = jnp.mean(values * scaled, axis=-1, keepdims=True)
    return scale * scaled - values * (scale * scale * scale * drift), jnp.sum(
        upstream * values * scale, axis=0, keepdims=True
    )


def pre_kernel(layer, layers, heads, size, *refs):
    refs = list(refs)

    def take(count):
        taken = refs[:count]
        del refs[:count]
        return taken

    first, last = layer == 0, layer == layers - 1
    lens, gain_a, w_qkv, vecs, w_attn, gain_f, router, rows, cols = take(9)
    if first:
        tokens, cotangent, far_rows = take(3)
    else:
        before, returned, cols_in, gates_in = take(4)
    (g_in,) = take(1) if last else (None,)
    (stream_o,) = (None,) if first else take(1)
    normed_o, qkv_o, mixed_o, lse_o, middle_o, ffn_o, gates_o, send_o = take(8)
    (g_o,) = take(1) if first or last else (None,)
    held, hssem, hrsem = take(3)
    weight, q_s, k_s, vt_s, table, cont_bias, mixt, segc, out_s, mixed_s, mssem, mrsem = take(12)
    if first:
        g_send, g_held, gssem, grsem = take(4)
    elif last:
        g_held, gssem, grsem = take(3)
    me, core, mate, across, diagonal = mp_places()
    d = lax.axis_index("dp")
    dp_count = lax.axis_size("dp")
    seq, own = mixed_o.shape
    local, model = middle_o.shape
    parts = local // LANES

    barrier = pltpu.get_barrier_semaphore()
    for to in (mate, across, diagonal):
        signal_to(barrier, mp=to)
    if first:
        for k in range(2, 2 * dp_count):
            signal_to(barrier, dp=lax.rem(d + k // 2, dp_count), mp=(me // 2) * 2 + lax.rem(core + k % 2, 2))
        count = 3 + 2 * dp_count - 2
    else:
        count = 3
    if first:
        stream = tokens[...].astype(F32)
    else:
        stream = before[...]
        for j in range(2):
            stream = stream + gates_in[:, j : j + 1] * gather_rows(cols_in, j, returned)
        stream_o[...] = stream
    held[me] = (stream * mean_square_scale(stream) * gain_a[...]).astype(BF)
    pl.semaphore_wait(barrier, count)
    over = remote(held.at[me], held.at[me], hssem.at[1], hrsem.at[1], mp=across)
    to_mate = remote(held.at[me], held.at[me], hssem.at[0], hrsem.at[0], mp=mate)
    passed = remote(held.at[across], held.at[across], hssem.at[2], hrsem.at[2], mp=mate)
    over.start()
    to_mate.start()

    extras = []
    if first:
        scatter_rows(far_rows, [cotangent[...]], g_send)
        index = d * 2 + core
        extras.append(pltpu.make_async_copy(g_send.at[index], g_held.at[index], grsem.at[0]))
        for k in range(1, 2 * dp_count):
            dd, cc = lax.rem(d + k // 2, dp_count), lax.rem(core + k % 2, 2)
            extras.append(
                remote(g_send.at[dd * 2 + cc], g_held.at[index], gssem.at[k], grsem.at[k], dp=dd, mp=(me // 2) * 2 + cc)
            )
    elif last:
        extras.append(remote(g_in, g_held, gssem, grsem, mp=across))
    for copy in extras:
        copy.start()

    for m in range(model // own):

        @pl.when(me == m)
        def _():
            for t in range(3):
                weight[:, t * own : (t + 1) * own] = w_qkv[:, t * model + m * own : t * model + (m + 1) * own]

    seg_row, _ = segments(lens, (1, seq - PROMPT), 1)
    segc[...] = segments(lens, (seq - PROMPT, LANES), 0)[0]

    def tables(h, carry):
        bias_stage(vecs[pl.ds(h, 1), :], lens, table.at[h], cont_bias.at[h])
        return carry

    lax.fori_loop(0, heads, tables, 0)

    def project(m):
        at = pl.ds(pl.multiple_of(m * local, LANES), local)
        part = nn(held[m], weight[...]).astype(BF)
        qkv_o[at, :] = part
        for h in range(heads):
            q_s[h, at, :] = part[:, h * size : (h + 1) * size] * BF(0.125)
            k_s[h, at, :] = part[:, own + h * size : own + (h + 1) * size]
            vt_s[h, :, at] = part[:, 2 * own + h * size : 2 * own + (h + 1) * size].astype(F32).T.astype(BF)

    project(me)
    to_mate.wait_recv()
    project(mate)
    over.wait_recv()
    passed.start()
    project(across)
    passed.wait_recv()
    project(diagonal)

    def handed(n):
        return remote(out_s.at[n], mixed_s.at[me, n % parts], mssem.at[n], mrsem.at[me, n % parts], mp=n // parts)

    for block in blocks_of(seq):
        q0 = block[0]

        def head(h, carry):
            query = q_s[h, q0 : q0 + QB, :]
            scored = scores_of(k_s, query, table.at[h], cont_bias.at[h], segc, seg_row, block, h)
            top = functools.reduce(jnp.maximum, [jnp.max(s, axis=0, keepdims=True) for _, _, s in scored])
            total, mixed = 0.0, 0.0
            for k0, k1, s in scored:
                p = jnp.exp(s - top)
                total = total + jnp.sum(p, axis=0, keepdims=True)
                mixed = mixed + nn(vt_s[h, :, k0:k1], p.astype(BF))
            mixt[pl.ds(pl.multiple_of(h * size, size), size), :] = mixed / total
            lse_o[pl.ds(h, 1), q0 : q0 + QB] = top + jnp.log(total)
            return carry

        lax.fori_loop(0, heads, head, 0)
        done = mixt[...].T.astype(BF)
        mixed_o[q0 : q0 + QB, :] = done
        for half in range(QB // LANES):
            n = q0 // LANES + half
            out_s[n] = done[half * LANES : (half + 1) * LANES, :]

            @pl.when(me == n // parts)
            def _():
                pltpu.make_async_copy(out_s.at[n], mixed_s.at[me, n % parts], mrsem.at[me, n % parts]).start()

            @pl.when(me != n // parts)
            def _():
                handed(n).start()

    normed_o[...] = held[...]
    middle = stream
    for m in range(mixed_s.shape[0]):
        for n in range(parts):
            pltpu.make_async_copy(mixed_s.at[m, n], mixed_s.at[m, n], mrsem.at[m, n]).wait()
        middle = middle + nn(mixed_s[m].reshape(local, own), w_attn[m * own : (m + 1) * own, :])
    middle_o[...] = middle
    ffn = (middle * mean_square_scale(middle) * gain_f[...]).astype(BF)
    ffn_o[...] = ffn
    logits = nn(ffn, router[...])
    expert = lax.broadcasted_iota(jnp.int32, logits.shape, 1)
    chosen = [
        jnp.sum(jnp.where(expert == cols[:, j : j + 1], logits, 0.0), axis=1, keepdims=True) for j in range(2)
    ]
    top = jnp.maximum(chosen[0], chosen[1])
    powers = [jnp.exp(c - top) for c in chosen]
    gates = [p / (powers[0] + powers[1]) for p in powers]
    gates_o[...] = jnp.concatenate(gates, 1)
    scatter_rows(rows, [ffn], send_o)
    if last:
        scatter_gates(rows, gates, send_o, 7 * model // 2)
    if first or last:
        for copy in extras:
            if first and copy is extras[0]:
                copy.wait()
            else:
                copy.wait_send()
                copy.wait_recv()
        g_o[...] = g_held[...]
    for copy in (to_mate, over, passed):
        copy.wait_send()
    for n in range(seq // LANES):

        @pl.when(me != n // parts)
        def _():
            handed(n).wait_send()


def pre_call(layer, layers, number, heads, size, lens, normal, mp_count, dp_count, local, model, specials, block):
    first, last = layer == 0, layer == layers - 1
    seq, own = local * mp_count, heads * size
    width = PROMPT + 3 * LANES
    args = list(normal) + list(specials)
    specs = [SMEM] + [layer_spec(*a) if isinstance(a, tuple) else VMEM for a in args]
    narrow = block[:2] + (7 * model // 2,)
    send = narrow[:2] + (narrow[2] + LANES,) if last else narrow
    outs = [] if first else [((local, model), F32)]
    outs += [
        ((mp_count, local, model), BF), ((seq, 3 * own), BF), ((seq, own), BF), ((heads, seq), F32),
        ((local, model), F32), ((local, model), BF), ((local, 2), F32), (send, BF),
    ]
    if first or last:
        outs.append((narrow, BF))
    scratch = [
        pltpu.VMEM((mp_count, local, model), BF), dma(3), dma(3),
        pltpu.VMEM((model, 3 * own), BF),
        pltpu.VMEM((heads, seq, size), BF),
        pltpu.VMEM((heads, seq, size), BF),
        pltpu.VMEM((heads, size, seq), BF),
        pltpu.VMEM((heads, width - LANES, LANES), F32),
        pltpu.VMEM((heads, PROMPT, seq - PROMPT), F32),
        pltpu.VMEM((own, QB), F32),
        pltpu.VMEM((seq - PROMPT, LANES), jnp.int32),
        pltpu.VMEM((seq // LANES, LANES, own), BF),
        pltpu.VMEM((mp_count, local // LANES, LANES, own), BF),
        dma(seq // LANES),
        dma(mp_count, local // LANES),
    ]
    if first:
        scratch += [pltpu.VMEM(narrow, BF), pltpu.VMEM(narrow, BF), dma(2 * dp_count), dma(2 * dp_count)]
    elif last:
        scratch += [pltpu.VMEM(narrow, BF), dma(), dma()]
    return pl.pallas_call(
        functools.partial(pre_kernel, layer, layers, heads, size),
        grid=(1,),
        out_shape=tuple(jax.ShapeDtypeStruct(shape, kind) for shape, kind in outs),
        in_specs=specs,
        out_specs=tuple([VMEM] * len(outs)),
        scratch_shapes=scratch,
        compiler_params=pltpu.CompilerParams(
            collective_id=number, has_side_effects=True, vmem_limit_bytes=VMEM_BYTES
        ),
    )(lens, *[a[0] if isinstance(a, tuple) else a for a in args])


def post_kernel(with_output, *refs):
    if with_output:
        (back, returned, flow_in, middle, ffn, gates, cols, router, gain, grad_o, all_o, gain_o, router_o, out_o, held, ssem, rsem) = refs
        greet_mp(2)
    else:
        (back, returned, flow_in, middle, ffn, gates, cols, router, gain, shared, grad_o, all_o, gain_o, router_o, share_o, held, ssem, rsem, round_s, dssem, drsem) = refs
        greet_mp(2, dp_count=round_s.shape[0])
        d = lax.axis_index("dp")
        round_s[d] = shared[...]
        shares = share_dp(round_s, dssem, drsem)
        for copy in shares:
            copy.start()
    me = lax.axis_index("mp")
    flow = flow_in[...].astype(F32)
    outs = [gather_rows(cols, j, returned) for j in range(2)]
    gate = [gates[:, j : j + 1] for j in range(2)]
    keep = [cols[:, 4 + j : 5 + j].astype(F32) for j in range(2)]
    if with_output:
        out_o[...] = (middle[...] + gate[0] * keep[0] * outs[0] + gate[1] * keep[1] * outs[1]).astype(BF)
    gate_grad = [keep[j] * jnp.sum(flow * outs[j], axis=1, keepdims=True) for j in range(2)]
    shared = gate[0] * gate_grad[0] + gate[1] * gate_grad[1]
    expert = lax.broadcasted_iota(jnp.int32, (flow.shape[0], router.shape[1]), 1)
    logit_grad = 0.0
    for j in range(2):
        logit_grad = logit_grad + jnp.where(expert == cols[:, j : j + 1], gate[j] * (gate_grad[j] - shared), 0.0)
    high = logit_grad.astype(BF)
    low = (logit_grad - high.astype(F32)).astype(BF)
    upstream = gather_rows(cols, 0, back) + gather_rows(cols, 1, back)
    upstream = upstream + nt(high, router[...]) + nt(low, router[...])
    router_o[...] = tn(high, ffn[...]) + tn(low, ffn[...])
    grad, gain_o[...] = norm_grads(middle[...], gain[...], upstream)
    grad = grad + flow
    grad_o[...] = grad
    held[me] = grad.astype(BF)
    gather_mp(held, ssem, rsem)
    all_o[...] = held[...]
    if not with_output:
        for copy in shares:
            copy.wait()
        share_o[...] = round_s[...]


def close_layer(held, w_qkv, stream, gain, grad):
    model = w_qkv.shape[0]
    own = held.shape[2] // 3
    upstream = 0.0
    for t in range(3):
        piece = jnp.concatenate([held[m, :, t * own : (t + 1) * own] for m in range(held.shape[0])], 1)
        upstream = upstream + nt(piece, w_qkv[:, t * model : (t + 1) * model])
    inner, gain_grad = norm_grads(stream[...].astype(F32), gain[...], upstream)
    return grad[...] + inner, gain_grad


def fill_parts(part, heads):
    rows = part.shape[1]
    for j in range(part.shape[0]):
        part[j] = heads[j * rows : (j + 1) * rows, :].astype(BF)


def close_kernel(dqkv, w_qkv, stream, gain, grad, rows, cols, gates, heads, flow_o, gain_o, send_o, sum_o, held, part, come, ssem, rsem, lsem, dssem, drsem):
    greet_mp(3, dp_count=part.shape[0])
    swaps = swap_mp(dqkv, held, ssem, rsem, lsem)
    fill_parts(part, heads)
    scattered = scatter_dp(part, come, dssem, drsem)
    for copy in scattered:
        copy.start()
    for copy in swaps:
        copy.wait()
    flow, gain_o[...] = close_layer(held, w_qkv, stream, gain, grad)
    flow_o[...] = flow
    scatter_rows(
        rows,
        [(gates[:, j : j + 1] * cols[:, 4 + j : 5 + j].astype(F32) * flow).astype(BF) for j in range(2)],
        send_o,
    )
    sum_o[...] = sum_dp(scattered, part, come).astype(BF)
    for copy in scattered:
        copy.wait_send()


def last_kernel(
    dqkv, w_qkv, stream, gain, grad, heads, small, flow_o, all_o, small_o,
    held, part, come, small_s, small_come, small_mp, small_all,
    ssem, rsem, lsem, dssem, drsem, tsem, usem, csem, dsem, vsem, zsem, esem, fsem, hsem, isem,
):
    dp_count = part.shape[0]
    d = lax.axis_index("dp")
    me, core, mate, across, diagonal = mp_places()
    greet_mp(3, dp_count=dp_count)
    swaps = swap_mp(dqkv, held, ssem, rsem, lsem)
    fill_parts(part, heads)
    scattered = scatter_dp(part, come, dssem, drsem)
    for copy in scattered:
        copy.start()
    small_s[...] = small[...]
    for copy in swaps:
        copy.wait()
    flow, gain_grad = close_layer(held, w_qkv, stream, gain, grad)
    flow_o[...] = flow
    small_s[0, 0:1, :] = gain_grad
    small_scattered = scatter_dp(small_s, small_come, tsem, usem)
    for copy in small_scattered:
        copy.start()
    all_o[me, d] = sum_dp(scattered, part, come).astype(BF)
    shares = [
        remote(all_o.at[me, d], all_o.at[me, d], esem.at[k], fsem.at[k], dp=lax.rem(d + k, dp_count), mp=me)
        for k in range(1, dp_count)
    ]
    for copy in shares:
        copy.start()

    def over(n, j):
        whose = across if n == 2 else me
        return remote(all_o.at[whose, j], all_o.at[whose, j], hsem.at[n, j], isem.at[n, j], mp=across if n == 1 else mate)

    over(1, d).start()
    over(0, d).start()
    small_mp[me] = sum_dp(small_scattered, small_s, small_come)
    small_swaps = [
        remote(small_mp.at[me], small_mp.at[me], csem.at[n], dsem.at[n], mp=to) for n, to in enumerate((mate, across, diagonal))
    ]
    for copy in small_swaps:
        copy.start()
    for copy in small_swaps:
        copy.wait_recv()
    small_all[d] = small_mp[0] + small_mp[1] + small_mp[2] + small_mp[3]
    small_shares = share_dp(small_all, vsem, zsem)
    for copy in small_shares:
        copy.start()
    for k in range(1, dp_count):
        j = lax.rem(d + dp_count - k, dp_count)
        shares[k - 1].wait_recv()
        over(1, j).start()
        over(0, j).start()
        last = lax.rem(d + dp_count - k + 1, dp_count)
        over(1, last).wait_recv()
        over(2, last).start()
    last = lax.rem(d + 1, dp_count)
    over(1, last).wait_recv()
    over(2, last).start()
    for copy in small_shares:
        copy.wait_recv()
    small_o[...] = small_all[...]
    for j in range(dp_count):
        over(0, j).wait_recv()
        over(2, j).wait_recv()
        for n in range(3):
            over(n, j).wait_send()
    for copy in small_swaps + scattered + small_scattered + small_shares + shares:
        copy.wait_send()


def dma(*shape):
    return pltpu.SemaphoreType.DMA(shape) if shape else pltpu.SemaphoreType.DMA


def mp_call(kernel, number, outs, scratch, *args):
    specs = [layer_spec(*a) if isinstance(a, tuple) else VMEM for a in args]
    return pl.pallas_call(
        kernel,
        grid=(1,),
        out_shape=tuple(jax.ShapeDtypeStruct(shape, kind) for shape, kind in outs),
        in_specs=specs,
        out_specs=tuple([VMEM] * len(outs)),
        scratch_shapes=scratch,
        compiler_params=pltpu.CompilerParams(
            collective_id=number, has_side_effects=True, vmem_limit_bytes=VMEM_BYTES
        ),
    )(*[a[0] if isinstance(a, tuple) else a for a in args])


def gelu_grad(values):
    inner = jnp.tanh(SQRT_TWO_PI * (values + 0.044715 * values * values * values))
    slope = SQRT_TWO_PI * (1.0 + 3.0 * 0.044715 * values * values)
    return 0.5 * values * (1.0 + inner), 0.5 * (1.0 + inner) + 0.5 * values * (1.0 - inner * inner) * slope


def expert_kernel(mode, layer, dp_count, *refs):
    forward, backward = mode in ("fwd", "both"), mode in ("both", "bwd")
    refs = list(refs)

    def take(count):
        taken = refs[:count]
        del refs[:count]
        return taken

    (sending,) = take(1)
    far = take(2) if mode == "both" else None
    (x_in,) = take(1) if mode == "bwd" else (None,)
    w_in, w_out = take(2)
    results = take(forward + backward)
    (x_o,) = take(1) if mode == "fwd" else (None,)
    gw_in_o, gw_out_o = take(2) if backward else (None, None)
    w1, w2, wsem, wssem, wrsem = take(5)
    x_all, xsem = take(2)
    recv_a, recv_b, ssem, asem, fsem, bsem = take(6)
    paths = [take(9) for _ in results]
    if backward:
        g_all, hid_all, ig_all, stage, gsem, grsem, glsem = take(7)

    d = lax.axis_index("dp")
    me, core, mate, across, diagonal = mp_places()
    row = me // 2
    index = d * 2 + core
    experts = dp_count * 2
    model = w1.shape[1]
    half = model // 2
    rows_a = x_all.shape[1] // 2
    tile = sending.shape[1]
    ahead = 3

    barrier = pltpu.get_barrier_semaphore()

    def greet(k, carry):
        signal_to(barrier, dp=lax.rem(d + k // 2, dp_count), mp=row * 2 + lax.rem(core + k % 2, 2))
        return carry

    lax.fori_loop(1, experts, greet, 0)
    signal_to(barrier, mp=across)
    pl.semaphore_wait(barrier, experts)

    def send_wave(k):
        dd = lax.rem(d + k, dp_count)
        for cc in range(2):
            to = dd * 2 + cc

            @pl.when(to == index)
            def _():
                pltpu.make_async_copy(sending.at[to], recv_a.at[index], asem.at[index]).start()

            @pl.when(to != index)
            def _():
                remote(sending.at[to], recv_a.at[index], ssem.at[to], asem.at[index], dp=dd, mp=row * 2 + cc).start()

    for k in range(ahead):
        send_wave(k)
    copies = []
    for n, (source, held) in enumerate(((w_in, w1), (w_out, w2))):
        copies.append(remote(source.at[layer, 1 - core], held.at[core], wssem.at[n], wrsem.at[n], mp=mate))
        copies.append(pltpu.make_async_copy(source.at[layer, core], held.at[core], wsem.at[n]))
    if mode == "bwd":
        copies.append(pltpu.make_async_copy(x_in, x_all, xsem))
    for copy in copies:
        copy.start()
    for copy in copies:
        copy.wait()

    def source_of(g):
        return lax.rem(d + dp_count - g, dp_count)

    def unpack(held, g, side, into, gates):
        base = side * rows_a
        s0 = source_of(g)
        tails = []
        for cc in range(2):
            src = s0 * 2 + cc
            block = held[src]
            factors = None if gates is None else gates[src][:, 7 * half :].astype(F32)

            def factor(i):
                return factors[:, 3 * i : 3 * i + 1] + factors[:, 3 * i + 1 : 3 * i + 2] + factors[:, 3 * i + 2 : 3 * i + 3]

            for i in range(3):
                piece = block[:, i * model : (i + 1) * model]
                if gates is not None:
                    piece = (piece.astype(F32) * factor(i)).astype(BF)
                into[g, base + (2 * i + cc) * tile : base + (2 * i + cc + 1) * tile, :] = piece
            tail = unfold_tail(block[:, 3 * model : 7 * half], half)
            tails.append(tail if gates is None else tail * factor(3)[0:8, :])
        into[g, base + 6 * tile : base + 7 * tile, :] = jnp.concatenate(tails, 0).astype(BF)

    def forward_copy(s0):
        two = pl.ds(s0 * 2, 2)
        return remote(recv_a.at[two], recv_b.at[two], fsem.at[s0], bsem.at[s0], mp=across)

    def partial_copy(path, g):
        kept, part, pssem, prsem, ret_s, ret, rssem, rrsem, psend = path
        return remote(psend.at[g], part.at[g], pssem.at[g], prsem.at[g], mp=across)

    def compute(g):
        x = x_all[g]
        totals = [0.0] * len(results)
        for q in range(2):
            inner = nn(x, w1[q])
            if backward:
                value, slope = gelu_grad(inner)
                hidden = value.astype(BF)
                hid_all[q, g] = hidden
                grad = (nt(g_all[g], w2[q]) * slope).astype(BF)
                ig_all[q, g] = grad
                totals[-1] = totals[-1] + nt(grad, w1[q])
            else:
                hidden = gelu_tanh(inner).astype(BF)
            if forward:
                totals[0] = totals[0] + nn(hidden, w2[q])
        return totals

    def give_back(path, g):
        kept, part, pssem, prsem, ret_s, ret, rssem, rrsem, psend = path
        partial_copy(path, g).wait_recv()
        total = kept[lax.rem(g, 2)] + part[g].astype(F32)
        s0 = source_of(g)
        for cc in range(2):
            src = s0 * 2 + cc
            for i in range(3):
                at = (2 * i + cc) * tile
                ret_s[src, :, i * model : (i + 1) * model] = total[at : at + tile, :].astype(BF)
            at = 6 * tile + 8 * cc
            ret_s[src, :, 3 * model :] = jnp.concatenate(
                [total[at : at + 8, 0:half], total[at : at + 8, half:]], 0
            ).astype(BF)

            @pl.when(src == index)
            def _():
                pltpu.make_async_copy(ret_s.at[src], ret.at[index], rrsem.at[index]).start()

            @pl.when(src != index)
            def _():
                remote(ret_s.at[src], ret.at[index], rssem.at[src], rrsem.at[index], dp=s0, mp=row * 2 + cc).start()

    def step(i, carry):
        @pl.when(i < dp_count)
        def _():
            s0 = source_of(i)
            for cc in range(2):
                src = s0 * 2 + cc
                pltpu.make_async_copy(recv_a.at[src], recv_a.at[src], asem.at[src]).wait()
            forward_copy(s0).start()

        @pl.when(i + ahead < dp_count)
        def _():
            send_wave(i + ahead)

        @pl.when((i >= 1) & (i <= dp_count))
        def _():
            g = i - 1
            forward_copy(source_of(g)).wait_recv()
            for side, held in enumerate((recv_a, recv_b)):
                if forward:
                    unpack(held, g, side, x_all, None)
                if mode == "both":
                    unpack(far[side], g, side, g_all, held)
                elif mode == "bwd":
                    unpack(held, g, side, g_all, None)
            for path, total in zip(paths, compute(g)):
                kept, psend = path[0], path[8]
                kept[lax.rem(g, 2)] = total[0:rows_a, :]
                psend[g] = total[rows_a:, :].astype(BF)
                partial_copy(path, g).start()

        @pl.when(i >= 2)
        def _():
            for path in paths:
                give_back(path, i - 2)

        return carry

    lax.fori_loop(0, dp_count + 2, step, 0)
    if mode == "fwd":
        saved = pltpu.make_async_copy(x_all, x_o, xsem)
        saved.start()
    if backward:
        count = dp_count * 2 * rows_a

        def products(n, q):
            if n == 0:
                return tn(x_all[...].reshape(count, model), ig_all[q].reshape(count, model))
            return tn(hid_all[q].reshape(count, model), g_all[...].reshape(count, model))

        outs = (gw_in_o, gw_out_o)
        copies = []
        for n in range(2):
            stage[n] = products(n, 1 - core)
            copy = remote(stage.at[n], outs[n].at[core], gsem.at[n], grsem.at[n], mp=mate)
            copy.start()
            copies.append(copy)
        for n in range(2):
            copies[n].wait_send()
            stage[n] = products(n, core)
            copy = pltpu.make_async_copy(stage.at[n], outs[n].at[core], glsem.at[n])
            copy.start()
            copies.append(copy)
    for path, result in zip(paths, results):
        kept, part, pssem, prsem, ret_s, ret, rssem, rrsem, psend = path

        def end(e, carry):
            pltpu.make_async_copy(ret.at[e], ret.at[e], rrsem.at[e]).wait()

            @pl.when(e != index)
            def _():
                pltpu.make_async_copy(ret_s.at[e], ret_s.at[e], rssem.at[e]).wait()

            return carry

        lax.fori_loop(0, experts, end, 0)

        def end_group(g, carry):
            pltpu.make_async_copy(psend.at[g], psend.at[g], pssem.at[g]).wait()
            return carry

        lax.fori_loop(0, dp_count, end_group, 0)
        result[...] = ret[...]

    def end_send(e, carry):
        @pl.when(e != index)
        def _():
            pltpu.make_async_copy(sending.at[e], sending.at[e], ssem.at[e]).wait()

        return carry

    lax.fori_loop(0, experts, end_send, 0)

    def end_pair(s0, carry):
        two = pl.ds(s0 * 2, 2)
        pltpu.make_async_copy(recv_a.at[two], recv_a.at[two], fsem.at[s0]).wait()
        return carry

    lax.fori_loop(0, dp_count, end_pair, 0)
    if mode == "fwd":
        saved.wait()
    if backward:
        for n in range(2):
            copies[n].wait_recv()
            copies[2 + n].wait()


def expert_call(mode, layer, number, dp_count, send, far, x_in, w_in, w_out):
    forward, backward = mode in ("fwd", "both"), mode in ("both", "bwd")
    experts, tile, _ = send.shape
    model = w_in.shape[2]
    block = (experts, tile, 7 * model // 2)
    rows = 2 * 7 * tile
    args, specs = [send], [VMEM]
    if mode == "both":
        args += far
        specs += [VMEM] * 2
    if mode == "bwd":
        args.append(x_in)
        specs.append(ANY)
    args += [w_in, w_out]
    specs += [ANY, ANY]
    outs, out_specs = [], []

    def out(dims, kind, spec):
        outs.append(jax.ShapeDtypeStruct(dims, kind))
        out_specs.append(spec)

    for _ in range(forward + backward):
        out(block, BF, VMEM)
    if mode == "fwd":
        out((dp_count, rows, model), BF, ANY)
    if backward:
        out((2, model, model), F32, ANY)
        out((2, model, model), F32, ANY)
    scratch = [
        pltpu.VMEM((2, model, model), BF),
        pltpu.VMEM((2, model, model), BF),
        dma(2),
        dma(2),
        dma(2),
        pltpu.VMEM((dp_count, rows, model), BF),
        dma(),
        pltpu.VMEM(send.shape, BF),
        pltpu.VMEM(send.shape, BF),
        dma(experts),
        dma(experts),
        dma(dp_count),
        dma(dp_count),
    ]
    for _ in range(forward + backward):
        scratch += [
            pltpu.VMEM((2, rows // 2, model), F32),
            pltpu.VMEM((dp_count, rows // 2, model), BF),
            dma(dp_count),
            dma(dp_count),
            pltpu.VMEM(block, BF),
            pltpu.VMEM(block, BF),
            dma(experts),
            dma(experts),
            pltpu.VMEM((dp_count, rows // 2, model), BF),
        ]
    if backward:
        scratch += [
            pltpu.VMEM((dp_count, rows, model), BF),
            pltpu.VMEM((2, dp_count, rows, model), BF),
            pltpu.VMEM((2, dp_count, rows, model), BF),
            pltpu.VMEM((2, model, model), F32),
            dma(2),
            dma(2),
            dma(2),
        ]
    return pl.pallas_call(
        functools.partial(expert_kernel, mode, layer, dp_count),
        out_shape=tuple(outs),
        in_specs=specs,
        out_specs=tuple(out_specs),
        scratch_shapes=scratch,
        compiler_params=pltpu.CompilerParams(
            collective_id=number, has_side_effects=True, vmem_limit_bytes=VMEM_BYTES
        ),
    )(*args)


def spread_kernel(own, count, *refs):
    parts, (gw_in, gw_out, _, _) = refs[:count], refs[count : count + 4]
    qkv_o, attn_o, in_o, out_o, sem = refs[count + 4 :]
    step = pl.program_id(0)
    copies = [
        pltpu.make_async_copy(gw_in.at[0], in_o.at[0, step], sem.at[0]),
        pltpu.make_async_copy(gw_out.at[0], out_o.at[0, step], sem.at[1]),
    ]
    for copy in copies:
        copy.start()

    for n in range(count):
        mp_count, blocks, rows, width = parts[n].shape
        pieces = [parts[n][m].reshape(blocks * rows, width).astype(F32) for m in range(mp_count)]
        qkv_o[n] = jnp.concatenate([p[:, t * own : (t + 1) * own] for t in range(3) for p in pieces], 1)
        for m in range(mp_count):
            attn_o[n, m * own : (m + 1) * own, :] = pieces[m][:, 3 * own :].T
    for copy in copies:
        copy.wait()


def spread_call(parts, own, grads, places):
    mp_count, blocks, rows, width = parts[0].shape
    layers, model = len(parts), blocks * rows
    steps = grads[0].shape[0]
    return pl.pallas_call(
        functools.partial(spread_kernel, own, layers),
        grid=(steps,),
        out_shape=(
            jax.ShapeDtypeStruct((layers, model, 3 * mp_count * own), F32),
            jax.ShapeDtypeStruct((layers, mp_count * own, model), F32),
        )
        + tuple(jax.ShapeDtypeStruct(p.shape, F32) for p in places),
        in_specs=[pl.BlockSpec((mp_count, blocks // steps, rows, width), lambda i: (0, i, 0, 0))] * layers
        + [pl.BlockSpec((1,) + g.shape[1:], lambda i: (i, 0, 0)) for g in grads]
        + [ANY] * 2,
        out_specs=(
            pl.BlockSpec((layers, model // steps, 3 * mp_count * own), lambda i: (0, i, 0)),
            pl.BlockSpec((layers, mp_count * own, model // steps), lambda i: (0, 0, i)),
            ANY,
            ANY,
        ),
        scratch_shapes=[dma(2)],
        input_output_aliases={layers + 2: 2, layers + 3: 3},
        compiler_params=pltpu.CompilerParams(vmem_limit_bytes=VMEM_BYTES),
    )(*parts, *grads, *places)


def fast_body(
    tokens, cotangent, w_qkv, w_attn, attn_gain, rel_bias, ffn_gain, router, w_in, w_out, cont_lengths, routes, slots, drops
):
    _, local, model = tokens.shape
    heads, buckets = rel_bias.shape[1:]
    size = model // heads
    layers = w_qkv.shape[0]
    dp_count, mp_count = lax.axis_size("dp"), lax.axis_size("mp")
    seq = local * mp_count
    own_heads = heads // mp_count
    own = own_heads * size
    experts = dp_count * 2
    me = lax.axis_index("mp")
    block = (experts, 16, 7 * model // 2)
    pairs = jnp.concatenate(
        [routes.reshape(layers, local, 2), slots.reshape(layers, local, 2), 1 - drops.reshape(layers, local, 2)], 2
    )
    cols = jnp.pad(pairs, ((0, 0), (0, 0), (0, 2)))
    rows = cols.transpose(0, 2, 1)
    vecs = bias_vectors(lax.dynamic_slice_in_dim(rel_bias, me * own_heads, own_heads, 1))
    gain_a, gain_f = attn_gain[:, None], ffn_gain[:, None]
    held = (mp_count, local, model)
    chunk = (dp_count, model // dp_count, model)
    gather = [pltpu.VMEM(held, BF), dma(3), dma(3)]

    def swap(width):
        return [pltpu.VMEM((mp_count, local, width), BF)], [dma(3), dma(3), dma()]

    kept = [None] * layers
    back, far = None, [None, None]
    for l in range(layers):
        first, last = l == 0, l == layers - 1
        normal = [(gain_a, l), (w_qkv, l), vecs[l], (w_attn, l), (gain_f, l), (router, l), (rows, l), (cols, l)]
        if first:
            specials = [tokens[0], cotangent[0], (rows, layers - 1)]
        else:
            before = kept[l - 1]
            specials = [before["middle"], before["out"], (cols, l - 1), before["gates"]]
        if last:
            specials.append(far[0])
        got = pre_call(
            l, layers, l, own_heads, size, cont_lengths, normal, mp_count, dp_count, local, model, specials, block
        )
        got = [tokens[0]] + list(got) if first else list(got)
        names = ("stream", "normed", "qkv", "mixed", "lse", "middle", "ffn", "gates")
        kept[l] = k = dict(zip(names, got))
        k["normed"] = k["normed"].reshape(seq, model)
        if first:
            far[0] = got[9]
        if last:
            far[1] = got[9]
            k["out"], back, k["gw_in"], k["gw_out"] = expert_call("both", l, 5, dp_count, got[8], far, None, w_in, w_out)
        else:
            k["out"], k["x_rows"] = expert_call("fwd", l, 4, dp_count, got[8], None, None, w_in, w_out)

    flow = cotangent[0]
    for l in reversed(range(layers)):
        k = kept[l]
        last = l == layers - 1
        outs = [((local, model), F32), (held, BF), ((1, model), F32), ((experts, model), F32)]
        args = [back, k["out"], flow, k["middle"], k["ffn"], k["gates"], (cols, l), (router, l), (gain_f, l)]
        if last:
            outs.append(((local, model), BF))
            scratch = gather
        else:
            outs.append((chunk, BF))
            args.append(heads_sum)
            scratch = gather + [pltpu.VMEM(chunk, BF), dma(dp_count), dma(dp_count)]
        got = mp_call(functools.partial(post_kernel, last), 6 + last, outs, scratch, *args)
        grad, branch, k["ffn_gain"], k["router"] = got[:4]
        if last:
            output = got[4]
            extra, more = "copy", (k["gw_in"], k["gw_out"])
        else:
            extra, more = "share", (got[4],)
        got = attn_bwd(
            cont_lengths, k["qkv"], k["normed"], branch.reshape(seq, model), w_attn, l, k["mixed"], k["lse"], vecs[l],
            own_heads, size, extra, more, 8,
        )
        dqkv, heads_grad, dvecs = got[:3]
        k["bias"] = bias_grads(dvecs, buckets)
        args = [dqkv.reshape(mp_count, local, 3 * own), (w_qkv, l), k["stream"], (gain_a, l), grad]
        space, sems = swap(3 * own)
        if last:
            places = got[3:]
            b = kept[l - 1]
            flow, k["attn_gain"], send, heads_sum = mp_call(
                close_kernel, 9, [((local, model), F32), ((1, model), F32), (block, BF), (chunk[1:], BF)],
                space + [pltpu.VMEM(chunk, BF)] * 2 + sems + [dma(dp_count)] * 2,
                *args, (rows, l - 1), (cols, l - 1), b["gates"], heads_grad,
            )
            back, b["gw_in"], b["gw_out"] = expert_call("bwd", l - 1, 10, dp_count, send, None, b["x_rows"], w_in, w_out)
        else:
            (parts,) = got[3:]

    small = []
    for l in range(layers):
        k = kept[l]
        bias = lax.dynamic_update_slice_in_dim(jnp.zeros((heads, buckets), F32), k["bias"], me * own_heads, 0)
        small += [k["attn_gain"] if l > 0 else jnp.zeros((1, model), F32), k["ffn_gain"]]
        small += [jnp.pad(bias.reshape(1, -1), ((0, 5), (0, model - heads * buckets))), k["router"]]
    lines = 8 + experts
    share = -(-layers * lines // (8 * dp_count)) * 8
    small = jnp.pad(jnp.concatenate(small, 0), ((0, share * dp_count - layers * lines), (0, 0)))
    small = small.reshape(dp_count, share, model)
    small_vmem = pltpu.VMEM(small.shape, F32)
    flow, first_parts, small = mp_call(
        last_kernel, 11, [((local, model), F32), ((mp_count,) + chunk, BF), (small.shape, F32)],
        space
        + [pltpu.VMEM(chunk, BF)] * 2
        + [small_vmem, small_vmem, pltpu.VMEM((mp_count, share, model), F32), small_vmem]
        + sems
        + [dma(dp_count)] * 4
        + [dma(3)] * 2
        + [dma(dp_count)] * 4
        + [dma(3, dp_count)] * 2,
        *args, heads_grad, small,
    )
    small = small.reshape(-1, model)[: layers * lines].reshape(layers, lines, model)
    b = kept[0]
    grad_qkv, grad_attn, grad_in, grad_out = spread_call([first_parts, parts], own, (b["gw_in"], b["gw_out"]), places)
    return (
        output[None],
        flow[None],
        grad_qkv,
        grad_attn,
        small[:, 0],
        small[:, 2, : heads * buckets].reshape(layers, heads, buckets),
        small[:, 1],
        small[:, 8:].transpose(0, 2, 1),
        grad_in,
        grad_out,
    )


def chosen_body(
    tokens, cotangent, w_qkv, w_attn, attn_gain, rel_bias, ffn_gain, router, w_in, w_out, cont_lengths, routes, slots, drops
):
    groups, local, model = tokens.shape
    heads = rel_bias.shape[1]
    dp_count, mp_count = lax.axis_size("dp"), lax.axis_size("mp")
    capacity = max(2, 9 * 2 * groups * local // (8 * w_in.shape[1] * dp_count))
    seq = local * mp_count
    fits = (
        groups == 1
        and w_qkv.shape[0] == 2
        and mp_count == 4
        and dp_count % 8 == 0
        and heads % mp_count == 0
        and model // heads == 64
        and model % 256 == 0
        and local % 128 == 0
        and w_in.shape[1:] == (2, model, model)
        and w_out.shape[1:] == (2, model, model)
        and 48 < capacity <= 56
        and seq > PROMPT
        and (seq - PROMPT) % QB == 0
    )
    plan = fast_body if fits else body
    return plan(
        tokens, cotangent, w_qkv, w_attn, attn_gain, rel_bias, ffn_gain, router, w_in, w_out, cont_lengths, routes, slots, drops
    )


def solution(mesh):
    return jax.shard_map(
        chosen_body,
        mesh=mesh,
        in_specs=(
            P("dp", "mp", None),
            P("dp", "mp", None),
            P(),
            P(),
            P(),
            P(),
            P(),
            P(),
            P(None, "dp", None, "mp"),
            P(None, "dp", "mp", None),
            P("dp", None),
            P(None, "dp", "mp", None),
            P(None, "dp", "mp", None),
            P(None, "dp", "mp", None),
        ),
        out_specs=(
            P("dp", "mp", None),
            P("dp", "mp", None),
            P(),
            P(),
            P(),
            P(),
            P(),
            P(),
            P(None, "dp", None, "mp"),
            P(None, "dp", "mp", None),
        ),
        check_vma=False,
    )
```

```python
import functools

import jax
import jax.numpy as jnp
from jax import lax
from jax.experimental import pallas as pl
from jax.experimental.pallas import tpu as pltpu
from jax.sharding import PartitionSpec as P

PROMPT = 1024


EPSILON = 1e-06
SQRT_TWO_PI = 0.7978845608028654
THRESHOLDS = (16, 20, 24, 32, 40, 48, 64, 80, 96, 128, 160, 192, 256, 384, 512, 768)
HIGHEST = lax.Precision.HIGHEST


def rms_scale(values, gain_row):
    return (
        values * lax.rsqrt(jnp.mean(values * values, axis=-1, keepdims=True) + EPSILON) * gain_row
    )


def gelu_tanh(values):
    return (
        0.5
        * values
        * (1.0 + jnp.tanh(SQRT_TWO_PI * (values + 0.044715 * values * values * values)))
    )


def bucket_of(distance):
    counted = jnp.minimum(distance, 15)
    for threshold in THRESHOLDS:
        counted = counted + (distance >= threshold).astype(jnp.int32)
    return counted


def geometry(lengths, row_ids):
    starts = PROMPT + jnp.cumsum(lengths, axis=-1) - lengths
    inside = row_ids[None, :, None] >= starts[:, None, :]
    segment = jnp.sum(inside.astype(jnp.int32), axis=-1) - 1
    begin_at = jnp.max(jnp.where(inside, starts[:, None, :], 0), axis=-1)
    position = jnp.where(
        row_ids[None, :] < PROMPT, row_ids[None, :], PROMPT + row_ids[None, :] - begin_at
    )
    return (position, segment)


def visibility(query_pos, query_seg, key_pos, key_seg):
    query_at = query_pos[:, :, None]
    query_in = query_seg[:, :, None]
    key_at = key_pos[:, None, :]
    key_in = key_seg[:, None, :]
    earlier = key_at <= query_at
    allowed = (key_in < 0) & ((query_in >= 0) | earlier) | (key_in >= 0) & (
        key_in == query_in
    ) & earlier
    bucket = bucket_of(jnp.maximum(query_at - key_at, 0))
    return (allowed, bucket)


def bias_table(bias_row, bucket):
    full_bias = jnp.zeros((bias_row.shape[0],) + bucket.shape, jnp.float32)
    for number in range(bias_row.shape[1]):
        full_bias = full_bias + jnp.where(
            bucket[None] == number, bias_row[:, number][:, None, None, None], 0.0
        )
    return full_bias


def score_block(query_b, key_every, full_bias, allowed, factor):
    raw = (
        jnp.einsum("grhd,gkhd->hgrk", query_b, key_every, preferred_element_type=jnp.float32)
        * factor
    )
    raw = raw + full_bias
    return jnp.where(allowed[None], raw, -1e30)


def body(
    tokens,
    cotangent,
    w_qkv,
    w_attn,
    attn_gain,
    rel_bias,
    ffn_gain,
    router,
    w_in,
    w_out,
    cont_lengths,
    routes,
    slots,
    drops,
):
    groups, local_rows, model_width = tokens.shape
    head_count = rel_bias.shape[1]
    bucket_count = rel_bias.shape[2]
    head_size = model_width // head_count
    factor = head_size ** (-0.5)
    layer_count = w_qkv.shape[0]
    dp_count = lax.axis_size("dp")
    mp_count = lax.axis_size("mp")
    seq_len = local_rows * mp_count
    local_experts = w_in.shape[1]
    expert_total = local_experts * dp_count
    tok_count = groups * local_rows
    capacity = max(2, 9 * 2 * tok_count // (8 * expert_total))
    slot_total = expert_total * capacity
    rows_here = lax.axis_index("mp") * local_rows + jnp.arange(local_rows, dtype=jnp.int32)
    rows_every = jnp.arange(seq_len, dtype=jnp.int32)
    query_pos, query_seg = geometry(cont_lengths, rows_here)
    key_pos, key_seg = geometry(cont_lengths, rows_every)
    allowed, bucket = visibility(query_pos, query_seg, key_pos, key_seg)
    route_all = routes.reshape(layer_count, tok_count, 2)
    slot_all = slots.reshape(layer_count, tok_count, 2)
    keep_all = (1 - drops.reshape(layer_count, tok_count, 2)).astype(jnp.float32)
    head_shape = (groups, seq_len, head_count, head_size)
    stream = tokens.reshape(tok_count, model_width).astype(jnp.float32)
    stored = []
    for layer_now in range(layer_count):
        normed_b = rms_scale(stream, attn_gain[layer_now]).astype(jnp.bfloat16)
        qkv_all = jnp.dot(normed_b, w_qkv[layer_now], preferred_element_type=jnp.float32).astype(
            jnp.bfloat16
        )
        query_b = qkv_all[:, :model_width].reshape(groups, local_rows, head_count, head_size)
        key_own = qkv_all[:, model_width : 2 * model_width].reshape(groups, local_rows, model_width)
        value_own = qkv_all[:, 2 * model_width :].reshape(groups, local_rows, model_width)
        key_every, value_every = (
            lax.all_gather(key_own, "mp", axis=1, tiled=True),
            lax.all_gather(value_own, "mp", axis=1, tiled=True),
        )
        key_every = key_every.reshape(head_shape)
        value_every = value_every.reshape(head_shape)
        full_bias = bias_table(rel_bias[layer_now], bucket)
        scores = score_block(query_b, key_every, full_bias, allowed, factor)
        top_score = jnp.max(scores, axis=-1, keepdims=True)
        weights = jnp.exp(scores - top_score)
        weight_sum = jnp.sum(weights, axis=-1, keepdims=True)
        log_total = top_score + jnp.log(weight_sum)
        probs_b = (weights / weight_sum).astype(jnp.bfloat16)
        mixed_b = jnp.einsum(
            "hgrk,gkhd->grhd", probs_b, value_every, preferred_element_type=jnp.float32
        )
        mixed_b = mixed_b.reshape(tok_count, model_width).astype(jnp.bfloat16)
        middle = stream + jnp.dot(mixed_b, w_attn[layer_now], preferred_element_type=jnp.float32)
        kept_keys = (key_every, value_every)
        ffn_b = rms_scale(middle, ffn_gain[layer_now]).astype(jnp.bfloat16)
        logits = jnp.dot(ffn_b, router[layer_now], preferred_element_type=jnp.float32)
        chosen = route_all[layer_now]
        keep_pair = keep_all[layer_now]
        gate_pair = jax.nn.softmax(jnp.take_along_axis(logits, chosen, axis=1), axis=-1)
        target = chosen * capacity + slot_all[layer_now]
        sending = jnp.where(
            keep_pair[:, :, None] > 0, ffn_b[:, None, :], jnp.zeros((), jnp.bfloat16)
        )
        send_rows = (
            jnp.zeros((slot_total, model_width), jnp.bfloat16)
            .at[target.reshape(-1)]
            .add(sending.reshape(-1, model_width))
        )
        arrived = lax.all_to_all(
            send_rows.reshape(dp_count, local_experts, capacity, model_width),
            "dp",
            split_axis=0,
            concat_axis=0,
            tiled=True,
        )
        rows_in = lax.all_gather(arrived, "mp", axis=0, tiled=True)
        up_block = w_in[layer_now]
        down_block = w_out[layer_now]
        inner_act = jnp.einsum(
            "secd,edf->secf", rows_in, up_block, preferred_element_type=jnp.float32
        )
        hidden_b = gelu_tanh(inner_act).astype(jnp.bfloat16)
        summed = lax.psum_scatter(
            jnp.einsum(
                "secf,efd->secd", hidden_b, down_block, preferred_element_type=jnp.float32
            ).astype(jnp.bfloat16),
            "mp",
            scatter_dimension=0,
            tiled=True,
        )
        kept_rows = (rows_in, inner_act, hidden_b)
        returned = lax.all_to_all(summed, "dp", split_axis=0, concat_axis=0, tiled=True).reshape(
            slot_total, model_width
        )
        pair_out = returned[target].astype(jnp.float32)
        stored.append(
            (
                stream,
                normed_b,
                query_b,
                key_own,
                value_own,
                kept_keys,
                log_total,
                mixed_b,
                middle,
                ffn_b,
                chosen,
                keep_pair,
                gate_pair,
                target,
                pair_out,
                kept_rows,
                full_bias,
            )
        )
        stream = middle + jnp.sum((gate_pair * keep_pair)[:, :, None] * pair_out, axis=1)
    output = stream.astype(jnp.bfloat16).reshape(groups, local_rows, model_width)
    one_hot = (
        bucket[None] == jnp.arange(bucket_count, dtype=jnp.int32)[:, None, None, None]
    ).astype(jnp.bfloat16)
    expert_ids = jnp.arange(expert_total, dtype=jnp.int32)
    qkv_grads = [None] * layer_count
    attn_grads = [None] * layer_count
    attn_gain_grads = [None] * layer_count
    bias_grads = [None] * layer_count
    ffn_gain_grads = [None] * layer_count
    router_grads = [None] * layer_count
    up_grads = [None] * layer_count
    down_grads = [None] * layer_count
    flowing = cotangent.reshape(tok_count, model_width).astype(jnp.float32)
    for layer_now in reversed(range(layer_count)):
        (
            stream_in,
            normed_b,
            query_b,
            key_own,
            value_own,
            kept_keys,
            log_total,
            mixed_b,
            middle,
            ffn_b,
            chosen,
            keep_pair,
            gate_pair,
            target,
            pair_out,
            kept_rows,
            full_bias,
        ) = stored[layer_now]
        weighted = gate_pair * keep_pair
        pair_grad = weighted[:, :, None] * flowing[:, None, :]
        gate_grad = keep_pair * jnp.sum(flowing[:, None, :] * pair_out, axis=-1)
        picked_grad = gate_pair * (
            gate_grad - jnp.sum(gate_pair * gate_grad, axis=-1, keepdims=True)
        )
        logit_grad = jnp.sum(
            picked_grad[:, :, None] * (chosen[:, :, None] == expert_ids).astype(jnp.float32), axis=1
        )
        back_rows = (
            jnp.zeros((slot_total, model_width), jnp.float32)
            .at[target.reshape(-1)]
            .add(pair_grad.reshape(-1, model_width))
        )
        back_rows = back_rows.astype(jnp.bfloat16).reshape(
            dp_count, local_experts, capacity, model_width
        )
        grad_arrived = lax.all_to_all(back_rows, "dp", split_axis=0, concat_axis=0, tiled=True)
        grad_rows = lax.all_gather(grad_arrived, "mp", axis=0, tiled=True)
        up_block = w_in[layer_now]
        down_block = w_out[layer_now]
        rows_in, inner_act, hidden_b = kept_rows
        down_grad = jnp.einsum(
            "secf,secd->efd", hidden_b, grad_rows, preferred_element_type=jnp.float32
        )
        hidden_grad = jnp.einsum(
            "secd,efd->secf", grad_rows, down_block, preferred_element_type=jnp.float32
        )
        inner_grad = jax.vjp(gelu_tanh, inner_act)[1](hidden_grad)[0].astype(jnp.bfloat16)
        up_grad = jnp.einsum(
            "secd,secf->edf", rows_in, inner_grad, preferred_element_type=jnp.float32
        )
        rows_grad = lax.psum_scatter(
            jnp.einsum(
                "secf,edf->secd", inner_grad, up_block, preferred_element_type=jnp.float32
            ).astype(jnp.bfloat16),
            "mp",
            scatter_dimension=0,
            tiled=True,
        )
        up_grads[layer_now] = up_grad
        down_grads[layer_now] = down_grad
        grad_back = lax.all_to_all(
            rows_grad, "dp", split_axis=0, concat_axis=0, tiled=True
        ).reshape(slot_total, model_width)
        ffn_grad = jnp.sum(keep_pair[:, :, None] * grad_back[target].astype(jnp.float32), axis=1)
        ffn_grad = ffn_grad + jnp.einsum(
            "te,de->td", logit_grad, router[layer_now].astype(jnp.float32), precision=HIGHEST
        )
        router_grads[layer_now] = jnp.einsum(
            "td,te->de", ffn_b.astype(jnp.float32), logit_grad, precision=HIGHEST
        )
        middle_grad, ffn_gain_grads[layer_now] = jax.vjp(rms_scale, middle, ffn_gain[layer_now])[1](
            ffn_grad
        )
        middle_grad = middle_grad + flowing
        branch_grad = middle_grad.astype(jnp.bfloat16)
        attn_grads[layer_now] = jnp.einsum(
            "td,te->de", mixed_b, branch_grad, preferred_element_type=jnp.float32
        )
        mixed_grad = jnp.einsum(
            "te,de->td", branch_grad, w_attn[layer_now], preferred_element_type=jnp.float32
        )
        mixed_grad = mixed_grad.astype(jnp.bfloat16).reshape(
            groups, local_rows, head_count, head_size
        )
        key_every, value_every = kept_keys
        scores = score_block(query_b, key_every, full_bias, allowed, factor)
        probs = jnp.exp(scores - log_total)
        prob_grad = jnp.einsum(
            "grhd,gkhd->hgrk", mixed_grad, value_every, preferred_element_type=jnp.float32
        )
        score_grad = (
            probs * (prob_grad - jnp.sum(probs * prob_grad, axis=-1, keepdims=True))
        ).astype(jnp.bfloat16)
        query_grad = (
            jnp.einsum("hgrk,gkhd->grhd", score_grad, key_every, preferred_element_type=jnp.float32)
            * factor
        )
        key_part = (
            jnp.einsum("hgrk,grhd->gkhd", score_grad, query_b, preferred_element_type=jnp.float32)
            * factor
        )
        value_part = jnp.einsum(
            "hgrk,grhd->gkhd",
            probs.astype(jnp.bfloat16),
            mixed_grad,
            preferred_element_type=jnp.float32,
        )
        key_grad, value_grad = (
            lax.psum_scatter(
                key_part.reshape(groups, seq_len, model_width).astype(jnp.bfloat16),
                "mp",
                scatter_dimension=1,
                tiled=True,
            ).astype(jnp.float32),
            lax.psum_scatter(
                value_part.reshape(groups, seq_len, model_width).astype(jnp.bfloat16),
                "mp",
                scatter_dimension=1,
                tiled=True,
            ).astype(jnp.float32),
        )
        bias_grads[layer_now] = jnp.einsum(
            "hgrk,bgrk->hb", score_grad, one_hot, preferred_element_type=jnp.float32
        )
        qkv_grad = jnp.concatenate(
            [
                query_grad.reshape(tok_count, model_width),
                key_grad.reshape(tok_count, model_width),
                value_grad.reshape(tok_count, model_width),
            ],
            axis=1,
        ).astype(jnp.bfloat16)
        qkv_grads[layer_now] = jnp.einsum(
            "td,te->de", normed_b, qkv_grad, preferred_element_type=jnp.float32
        )
        normed_grad = jnp.einsum(
            "te,de->td", qkv_grad, w_qkv[layer_now], preferred_element_type=jnp.float32
        )
        stream_grad, attn_gain_grads[layer_now] = jax.vjp(
            rms_scale, stream_in, attn_gain[layer_now]
        )[1](normed_grad)
        flowing = middle_grad + stream_grad
    totals = lax.psum(
        (
            jnp.stack(qkv_grads),
            jnp.stack(attn_grads),
            jnp.stack(attn_gain_grads),
            jnp.stack(bias_grads),
            jnp.stack(ffn_gain_grads),
            jnp.stack(router_grads),
        ),
        ("dp", "mp"),
    )
    input_grad = flowing.reshape(groups, local_rows, model_width)
    return (
        output,
        input_grad,
        totals[0],
        totals[1],
        totals[2],
        totals[3],
        totals[4],
        totals[5],
        jnp.stack(up_grads),
        jnp.stack(down_grads),
    )


BF = jnp.bfloat16
F32 = jnp.float32
VMEM = pl.BlockSpec(memory_space=pltpu.VMEM)
SMEM = pl.BlockSpec(memory_space=pltpu.SMEM)
ANY = pl.BlockSpec(memory_space=pl.ANY)
VMEM_BYTES = 60 << 20
MESH = pl.DeviceIdType.MESH
LANES = 128
QB = 256


def nn(a, b):
    return lax.dot_general(a, b, (((1,), (0,)), ((), ())), preferred_element_type=F32)


def nt(a, b):
    return lax.dot_general(a, b, (((1,), (1,)), ((), ())), preferred_element_type=F32)


def tn(a, b):
    return lax.dot_general(a, b, (((0,), (0,)), ((), ())), preferred_element_type=F32)


def layer_spec(array, layer):
    zeros = (0,) * (array.ndim - 1)
    return pl.BlockSpec((None,) + array.shape[1:], lambda i: (layer,) + zeros, pipeline_mode=pl.Buffered(1))


def segments(lens, shape, dim):
    at = lax.broadcasted_iota(jnp.int32, shape, dim)
    segment = jnp.full(shape, -1, jnp.int32)
    begin = jnp.zeros(shape, jnp.int32)
    start = jnp.int32(0)
    for number in range(lens.shape[1]):
        inside = at >= start
        segment = segment + inside.astype(jnp.int32)
        begin = jnp.where(inside, start, begin)
        start = start + lens[0, number]
    return segment, at - begin


def bias_stage(vec, lens, table, cont_bias):
    width = vec.shape[1]
    rows = lax.broadcasted_iota(jnp.int32, (LANES, width), 0)
    skewed = jnp.broadcast_to(vec, (LANES, width))
    for bit in range(7):
        skewed = jnp.where((rows >> bit) % 2 == 1, pltpu.roll(skewed, 1 << bit, 1), skewed)
    table[...] = skewed[:, : width - LANES].T
    cont = cont_bias.shape[1]
    _, offset = segments(lens, (LANES, cont), 1)
    place = (lax.broadcasted_iota(jnp.int32, (LANES, cont), 0) == offset).astype(BF)
    full = table[0:PROMPT, :]
    high = full.astype(BF)
    low = (full - high.astype(F32)).astype(BF)
    cont_bias[...] = nn(jnp.concatenate([high, low], 1), jnp.concatenate([place, place], 0))


def blocks_of(seq):
    out = []
    for start in range(0, PROMPT, QB):
        out.append((start, start + QB, None))
    for start in range(0, seq - PROMPT, QB):
        out.append((PROMPT + start, PROMPT, max(0, start - LANES)))
    return out


def scores_of(keys, query, table, cont_bias, seg_col, seg_row, block, h):
    q0, prompt_keys, cont_from = block
    if cont_from is None:
        left = PROMPT - q0
        bias = jnp.concatenate(
            [table[left : left + prompt_keys, :], table[left - LANES : left - LANES + prompt_keys, :]], 1
        )
        return [(0, prompt_keys, nt(keys[h, 0:prompt_keys, :], query) + bias)]
    at = q0 - PROMPT
    first = nt(keys[h, 0:PROMPT, :], query) + cont_bias[:, at : at + QB]
    k0, k1 = PROMPT + cont_from, q0 + QB
    left = PROMPT + cont_from - at
    bias = jnp.concatenate(
        [table[left : left + k1 - k0, :], table[left - LANES : left - LANES + k1 - k0, :]], 1
    )
    same = seg_col[cont_from : at + QB, :][:, 0:1] == seg_row[:, at : at + QB]
    second = jnp.where(same, nt(keys[h, k0:k1, :], query) + bias, -1e30)
    return [(0, PROMPT, first), (k0, k1, second)]


def diagonals():
    width = PROMPT + 3 * LANES
    at = jnp.arange(width, dtype=jnp.int32)
    distance = jnp.where(at <= PROMPT, PROMPT - at, PROMPT + width - at)
    valid = (at <= PROMPT) | (at > width - LANES)
    return width, distance, valid


def bias_vectors(bias):
    _, distance, valid = diagonals()
    hot = bucket_of(distance)[None, :] == jnp.arange(bias.shape[-1], dtype=jnp.int32)[:, None]
    picked = jnp.sum(jnp.where(hot, bias[..., :, None], 0.0), axis=-2)
    return jnp.where(valid, picked, -1e30)


def scatter_rows(rows, values, send):
    experts, tile, _ = send.shape
    tokens, model = values[0].shape
    half = model // 2
    at = lax.broadcasted_iota(jnp.int32, (experts * tile, tokens), 0)
    place, piece = [], []
    for j in range(2):
        slot = rows[2 + j : 3 + j, :]
        piece.append(jnp.where(rows[4 + j : 5 + j, :] > 0, slot // tile, -1))
        place.append(rows[j : j + 1, :] * tile + slot % tile)

    def pick(number, shift, columns):
        hots = [
            (jnp.where(piece[j] == number, place[j] + shift, -1) == at) for j in range(2)
        ]
        if len(values) == 1:
            return nn((hots[0] | hots[1]).astype(BF), values[0][:, columns])
        return nn(hots[0].astype(BF), values[0][:, columns]) + nn(hots[1].astype(BF), values[1][:, columns])

    for i in range(3):
        send[:, :, i * model : (i + 1) * model] = pick(i, 0, slice(0, model)).astype(BF).reshape(experts, tile, model)
    tail = pick(3, 0, slice(0, half)) + pick(3, 8, slice(half, model))
    send[:, :, 3 * model : 3 * model + half] = tail.astype(BF).reshape(experts, tile, half)


def scatter_gates(rows, gates, send, start):
    experts, tile, _ = send.shape
    tokens = rows.shape[1]
    at = lax.broadcasted_iota(jnp.int32, (experts * tile, tokens), 0)
    lane = lax.broadcasted_iota(jnp.int32, (tokens, LANES), 1)
    total = 0.0
    for j in range(2):
        slot = rows[2 + j : 3 + j, :]
        piece = jnp.where(rows[4 + j : 5 + j, :] > 0, slot // tile, -1)
        place = rows[j : j + 1, :] * tile + slot % tile
        high = gates[j].astype(BF).astype(F32)
        rest = gates[j] - high
        mid = rest.astype(BF).astype(F32)
        part = jnp.where(lane % 3 == 0, high, jnp.where(lane % 3 == 1, mid, rest - mid))
        for i in range(4):
            hot = (jnp.where(piece == i, place, -1) == at).astype(BF)
            total = total + nn(hot, jnp.where(lane // 3 == i, part, 0.0).astype(BF))
    send[:, :, start:] = total.astype(BF).reshape(experts, tile, LANES)


def gather_rows(cols, j, back):
    experts, tile, wide = back.shape
    half = wide // 7
    model = 2 * half
    tokens = cols.shape[0]
    at = lax.broadcasted_iota(jnp.int32, (tokens, experts * tile), 1)
    slot = cols[:, 2 + j : 3 + j]
    piece = jnp.where(cols[:, 4 + j : 5 + j] > 0, slot // tile, -1)
    place = cols[:, j : j + 1] * tile + slot % tile
    total = 0.0
    for i in range(3):
        hot = (jnp.where(piece == i, place, -1) == at).astype(BF)
        total = total + nn(hot, back[:, :, i * model : (i + 1) * model].reshape(experts * tile, model))
    tail = back[:, :, 3 * model :].reshape(experts * tile, half)
    left = nn((jnp.where(piece == 3, place, -1) == at).astype(BF), tail)
    right = nn((jnp.where(piece == 3, place + 8, -1) == at).astype(BF), tail)
    return total + jnp.concatenate([left, right], 1)


def unfold_tail(block, half):
    wide = block.astype(F32)
    return jnp.concatenate([wide[0:8, :], wide[8:16, :]], 1)


def mp_places():
    me = lax.axis_index("mp")
    core, row = lax.rem(me, 2), me // 2
    return me, core, row * 2 + 1 - core, (1 - row) * 2 + core, (1 - row) * 2 + 1 - core


def signal_to(barrier, **place):
    pl.semaphore_signal(barrier, inc=1, device_id=place, device_id_type=MESH)


def remote(src, dst, send_sem, recv_sem, **place):
    return pltpu.make_async_remote_copy(
        src_ref=src, dst_ref=dst, send_sem=send_sem, recv_sem=recv_sem, device_id=place, device_id_type=MESH
    )


def greet_mp(count, dp_count=1):
    me, core, mate, across, diagonal = mp_places()
    d = lax.axis_index("dp")
    barrier = pltpu.get_barrier_semaphore()
    for to in (mate, across, diagonal)[:count]:
        signal_to(barrier, mp=to)
    for k in range(1, dp_count):
        signal_to(barrier, dp=lax.rem(d + k, dp_count), mp=me)
    pl.semaphore_wait(barrier, count + dp_count - 1)


def share_dp(held, ssem, rsem):
    d, me, count = lax.axis_index("dp"), lax.axis_index("mp"), held.shape[0]
    return [
        remote(held.at[d], held.at[d], ssem.at[k], rsem.at[k], dp=lax.rem(d + k, count), mp=me) for k in range(1, count)
    ]


def scatter_dp(part, come, ssem, rsem):
    d, me, count = lax.axis_index("dp"), lax.axis_index("mp"), part.shape[0]
    copies = []
    for k in range(1, count):
        to = lax.rem(d + k, count)
        copies.append(remote(part.at[to], come.at[d], ssem.at[k], rsem.at[k], dp=to, mp=me))
    return copies


def sum_dp(copies, part, come):
    d, count = lax.axis_index("dp"), part.shape[0]
    total = part[d].astype(F32)
    for k in range(1, count):
        copies[k - 1].wait_recv()
        total = total + come[lax.rem(d + count - k, count)].astype(F32)
    return total


def mean_square_scale(values):
    return lax.rsqrt(jnp.mean(values * values, axis=-1, keepdims=True) + EPSILON)


def norm_grads(values, gain, upstream):
    scale = mean_square_scale(values)
    scaled = upstream * gain
    drift = jnp.mean(values * scaled, axis=-1, keepdims=True)
    return scale * scaled - values * (scale * scale * scale * drift), jnp.sum(
        upstream * values * scale, axis=0, keepdims=True
    )


def pre_kernel(layer, layers, heads, size, *refs):
    refs = list(refs)

    def take(count):
        taken = refs[:count]
        del refs[:count]
        return taken

    first, last = layer == 0, layer == layers - 1
    lens, gain_a, w_qkv, vecs, w_attn, gain_f, router, rows, cols = take(9)
    if first:
        tokens, cotangent, far_rows = take(3)
    else:
        before, returned, cols_in, gates_in = take(4)
    g_in, g_half = take(2) if last else (None, None)
    (stream_o,) = (None,) if first else take(1)
    normed_o, qkv_o, mixed_o, lse_o, middle_o, ffn_o, gates_o, send_o = take(8)
    (g_o,) = take(1) if first or last else (None,)
    (g_half_o,) = take(1) if first else (None,)
    held, hssem, hrsem = take(3)
    weight, q_s, k_s, vt_s, table, cont_bias, mixt, segc, out_s, mixed_s, mssem, mrsem = take(12)
    if first:
        g_send, g_held, gssem, grsem = take(4)
    if first or last:
        g_over, gfsem, gbsem = take(3)
    me, core, mate, across, diagonal = mp_places()
    d = lax.axis_index("dp")
    dp_count = lax.axis_size("dp")
    seq, own = mixed_o.shape
    local, model = middle_o.shape
    parts = local // LANES

    barrier = pltpu.get_barrier_semaphore()
    for to in (mate, across, diagonal):
        signal_to(barrier, mp=to)
    if first:
        for k in range(2, 2 * dp_count):
            signal_to(barrier, dp=lax.rem(d + k // 2, dp_count), mp=(me // 2) * 2 + lax.rem(core + k % 2, 2))
        count = 3 + 2 * dp_count - 2
    else:
        count = 3
    if first:
        stream = tokens[...].astype(F32)
    else:
        stream = before[...]
        for j in range(2):
            stream = stream + gates_in[:, j : j + 1] * gather_rows(cols_in, j, returned)
        stream_o[...] = stream
    held[me] = (stream * mean_square_scale(stream) * gain_a[layer : layer + 1, :]).astype(BF)
    pl.semaphore_wait(barrier, count)
    over = remote(held.at[me], held.at[me], hssem.at[1], hrsem.at[1], mp=across)
    to_mate = remote(held.at[me], held.at[me], hssem.at[0], hrsem.at[0], mp=mate)
    passed = remote(held.at[across], held.at[across], hssem.at[2], hrsem.at[2], mp=mate)
    over.start()
    to_mate.start()

    index = d * 2 + core

    def far_copy(k):
        dd, cc = lax.rem(d + k // 2, dp_count), lax.rem(core + k % 2, 2)
        if k == 0:
            return pltpu.make_async_copy(g_send.at[index], g_held.at[index], grsem.at[0])
        return remote(g_send.at[dd * 2 + cc], g_held.at[index], gssem.at[k], grsem.at[k], dp=dd, mp=(me // 2) * 2 + cc)

    def far_over(source, n):
        two = pl.ds(lax.rem(d + dp_count - n, dp_count) * 2, 2)
        return remote(source.at[two], g_over.at[two], gfsem.at[n], gbsem.at[n], mp=across)

    def far_wave(n):
        if n < dp_count:
            far_copy(2 * n).start()
            far_copy(2 * n + 1).start()

    def far_arrived(n):
        far_copy(2 * n).wait() if n == 0 else far_copy(2 * n).wait_recv()
        far_copy(2 * n + 1).wait_recv()

    if first:
        scatter_rows(far_rows, [cotangent[...]], g_send)
        for n in range(dp_count):
            far_wave(n)
    elif last:
        for n in range(2, dp_count):
            far_over(g_in, n).start()

    for m in range(model // own):

        @pl.when(me == m)
        def _():
            for t in range(3):
                weight[:, t * own : (t + 1) * own] = w_qkv[:, t * model + m * own : t * model + (m + 1) * own]

    seg_row, _ = segments(lens, (1, seq - PROMPT), 1)
    segc[...] = segments(lens, (seq - PROMPT, LANES), 0)[0]

    def tables(h, carry):
        bias_stage(vecs[pl.ds(h, 1), :], lens, table.at[h], cont_bias.at[h])
        return carry

    lax.fori_loop(0, heads, tables, 0)

    def project(m):
        at = pl.ds(pl.multiple_of(m * local, LANES), local)
        part = nn(held[m], weight[...]).astype(BF)
        qkv_o[at, :] = part
        for h in range(heads):
            q_s[h, at, :] = part[:, h * size : (h + 1) * size] * BF(0.125)
            k_s[h, at, :] = part[:, own + h * size : own + (h + 1) * size]
            vt_s[h, :, at] = part[:, 2 * own + h * size : 2 * own + (h + 1) * size].astype(F32).T.astype(BF)

    project(me)
    to_mate.wait_recv()
    project(mate)
    over.wait_recv()
    passed.start()
    project(across)
    passed.wait_recv()
    project(diagonal)

    def handed(n):
        return remote(out_s.at[n], mixed_s.at[me, n % parts], mssem.at[n], mrsem.at[me, n % parts], mp=n // parts)

    early = {1: 0, 3: 1}
    for number, block in enumerate(blocks_of(seq)):
        q0 = block[0]
        if first and number in early:
            far_arrived(early[number])
            far_over(g_held, early[number]).start()

        def head(h, carry):
            query = q_s[h, q0 : q0 + QB, :]
            scored = scores_of(k_s, query, table.at[h], cont_bias.at[h], segc, seg_row, block, h)
            top = functools.reduce(jnp.maximum, [jnp.max(s, axis=0, keepdims=True) for _, _, s in scored])
            total, mixed = 0.0, 0.0
            for k0, k1, s in scored:
                p = jnp.exp(s - top)
                total = total + jnp.sum(p, axis=0, keepdims=True)
                mixed = mixed + nn(vt_s[h, :, k0:k1], p.astype(BF))
            mixt[pl.ds(pl.multiple_of(h * size, size), size), :] = mixed / total
            lse_o[pl.ds(h, 1), q0 : q0 + QB] = top + jnp.log(total)
            return carry

        lax.fori_loop(0, heads, head, 0)
        done = mixt[...].T.astype(BF)
        mixed_o[q0 : q0 + QB, :] = done
        for half in range(QB // LANES):
            n = q0 // LANES + half
            out_s[n] = done[half * LANES : (half + 1) * LANES, :]

            @pl.when(me == n // parts)
            def _():
                pltpu.make_async_copy(out_s.at[n], mixed_s.at[me, n % parts], mrsem.at[me, n % parts]).start()

            @pl.when(me != n // parts)
            def _():
                handed(n).start()

    normed_o[...] = held[...]
    middle = stream
    for m in range(mixed_s.shape[0]):
        for n in range(parts):
            pltpu.make_async_copy(mixed_s.at[m, n], mixed_s.at[m, n], mrsem.at[m, n]).wait()
        middle = middle + nn(mixed_s[m].reshape(local, own), w_attn[m * own : (m + 1) * own, :])
    middle_o[...] = middle
    ffn = (middle * mean_square_scale(middle) * gain_f[layer : layer + 1, :]).astype(BF)
    ffn_o[...] = ffn
    logits = nn(ffn, router[...])
    expert = lax.broadcasted_iota(jnp.int32, logits.shape, 1)
    chosen = [
        jnp.sum(jnp.where(expert == cols[:, j : j + 1], logits, 0.0), axis=1, keepdims=True) for j in range(2)
    ]
    top = jnp.maximum(chosen[0], chosen[1])
    powers = [jnp.exp(c - top) for c in chosen]
    gates = [p / (powers[0] + powers[1]) for p in powers]
    gates_o[...] = jnp.concatenate(gates, 1)
    scatter_rows(rows, [ffn], send_o)
    if last:
        scatter_gates(rows, gates, send_o, 7 * model // 2)
    if first:
        for n in range(2, dp_count):
            far_arrived(n)
        g_o[...] = g_held[...]
        for k in range(1, 2 * dp_count):
            far_copy(k).wait_send()
        for n in range(2):
            far_over(g_held, n).wait()
            two = pl.ds(lax.rem(d + dp_count - n, dp_count) * 2, 2)
            g_half_o[two] = g_over[two]
    elif last:
        for n in range(2):
            two = pl.ds(lax.rem(d + dp_count - n, dp_count) * 2, 2)
            g_o[two] = g_half[two]
        for n in range(2, dp_count):
            far_over(g_in, n).wait()
            two = pl.ds(lax.rem(d + dp_count - n, dp_count) * 2, 2)
            g_o[two] = g_over[two]
    for copy in (to_mate, over, passed):
        copy.wait_send()
    for n in range(seq // LANES):

        @pl.when(me != n // parts)
        def _():
            handed(n).wait_send()


def pre_call(layer, layers, number, heads, size, lens, normal, mp_count, dp_count, local, model, specials, block):
    first, last = layer == 0, layer == layers - 1
    seq, own = local * mp_count, heads * size
    width = PROMPT + 3 * LANES
    args = list(normal) + list(specials)
    specs = [SMEM] + [layer_spec(*a) if isinstance(a, tuple) else VMEM for a in args]
    narrow = block[:2] + (7 * model // 2,)
    send = narrow[:2] + (narrow[2] + LANES,) if last else narrow
    outs = [] if first else [((local, model), F32)]
    outs += [
        ((mp_count, local, model), BF), ((seq, 3 * own), BF), ((seq, own), BF), ((heads, seq), F32),
        ((local, model), F32), ((local, model), BF), ((local, 2), F32), (send, BF),
    ]
    if first or last:
        outs.append((narrow, BF))
    if first:
        outs.append((narrow, BF))
    scratch = [
        pltpu.VMEM((mp_count, local, model), BF), dma(3), dma(3),
        pltpu.VMEM((model, 3 * own), BF),
        pltpu.VMEM((heads, seq, size), BF),
        pltpu.VMEM((heads, seq, size), BF),
        pltpu.VMEM((heads, size, seq), BF),
        pltpu.VMEM((heads, width - LANES, LANES), F32),
        pltpu.VMEM((heads, PROMPT, seq - PROMPT), F32),
        pltpu.VMEM((own, QB), F32),
        pltpu.VMEM((seq - PROMPT, LANES), jnp.int32),
        pltpu.VMEM((seq // LANES, LANES, own), BF),
        pltpu.VMEM((mp_count, local // LANES, LANES, own), BF),
        dma(seq // LANES),
        dma(mp_count, local // LANES),
    ]
    if first:
        scratch += [pltpu.VMEM(narrow, BF), pltpu.VMEM(narrow, BF), dma(2 * dp_count), dma(2 * dp_count)]
    if first or last:
        scratch += [pltpu.VMEM(narrow, BF), dma(dp_count), dma(dp_count)]
    return pl.pallas_call(
        functools.partial(pre_kernel, layer, layers, heads, size),
        grid=(1,),
        out_shape=tuple(jax.ShapeDtypeStruct(shape, kind) for shape, kind in outs),
        in_specs=specs,
        out_specs=tuple([VMEM] * len(outs)),
        scratch_shapes=scratch,
        compiler_params=pltpu.CompilerParams(
            collective_id=number, has_side_effects=True, vmem_limit_bytes=VMEM_BYTES
        ),
    )(lens, *[a[0] if isinstance(a, tuple) else a for a in args])


def shift_table(flat, width):
    rows = lax.broadcasted_iota(jnp.int32, flat.shape, 0)
    for bit in range(7):
        flat = jnp.where((rows >> bit) % 2 == 1, pltpu.roll(flat, width - (1 << bit), 1), flat)
    return jnp.sum(flat, axis=0, keepdims=True)


def back_kernel(layer, layers, heads, size, buckets, *refs):
    refs = list(refs)

    def take(count):
        taken = refs[:count]
        del refs[:count]
        return taken

    first, last = layer == 0, layer == layers - 1
    lens, vecs, back, returned, flow_in, middle, ffn, gates, cols, router, gain_f = take(11)
    normed, qkv, mixed, lse, w_attn, w_qkv, stream, gain_a = take(8)
    if first:
        above, small_above = take(2)
    else:
        rows_below, cols_below, gates_below = take(3)
    (flow_o,) = take(1)
    if first:
        up_o, all_o, small_o = take(3)
    else:
        out_o, send_o, sum_o, small_o = take(4)
    held, hssem, hrsem = take(3)
    normed_t, q_s, k_s, v_s, kt_s, do_s, table, cont_bias, fold, dtable, dk_s, dv_s, dqt, segc, hot, bias_s, gw_a, router_s = take(18)
    dq_s, dq_held, qssem, qrsem, part, come, pssem, prsem = take(8)
    if first:
        small_s, small_come, small_mp, tsem, usem, csem, dsem, vsem, zsem = take(9)
        assem, arsem, ossem, orsem = take(4)
        ussem, ursem, wssem, wrsem = take(4)
    me, core, mate, across, diagonal = mp_places()
    d = lax.axis_index("dp")
    dp_count = part.shape[0]
    local, model = middle.shape
    seq, own = mixed.shape
    cont = seq - PROMPT
    width = vecs.shape[1]
    places = mixed.shape[0] // local

    def dp_share(held_all, ssem, rsem, k):
        return remote(held_all.at[me, d], held_all.at[me, d], ssem.at[k], rsem.at[k], dp=lax.rem(d + k, dp_count), mp=me)

    def mp_share(held_all, ssem, rsem, n, j):
        whose = across if n == 2 else me
        return remote(
            held_all.at[whose, j], held_all.at[whose, j], ssem.at[n, j], rsem.at[n, j], mp=across if n == 1 else mate
        )

    greet_mp(3, dp_count=dp_count)
    if first:
        up_o[me, d] = above[...]
        for k in range(1, dp_count - 2):
            dp_share(up_o, ussem, ursem, k).start()

    flow = flow_in[...].astype(F32)
    outs = [gather_rows(cols, j, returned) for j in range(2)]
    gate = [gates[:, j : j + 1] for j in range(2)]
    keep = [cols[:, 4 + j : 5 + j].astype(F32) for j in range(2)]
    if last:
        out_o[...] = (middle[...] + gate[0] * keep[0] * outs[0] + gate[1] * keep[1] * outs[1]).astype(BF)
    gate_grad = [keep[j] * jnp.sum(flow * outs[j], axis=1, keepdims=True) for j in range(2)]
    shared = gate[0] * gate_grad[0] + gate[1] * gate_grad[1]
    expert = lax.broadcasted_iota(jnp.int32, (local, router.shape[1]), 1)
    logit_grad = 0.0
    for j in range(2):
        logit_grad = logit_grad + jnp.where(expert == cols[:, j : j + 1], gate[j] * (gate_grad[j] - shared), 0.0)
    high = logit_grad.astype(BF)
    low = (logit_grad - high.astype(F32)).astype(BF)
    upstream = gather_rows(cols, 0, back) + gather_rows(cols, 1, back)
    upstream = upstream + nt(high, router[...]) + nt(low, router[...])
    grad, gain_f_grad = norm_grads(middle[...], gain_f[layer : layer + 1, :], upstream)
    grad = grad + flow
    flow_o[...] = grad
    held[me] = grad.astype(BF)
    to_mate = remote(held.at[me], held.at[me], hssem.at[0], hrsem.at[0], mp=mate)
    over = remote(held.at[me], held.at[me], hssem.at[1], hrsem.at[1], mp=across)
    passed = remote(held.at[across], held.at[across], hssem.at[2], hrsem.at[2], mp=mate)
    over.start()
    to_mate.start()

    router_s[...] = tn(jnp.concatenate([high, low], 1), ffn[...])
    for i in range(seq // local):
        rows = pl.ds(i * local, local)
        normed_t[:, i * local : (i + 1) * local] = normed[i].astype(F32).T.astype(BF)
        piece = qkv[rows, :]
        for h in range(heads):
            q_s[h, rows, :] = piece[:, h * size : (h + 1) * size] * BF(0.125)
            key = piece[:, own + h * size : own + (h + 1) * size]
            k_s[h, rows, :] = key
            kt_s[h, :, i * local : (i + 1) * local] = (key.astype(F32) * 0.125).T.astype(BF)
            v_s[h, rows, :] = piece[:, 2 * own + h * size : 2 * own + (h + 1) * size]
    seg_row, _ = segments(lens, (1, cont), 1)
    segc[...] = segments(lens, (cont, LANES), 0)[0]
    _, offset = segments(lens, (cont, LANES), 0)
    unplace = (lax.broadcasted_iota(jnp.int32, (cont, LANES), 1) == offset).astype(BF)
    at = lax.broadcasted_iota(jnp.int32, (1, width), 1)
    distance = jnp.where(at <= PROMPT, PROMPT - at, PROMPT + width - at)
    bucket = jnp.where((at <= PROMPT) | (at > width - LANES), bucket_of(distance), -1)
    hot[...] = (lax.broadcasted_iota(jnp.int32, (buckets, width), 0) == bucket).astype(F32)
    bias_s[...] = jnp.zeros_like(bias_s)

    def receive(m):
        dmix = nt(held[m], w_attn[pl.ds(pl.multiple_of(me * own, size), own), :]).astype(BF)
        for h in range(heads):
            do_s[h, pl.ds(pl.multiple_of(m * local, LANES), local), :] = dmix[:, h * size : (h + 1) * size]

    receive(me)
    to_mate.wait_recv()
    receive(mate)
    over.wait_recv()
    passed.start()
    receive(across)
    passed.wait_recv()
    receive(diagonal)
    gw_a[...] = tn(held[...].reshape(seq, model), mixed[...])

    def swap_copy(h, n):
        to = (mate, across, diagonal)[n]
        return remote(dq_s.at[h, to], dq_held.at[h, me], qssem.at[h, n], qrsem.at[h, me], mp=to)

    def sum_copy(h, k):
        to = lax.rem(d + k, dp_count)
        return remote(part.at[to, h], come.at[d, h], pssem.at[h, k], prsem.at[h, k], dp=to, mp=me)

    def summed(h):
        total = part[d, h].astype(F32)
        for k in range(1, dp_count):
            sum_copy(h, k).wait_recv()
            total = total + come[lax.rem(d + dp_count - k, dp_count), h].astype(F32)
        return total.astype(BF)

    def head_share(h, k):
        place = all_o.at[me, d, h]
        return remote(place, place, assem.at[h, k], arsem.at[h, k], dp=lax.rem(d + k, dp_count), mp=me)

    def head_pass(n, h, j):
        place = all_o.at[across if n == 2 else me, j, h]
        return remote(place, place, ossem.at[n, h, j], orsem.at[n, h, j], mp=across if n == 1 else mate)

    def finish_sum(h):
        all_o[me, d, h] = summed(h)
        for k in range(1, dp_count):
            head_share(h, k).start()

    def hand_on(h):
        for k in range(dp_count):
            j = lax.rem(d + dp_count - k, dp_count)
            if k > 0:
                head_share(h, k).wait_recv()
            head_pass(1, h, j).start()
            head_pass(0, h, j).start()

    def pass_on(h):
        for k in range(dp_count):
            j = lax.rem(d + dp_count - k, dp_count)
            head_pass(1, h, j).wait_recv()
            head_pass(2, h, j).start()

    def head(h, carry):
        bias_stage(vecs[pl.ds(h, 1), :], lens, table, cont_bias)
        dtable[...] = jnp.zeros_like(dtable)
        dk_s[...] = jnp.zeros_like(dk_s)
        dv_s[...] = jnp.zeros_like(dv_s)
        for number, block in enumerate(blocks_of(seq)):
            q0, prompt_keys, cont_from = block
            if first:

                @pl.when(h == 0)
                def _():
                    for k in ((0,), (1,), (2,), (3,), (4, 5), (6, 7))[number]:
                        if k > 0:
                            dp_share(up_o, ussem, ursem, k).wait_recv()
                        if number == 1:
                            for later in range(dp_count - 2, dp_count):
                                dp_share(up_o, ussem, ursem, later).start()
                        j = lax.rem(d + dp_count - k, dp_count)
                        mp_share(up_o, wssem, wrsem, 1, j).start()
                        mp_share(up_o, wssem, wrsem, 0, j).start()

            query = q_s[h, q0 : q0 + QB, :]
            dout = do_s[h, q0 : q0 + QB, :]
            scored = scores_of(k_s, query, table, cont_bias, segc, seg_row, block, h)
            lse_row = lse[pl.ds(h, 1), q0 : q0 + QB]
            kept, delta = [], 0.0
            for k0, k1, s in scored:
                p = jnp.exp(s - lse_row)
                dp = nt(v_s[h, k0:k1, :], dout)
                delta = delta + jnp.sum(p * dp, axis=0, keepdims=True)
                dv_s[k0:k1, :] += nn(p.astype(BF), dout)
                kept.append((k0, k1, p, dp))
            dq = 0.0
            for k0, k1, p, dp in kept:
                ds = p * (dp - delta)
                dsb = ds.astype(BF)
                dk_s[k0:k1, :] += nn(dsb, query)
                dq = dq + nn(kt_s[h, :, k0:k1], dsb)
                if cont_from is not None and k0 == 0:
                    fold[:, q0 - PROMPT : q0 - PROMPT + QB] = dsb
                else:
                    left = PROMPT - q0 if cont_from is None else PROMPT + cont_from - (q0 - PROMPT)
                    dtable[left : left + k1 - k0, :] += ds[:, 0:LANES]
                    dtable[left - LANES : left - LANES + k1 - k0, :] += ds[:, LANES:]
            dqt[:, q0 : q0 + QB] = dq
        for m in range(places):
            rows = slice(m * local, (m + 1) * local)
            dq_s[h, m] = jnp.concatenate(
                [dqt[:, rows].T.astype(BF), dk_s[rows, :].astype(BF), dv_s[rows, :].astype(BF)], 1
            )
        for n in (2, 1, 0):
            swap_copy(h, n).start()
        pltpu.make_async_copy(dq_s.at[h, me], dq_held.at[h, me], qrsem.at[h, me]).start()
        grads = nn(normed_t[...], dq_s[h].reshape(seq, 3 * size))
        for j in range(dp_count):
            rows = slice(j * part.shape[2], (j + 1) * part.shape[2])
            part[j, h, :, 0 : 3 * size] = grads[rows, :].astype(BF)
        for k in range(1, dp_count):
            sum_copy(h, k).start()
        dtable[0:PROMPT, :] += nn(fold[...], unplace)
        flat = jnp.concatenate([dtable[...].T, jnp.zeros((LANES, LANES), F32)], 1)
        found = jnp.sum(hot[...] * shift_table(flat, width), axis=1, keepdims=True)
        lane = lax.broadcasted_iota(jnp.int32, bias_s.shape, 1)
        bias_s[...] += jnp.where(lane == me * heads + h, found, 0.0)
        if first:

            @pl.when(h == heads - 1)
            def _():
                for j in range(dp_count):
                    mp_share(up_o, wssem, wrsem, 1, j).wait_recv()
                    mp_share(up_o, wssem, wrsem, 2, j).start()

            @pl.when(h > 0)
            def _():
                finish_sum(h - 1)

        return carry

    for j in range(dp_count):
        rows = slice(j * part.shape[2], (j + 1) * part.shape[2])
        for h in range(heads):
            part[j, h, :, 3 * size :] = gw_a[rows, h * size : (h + 1) * size].astype(BF)
    lax.fori_loop(0, heads, head, 0)
    if first:
        hand_on(0)
    for h in range(heads):
        for m in range(places):
            pltpu.make_async_copy(dq_held.at[h, m], dq_held.at[h, m], qrsem.at[h, m]).wait()
    upstream = 0.0
    for t in range(3):
        piece = jnp.concatenate(
            [dq_held[h, m, :, t * size : (t + 1) * size] for m in range(places) for h in range(heads)], 1
        )
        upstream = upstream + nt(piece, w_qkv[:, t * model : (t + 1) * model])
    inner, gain_a_grad = norm_grads(stream[...].astype(F32), gain_a[layer : layer + 1, :], upstream)
    flow = flow_o[...] + inner
    flow_o[...] = flow
    gains = jnp.concatenate([gain_a_grad, gain_f_grad, jnp.zeros((6, model), F32)], 0)
    tiles = [bias_s[8 * i : 8 * i + 8, :] for i in range(buckets // 8)]
    bias_rows = jnp.concatenate(tiles + [jnp.zeros((8, model - LANES * len(tiles)), F32)], 1)
    router_grad = router_s[0 : router.shape[1], :] + router_s[router.shape[1] :, :]
    small = [gains, bias_rows] + [router_grad[8 * i : 8 * i + 8, :] for i in range(router.shape[1] // 8)]

    if not first:
        scatter_rows(
            rows_below,
            [(gates_below[:, j : j + 1] * cols_below[:, 4 + j : 5 + j].astype(F32) * flow).astype(BF) for j in range(2)],
            send_o,
        )
        for n, block in enumerate(small):
            small_o[n] = block
        for h in range(heads):
            sum_o[h] = summed(h)
    else:
        for n, block in enumerate(small):
            small_s[n] = block
        small_s[len(small) :] = small_above[...]
        small_scattered = scatter_dp(small_s, small_come, tsem, usem)
        for copy in small_scattered:
            copy.start()
        finish_sum(heads - 1)
        hand_on(1)
        small_mp[me] = sum_dp(small_scattered, small_s, small_come)
        small_swaps = [
            remote(small_mp.at[me], small_mp.at[me], csem.at[n], dsem.at[n], mp=to) for n, to in enumerate((mate, across, diagonal))
        ]
        for copy in small_swaps:
            copy.start()
        pass_on(0)
        for copy in small_swaps:
            copy.wait_recv()
        small_o[d] = small_mp[0] + small_mp[1] + small_mp[2] + small_mp[3]
        small_shares = share_dp(small_o, vsem, zsem)
        for copy in small_shares:
            copy.start()
        for h in range(2, heads):
            hand_on(h)
        for h in range(1, heads):
            pass_on(h)
        for copy in small_shares:
            copy.wait_recv()
        for j in range(dp_count):
            for n in range(3):
                if n != 1:
                    mp_share(up_o, wssem, wrsem, n, j).wait_recv()
                mp_share(up_o, wssem, wrsem, n, j).wait_send()
                for h in range(heads):
                    if n != 1:
                        head_pass(n, h, j).wait_recv()
                    head_pass(n, h, j).wait_send()
        for k in range(1, dp_count):
            dp_share(up_o, ussem, ursem, k).wait_send()
            for h in range(heads):
                head_share(h, k).wait_send()
        for copy in small_swaps + small_scattered + small_shares:
            copy.wait_send()
    for copy in (to_mate, over, passed):
        copy.wait_send()
    for h in range(heads):
        for n in range(3):
            swap_copy(h, n).wait_send()
        for k in range(1, dp_count):
            sum_copy(h, k).wait_send()


def back_call(layer, layers, number, heads, size, buckets, lens, normal, mp_count, dp_count, local, model, block, extra):
    first, last = layer == 0, layer == layers - 1
    seq, own = local * mp_count, heads * size
    width = PROMPT + 3 * LANES
    cont = seq - PROMPT
    args = list(normal) + list(extra)
    specs = [SMEM] + [layer_spec(*a) if isinstance(a, tuple) else VMEM for a in args]
    chunk = (heads, model // dp_count, 4 * size)
    smalls = dp_count // layers
    outs = [((local, model), F32)]
    if first:
        outs += [((mp_count, dp_count) + chunk, BF), ((mp_count, dp_count) + chunk, BF), ((dp_count, 8, model), F32)]
    else:
        outs += [((local, model), BF), (block, BF), (chunk, BF), ((smalls, 8, model), F32)]
    scratch = [
        pltpu.VMEM((mp_count, local, model), BF), dma(3), dma(3),
        pltpu.VMEM((model, seq), BF),
        pltpu.VMEM((heads, seq, size), BF),
        pltpu.VMEM((heads, seq, size), BF),
        pltpu.VMEM((heads, seq, size), BF),
        pltpu.VMEM((heads, size, seq), BF),
        pltpu.VMEM((heads, seq, size), BF),
        pltpu.VMEM((width - LANES, LANES), F32),
        pltpu.VMEM((PROMPT, cont), F32),
        pltpu.VMEM((PROMPT, cont), BF),
        pltpu.VMEM((width - LANES, LANES), F32),
        pltpu.VMEM((seq, size), F32),
        pltpu.VMEM((seq, size), F32),
        pltpu.VMEM((size, seq), F32),
        pltpu.VMEM((cont, LANES), jnp.int32),
        pltpu.VMEM((buckets, width), F32),
        pltpu.VMEM((buckets, LANES), F32),
        pltpu.VMEM((model, own), F32),
        pltpu.VMEM((4 * dp_count, model), F32),
        pltpu.VMEM((heads, mp_count, local, 3 * size), BF),
        pltpu.VMEM((heads, mp_count, local, 3 * size), BF),
        dma(heads, 3),
        dma(heads, mp_count),
        pltpu.VMEM((dp_count,) + chunk, BF),
        pltpu.VMEM((dp_count,) + chunk, BF),
        dma(heads, dp_count),
        dma(heads, dp_count),
    ]
    if first:
        scratch += [
            pltpu.VMEM((dp_count, 8, model), F32),
            pltpu.VMEM((dp_count, 8, model), F32),
            pltpu.VMEM((mp_count, 8, model), F32),
        ]
        scratch += [dma(dp_count)] * 2 + [dma(3)] * 2 + [dma(dp_count)] * 2
        scratch += [dma(heads, dp_count)] * 2 + [dma(3, heads, dp_count)] * 2 + [dma(dp_count)] * 2 + [dma(3, dp_count)] * 2
    return pl.pallas_call(
        functools.partial(back_kernel, layer, layers, heads, size, buckets),
        grid=(1,),
        out_shape=tuple(jax.ShapeDtypeStruct(shape, kind) for shape, kind in outs),
        in_specs=specs,
        out_specs=tuple([VMEM] * len(outs)),
        scratch_shapes=scratch,
        compiler_params=pltpu.CompilerParams(
            collective_id=number, has_side_effects=True, vmem_limit_bytes=VMEM_BYTES
        ),
    )(lens, *[a[0] if isinstance(a, tuple) else a for a in args])


def dma(*shape):
    return pltpu.SemaphoreType.DMA(shape) if shape else pltpu.SemaphoreType.DMA


def gelu_grad(values):
    inner = jnp.tanh(SQRT_TWO_PI * (values + 0.044715 * values * values * values))
    slope = SQRT_TWO_PI * (1.0 + 3.0 * 0.044715 * values * values)
    return 0.5 * values * (1.0 + inner), 0.5 * (1.0 + inner) + 0.5 * values * (1.0 - inner * inner) * slope


def expert_kernel(mode, layer, dp_count, *refs):
    forward, backward = mode in ("fwd", "both"), mode in ("both", "bwd")
    refs = list(refs)

    def take(count):
        taken = refs[:count]
        del refs[:count]
        return taken

    (sending,) = take(1)
    far = take(2) if mode == "both" else None
    (x_in,) = take(1) if mode == "bwd" else (None,)
    w_in, w_out = take(2)
    results = take(forward + backward)
    (x_o,) = take(1) if mode == "fwd" else (None,)
    gw_in_o, gw_out_o = take(2) if backward else (None, None)
    w1, w2, wsem, wssem, wrsem = take(5)
    x_all, xsem = take(2)
    recv_a, recv_b, ssem, asem, fsem, bsem = take(6)
    paths = [take(9) for _ in results]
    if backward:
        g_all, hid_all, ig_all, stage, gsem, grsem, glsem = take(7)

    d = lax.axis_index("dp")
    me, core, mate, across, diagonal = mp_places()
    row = me // 2
    index = d * 2 + core
    experts = dp_count * 2
    model = w1.shape[1]
    half = model // 2
    rows_a = x_all.shape[1] // 2
    tile = sending.shape[1]
    ahead = 3

    barrier = pltpu.get_barrier_semaphore()

    def greet(k, carry):
        signal_to(barrier, dp=lax.rem(d + k // 2, dp_count), mp=row * 2 + lax.rem(core + k % 2, 2))
        return carry

    lax.fori_loop(1, experts, greet, 0)
    signal_to(barrier, mp=across)
    pl.semaphore_wait(barrier, experts)

    def send_wave(k):
        dd = lax.rem(d + k, dp_count)
        for cc in range(2):
            to = dd * 2 + cc

            @pl.when(to == index)
            def _():
                pltpu.make_async_copy(sending.at[to], recv_a.at[index], asem.at[index]).start()

            @pl.when(to != index)
            def _():
                remote(sending.at[to], recv_a.at[index], ssem.at[to], asem.at[index], dp=dd, mp=row * 2 + cc).start()

    for k in range(ahead):
        send_wave(k)
    copies = []
    for n, (source, held) in enumerate(((w_in, w1), (w_out, w2))):
        copies.append(remote(source.at[layer, 1 - core], held.at[core], wssem.at[n], wrsem.at[n], mp=mate))
        copies.append(pltpu.make_async_copy(source.at[layer, core], held.at[core], wsem.at[n]))
    if mode == "bwd":
        copies.append(pltpu.make_async_copy(x_in, x_all, xsem))
    for copy in copies:
        copy.start()
    for copy in copies:
        copy.wait()

    def source_of(g):
        return lax.rem(d + dp_count - g, dp_count)

    def unpack(held, g, side, into, gates):
        base = side * rows_a
        s0 = source_of(g)
        tails = []
        for cc in range(2):
            src = s0 * 2 + cc
            block = held[src]
            factors = None if gates is None else gates[src][:, 7 * half :].astype(F32)

            def factor(i):
                return factors[:, 3 * i : 3 * i + 1] + factors[:, 3 * i + 1 : 3 * i + 2] + factors[:, 3 * i + 2 : 3 * i + 3]

            for i in range(3):
                piece = block[:, i * model : (i + 1) * model]
                if gates is not None:
                    piece = (piece.astype(F32) * factor(i)).astype(BF)
                into[g, base + (2 * i + cc) * tile : base + (2 * i + cc + 1) * tile, :] = piece
            tail = unfold_tail(block[:, 3 * model : 7 * half], half)
            tails.append(tail if gates is None else tail * factor(3)[0:8, :])
        into[g, base + 6 * tile : base + 7 * tile, :] = jnp.concatenate(tails, 0).astype(BF)

    def forward_copy(s0):
        two = pl.ds(s0 * 2, 2)
        return remote(recv_a.at[two], recv_b.at[two], fsem.at[s0], bsem.at[s0], mp=across)

    def partial_copy(path, g):
        kept, part, pssem, prsem, ret_s, ret, rssem, rrsem, psend = path
        return remote(psend.at[g], part.at[g], pssem.at[g], prsem.at[g], mp=across)

    def compute(g):
        x = x_all[g]
        totals = [0.0] * len(results)
        for q in range(2):
            inner = nn(x, w1[q])
            if backward:
                value, slope = gelu_grad(inner)
                hidden = value.astype(BF)
                hid_all[q, g] = hidden
                grad = (nt(g_all[g], w2[q]) * slope).astype(BF)
                ig_all[q, g] = grad
                totals[-1] = totals[-1] + nt(grad, w1[q])
            else:
                hidden = gelu_tanh(inner).astype(BF)
            if forward:
                totals[0] = totals[0] + nn(hidden, w2[q])
        return totals

    def give_back(path, g):
        kept, part, pssem, prsem, ret_s, ret, rssem, rrsem, psend = path
        partial_copy(path, g).wait_recv()
        total = kept[lax.rem(g, 2)] + part[g].astype(F32)
        s0 = source_of(g)
        for cc in range(2):
            src = s0 * 2 + cc
            for i in range(3):
                at = (2 * i + cc) * tile
                ret_s[src, :, i * model : (i + 1) * model] = total[at : at + tile, :].astype(BF)
            at = 6 * tile + 8 * cc
            ret_s[src, :, 3 * model :] = jnp.concatenate(
                [total[at : at + 8, 0:half], total[at : at + 8, half:]], 0
            ).astype(BF)

            @pl.when(src == index)
            def _():
                pltpu.make_async_copy(ret_s.at[src], ret.at[index], rrsem.at[index]).start()

            @pl.when(src != index)
            def _():
                remote(ret_s.at[src], ret.at[index], rssem.at[src], rrsem.at[index], dp=s0, mp=row * 2 + cc).start()

    def products(n, q, part):
        half_groups = pl.ds(part * dp_count // 2, dp_count // 2)
        count = dp_count * rows_a
        if n == 0:
            left, right = x_all[half_groups], ig_all[q, half_groups]
        else:
            left, right = hid_all[q, half_groups], g_all[half_groups]
        return tn(left.reshape(count, model), right.reshape(count, model))

    def step(i, carry):
        @pl.when(i < dp_count)
        def _():
            s0 = source_of(i)
            for cc in range(2):
                src = s0 * 2 + cc
                pltpu.make_async_copy(recv_a.at[src], recv_a.at[src], asem.at[src]).wait()
            forward_copy(s0).start()

        @pl.when(i + ahead < dp_count)
        def _():
            send_wave(i + ahead)

        @pl.when((i >= 1) & (i <= dp_count))
        def _():
            g = i - 1
            forward_copy(source_of(g)).wait_recv()
            for side, held in enumerate((recv_a, recv_b)):
                if forward:
                    unpack(held, g, side, x_all, None)
                if mode == "both":
                    unpack(far[side], g, side, g_all, held)
                elif mode == "bwd":
                    unpack(held, g, side, g_all, None)
            for path, total in zip(paths, compute(g)):
                kept, psend = path[0], path[8]
                kept[lax.rem(g, 2)] = total[0:rows_a, :]
                psend[g] = total[rows_a:, :].astype(BF)
                partial_copy(path, g).start()

        @pl.when(i >= 2)
        def _():
            for path in paths:
                give_back(path, i - 2)

        if backward:
            for n in range(2):
                for q in range(2):

                    @pl.when(i == dp_count // 2 + 1 + 2 * n + q)
                    def _():
                        stage[n, q] = products(n, q, 0)

        return carry

    lax.fori_loop(0, dp_count + 2, step, 0)
    if mode == "fwd":
        saved = pltpu.make_async_copy(x_all, x_o, xsem)
        saved.start()
    if backward:
        outs = (gw_in_o, gw_out_o)
        copies = []
        for n in range(2):
            stage[n, 1 - core] += products(n, 1 - core, 1)
            copy = remote(stage.at[n, 1 - core], outs[n].at[core], gsem.at[n], grsem.at[n], mp=mate)
            copy.start()
            copies.append(copy)
        for n in range(2):
            stage[n, core] += products(n, core, 1)
            copy = pltpu.make_async_copy(stage.at[n, core], outs[n].at[core], glsem.at[n])
            copy.start()
            copies.append(copy)
    for path, result in zip(paths, results):
        kept, part, pssem, prsem, ret_s, ret, rssem, rrsem, psend = path

        def end(e, carry):
            pltpu.make_async_copy(ret.at[e], ret.at[e], rrsem.at[e]).wait()

            @pl.when(e != index)
            def _():
                pltpu.make_async_copy(ret_s.at[e], ret_s.at[e], rssem.at[e]).wait()

            return carry

        lax.fori_loop(0, experts, end, 0)

        def end_group(g, carry):
            pltpu.make_async_copy(psend.at[g], psend.at[g], pssem.at[g]).wait()
            return carry

        lax.fori_loop(0, dp_count, end_group, 0)
        result[...] = ret[...]

    def end_send(e, carry):
        @pl.when(e != index)
        def _():
            pltpu.make_async_copy(sending.at[e], sending.at[e], ssem.at[e]).wait()

        return carry

    lax.fori_loop(0, experts, end_send, 0)

    def end_pair(s0, carry):
        two = pl.ds(s0 * 2, 2)
        pltpu.make_async_copy(recv_a.at[two], recv_a.at[two], fsem.at[s0]).wait()
        return carry

    lax.fori_loop(0, dp_count, end_pair, 0)
    if mode == "fwd":
        saved.wait()
    if backward:
        for n in range(2):
            copies[n].wait()
            copies[2 + n].wait()


def expert_call(mode, layer, number, dp_count, send, far, x_in, w_in, w_out):
    forward, backward = mode in ("fwd", "both"), mode in ("both", "bwd")
    experts, tile, _ = send.shape
    model = w_in.shape[2]
    block = (experts, tile, 7 * model // 2)
    rows = 2 * 7 * tile
    args, specs = [send], [VMEM]
    if mode == "both":
        args += far
        specs += [VMEM] * 2
    if mode == "bwd":
        args.append(x_in)
        specs.append(ANY)
    args += [w_in, w_out]
    specs += [ANY, ANY]
    outs, out_specs = [], []

    def out(dims, kind, spec):
        outs.append(jax.ShapeDtypeStruct(dims, kind))
        out_specs.append(spec)

    for _ in range(forward + backward):
        out(block, BF, VMEM)
    if mode == "fwd":
        out((dp_count, rows, model), BF, ANY)
    if backward:
        out((2, model, model), F32, ANY)
        out((2, model, model), F32, ANY)
    scratch = [
        pltpu.VMEM((2, model, model), BF),
        pltpu.VMEM((2, model, model), BF),
        dma(2),
        dma(2),
        dma(2),
        pltpu.VMEM((dp_count, rows, model), BF),
        dma(),
        pltpu.VMEM(send.shape, BF),
        pltpu.VMEM(send.shape, BF),
        dma(experts),
        dma(experts),
        dma(dp_count),
        dma(dp_count),
    ]
    for _ in range(forward + backward):
        scratch += [
            pltpu.VMEM((2, rows // 2, model), F32),
            pltpu.VMEM((dp_count, rows // 2, model), BF),
            dma(dp_count),
            dma(dp_count),
            pltpu.VMEM(block, BF),
            pltpu.VMEM(block, BF),
            dma(experts),
            dma(experts),
            pltpu.VMEM((dp_count, rows // 2, model), BF),
        ]
    if backward:
        scratch += [
            pltpu.VMEM((dp_count, rows, model), BF),
            pltpu.VMEM((2, dp_count, rows, model), BF),
            pltpu.VMEM((2, dp_count, rows, model), BF),
            pltpu.VMEM((2, 2, model, model), F32),
            dma(2),
            dma(2),
            dma(2),
        ]
    return pl.pallas_call(
        functools.partial(expert_kernel, mode, layer, dp_count),
        out_shape=tuple(outs),
        in_specs=specs,
        out_specs=tuple(out_specs),
        scratch_shapes=scratch,
        compiler_params=pltpu.CompilerParams(
            collective_id=number, has_side_effects=True, vmem_limit_bytes=VMEM_BYTES
        ),
    )(*args)


def spread_kernel(size, buckets, count, *refs):
    parts, grads, small = refs[:count], refs[count : 3 * count], refs[3 * count]
    qkv_o, attn_o, in_o, out_o, gain_a_o, bias_o, gain_f_o, router_o, sem = refs[3 * count + 1 :]
    step = pl.program_id(0)
    copies = []
    for n in range(count):
        copies.append(pltpu.make_async_copy(grads[2 * n].at[0], in_o.at[n, step], sem.at[2 * n]))
        copies.append(pltpu.make_async_copy(grads[2 * n + 1].at[0], out_o.at[n, step], sem.at[2 * n + 1]))
    for copy in copies:
        copy.start()
    for n in range(count):
        mp_count, blocks, heads, rows, _ = parts[n].shape
        pieces = [
            parts[n][m, :, h].reshape(blocks * rows, 4 * size).astype(F32) for m in range(mp_count) for h in range(heads)
        ]
        qkv_o[n] = jnp.concatenate([p[:, t * size : (t + 1) * size] for t in range(3) for p in pieces], 1)
        for number, p in enumerate(pieces):
            attn_o[n, number * size : (number + 1) * size, :] = p[:, 3 * size :].T
    lines = small.shape[0] // count
    for n in range(count):
        gain_a_o[n : n + 1, :] = small[n * lines, 0:1, :]
        gain_f_o[n : n + 1, :] = small[n * lines, 1:2, :]
        tiles = [small[n * lines + 1, :, i * LANES : (i + 1) * LANES] for i in range(buckets // 8)]
        bias_o[n] = jnp.concatenate(tiles, 0).T[0 : bias_o.shape[1], :]
        router_o[n] = jnp.concatenate([small[n * lines + i] for i in range(2, lines)], 0)
    for copy in copies:
        copy.wait()


def spread_call(parts, grads, small, size, heads, buckets, experts):
    mp_count, blocks, own_heads, rows, wide = parts[0].shape
    layers, model = len(parts), blocks * rows
    steps = grads[0].shape[0]
    return pl.pallas_call(
        functools.partial(spread_kernel, size, buckets, layers),
        grid=(steps,),
        out_shape=(
            jax.ShapeDtypeStruct((layers, model, 3 * heads * size), F32),
            jax.ShapeDtypeStruct((layers, heads * size, model), F32),
            jax.ShapeDtypeStruct((layers,) + grads[0].shape, F32),
            jax.ShapeDtypeStruct((layers,) + grads[1].shape, F32),
            jax.ShapeDtypeStruct((layers, model), F32),
            jax.ShapeDtypeStruct((layers, heads, buckets), F32),
            jax.ShapeDtypeStruct((layers, model), F32),
            jax.ShapeDtypeStruct((layers, experts, model), F32),
        ),
        in_specs=[pl.BlockSpec((mp_count, blocks // steps, own_heads, rows, wide), lambda i: (0, i, 0, 0, 0))] * layers
        + [pl.BlockSpec((1,) + g.shape[1:], lambda i: (i, 0, 0)) for g in grads]
        + [VMEM],
        out_specs=(
            pl.BlockSpec((layers, model // steps, 3 * heads * size), lambda i: (0, i, 0)),
            pl.BlockSpec((layers, heads * size, model // steps), lambda i: (0, 0, i)),
            ANY,
            ANY,
            VMEM,
            VMEM,
            VMEM,
            VMEM,
        ),
        scratch_shapes=[dma(2 * layers)],
        compiler_params=pltpu.CompilerParams(vmem_limit_bytes=VMEM_BYTES),
    )(*parts, *grads, small)


def fast_body(
    tokens, cotangent, w_qkv, w_attn, attn_gain, rel_bias, ffn_gain, router, w_in, w_out, cont_lengths, routes, slots, drops
):
    _, local, model = tokens.shape
    heads, buckets = rel_bias.shape[1:]
    size = model // heads
    layers = w_qkv.shape[0]
    dp_count, mp_count = lax.axis_size("dp"), lax.axis_size("mp")
    own_heads = heads // mp_count
    experts = dp_count * 2
    me = lax.axis_index("mp")
    block = (experts, 16, 7 * model // 2)
    pairs = jnp.concatenate(
        [routes.reshape(layers, local, 2), slots.reshape(layers, local, 2), 1 - drops.reshape(layers, local, 2)], 2
    )
    cols = jnp.pad(pairs, ((0, 0), (0, 0), (0, 2)))
    rows = cols.transpose(0, 2, 1)
    vecs = bias_vectors(lax.dynamic_slice_in_dim(rel_bias, me * own_heads, own_heads, 1))

    kept = [None] * layers
    back, far = None, None
    for l in range(layers):
        first, last = l == 0, l == layers - 1
        normal = [attn_gain, (w_qkv, l), vecs[l], (w_attn, l), ffn_gain, (router, l), (rows, l), (cols, l)]
        if first:
            specials = [tokens[0], cotangent[0], (rows, layers - 1)]
        else:
            before = kept[l - 1]
            specials = [before["middle"], before["out"], (cols, l - 1), before["gates"]]
        if last:
            specials += far
        got = pre_call(
            l, layers, l, own_heads, size, cont_lengths, normal, mp_count, dp_count, local, model, specials, block
        )
        got = [tokens[0]] + list(got) if first else list(got)
        names = ("stream", "normed", "qkv", "mixed", "lse", "middle", "ffn", "gates")
        kept[l] = k = dict(zip(names, got))
        if first:
            far = got[9:11]
        if last:
            far = [far[0], got[9]]
            k["out"], back, k["gw_in"], k["gw_out"] = expert_call("both", l, 5, dp_count, got[8], far, None, w_in, w_out)
        else:
            k["out"], k["x_rows"] = expert_call("fwd", l, 4, dp_count, got[8], None, None, w_in, w_out)

    flow = cotangent[0]
    for l in reversed(range(layers)):
        k = kept[l]
        last = l == layers - 1
        normal = [
            vecs[l], back, k["out"], flow, k["middle"], k["ffn"], k["gates"], (cols, l), (router, l), ffn_gain,
            k["normed"], k["qkv"], k["mixed"], k["lse"], (w_attn, l), (w_qkv, l), k["stream"], attn_gain,
        ]
        extra = [(rows, l - 1), (cols, l - 1), kept[l - 1]["gates"]] if last else [heads_sum, small]
        got = back_call(
            l, layers, 6 + last, own_heads, size, buckets, cont_lengths, normal, mp_count, dp_count, local, model, block, extra
        )
        if last:
            flow, output, send, heads_sum, small = got
            b = kept[l - 1]
            back, b["gw_in"], b["gw_out"] = expert_call("bwd", l - 1, 10, dp_count, send, None, b["x_rows"], w_in, w_out)
        else:
            flow, upper, lower, small = got
    grads = [kept[l][name] for l in range(layers) for name in ("gw_in", "gw_out")]
    grad_qkv, grad_attn, grad_in, grad_out, grad_a, grad_bias, grad_f, grad_router = spread_call(
        [lower, upper], grads, small, size, heads, buckets, experts
    )
    return (
        output[None], flow[None], grad_qkv, grad_attn, grad_a, grad_bias, grad_f, grad_router.transpose(0, 2, 1), grad_in, grad_out,
    )


def chosen_body(
    tokens, cotangent, w_qkv, w_attn, attn_gain, rel_bias, ffn_gain, router, w_in, w_out, cont_lengths, routes, slots, drops
):
    groups, local, model = tokens.shape
    heads = rel_bias.shape[1]
    dp_count, mp_count = lax.axis_size("dp"), lax.axis_size("mp")
    capacity = max(2, 9 * 2 * groups * local // (8 * w_in.shape[1] * dp_count))
    seq = local * mp_count
    fits = (
        groups == 1
        and w_qkv.shape[0] == 2
        and mp_count == 4
        and dp_count == 8
        and router.shape[2] == 16
        and rel_bias.shape[2] == 32
        and heads % mp_count == 0
        and model // heads == 64
        and model % 256 == 0
        and local % 128 == 0
        and w_in.shape[1:] == (2, model, model)
        and w_out.shape[1:] == (2, model, model)
        and 48 < capacity <= 56
        and seq > PROMPT
        and (seq - PROMPT) % QB == 0
    )
    plan = fast_body if fits else body
    return plan(
        tokens, cotangent, w_qkv, w_attn, attn_gain, rel_bias, ffn_gain, router, w_in, w_out, cont_lengths, routes, slots, drops
    )


def solution(mesh):
    return jax.shard_map(
        chosen_body,
        mesh=mesh,
        in_specs=(
            P("dp", "mp", None),
            P("dp", "mp", None),
            P(),
            P(),
            P(),
            P(),
            P(),
            P(),
            P(None, "dp", None, "mp"),
            P(None, "dp", "mp", None),
            P("dp", None),
            P(None, "dp", "mp", None),
            P(None, "dp", "mp", None),
            P(None, "dp", "mp", None),
        ),
        out_specs=(
            P("dp", "mp", None),
            P("dp", "mp", None),
            P(),
            P(),
            P(),
            P(),
            P(),
            P(),
            P(None, "dp", None, "mp"),
            P(None, "dp", "mp", None),
        ),
        check_vma=False,
    )
```

```python
import functools

import jax
import jax.numpy as jnp
from jax import lax
from jax.experimental import pallas as pl
from jax.experimental.pallas import tpu as pltpu
from jax.sharding import PartitionSpec as P

PROMPT = 1024


EPSILON = 1e-06
SQRT_TWO_PI = 0.7978845608028654
THRESHOLDS = (16, 20, 24, 32, 40, 48, 64, 80, 96, 128, 160, 192, 256, 384, 512, 768)
HIGHEST = lax.Precision.HIGHEST


def rms_scale(values, gain_row):
    return (
        values * lax.rsqrt(jnp.mean(values * values, axis=-1, keepdims=True) + EPSILON) * gain_row
    )


def gelu_tanh(values):
    return (
        0.5
        * values
        * (1.0 + jnp.tanh(SQRT_TWO_PI * (values + 0.044715 * values * values * values)))
    )


def bucket_of(distance):
    counted = jnp.minimum(distance, 15)
    for threshold in THRESHOLDS:
        counted = counted + (distance >= threshold).astype(jnp.int32)
    return counted


def geometry(lengths, row_ids):
    starts = PROMPT + jnp.cumsum(lengths, axis=-1) - lengths
    inside = row_ids[None, :, None] >= starts[:, None, :]
    segment = jnp.sum(inside.astype(jnp.int32), axis=-1) - 1
    begin_at = jnp.max(jnp.where(inside, starts[:, None, :], 0), axis=-1)
    position = jnp.where(
        row_ids[None, :] < PROMPT, row_ids[None, :], PROMPT + row_ids[None, :] - begin_at
    )
    return (position, segment)


def visibility(query_pos, query_seg, key_pos, key_seg):
    query_at = query_pos[:, :, None]
    query_in = query_seg[:, :, None]
    key_at = key_pos[:, None, :]
    key_in = key_seg[:, None, :]
    earlier = key_at <= query_at
    allowed = (key_in < 0) & ((query_in >= 0) | earlier) | (key_in >= 0) & (
        key_in == query_in
    ) & earlier
    bucket = bucket_of(jnp.maximum(query_at - key_at, 0))
    return (allowed, bucket)


def bias_table(bias_row, bucket):
    full_bias = jnp.zeros((bias_row.shape[0],) + bucket.shape, jnp.float32)
    for number in range(bias_row.shape[1]):
        full_bias = full_bias + jnp.where(
            bucket[None] == number, bias_row[:, number][:, None, None, None], 0.0
        )
    return full_bias


def score_block(query_b, key_every, full_bias, allowed, factor):
    raw = (
        jnp.einsum("grhd,gkhd->hgrk", query_b, key_every, preferred_element_type=jnp.float32)
        * factor
    )
    raw = raw + full_bias
    return jnp.where(allowed[None], raw, -1e30)


def body(
    tokens,
    cotangent,
    w_qkv,
    w_attn,
    attn_gain,
    rel_bias,
    ffn_gain,
    router,
    w_in,
    w_out,
    cont_lengths,
    routes,
    slots,
    drops,
):
    groups, local_rows, model_width = tokens.shape
    head_count = rel_bias.shape[1]
    bucket_count = rel_bias.shape[2]
    head_size = model_width // head_count
    factor = head_size ** (-0.5)
    layer_count = w_qkv.shape[0]
    dp_count = lax.axis_size("dp")
    mp_count = lax.axis_size("mp")
    seq_len = local_rows * mp_count
    local_experts = w_in.shape[1]
    expert_total = local_experts * dp_count
    tok_count = groups * local_rows
    capacity = max(2, 9 * 2 * tok_count // (8 * expert_total))
    slot_total = expert_total * capacity
    rows_here = lax.axis_index("mp") * local_rows + jnp.arange(local_rows, dtype=jnp.int32)
    rows_every = jnp.arange(seq_len, dtype=jnp.int32)
    query_pos, query_seg = geometry(cont_lengths, rows_here)
    key_pos, key_seg = geometry(cont_lengths, rows_every)
    allowed, bucket = visibility(query_pos, query_seg, key_pos, key_seg)
    route_all = routes.reshape(layer_count, tok_count, 2)
    slot_all = slots.reshape(layer_count, tok_count, 2)
    keep_all = (1 - drops.reshape(layer_count, tok_count, 2)).astype(jnp.float32)
    head_shape = (groups, seq_len, head_count, head_size)
    stream = tokens.reshape(tok_count, model_width).astype(jnp.float32)
    stored = []
    for layer_now in range(layer_count):
        normed_b = rms_scale(stream, attn_gain[layer_now]).astype(jnp.bfloat16)
        qkv_all = jnp.dot(normed_b, w_qkv[layer_now], preferred_element_type=jnp.float32).astype(
            jnp.bfloat16
        )
        query_b = qkv_all[:, :model_width].reshape(groups, local_rows, head_count, head_size)
        key_own = qkv_all[:, model_width : 2 * model_width].reshape(groups, local_rows, model_width)
        value_own = qkv_all[:, 2 * model_width :].reshape(groups, local_rows, model_width)
        key_every, value_every = (
            lax.all_gather(key_own, "mp", axis=1, tiled=True),
            lax.all_gather(value_own, "mp", axis=1, tiled=True),
        )
        key_every = key_every.reshape(head_shape)
        value_every = value_every.reshape(head_shape)
        full_bias = bias_table(rel_bias[layer_now], bucket)
        scores = score_block(query_b, key_every, full_bias, allowed, factor)
        top_score = jnp.max(scores, axis=-1, keepdims=True)
        weights = jnp.exp(scores - top_score)
        weight_sum = jnp.sum(weights, axis=-1, keepdims=True)
        log_total = top_score + jnp.log(weight_sum)
        probs_b = (weights / weight_sum).astype(jnp.bfloat16)
        mixed_b = jnp.einsum(
            "hgrk,gkhd->grhd", probs_b, value_every, preferred_element_type=jnp.float32
        )
        mixed_b = mixed_b.reshape(tok_count, model_width).astype(jnp.bfloat16)
        middle = stream + jnp.dot(mixed_b, w_attn[layer_now], preferred_element_type=jnp.float32)
        kept_keys = (key_every, value_every)
        ffn_b = rms_scale(middle, ffn_gain[layer_now]).astype(jnp.bfloat16)
        logits = jnp.dot(ffn_b, router[layer_now], preferred_element_type=jnp.float32)
        chosen = route_all[layer_now]
        keep_pair = keep_all[layer_now]
        gate_pair = jax.nn.softmax(jnp.take_along_axis(logits, chosen, axis=1), axis=-1)
        target = chosen * capacity + slot_all[layer_now]
        sending = jnp.where(
            keep_pair[:, :, None] > 0, ffn_b[:, None, :], jnp.zeros((), jnp.bfloat16)
        )
        send_rows = (
            jnp.zeros((slot_total, model_width), jnp.bfloat16)
            .at[target.reshape(-1)]
            .add(sending.reshape(-1, model_width))
        )
        arrived = lax.all_to_all(
            send_rows.reshape(dp_count, local_experts, capacity, model_width),
            "dp",
            split_axis=0,
            concat_axis=0,
            tiled=True,
        )
        rows_in = lax.all_gather(arrived, "mp", axis=0, tiled=True)
        up_block = w_in[layer_now]
        down_block = w_out[layer_now]
        inner_act = jnp.einsum(
            "secd,edf->secf", rows_in, up_block, preferred_element_type=jnp.float32
        )
        hidden_b = gelu_tanh(inner_act).astype(jnp.bfloat16)
        summed = lax.psum_scatter(
            jnp.einsum(
                "secf,efd->secd", hidden_b, down_block, preferred_element_type=jnp.float32
            ).astype(jnp.bfloat16),
            "mp",
            scatter_dimension=0,
            tiled=True,
        )
        kept_rows = (rows_in, inner_act, hidden_b)
        returned = lax.all_to_all(summed, "dp", split_axis=0, concat_axis=0, tiled=True).reshape(
            slot_total, model_width
        )
        pair_out = returned[target].astype(jnp.float32)
        stored.append(
            (
                stream,
                normed_b,
                query_b,
                key_own,
                value_own,
                kept_keys,
                log_total,
                mixed_b,
                middle,
                ffn_b,
                chosen,
                keep_pair,
                gate_pair,
                target,
                pair_out,
                kept_rows,
                full_bias,
            )
        )
        stream = middle + jnp.sum((gate_pair * keep_pair)[:, :, None] * pair_out, axis=1)
    output = stream.astype(jnp.bfloat16).reshape(groups, local_rows, model_width)
    one_hot = (
        bucket[None] == jnp.arange(bucket_count, dtype=jnp.int32)[:, None, None, None]
    ).astype(jnp.bfloat16)
    expert_ids = jnp.arange(expert_total, dtype=jnp.int32)
    qkv_grads = [None] * layer_count
    attn_grads = [None] * layer_count
    attn_gain_grads = [None] * layer_count
    bias_grads = [None] * layer_count
    ffn_gain_grads = [None] * layer_count
    router_grads = [None] * layer_count
    up_grads = [None] * layer_count
    down_grads = [None] * layer_count
    flowing = cotangent.reshape(tok_count, model_width).astype(jnp.float32)
    for layer_now in reversed(range(layer_count)):
        (
            stream_in,
            normed_b,
            query_b,
            key_own,
            value_own,
            kept_keys,
            log_total,
            mixed_b,
            middle,
            ffn_b,
            chosen,
            keep_pair,
            gate_pair,
            target,
            pair_out,
            kept_rows,
            full_bias,
        ) = stored[layer_now]
        weighted = gate_pair * keep_pair
        pair_grad = weighted[:, :, None] * flowing[:, None, :]
        gate_grad = keep_pair * jnp.sum(flowing[:, None, :] * pair_out, axis=-1)
        picked_grad = gate_pair * (
            gate_grad - jnp.sum(gate_pair * gate_grad, axis=-1, keepdims=True)
        )
        logit_grad = jnp.sum(
            picked_grad[:, :, None] * (chosen[:, :, None] == expert_ids).astype(jnp.float32), axis=1
        )
        back_rows = (
            jnp.zeros((slot_total, model_width), jnp.float32)
            .at[target.reshape(-1)]
            .add(pair_grad.reshape(-1, model_width))
        )
        back_rows = back_rows.astype(jnp.bfloat16).reshape(
            dp_count, local_experts, capacity, model_width
        )
        grad_arrived = lax.all_to_all(back_rows, "dp", split_axis=0, concat_axis=0, tiled=True)
        grad_rows = lax.all_gather(grad_arrived, "mp", axis=0, tiled=True)
        up_block = w_in[layer_now]
        down_block = w_out[layer_now]
        rows_in, inner_act, hidden_b = kept_rows
        down_grad = jnp.einsum(
            "secf,secd->efd", hidden_b, grad_rows, preferred_element_type=jnp.float32
        )
        hidden_grad = jnp.einsum(
            "secd,efd->secf", grad_rows, down_block, preferred_element_type=jnp.float32
        )
        inner_grad = jax.vjp(gelu_tanh, inner_act)[1](hidden_grad)[0].astype(jnp.bfloat16)
        up_grad = jnp.einsum(
            "secd,secf->edf", rows_in, inner_grad, preferred_element_type=jnp.float32
        )
        rows_grad = lax.psum_scatter(
            jnp.einsum(
                "secf,edf->secd", inner_grad, up_block, preferred_element_type=jnp.float32
            ).astype(jnp.bfloat16),
            "mp",
            scatter_dimension=0,
            tiled=True,
        )
        up_grads[layer_now] = up_grad
        down_grads[layer_now] = down_grad
        grad_back = lax.all_to_all(
            rows_grad, "dp", split_axis=0, concat_axis=0, tiled=True
        ).reshape(slot_total, model_width)
        ffn_grad = jnp.sum(keep_pair[:, :, None] * grad_back[target].astype(jnp.float32), axis=1)
        ffn_grad = ffn_grad + jnp.einsum(
            "te,de->td", logit_grad, router[layer_now].astype(jnp.float32), precision=HIGHEST
        )
        router_grads[layer_now] = jnp.einsum(
            "td,te->de", ffn_b.astype(jnp.float32), logit_grad, precision=HIGHEST
        )
        middle_grad, ffn_gain_grads[layer_now] = jax.vjp(rms_scale, middle, ffn_gain[layer_now])[1](
            ffn_grad
        )
        middle_grad = middle_grad + flowing
        branch_grad = middle_grad.astype(jnp.bfloat16)
        attn_grads[layer_now] = jnp.einsum(
            "td,te->de", mixed_b, branch_grad, preferred_element_type=jnp.float32
        )
        mixed_grad = jnp.einsum(
            "te,de->td", branch_grad, w_attn[layer_now], preferred_element_type=jnp.float32
        )
        mixed_grad = mixed_grad.astype(jnp.bfloat16).reshape(
            groups, local_rows, head_count, head_size
        )
        key_every, value_every = kept_keys
        scores = score_block(query_b, key_every, full_bias, allowed, factor)
        probs = jnp.exp(scores - log_total)
        prob_grad = jnp.einsum(
            "grhd,gkhd->hgrk", mixed_grad, value_every, preferred_element_type=jnp.float32
        )
        score_grad = (
            probs * (prob_grad - jnp.sum(probs * prob_grad, axis=-1, keepdims=True))
        ).astype(jnp.bfloat16)
        query_grad = (
            jnp.einsum("hgrk,gkhd->grhd", score_grad, key_every, preferred_element_type=jnp.float32)
            * factor
        )
        key_part = (
            jnp.einsum("hgrk,grhd->gkhd", score_grad, query_b, preferred_element_type=jnp.float32)
            * factor
        )
        value_part = jnp.einsum(
            "hgrk,grhd->gkhd",
            probs.astype(jnp.bfloat16),
            mixed_grad,
            preferred_element_type=jnp.float32,
        )
        key_grad, value_grad = (
            lax.psum_scatter(
                key_part.reshape(groups, seq_len, model_width).astype(jnp.bfloat16),
                "mp",
                scatter_dimension=1,
                tiled=True,
            ).astype(jnp.float32),
            lax.psum_scatter(
                value_part.reshape(groups, seq_len, model_width).astype(jnp.bfloat16),
                "mp",
                scatter_dimension=1,
                tiled=True,
            ).astype(jnp.float32),
        )
        bias_grads[layer_now] = jnp.einsum(
            "hgrk,bgrk->hb", score_grad, one_hot, preferred_element_type=jnp.float32
        )
        qkv_grad = jnp.concatenate(
            [
                query_grad.reshape(tok_count, model_width),
                key_grad.reshape(tok_count, model_width),
                value_grad.reshape(tok_count, model_width),
            ],
            axis=1,
        ).astype(jnp.bfloat16)
        qkv_grads[layer_now] = jnp.einsum(
            "td,te->de", normed_b, qkv_grad, preferred_element_type=jnp.float32
        )
        normed_grad = jnp.einsum(
            "te,de->td", qkv_grad, w_qkv[layer_now], preferred_element_type=jnp.float32
        )
        stream_grad, attn_gain_grads[layer_now] = jax.vjp(
            rms_scale, stream_in, attn_gain[layer_now]
        )[1](normed_grad)
        flowing = middle_grad + stream_grad
    totals = lax.psum(
        (
            jnp.stack(qkv_grads),
            jnp.stack(attn_grads),
            jnp.stack(attn_gain_grads),
            jnp.stack(bias_grads),
            jnp.stack(ffn_gain_grads),
            jnp.stack(router_grads),
        ),
        ("dp", "mp"),
    )
    input_grad = flowing.reshape(groups, local_rows, model_width)
    return (
        output,
        input_grad,
        totals[0],
        totals[1],
        totals[2],
        totals[3],
        totals[4],
        totals[5],
        jnp.stack(up_grads),
        jnp.stack(down_grads),
    )


BF = jnp.bfloat16
F32 = jnp.float32
VMEM = pl.BlockSpec(memory_space=pltpu.VMEM)
SMEM = pl.BlockSpec(memory_space=pltpu.SMEM)
ANY = pl.BlockSpec(memory_space=pl.ANY)
VMEM_BYTES = 60 << 20
MESH = pl.DeviceIdType.MESH
LANES = 128
QB = 256


def nn(a, b):
    return lax.dot_general(a, b, (((1,), (0,)), ((), ())), preferred_element_type=F32)


def nt(a, b):
    return lax.dot_general(a, b, (((1,), (1,)), ((), ())), preferred_element_type=F32)


def tn(a, b):
    return lax.dot_general(a, b, (((0,), (0,)), ((), ())), preferred_element_type=F32)


def layer_spec(array, layer):
    zeros = (0,) * (array.ndim - 1)
    return pl.BlockSpec((None,) + array.shape[1:], lambda i: (layer,) + zeros, pipeline_mode=pl.Buffered(1))


def segments(lens, shape, dim):
    at = lax.broadcasted_iota(jnp.int32, shape, dim)
    segment = jnp.full(shape, -1, jnp.int32)
    begin = jnp.zeros(shape, jnp.int32)
    start = jnp.int32(0)
    for number in range(lens.shape[1]):
        inside = at >= start
        segment = segment + inside.astype(jnp.int32)
        begin = jnp.where(inside, start, begin)
        start = start + lens[0, number]
    return segment, at - begin


def bias_stage(vec, lens, table, cont_bias):
    width = vec.shape[1]
    rows = lax.broadcasted_iota(jnp.int32, (LANES, width), 0)
    skewed = jnp.broadcast_to(vec, (LANES, width))
    for bit in range(7):
        skewed = jnp.where((rows >> bit) % 2 == 1, pltpu.roll(skewed, 1 << bit, 1), skewed)
    table[...] = skewed[:, : width - LANES].T
    cont = cont_bias.shape[1]
    _, offset = segments(lens, (LANES, cont), 1)
    place = (lax.broadcasted_iota(jnp.int32, (LANES, cont), 0) == offset).astype(BF)
    full = table[0:PROMPT, :]
    high = full.astype(BF)
    low = (full - high.astype(F32)).astype(BF)
    cont_bias[...] = nn(jnp.concatenate([high, low], 1), jnp.concatenate([place, place], 0))


def blocks_of(seq):
    out = []
    for start in range(0, PROMPT, QB):
        out.append((start, start + QB, None))
    for start in range(0, seq - PROMPT, QB):
        out.append((PROMPT + start, PROMPT, max(0, start - LANES)))
    return out


def scores_of(keys, query, table, cont_bias, seg_col, seg_row, block, h):
    q0, prompt_keys, cont_from = block
    if cont_from is None:
        left = PROMPT - q0
        bias = jnp.concatenate(
            [table[left : left + prompt_keys, :], table[left - LANES : left - LANES + prompt_keys, :]], 1
        )
        return [(0, prompt_keys, nt(keys[h, 0:prompt_keys, :], query) + bias)]
    at = q0 - PROMPT
    first = nt(keys[h, 0:PROMPT, :], query) + cont_bias[:, at : at + QB]
    k0, k1 = PROMPT + cont_from, q0 + QB
    left = PROMPT + cont_from - at
    bias = jnp.concatenate(
        [table[left : left + k1 - k0, :], table[left - LANES : left - LANES + k1 - k0, :]], 1
    )
    same = seg_col[cont_from : at + QB, :][:, 0:1] == seg_row[:, at : at + QB]
    second = jnp.where(same, nt(keys[h, k0:k1, :], query) + bias, -1e30)
    return [(0, PROMPT, first), (k0, k1, second)]


def diagonals():
    width = PROMPT + 3 * LANES
    at = jnp.arange(width, dtype=jnp.int32)
    distance = jnp.where(at <= PROMPT, PROMPT - at, PROMPT + width - at)
    valid = (at <= PROMPT) | (at > width - LANES)
    return width, distance, valid


def bias_vectors(bias):
    _, distance, valid = diagonals()
    hot = bucket_of(distance)[None, :] == jnp.arange(bias.shape[-1], dtype=jnp.int32)[:, None]
    picked = jnp.sum(jnp.where(hot, bias[..., :, None], 0.0), axis=-2)
    return jnp.where(valid, picked, -1e30)


def scatter_rows(rows, values, send):
    experts, tile, _ = send.shape
    tokens, model = values[0].shape
    half = model // 2
    at = lax.broadcasted_iota(jnp.int32, (experts * tile, tokens), 0)
    place, piece = [], []
    for j in range(2):
        slot = rows[2 + j : 3 + j, :]
        piece.append(jnp.where(rows[4 + j : 5 + j, :] > 0, slot // tile, -1))
        place.append(rows[j : j + 1, :] * tile + slot % tile)

    def pick(number, shift, columns):
        hots = [
            (jnp.where(piece[j] == number, place[j] + shift, -1) == at) for j in range(2)
        ]
        if len(values) == 1:
            return nn((hots[0] | hots[1]).astype(BF), values[0][:, columns])
        return nn(hots[0].astype(BF), values[0][:, columns]) + nn(hots[1].astype(BF), values[1][:, columns])

    for i in range(3):
        send[:, :, i * model : (i + 1) * model] = pick(i, 0, slice(0, model)).astype(BF).reshape(experts, tile, model)
    tail = pick(3, 0, slice(0, half)) + pick(3, 8, slice(half, model))
    send[:, :, 3 * model : 3 * model + half] = tail.astype(BF).reshape(experts, tile, half)


def columns(rows):
    return rows[...].astype(F32).T.astype(jnp.int32)


def scatter_gates(rows, gates, send, start):
    experts, tile, _ = send.shape
    tokens = rows.shape[1]
    at = lax.broadcasted_iota(jnp.int32, (experts * tile, tokens), 0)
    lane = lax.broadcasted_iota(jnp.int32, (tokens, LANES), 1)
    total = 0.0
    for j in range(2):
        slot = rows[2 + j : 3 + j, :]
        piece = jnp.where(rows[4 + j : 5 + j, :] > 0, slot // tile, -1)
        place = rows[j : j + 1, :] * tile + slot % tile
        high = gates[j].astype(BF).astype(F32)
        rest = gates[j] - high
        mid = rest.astype(BF).astype(F32)
        part = jnp.where(lane % 3 == 0, high, jnp.where(lane % 3 == 1, mid, rest - mid))
        for i in range(4):
            hot = (jnp.where(piece == i, place, -1) == at).astype(BF)
            total = total + nn(hot, jnp.where(lane // 3 == i, part, 0.0).astype(BF))
    send[:, :, start:] = total.astype(BF).reshape(experts, tile, LANES)


def gather_rows(cols, j, back):
    experts, tile, wide = back.shape
    half = wide // 7
    model = 2 * half
    tokens = cols.shape[0]
    at = lax.broadcasted_iota(jnp.int32, (tokens, experts * tile), 1)
    slot = cols[:, 2 + j : 3 + j]
    piece = jnp.where(cols[:, 4 + j : 5 + j] > 0, slot // tile, -1)
    place = cols[:, j : j + 1] * tile + slot % tile
    total = 0.0
    for i in range(3):
        hot = (jnp.where(piece == i, place, -1) == at).astype(BF)
        total = total + nn(hot, back[:, :, i * model : (i + 1) * model].reshape(experts * tile, model))
    tail = back[:, :, 3 * model :].reshape(experts * tile, half)
    left = nn((jnp.where(piece == 3, place, -1) == at).astype(BF), tail)
    right = nn((jnp.where(piece == 3, place + 8, -1) == at).astype(BF), tail)
    return total + jnp.concatenate([left, right], 1)


def unfold_tail(block, half):
    wide = block.astype(F32)
    return jnp.concatenate([wide[0:8, :], wide[8:16, :]], 1)


def mp_places():
    me = lax.axis_index("mp")
    core, row = lax.rem(me, 2), me // 2
    return me, core, row * 2 + 1 - core, (1 - row) * 2 + core, (1 - row) * 2 + 1 - core


def signal_to(barrier, **place):
    pl.semaphore_signal(barrier, inc=1, device_id=place, device_id_type=MESH)


def remote(src, dst, send_sem, recv_sem, **place):
    return pltpu.make_async_remote_copy(
        src_ref=src, dst_ref=dst, send_sem=send_sem, recv_sem=recv_sem, device_id=place, device_id_type=MESH
    )


def greet_mp(count, dp_count=1):
    me, core, mate, across, diagonal = mp_places()
    d = lax.axis_index("dp")
    barrier = pltpu.get_barrier_semaphore()
    for to in (mate, across, diagonal)[:count]:
        signal_to(barrier, mp=to)
    for k in range(1, dp_count):
        signal_to(barrier, dp=lax.rem(d + k, dp_count), mp=me)
    pl.semaphore_wait(barrier, count + dp_count - 1)


def share_dp(held, ssem, rsem):
    d, me, count = lax.axis_index("dp"), lax.axis_index("mp"), held.shape[0]
    return [
        remote(held.at[d], held.at[d], ssem.at[k], rsem.at[k], dp=lax.rem(d + k, count), mp=me) for k in range(1, count)
    ]


def scatter_dp(part, come, ssem, rsem):
    d, me, count = lax.axis_index("dp"), lax.axis_index("mp"), part.shape[0]
    copies = []
    for k in range(1, count):
        to = lax.rem(d + k, count)
        copies.append(remote(part.at[to], come.at[d], ssem.at[k], rsem.at[k], dp=to, mp=me))
    return copies


def sum_dp(copies, part, come):
    d, count = lax.axis_index("dp"), part.shape[0]
    total = part[d].astype(F32)
    for k in range(1, count):
        copies[k - 1].wait_recv()
        total = total + come[lax.rem(d + count - k, count)].astype(F32)
    return total


def mean_square_scale(values):
    return lax.rsqrt(jnp.mean(values * values, axis=-1, keepdims=True) + EPSILON)


def norm_grads(values, gain, upstream):
    scale = mean_square_scale(values)
    scaled = upstream * gain
    drift = jnp.mean(values * scaled, axis=-1, keepdims=True)
    return scale * scaled - values * (scale * scale * scale * drift), jnp.sum(
        upstream * values * scale, axis=0, keepdims=True
    )


def pre_kernel(layer, layers, heads, size, *refs):
    refs = list(refs)

    def take(count):
        taken = refs[:count]
        del refs[:count]
        return taken

    first, last = layer == 0, layer == layers - 1
    lens, gain_a, w_qkv_in, vecs, w_attn_in, gain_f, router, rows = take(8)
    if first:
        tokens, cotangent, far_rows = take(3)
    else:
        before, returned, rows_in, gates_in = take(4)
        cols_in = columns(rows_in)
    g_in, g_half = take(2) if last else (None, None)
    (stream_o,) = (None,) if first else take(1)
    normed_o, qkv_o, mixed_o, lse_o, middle_o, ffn_o, gates_o, send_o = take(8)
    (g_o,) = take(1) if first or last else (None,)
    (g_half_o,) = take(1) if first else (None,)
    held, hssem, hrsem = take(3)
    w_qkv, w_attn, qkv_s, iosem = take(4)
    (stream_s,) = (None,) if first else take(1)
    weight, q_s, k_s, vt_s, table, cont_bias, mixt, segc, out_s, mixed_s, mssem, mrsem = take(12)
    if first:
        g_send, g_held, gssem, grsem = take(4)
    if first or last:
        g_over, gfsem, gbsem = take(3)
    me, core, mate, across, diagonal = mp_places()
    d = lax.axis_index("dp")
    dp_count = lax.axis_size("dp")
    seq, own = mixed_o.shape
    local, model = middle_o.shape
    parts = local // LANES
    cols = columns(rows)
    w_qkv_come = pltpu.make_async_copy(w_qkv_in.at[layer], w_qkv, iosem.at[0])
    w_attn_come = pltpu.make_async_copy(w_attn_in.at[layer], w_attn, iosem.at[1])
    normed_go = pltpu.make_async_copy(held, normed_o, iosem.at[2])
    qkv_go = pltpu.make_async_copy(qkv_s, qkv_o, iosem.at[3])
    goes = [normed_go, qkv_go]
    if not first:
        goes.append(pltpu.make_async_copy(stream_s, stream_o, iosem.at[4]))
    w_qkv_come.start()
    w_attn_come.start()

    barrier = pltpu.get_barrier_semaphore()
    for to in (mate, across, diagonal):
        signal_to(barrier, mp=to)
    if first:
        for k in range(2, 2 * dp_count):
            signal_to(barrier, dp=lax.rem(d + k // 2, dp_count), mp=(me // 2) * 2 + lax.rem(core + k % 2, 2))
        count = 3 + 2 * dp_count - 2
    else:
        count = 3
    if first:
        stream = tokens[...].astype(F32)
    else:
        stream = before[...]
        for j in range(2):
            stream = stream + gates_in[:, j : j + 1] * gather_rows(cols_in, j, returned)
        stream_s[...] = stream
        goes[2].start()
    held[me] = (stream * mean_square_scale(stream) * gain_a[layer : layer + 1, :]).astype(BF)
    pl.semaphore_wait(barrier, count)
    over = remote(held.at[me], held.at[me], hssem.at[1], hrsem.at[1], mp=across)
    to_mate = remote(held.at[me], held.at[me], hssem.at[0], hrsem.at[0], mp=mate)
    passed = remote(held.at[across], held.at[across], hssem.at[2], hrsem.at[2], mp=mate)
    over.start()
    to_mate.start()

    index = d * 2 + core

    def far_copy(k):
        dd, cc = lax.rem(d + k // 2, dp_count), lax.rem(core + k % 2, 2)
        if k == 0:
            return pltpu.make_async_copy(g_send.at[index], g_held.at[index], grsem.at[0])
        return remote(g_send.at[dd * 2 + cc], g_held.at[index], gssem.at[k], grsem.at[k], dp=dd, mp=(me // 2) * 2 + cc)

    def far_over(source, n):
        two = pl.ds(lax.rem(d + dp_count - n, dp_count) * 2, 2)
        return remote(source.at[two], g_over.at[two], gfsem.at[n], gbsem.at[n], mp=across)

    def far_wave(n):
        if n < dp_count:
            far_copy(2 * n).start()
            far_copy(2 * n + 1).start()

    def far_arrived(n):
        far_copy(2 * n).wait() if n == 0 else far_copy(2 * n).wait_recv()
        far_copy(2 * n + 1).wait_recv()

    if first:
        scatter_rows(far_rows, [cotangent[...]], g_send)
        for n in range(dp_count):
            far_wave(n)
    elif last:
        for n in range(2, dp_count):
            far_over(g_in, n).start()

    w_qkv_come.wait()
    for m in range(model // own):

        @pl.when(me == m)
        def _():
            for t in range(3):
                weight[:, t * own : (t + 1) * own] = w_qkv[:, t * model + m * own : t * model + (m + 1) * own]

    seg_row, _ = segments(lens, (1, seq - PROMPT), 1)
    segc[...] = segments(lens, (seq - PROMPT, LANES), 0)[0]

    def tables(h, carry):
        bias_stage(vecs[pl.ds(h, 1), :], lens, table.at[h], cont_bias.at[h])
        return carry

    lax.fori_loop(0, heads, tables, 0)

    def project(m):
        at = pl.ds(pl.multiple_of(m * local, LANES), local)
        part = nn(held[m], weight[...]).astype(BF)
        qkv_s[at, :] = part
        for h in range(heads):
            q_s[h, at, :] = part[:, h * size : (h + 1) * size] * BF(0.125)
            k_s[h, at, :] = part[:, own + h * size : own + (h + 1) * size]
            vt_s[h, :, at] = part[:, 2 * own + h * size : 2 * own + (h + 1) * size].astype(F32).T.astype(BF)

    project(me)
    to_mate.wait_recv()
    project(mate)
    over.wait_recv()
    passed.start()
    project(across)
    passed.wait_recv()
    project(diagonal)
    normed_go.start()
    qkv_go.start()

    def handed(n):
        return remote(out_s.at[n], mixed_s.at[me, n % parts], mssem.at[n], mrsem.at[me, n % parts], mp=n // parts)

    early = {1: 0, 3: 1}
    for number, block in enumerate(blocks_of(seq)):
        q0 = block[0]
        if first and number in early:
            far_arrived(early[number])
            far_over(g_held, early[number]).start()

        def head(h, carry):
            query = q_s[h, q0 : q0 + QB, :]
            scored = scores_of(k_s, query, table.at[h], cont_bias.at[h], segc, seg_row, block, h)
            top = functools.reduce(jnp.maximum, [jnp.max(s, axis=0, keepdims=True) for _, _, s in scored])
            total, mixed = 0.0, 0.0
            for k0, k1, s in scored:
                p = jnp.exp(s - top)
                total = total + jnp.sum(p, axis=0, keepdims=True)
                mixed = mixed + nn(vt_s[h, :, k0:k1], p.astype(BF))
            mixt[pl.ds(pl.multiple_of(h * size, size), size), :] = mixed / total
            lse_o[pl.ds(h, 1), q0 : q0 + QB] = top + jnp.log(total)
            return carry

        lax.fori_loop(0, heads, head, 0)
        done = mixt[...].T.astype(BF)
        mixed_o[q0 : q0 + QB, :] = done
        for half in range(QB // LANES):
            n = q0 // LANES + half
            middle_row = half * LANES + LANES // 2
            out_s[n] = jnp.concatenate(
                [done[half * LANES : middle_row, :], done[middle_row : (half + 1) * LANES, :]], 1
            )

            @pl.when(me == n // parts)
            def _():
                pltpu.make_async_copy(out_s.at[n], mixed_s.at[me, n % parts], mrsem.at[me, n % parts]).start()

            @pl.when(me != n // parts)
            def _():
                handed(n).start()

    w_attn_come.wait()
    middle = stream
    for m in range(mixed_s.shape[0]):
        for n in range(parts):
            pltpu.make_async_copy(mixed_s.at[m, n], mixed_s.at[m, n], mrsem.at[m, n]).wait()
        halves = [mixed_s[m, n][:, i * own : (i + 1) * own] for n in range(parts) for i in range(2)]
        middle = middle + nn(jnp.concatenate(halves, 0), w_attn[m * own : (m + 1) * own, :])
    middle_o[...] = middle
    ffn = (middle * mean_square_scale(middle) * gain_f[layer : layer + 1, :]).astype(BF)
    ffn_o[...] = ffn
    logits = nt(ffn, router[...])
    expert = lax.broadcasted_iota(jnp.int32, logits.shape, 1)
    chosen = [
        jnp.sum(jnp.where(expert == cols[:, j : j + 1], logits, 0.0), axis=1, keepdims=True) for j in range(2)
    ]
    top = jnp.maximum(chosen[0], chosen[1])
    powers = [jnp.exp(c - top) for c in chosen]
    gates = [p / (powers[0] + powers[1]) for p in powers]
    gates_o[...] = jnp.concatenate(gates, 1)
    scatter_rows(rows, [ffn], send_o)
    if last:
        scatter_gates(rows, gates, send_o, 7 * model // 2)
    if first:
        for n in range(2, dp_count):
            far_arrived(n)
        g_o[...] = g_held[...]
        for k in range(1, 2 * dp_count):
            far_copy(k).wait_send()
        for n in range(2):
            far_over(g_held, n).wait()
            two = pl.ds(lax.rem(d + dp_count - n, dp_count) * 2, 2)
            g_half_o[two] = g_over[two]
    elif last:
        for n in range(2):
            two = pl.ds(lax.rem(d + dp_count - n, dp_count) * 2, 2)
            g_o[two] = g_half[two]
        for n in range(2, dp_count):
            far_over(g_in, n).wait()
            two = pl.ds(lax.rem(d + dp_count - n, dp_count) * 2, 2)
            g_o[two] = g_over[two]
    for copy in goes:
        copy.wait()
    for copy in (to_mate, over, passed):
        copy.wait_send()
    for n in range(seq // LANES):

        @pl.when(me != n // parts)
        def _():
            handed(n).wait_send()


def pre_call(layer, layers, number, heads, size, lens, normal, mp_count, dp_count, local, model, specials, block):
    first, last = layer == 0, layer == layers - 1
    seq, own = local * mp_count, heads * size
    width = PROMPT + 3 * LANES
    args = list(normal) + list(specials)
    specs = [SMEM] + [layer_spec(*a) if isinstance(a, tuple) else VMEM for a in args]
    specs[2] = specs[4] = ANY
    narrow = block[:2] + (7 * model // 2,)
    send = narrow[:2] + (narrow[2] + LANES,) if last else narrow
    outs = [] if first else [((local, model), F32)]
    outs += [
        ((mp_count, local, model), BF), ((seq, 3 * own), BF), ((seq, own), BF), ((heads, seq), F32),
        ((local, model), F32), ((local, model), BF), ((local, 2), F32), (send, BF),
    ]
    if first or last:
        outs.append((narrow, BF))
    if first:
        outs.append((narrow, BF))
    out_specs = [VMEM] * len(outs)
    for n in (0, 1) if first else (0, 1, 2):
        out_specs[n] = ANY
    scratch = [
        pltpu.VMEM((mp_count, local, model), BF), dma(3), dma(3),
        pltpu.VMEM((model, 3 * model), BF), pltpu.VMEM((model, model), BF), pltpu.VMEM((seq, 3 * own), BF), dma(5),
        *([] if first else [pltpu.VMEM((local, model), F32)]),
        pltpu.VMEM((model, 3 * own), BF),
        pltpu.VMEM((heads, seq, size), BF),
        pltpu.VMEM((heads, seq, size), BF),
        pltpu.VMEM((heads, size, seq), BF),
        pltpu.VMEM((heads, width - LANES, LANES), F32),
        pltpu.VMEM((heads, PROMPT, seq - PROMPT), F32),
        pltpu.VMEM((own, QB), F32),
        pltpu.VMEM((seq - PROMPT, LANES), jnp.int32),
        pltpu.VMEM((seq // LANES, LANES // 2, 2 * own), BF),
        pltpu.VMEM((mp_count, local // LANES, LANES // 2, 2 * own), BF),
        dma(seq // LANES),
        dma(mp_count, local // LANES),
    ]
    if first:
        scratch += [pltpu.VMEM(narrow, BF), pltpu.VMEM(narrow, BF), dma(2 * dp_count), dma(2 * dp_count)]
    if first or last:
        scratch += [pltpu.VMEM(narrow, BF), dma(dp_count), dma(dp_count)]
    return pl.pallas_call(
        functools.partial(pre_kernel, layer, layers, heads, size),
        grid=(1,),
        out_shape=tuple(jax.ShapeDtypeStruct(shape, kind) for shape, kind in outs),
        in_specs=specs,
        out_specs=tuple(out_specs),
        scratch_shapes=scratch,
        compiler_params=pltpu.CompilerParams(
            collective_id=number, has_side_effects=True, vmem_limit_bytes=VMEM_BYTES
        ),
    )(lens, *[a[0] if isinstance(a, tuple) else a for a in args])


def shift_table(flat, width):
    rows = lax.broadcasted_iota(jnp.int32, flat.shape, 0)
    for bit in range(7):
        flat = jnp.where((rows >> bit) % 2 == 1, pltpu.roll(flat, width - (1 << bit), 1), flat)
    return jnp.sum(flat, axis=0, keepdims=True)


def back_kernel(layer, layers, heads, size, buckets, *refs):
    refs = list(refs)

    def take(count):
        taken = refs[:count]
        del refs[:count]
        return taken

    first, last = layer == 0, layer == layers - 1
    lens, vecs, back, returned, flow_in, middle, ffn, gates, rows_own, router, gain_f = take(11)
    normed_in, qkv_in, mixed, lse, w_attn_in, w_qkv_in, stream, gain_a = take(8)
    if first:
        above, small_above = take(2)
    else:
        rows_below, gates_below = take(2)
    (flow_o,) = take(1)
    if first:
        up_out, all_out, small_o = take(3)
    else:
        out_o, send_o, sum_o, small_o = take(4)
    held, hssem, hrsem = take(3)
    normed, qkv, w_attn, w_qkv, insem = take(5)
    normed_t, q_s, k_s, v_s, kt_s, do_s, table, cont_bias, fold, dtable, dk_s, dv_s, dqt, segc, hot, bias_s, gw_a, router_s = take(18)
    dq_s, dq_fold, dq_held, qssem, qrsem, part, come, pssem, prsem = take(9)
    if first:
        small_s, small_come, small_mp, tsem, usem, csem, dsem, vsem, zsem = take(9)
        assem, arsem, ossem, orsem = take(4)
        ussem, ursem, wssem, wrsem = take(4)
        up_o, all_o, outsem = take(3)
    me, core, mate, across, diagonal = mp_places()
    d = lax.axis_index("dp")
    dp_count = part.shape[0]
    local, model = middle.shape
    seq, own = mixed.shape
    cont = seq - PROMPT
    width = vecs.shape[1]
    places = mixed.shape[0] // local
    cols = columns(rows_own)
    sources = (normed_in, qkv_in, w_attn_in.at[layer], w_qkv_in.at[layer])
    come_in = [pltpu.make_async_copy(s, h, insem.at[n]) for n, (s, h) in enumerate(zip(sources, (normed, qkv, w_attn, w_qkv)))]
    for copy in come_in:
        copy.start()

    def dp_share(held_all, ssem, rsem, k):
        return remote(held_all.at[me, d], held_all.at[me, d], ssem.at[k], rsem.at[k], dp=lax.rem(d + k, dp_count), mp=me)

    def mp_share(held_all, ssem, rsem, n, j):
        whose = across if n == 2 else me
        return remote(
            held_all.at[whose, j], held_all.at[whose, j], ssem.at[n, j], rsem.at[n, j], mp=across if n == 1 else mate
        )

    greet_mp(3, dp_count=dp_count)
    if first:
        up_o[me, d] = above[...]
        for k in range(1, dp_count - 2):
            dp_share(up_o, ussem, ursem, k).start()

    flow = flow_in[...].astype(F32)
    outs = [gather_rows(cols, j, returned) for j in range(2)]
    gate = [gates[:, j : j + 1] for j in range(2)]
    keep = [cols[:, 4 + j : 5 + j].astype(F32) for j in range(2)]
    if last:
        out_o[...] = (middle[...] + gate[0] * keep[0] * outs[0] + gate[1] * keep[1] * outs[1]).astype(BF)
    gate_grad = [keep[j] * jnp.sum(flow * outs[j], axis=1, keepdims=True) for j in range(2)]
    shared = gate[0] * gate_grad[0] + gate[1] * gate_grad[1]
    expert = lax.broadcasted_iota(jnp.int32, (local, router.shape[0]), 1)
    logit_grad = 0.0
    for j in range(2):
        logit_grad = logit_grad + jnp.where(expert == cols[:, j : j + 1], gate[j] * (gate_grad[j] - shared), 0.0)
    high = logit_grad.astype(BF)
    low = (logit_grad - high.astype(F32)).astype(BF)
    upstream = gather_rows(cols, 0, back) + gather_rows(cols, 1, back)
    upstream = upstream + nn(high, router[...]) + nn(low, router[...])
    grad, gain_f_grad = norm_grads(middle[...], gain_f[layer : layer + 1, :], upstream)
    grad = grad + flow
    flow_o[...] = grad
    held[me] = grad.astype(BF)
    to_mate = remote(held.at[me], held.at[me], hssem.at[0], hrsem.at[0], mp=mate)
    over = remote(held.at[me], held.at[me], hssem.at[1], hrsem.at[1], mp=across)
    passed = remote(held.at[across], held.at[across], hssem.at[2], hrsem.at[2], mp=mate)
    over.start()
    to_mate.start()

    router_s[...] = tn(jnp.concatenate([high, low], 1), ffn[...])
    for copy in come_in[:3]:
        copy.wait()
    for i in range(seq // local):
        rows = pl.ds(i * local, local)
        normed_t[:, i * local : (i + 1) * local] = normed[i].astype(F32).T.astype(BF)
        piece = qkv[rows, :]
        for h in range(heads):
            q_s[h, rows, :] = piece[:, h * size : (h + 1) * size] * BF(0.125)
            key = piece[:, own + h * size : own + (h + 1) * size]
            k_s[h, rows, :] = key
            kt_s[h, :, i * local : (i + 1) * local] = (key.astype(F32) * 0.125).T.astype(BF)
            v_s[h, rows, :] = piece[:, 2 * own + h * size : 2 * own + (h + 1) * size]
    seg_row, _ = segments(lens, (1, cont), 1)
    segc[...] = segments(lens, (cont, LANES), 0)[0]
    _, offset = segments(lens, (cont, LANES), 0)
    unplace = (lax.broadcasted_iota(jnp.int32, (cont, LANES), 1) == offset).astype(BF)
    at = lax.broadcasted_iota(jnp.int32, (1, width), 1)
    distance = jnp.where(at <= PROMPT, PROMPT - at, PROMPT + width - at)
    bucket = jnp.where((at <= PROMPT) | (at > width - LANES), bucket_of(distance), -1)
    hot[...] = (lax.broadcasted_iota(jnp.int32, (buckets, width), 0) == bucket).astype(F32)
    bias_s[...] = jnp.zeros_like(bias_s)

    def receive(m):
        dmix = nt(held[m], w_attn[pl.ds(pl.multiple_of(me * own, size), own), :]).astype(BF)
        for h in range(heads):
            do_s[h, pl.ds(pl.multiple_of(m * local, LANES), local), :] = dmix[:, h * size : (h + 1) * size]

    receive(me)
    to_mate.wait_recv()
    receive(mate)
    over.wait_recv()
    passed.start()
    receive(across)
    passed.wait_recv()
    receive(diagonal)
    gw_a[...] = tn(held[...].reshape(seq, model), mixed[...])

    def swap_copy(h, n):
        to = (mate, across, diagonal)[n]
        return remote(dq_fold.at[h, to], dq_held.at[h, me], qssem.at[h, n], qrsem.at[h, me], mp=to)

    def sum_copy(h, k):
        to = lax.rem(d + k, dp_count)
        return remote(part.at[to, h], come.at[d, h], pssem.at[h, k], prsem.at[h, k], dp=to, mp=me)

    def summed(h):
        total = part[d, h].astype(F32)
        for k in range(1, dp_count):
            sum_copy(h, k).wait_recv()
            total = total + come[lax.rem(d + dp_count - k, dp_count), h].astype(F32)
        return total.astype(BF)

    def head_share(h, k):
        place = all_o.at[me, d, h]
        return remote(place, place, assem.at[h, k], arsem.at[h, k], dp=lax.rem(d + k, dp_count), mp=me)

    def head_pass(n, h, j):
        place = all_o.at[across if n == 2 else me, j, h]
        return remote(place, place, ossem.at[n, h, j], orsem.at[n, h, j], mp=across if n == 1 else mate)

    def finish_sum(h):
        all_o[me, d, h] = summed(h)
        for k in range(1, dp_count):
            head_share(h, k).start()

    def hand_on(h):
        for k in range(dp_count):
            j = lax.rem(d + dp_count - k, dp_count)
            if k > 0:
                head_share(h, k).wait_recv()
            head_pass(1, h, j).start()
            head_pass(0, h, j).start()

    def pass_on(h):
        for k in range(dp_count):
            j = lax.rem(d + dp_count - k, dp_count)
            head_pass(1, h, j).wait_recv()
            head_pass(2, h, j).start()

    def head(h, carry):
        bias_stage(vecs[pl.ds(h, 1), :], lens, table, cont_bias)
        dtable[...] = jnp.zeros_like(dtable)
        dk_s[...] = jnp.zeros_like(dk_s)
        dv_s[...] = jnp.zeros_like(dv_s)
        for number, block in enumerate(blocks_of(seq)):
            q0, prompt_keys, cont_from = block
            if first:

                @pl.when(h == 0)
                def _():
                    for k in ((0,), (1,), (2,), (3,), (4, 5), (6, 7))[number]:
                        if k > 0:
                            dp_share(up_o, ussem, ursem, k).wait_recv()
                        if number == 1:
                            for later in range(dp_count - 2, dp_count):
                                dp_share(up_o, ussem, ursem, later).start()
                        j = lax.rem(d + dp_count - k, dp_count)
                        mp_share(up_o, wssem, wrsem, 1, j).start()
                        mp_share(up_o, wssem, wrsem, 0, j).start()

            query = q_s[h, q0 : q0 + QB, :]
            dout = do_s[h, q0 : q0 + QB, :]
            scored = scores_of(k_s, query, table, cont_bias, segc, seg_row, block, h)
            lse_row = lse[pl.ds(h, 1), q0 : q0 + QB]
            kept, delta = [], 0.0
            for k0, k1, s in scored:
                p = jnp.exp(s - lse_row)
                dp = nt(v_s[h, k0:k1, :], dout)
                delta = delta + jnp.sum(p * dp, axis=0, keepdims=True)
                dv_s[k0:k1, :] += nn(p.astype(BF), dout)
                kept.append((k0, k1, p, dp))
            dq = 0.0
            for k0, k1, p, dp in kept:
                ds = p * (dp - delta)
                dsb = ds.astype(BF)
                dk_s[k0:k1, :] += nn(dsb, query)
                dq = dq + nn(kt_s[h, :, k0:k1], dsb)
                if cont_from is not None and k0 == 0:
                    fold[:, q0 - PROMPT : q0 - PROMPT + QB] = dsb
                else:
                    left = PROMPT - q0 if cont_from is None else PROMPT + cont_from - (q0 - PROMPT)
                    dtable[left : left + k1 - k0, :] += ds[:, 0:LANES]
                    dtable[left - LANES : left - LANES + k1 - k0, :] += ds[:, LANES:]
            dqt[:, q0 : q0 + QB] = dq
        for m in range(places):
            rows = slice(m * local, (m + 1) * local)
            piece = jnp.concatenate([dqt[:, rows].T.astype(BF), dk_s[rows, :].astype(BF), dv_s[rows, :].astype(BF)], 1)
            dq_s[m] = piece
            dq_fold[h, m] = jnp.concatenate([piece[0 : local // 2, :], piece[local // 2 :, :]], 1)
        for n in (2, 1, 0):
            swap_copy(h, n).start()
        pltpu.make_async_copy(dq_fold.at[h, me], dq_held.at[h, me], qrsem.at[h, me]).start()
        grads = nn(normed_t[...], dq_s[...].reshape(seq, 3 * size))
        for j in range(dp_count):
            rows = slice(j * part.shape[2], (j + 1) * part.shape[2])
            part[j, h, :, 0 : 3 * size] = grads[rows, :].astype(BF)
        for k in range(1, dp_count):
            sum_copy(h, k).start()
        dtable[0:PROMPT, :] += nn(fold[...], unplace)
        flat = jnp.concatenate([dtable[...].T, jnp.zeros((LANES, LANES), F32)], 1)
        found = jnp.sum(hot[...] * shift_table(flat, width), axis=1, keepdims=True)
        lane = lax.broadcasted_iota(jnp.int32, bias_s.shape, 1)
        bias_s[...] += jnp.where(lane == me * heads + h, found, 0.0)
        if first:

            @pl.when(h == heads - 1)
            def _():
                for j in range(dp_count):
                    mp_share(up_o, wssem, wrsem, 1, j).wait_recv()
                    mp_share(up_o, wssem, wrsem, 2, j).start()

            @pl.when(h > 0)
            def _():
                finish_sum(h - 1)

        return carry

    for j in range(dp_count):
        rows = slice(j * part.shape[2], (j + 1) * part.shape[2])
        for h in range(heads):
            part[j, h, :, 3 * size :] = gw_a[rows, h * size : (h + 1) * size].astype(BF)
    lax.fori_loop(0, heads, head, 0, unroll=True)
    if first:
        hand_on(0)
    for h in range(heads):
        for m in range(places):
            pltpu.make_async_copy(dq_held.at[h, m], dq_held.at[h, m], qrsem.at[h, m]).wait()
    come_in[3].wait()
    upstream = 0.0
    for t in range(3):
        halves = []
        for lane in (t * size, own + t * size):
            found = [dq_held[h, m, :, lane : lane + size] for m in range(places) for h in range(heads)]
            halves.append(jnp.concatenate(found, 1))
        piece = jnp.concatenate(halves, 0)
        upstream = upstream + nt(piece, w_qkv[:, t * model : (t + 1) * model])
    inner, gain_a_grad = norm_grads(stream[...].astype(F32), gain_a[layer : layer + 1, :], upstream)
    flow = flow_o[...] + inner
    flow_o[...] = flow
    gains = jnp.concatenate([gain_a_grad, gain_f_grad, jnp.zeros((6, model), F32)], 0)
    tiles = [bias_s[8 * i : 8 * i + 8, :] for i in range(buckets // 8)]
    bias_rows = jnp.concatenate(tiles + [jnp.zeros((8, model - LANES * len(tiles)), F32)], 1)
    router_grad = router_s[0 : router.shape[0], :] + router_s[router.shape[0] :, :]
    small = [gains, bias_rows] + [router_grad[8 * i : 8 * i + 8, :] for i in range(router.shape[0] // 8)]

    if not first:
        cols_below = columns(rows_below)
        scatter_rows(
            rows_below,
            [(gates_below[:, j : j + 1] * cols_below[:, 4 + j : 5 + j].astype(F32) * flow).astype(BF) for j in range(2)],
            send_o,
        )
        for n, block in enumerate(small):
            small_o[n] = block
        for h in range(heads):
            sum_o[h] = summed(h)
    else:
        for n, block in enumerate(small):
            small_s[n] = block
        small_s[len(small) :] = small_above[...]
        small_scattered = scatter_dp(small_s, small_come, tsem, usem)
        for copy in small_scattered:
            copy.start()
        finish_sum(heads - 1)
        for j in range(dp_count):
            mp_share(up_o, wssem, wrsem, 0, j).wait_recv()
            mp_share(up_o, wssem, wrsem, 2, j).wait_recv()
        up_go = pltpu.make_async_copy(up_o, up_out, outsem.at[0])
        all_go = pltpu.make_async_copy(all_o, all_out, outsem.at[1])
        up_go.start()
        hand_on(1)
        small_mp[me] = sum_dp(small_scattered, small_s, small_come)
        small_swaps = [
            remote(small_mp.at[me], small_mp.at[me], csem.at[n], dsem.at[n], mp=to) for n, to in enumerate((mate, across, diagonal))
        ]
        for copy in small_swaps:
            copy.start()
        pass_on(0)
        for copy in small_swaps:
            copy.wait_recv()
        small_o[d] = small_mp[0] + small_mp[1] + small_mp[2] + small_mp[3]
        small_shares = share_dp(small_o, vsem, zsem)
        for copy in small_shares:
            copy.start()
        for h in range(2, heads):
            hand_on(h)
        for h in range(1, heads):
            pass_on(h)
        for copy in small_shares:
            copy.wait_recv()
        for j in range(dp_count):
            for h in range(heads):
                head_pass(0, h, j).wait_recv()
                head_pass(2, h, j).wait_recv()
        all_go.start()
        for j in range(dp_count):
            for n in range(3):
                mp_share(up_o, wssem, wrsem, n, j).wait_send()
                for h in range(heads):
                    head_pass(n, h, j).wait_send()
        for k in range(1, dp_count):
            dp_share(up_o, ussem, ursem, k).wait_send()
            for h in range(heads):
                head_share(h, k).wait_send()
        for copy in small_swaps + small_scattered + small_shares:
            copy.wait_send()
        up_go.wait()
        all_go.wait()
    for copy in (to_mate, over, passed):
        copy.wait_send()
    for h in range(heads):
        for n in range(3):
            swap_copy(h, n).wait_send()
        for k in range(1, dp_count):
            sum_copy(h, k).wait_send()


def back_call(layer, layers, number, heads, size, buckets, lens, normal, mp_count, dp_count, local, model, block, extra):
    first, last = layer == 0, layer == layers - 1
    seq, own = local * mp_count, heads * size
    width = PROMPT + 3 * LANES
    cont = seq - PROMPT
    args = list(normal) + list(extra)
    specs = [SMEM] + [layer_spec(*a) if isinstance(a, tuple) else VMEM for a in args]
    for n in (11, 12, 15, 16):
        specs[n] = ANY
    chunk = (heads, model // dp_count, 4 * size)
    smalls = dp_count // layers
    outs = [((local, model), F32)]
    if first:
        outs += [((mp_count, dp_count) + chunk, BF), ((mp_count, dp_count) + chunk, BF), ((dp_count, 8, model), F32)]
    else:
        outs += [((local, model), BF), (block, BF), (chunk, BF), ((smalls, 8, model), F32)]
    out_specs = [VMEM] * len(outs)
    scratch = [
        pltpu.VMEM((mp_count, local, model), BF), dma(3), dma(3),
        pltpu.VMEM((mp_count, local, model), BF), pltpu.VMEM((seq, 3 * own), BF),
        pltpu.VMEM((model, model), BF), pltpu.VMEM((model, 3 * model), BF), dma(4),
        pltpu.VMEM((model, seq), BF),
        pltpu.VMEM((heads, seq, size), BF),
        pltpu.VMEM((heads, seq, size), BF),
        pltpu.VMEM((heads, seq, size), BF),
        pltpu.VMEM((heads, size, seq), BF),
        pltpu.VMEM((heads, seq, size), BF),
        pltpu.VMEM((width - LANES, LANES), F32),
        pltpu.VMEM((PROMPT, cont), F32),
        pltpu.VMEM((PROMPT, cont), BF),
        pltpu.VMEM((width - LANES, LANES), F32),
        pltpu.VMEM((seq, size), F32),
        pltpu.VMEM((seq, size), F32),
        pltpu.VMEM((size, seq), F32),
        pltpu.VMEM((cont, LANES), jnp.int32),
        pltpu.VMEM((buckets, width), F32),
        pltpu.VMEM((buckets, LANES), F32),
        pltpu.VMEM((model, own), F32),
        pltpu.VMEM((4 * dp_count, model), F32),
        pltpu.VMEM((mp_count, local, 3 * size), BF),
        pltpu.VMEM((heads, mp_count, local // 2, 6 * size), BF),
        pltpu.VMEM((heads, mp_count, local // 2, 6 * size), BF),
        dma(heads, 3),
        dma(heads, mp_count),
        pltpu.VMEM((dp_count,) + chunk, BF),
        pltpu.VMEM((dp_count,) + chunk, BF),
        dma(heads, dp_count),
        dma(heads, dp_count),
    ]
    if first:
        scratch += [
            pltpu.VMEM((dp_count, 8, model), F32),
            pltpu.VMEM((dp_count, 8, model), F32),
            pltpu.VMEM((mp_count, 8, model), F32),
        ]
        scratch += [dma(dp_count)] * 2 + [dma(3)] * 2 + [dma(dp_count)] * 2
        scratch += [dma(heads, dp_count)] * 2 + [dma(3, heads, dp_count)] * 2 + [dma(dp_count)] * 2 + [dma(3, dp_count)] * 2
        scratch += [pltpu.VMEM((mp_count, dp_count) + chunk, BF)] * 2 + [dma(2)]
        out_specs[1] = out_specs[2] = ANY
    return pl.pallas_call(
        functools.partial(back_kernel, layer, layers, heads, size, buckets),
        grid=(1,),
        out_shape=tuple(jax.ShapeDtypeStruct(shape, kind) for shape, kind in outs),
        in_specs=specs,
        out_specs=tuple(out_specs),
        scratch_shapes=scratch,
        compiler_params=pltpu.CompilerParams(
            collective_id=number, has_side_effects=True, vmem_limit_bytes=VMEM_BYTES
        ),
    )(lens, *[a[0] if isinstance(a, tuple) else a for a in args])


def dma(*shape):
    return pltpu.SemaphoreType.DMA(shape) if shape else pltpu.SemaphoreType.DMA


def gelu_grad(values):
    inner = jnp.tanh(SQRT_TWO_PI * (values + 0.044715 * values * values * values))
    slope = SQRT_TWO_PI * (1.0 + 3.0 * 0.044715 * values * values)
    return 0.5 * values * (1.0 + inner), 0.5 * (1.0 + inner) + 0.5 * values * (1.0 - inner * inner) * slope


def expert_kernel(mode, layer, dp_count, *refs):
    forward, backward = mode in ("fwd", "both"), mode in ("both", "bwd")
    refs = list(refs)

    def take(count):
        taken = refs[:count]
        del refs[:count]
        return taken

    (sending,) = take(1)
    far = take(2) if mode == "both" else None
    (x_in,) = take(1) if mode == "bwd" else (None,)
    w_in, w_out = take(2)
    results = take(forward + backward)
    (x_o,) = take(1) if mode == "fwd" else (None,)
    gw_in_o, gw_out_o = take(2) if backward else (None, None)
    w1, w2, wsem, wssem, wrsem = take(5)
    x_all, xsem = take(2)
    recv_a, recv_b, ssem, asem, fsem, bsem = take(6)
    paths = [take(9) for _ in results]
    if backward:
        g_all, hid_all, ig_all, stage, gsem, grsem, glsem = take(7)

    d = lax.axis_index("dp")
    me, core, mate, across, diagonal = mp_places()
    row = me // 2
    index = d * 2 + core
    experts = dp_count * 2
    model = w1.shape[1]
    half = model // 2
    rows_a = x_all.shape[1] // 2
    tile = sending.shape[1]
    ahead = 3

    barrier = pltpu.get_barrier_semaphore()

    def greet(k, carry):
        signal_to(barrier, dp=lax.rem(d + k // 2, dp_count), mp=row * 2 + lax.rem(core + k % 2, 2))
        return carry

    lax.fori_loop(1, experts, greet, 0)
    signal_to(barrier, mp=across)
    pl.semaphore_wait(barrier, experts)

    def send_wave(k):
        dd = lax.rem(d + k, dp_count)
        for cc in range(2):
            to = dd * 2 + cc

            @pl.when(to == index)
            def _():
                pltpu.make_async_copy(sending.at[to], recv_a.at[index], asem.at[index]).start()

            @pl.when(to != index)
            def _():
                remote(sending.at[to], recv_a.at[index], ssem.at[to], asem.at[index], dp=dd, mp=row * 2 + cc).start()

    for k in range(ahead):
        send_wave(k)
    copies = []
    for n, (source, held) in enumerate(((w_in, w1), (w_out, w2))):
        copies.append(remote(source.at[layer, 1 - core], held.at[core], wssem.at[n], wrsem.at[n], mp=mate))
        copies.append(pltpu.make_async_copy(source.at[layer, core], held.at[core], wsem.at[n]))
    if mode == "bwd":
        copies.append(pltpu.make_async_copy(x_in, x_all, xsem))
    for copy in copies:
        copy.start()

    def source_of(g):
        return lax.rem(d + dp_count - g, dp_count)

    def unpack(held, g, side, into, gates):
        base = side * rows_a
        s0 = source_of(g)
        tails = []
        for cc in range(2):
            src = s0 * 2 + cc
            block = held[src]
            factors = None if gates is None else gates[src][:, 7 * half :].astype(F32)

            def factor(i):
                return factors[:, 3 * i : 3 * i + 1] + factors[:, 3 * i + 1 : 3 * i + 2] + factors[:, 3 * i + 2 : 3 * i + 3]

            for i in range(3):
                piece = block[:, i * model : (i + 1) * model]
                if gates is not None:
                    piece = (piece.astype(F32) * factor(i)).astype(BF)
                into[g, base + (2 * i + cc) * tile : base + (2 * i + cc + 1) * tile, :] = piece
            tail = unfold_tail(block[:, 3 * model : 7 * half], half)
            tails.append(tail if gates is None else tail * factor(3)[0:8, :])
        into[g, base + 6 * tile : base + 7 * tile, :] = jnp.concatenate(tails, 0).astype(BF)

    def forward_copy(s0):
        two = pl.ds(s0 * 2, 2)
        return remote(recv_a.at[two], recv_b.at[two], fsem.at[s0], bsem.at[s0], mp=across)

    def partial_copy(path, g):
        kept, part, pssem, prsem, ret_s, ret, rssem, rrsem, psend = path
        return remote(psend.at[g], part.at[g], pssem.at[g], prsem.at[g], mp=across)

    def compute(g):
        x = x_all[g]
        totals = [0.0] * len(results)
        for q in range(2):
            inner = nn(x, w1[q])
            if backward:
                value, slope = gelu_grad(inner)
                hidden = value.astype(BF)
                hid_all[q, g] = hidden
                grad = (nt(g_all[g], w2[q]) * slope).astype(BF)
                ig_all[q, g] = grad
                totals[-1] = totals[-1] + nt(grad, w1[q])
            else:
                hidden = gelu_tanh(inner).astype(BF)
            if forward:
                totals[0] = totals[0] + nn(hidden, w2[q])
        return totals

    def give_back(path, g):
        kept, part, pssem, prsem, ret_s, ret, rssem, rrsem, psend = path
        partial_copy(path, g).wait_recv()
        total = kept[lax.rem(g, 2)] + part[g].astype(F32)
        s0 = source_of(g)
        for cc in range(2):
            src = s0 * 2 + cc
            for i in range(3):
                at = (2 * i + cc) * tile
                ret_s[src, :, i * model : (i + 1) * model] = total[at : at + tile, :].astype(BF)
            at = 6 * tile + 8 * cc
            ret_s[src, :, 3 * model :] = jnp.concatenate(
                [total[at : at + 8, 0:half], total[at : at + 8, half:]], 0
            ).astype(BF)

            @pl.when(src == index)
            def _():
                pltpu.make_async_copy(ret_s.at[src], ret.at[index], rrsem.at[index]).start()

            @pl.when(src != index)
            def _():
                remote(ret_s.at[src], ret.at[index], rssem.at[src], rrsem.at[index], dp=s0, mp=row * 2 + cc).start()

    def products(n, q, part):
        half_groups = pl.ds(part * dp_count // 2, dp_count // 2)
        count = dp_count * rows_a
        if n == 0:
            left, right = x_all[half_groups], ig_all[q, half_groups]
        else:
            left, right = hid_all[q, half_groups], g_all[half_groups]
        return tn(left.reshape(count, model), right.reshape(count, model))

    def arrive(g):
        s0 = source_of(g)
        for cc in range(2):
            src = s0 * 2 + cc
            pltpu.make_async_copy(recv_a.at[src], recv_a.at[src], asem.at[src]).wait()
        forward_copy(s0).start()

    def step(i, carry):
        @pl.when(i < dp_count)
        def _():
            arrive(i)

        @pl.when(i + ahead < dp_count)
        def _():
            send_wave(i + ahead)

        @pl.when((i >= 1) & (i <= dp_count))
        def _():
            g = i - 1
            forward_copy(source_of(g)).wait_recv()
            for side, held in enumerate((recv_a, recv_b)):
                if forward:
                    unpack(held, g, side, x_all, None)
                if mode == "both":
                    unpack(far[side], g, side, g_all, held)
                elif mode == "bwd":
                    unpack(held, g, side, g_all, None)
            for path, total in zip(paths, compute(g)):
                kept, psend = path[0], path[8]
                kept[lax.rem(g, 2)] = total[0:rows_a, :]
                psend[g] = total[rows_a:, :].astype(BF)
                partial_copy(path, g).start()

        @pl.when(i >= 2)
        def _():
            for path in paths:
                give_back(path, i - 2)

        if backward:
            for n in range(2):
                for q in range(2):

                    @pl.when(i == dp_count // 2 + 1 + 2 * n + q)
                    def _():
                        stage[n, q] = products(n, q, 0)

        return carry

    arrive(0)
    send_wave(ahead)
    for copy in copies:
        copy.wait()
    lax.fori_loop(1, dp_count + 2, step, 0)
    if mode == "fwd":
        saved = pltpu.make_async_copy(x_all, x_o, xsem)
        saved.start()
    if backward:
        outs = (gw_in_o, gw_out_o)
        copies = []
        for n in range(2):
            stage[n, 1 - core] += products(n, 1 - core, 1)
            copy = remote(stage.at[n, 1 - core], outs[n].at[core], gsem.at[n], grsem.at[n], mp=mate)
            copy.start()
            copies.append(copy)
        for n in range(2):
            stage[n, core] += products(n, core, 1)
            copy = pltpu.make_async_copy(stage.at[n, core], outs[n].at[core], glsem.at[n])
            copy.start()
            copies.append(copy)
    for path, result in zip(paths, results):
        kept, part, pssem, prsem, ret_s, ret, rssem, rrsem, psend = path

        def end(e, carry):
            pltpu.make_async_copy(ret.at[e], ret.at[e], rrsem.at[e]).wait()

            @pl.when(e != index)
            def _():
                pltpu.make_async_copy(ret_s.at[e], ret_s.at[e], rssem.at[e]).wait()

            return carry

        lax.fori_loop(0, experts, end, 0)

        def end_group(g, carry):
            pltpu.make_async_copy(psend.at[g], psend.at[g], pssem.at[g]).wait()
            return carry

        lax.fori_loop(0, dp_count, end_group, 0)
        result[...] = ret[...]

    def end_send(e, carry):
        @pl.when(e != index)
        def _():
            pltpu.make_async_copy(sending.at[e], sending.at[e], ssem.at[e]).wait()

        return carry

    lax.fori_loop(0, experts, end_send, 0)

    def end_pair(s0, carry):
        two = pl.ds(s0 * 2, 2)
        pltpu.make_async_copy(recv_a.at[two], recv_a.at[two], fsem.at[s0]).wait()
        return carry

    lax.fori_loop(0, dp_count, end_pair, 0)
    if mode == "fwd":
        saved.wait()
    if backward:
        for n in range(2):
            copies[n].wait()
            copies[2 + n].wait()


def expert_call(mode, layer, number, dp_count, send, far, x_in, w_in, w_out):
    forward, backward = mode in ("fwd", "both"), mode in ("both", "bwd")
    experts, tile, _ = send.shape
    model = w_in.shape[2]
    block = (experts, tile, 7 * model // 2)
    rows = 2 * 7 * tile
    args, specs = [send], [VMEM]
    if mode == "both":
        args += far
        specs += [VMEM] * 2
    if mode == "bwd":
        args.append(x_in)
        specs.append(ANY)
    args += [w_in, w_out]
    specs += [ANY, ANY]
    outs, out_specs = [], []

    def out(dims, kind, spec):
        outs.append(jax.ShapeDtypeStruct(dims, kind))
        out_specs.append(spec)

    for _ in range(forward + backward):
        out(block, BF, VMEM)
    if mode == "fwd":
        out((dp_count, rows, model), BF, ANY)
    if backward:
        out((2, model, model), F32, ANY)
        out((2, model, model), F32, ANY)
    scratch = [
        pltpu.VMEM((2, model, model), BF),
        pltpu.VMEM((2, model, model), BF),
        dma(2),
        dma(2),
        dma(2),
        pltpu.VMEM((dp_count, rows, model), BF),
        dma(),
        pltpu.VMEM(send.shape, BF),
        pltpu.VMEM(send.shape, BF),
        dma(experts),
        dma(experts),
        dma(dp_count),
        dma(dp_count),
    ]
    for _ in range(forward + backward):
        scratch += [
            pltpu.VMEM((2, rows // 2, model), F32),
            pltpu.VMEM((dp_count, rows // 2, model), BF),
            dma(dp_count),
            dma(dp_count),
            pltpu.VMEM(block, BF),
            pltpu.VMEM(block, BF),
            dma(experts),
            dma(experts),
            pltpu.VMEM((dp_count, rows // 2, model), BF),
        ]
    if backward:
        scratch += [
            pltpu.VMEM((dp_count, rows, model), BF),
            pltpu.VMEM((2, dp_count, rows, model), BF),
            pltpu.VMEM((2, dp_count, rows, model), BF),
            pltpu.VMEM((2, 2, model, model), F32),
            dma(2),
            dma(2),
            dma(2),
        ]
    return pl.pallas_call(
        functools.partial(expert_kernel, mode, layer, dp_count),
        out_shape=tuple(outs),
        in_specs=specs,
        out_specs=tuple(out_specs),
        scratch_shapes=scratch,
        compiler_params=pltpu.CompilerParams(
            collective_id=number, has_side_effects=True, vmem_limit_bytes=VMEM_BYTES
        ),
    )(*args)


def spread_kernel(size, buckets, count, *refs):
    parts, grads, small = refs[:count], refs[count : 3 * count], refs[3 * count]
    qkv_o, attn_o, in_o, out_o, gain_a_o, bias_o, gain_f_o, router_o, sem = refs[3 * count + 1 :]
    step = pl.program_id(0)
    copies = []
    for n in range(count):
        copies.append(pltpu.make_async_copy(grads[2 * n].at[0], in_o.at[n, step], sem.at[2 * n]))
        copies.append(pltpu.make_async_copy(grads[2 * n + 1].at[0], out_o.at[n, step], sem.at[2 * n + 1]))
    for copy in copies:
        copy.start()
    for n in range(count):
        mp_count, blocks, heads, rows, _ = parts[n].shape
        pieces = [
            parts[n][m, :, h].reshape(blocks * rows, 4 * size).astype(F32) for m in range(mp_count) for h in range(heads)
        ]
        qkv_o[n] = jnp.concatenate([p[:, t * size : (t + 1) * size] for t in range(3) for p in pieces], 1)
        for number, p in enumerate(pieces):
            attn_o[n, number * size : (number + 1) * size, :] = p[:, 3 * size :].T
    lines = small.shape[0] // count
    for n in range(count):
        gain_a_o[n : n + 1, :] = small[n * lines, 0:1, :]
        gain_f_o[n : n + 1, :] = small[n * lines, 1:2, :]
        tiles = [small[n * lines + 1, :, i * LANES : (i + 1) * LANES] for i in range(buckets // 8)]
        bias_o[n] = jnp.concatenate(tiles, 0).T[0 : bias_o.shape[1], :]
        router_o[n] = jnp.concatenate([small[n * lines + i] for i in range(2, lines)], 0)
    for copy in copies:
        copy.wait()


def spread_call(parts, grads, small, size, heads, buckets, experts):
    mp_count, blocks, own_heads, rows, wide = parts[0].shape
    layers, model = len(parts), blocks * rows
    steps = grads[0].shape[0]
    return pl.pallas_call(
        functools.partial(spread_kernel, size, buckets, layers),
        grid=(steps,),
        out_shape=(
            jax.ShapeDtypeStruct((layers, model, 3 * heads * size), F32),
            jax.ShapeDtypeStruct((layers, heads * size, model), F32),
            jax.ShapeDtypeStruct((layers,) + grads[0].shape, F32),
            jax.ShapeDtypeStruct((layers,) + grads[1].shape, F32),
            jax.ShapeDtypeStruct((layers, model), F32),
            jax.ShapeDtypeStruct((layers, heads, buckets), F32),
            jax.ShapeDtypeStruct((layers, model), F32),
            jax.ShapeDtypeStruct((layers, experts, model), F32),
        ),
        in_specs=[pl.BlockSpec((mp_count, blocks // steps, own_heads, rows, wide), lambda i: (0, i, 0, 0, 0))] * layers
        + [pl.BlockSpec((1,) + g.shape[1:], lambda i: (i, 0, 0)) for g in grads]
        + [VMEM],
        out_specs=(
            pl.BlockSpec((layers, model // steps, 3 * heads * size), lambda i: (0, i, 0)),
            pl.BlockSpec((layers, heads * size, model // steps), lambda i: (0, 0, i)),
            ANY,
            ANY,
            VMEM,
            VMEM,
            VMEM,
            VMEM,
        ),
        scratch_shapes=[dma(2 * layers)],
        compiler_params=pltpu.CompilerParams(vmem_limit_bytes=VMEM_BYTES),
    )(*parts, *grads, small)


def fast_body(
    tokens, cotangent, w_qkv, w_attn, attn_gain, rel_bias, ffn_gain, router, w_in, w_out, cont_lengths, routes, slots, drops
):
    _, local, model = tokens.shape
    heads, buckets = rel_bias.shape[1:]
    size = model // heads
    layers = w_qkv.shape[0]
    dp_count, mp_count = lax.axis_size("dp"), lax.axis_size("mp")
    own_heads = heads // mp_count
    experts = dp_count * 2
    me = lax.axis_index("mp")
    block = (experts, 16, 7 * model // 2)
    pairs = jnp.concatenate(
        [routes.reshape(layers, local, 2), slots.reshape(layers, local, 2), 1 - drops.reshape(layers, local, 2)], 2
    )
    rows = jnp.pad(pairs.transpose(0, 2, 1), ((0, 0), (0, 2), (0, 0)))
    router = router.transpose(0, 2, 1)
    vecs = bias_vectors(lax.dynamic_slice_in_dim(rel_bias, me * own_heads, own_heads, 1))

    kept = [None] * layers
    back, far = None, None
    for l in range(layers):
        first, last = l == 0, l == layers - 1
        normal = [attn_gain, w_qkv, vecs[l], w_attn, ffn_gain, (router, l), (rows, l)]
        if first:
            specials = [tokens[0], cotangent[0], (rows, layers - 1)]
        else:
            before = kept[l - 1]
            specials = [before["middle"], before["out"], (rows, l - 1), before["gates"]]
        if last:
            specials += far
        got = pre_call(
            l, layers, l, own_heads, size, cont_lengths, normal, mp_count, dp_count, local, model, specials, block
        )
        got = [tokens[0]] + list(got) if first else list(got)
        names = ("stream", "normed", "qkv", "mixed", "lse", "middle", "ffn", "gates")
        kept[l] = k = dict(zip(names, got))
        if first:
            far = got[9:11]
        if last:
            far = [far[0], got[9]]
            k["out"], back, k["gw_in"], k["gw_out"] = expert_call("both", l, 5, dp_count, got[8], far, None, w_in, w_out)
        else:
            k["out"], k["x_rows"] = expert_call("fwd", l, 4, dp_count, got[8], None, None, w_in, w_out)

    flow = cotangent[0]
    for l in reversed(range(layers)):
        k = kept[l]
        last = l == layers - 1
        normal = [
            vecs[l], back, k["out"], flow, k["middle"], k["ffn"], k["gates"], (rows, l), (router, l), ffn_gain,
            k["normed"], k["qkv"], k["mixed"], k["lse"], w_attn, w_qkv, k["stream"], attn_gain,
        ]
        extra = [(rows, l - 1), kept[l - 1]["gates"]] if last else [heads_sum, small]
        got = back_call(
            l, layers, 6 + last, own_heads, size, buckets, cont_lengths, normal, mp_count, dp_count, local, model, block, extra
        )
        if last:
            flow, output, send, heads_sum, small = got
            b = kept[l - 1]
            back, b["gw_in"], b["gw_out"] = expert_call("bwd", l - 1, 10, dp_count, send, None, b["x_rows"], w_in, w_out)
        else:
            flow, upper, lower, small = got
    grads = [kept[l][name] for l in range(layers) for name in ("gw_in", "gw_out")]
    grad_qkv, grad_attn, grad_in, grad_out, grad_a, grad_bias, grad_f, grad_router = spread_call(
        [lower, upper], grads, small, size, heads, buckets, experts
    )
    return (
        output[None], flow[None], grad_qkv, grad_attn, grad_a, grad_bias, grad_f, grad_router.transpose(0, 2, 1), grad_in, grad_out,
    )


def chosen_body(
    tokens, cotangent, w_qkv, w_attn, attn_gain, rel_bias, ffn_gain, router, w_in, w_out, cont_lengths, routes, slots, drops
):
    groups, local, model = tokens.shape
    heads = rel_bias.shape[1]
    dp_count, mp_count = lax.axis_size("dp"), lax.axis_size("mp")
    capacity = max(2, 9 * 2 * groups * local // (8 * w_in.shape[1] * dp_count))
    seq = local * mp_count
    fits = (
        groups == 1
        and w_qkv.shape[0] == 2
        and mp_count == 4
        and dp_count == 8
        and router.shape[2] == 16
        and rel_bias.shape[2] == 32
        and heads % mp_count == 0
        and model // heads == 64
        and model % 256 == 0
        and local % 128 == 0
        and w_in.shape[1:] == (2, model, model)
        and w_out.shape[1:] == (2, model, model)
        and 48 < capacity <= 56
        and seq > PROMPT
        and (seq - PROMPT) % QB == 0
    )
    plan = fast_body if fits else body
    return plan(
        tokens, cotangent, w_qkv, w_attn, attn_gain, rel_bias, ffn_gain, router, w_in, w_out, cont_lengths, routes, slots, drops
    )


def solution(mesh):
    return jax.shard_map(
        chosen_body,
        mesh=mesh,
        in_specs=(
            P("dp", "mp", None),
            P("dp", "mp", None),
            P(),
            P(),
            P(),
            P(),
            P(),
            P(),
            P(None, "dp", None, "mp"),
            P(None, "dp", "mp", None),
            P("dp", None),
            P(None, "dp", "mp", None),
            P(None, "dp", "mp", None),
            P(None, "dp", "mp", None),
        ),
        out_specs=(
            P("dp", "mp", None),
            P("dp", "mp", None),
            P(),
            P(),
            P(),
            P(),
            P(),
            P(),
            P(None, "dp", None, "mp"),
            P(None, "dp", "mp", None),
        ),
        check_vma=False,
    )
```

```python
import functools

import jax
import jax.numpy as jnp
from jax import lax
from jax.experimental import pallas as pl
from jax.experimental.pallas import tpu as pltpu
from jax.sharding import PartitionSpec as P

PROMPT = 1024


EPSILON = 1e-06
SQRT_TWO_PI = 0.7978845608028654
THRESHOLDS = (16, 20, 24, 32, 40, 48, 64, 80, 96, 128, 160, 192, 256, 384, 512, 768)
HIGHEST = lax.Precision.HIGHEST


def rms_scale(values, gain_row):
    return (
        values * lax.rsqrt(jnp.mean(values * values, axis=-1, keepdims=True) + EPSILON) * gain_row
    )


def gelu_tanh(values):
    return (
        0.5
        * values
        * (1.0 + jnp.tanh(SQRT_TWO_PI * (values + 0.044715 * values * values * values)))
    )


def bucket_of(distance):
    counted = jnp.minimum(distance, 15)
    for threshold in THRESHOLDS:
        counted = counted + (distance >= threshold).astype(jnp.int32)
    return counted


def geometry(lengths, row_ids):
    starts = PROMPT + jnp.cumsum(lengths, axis=-1) - lengths
    inside = row_ids[None, :, None] >= starts[:, None, :]
    segment = jnp.sum(inside.astype(jnp.int32), axis=-1) - 1
    begin_at = jnp.max(jnp.where(inside, starts[:, None, :], 0), axis=-1)
    position = jnp.where(
        row_ids[None, :] < PROMPT, row_ids[None, :], PROMPT + row_ids[None, :] - begin_at
    )
    return (position, segment)


def visibility(query_pos, query_seg, key_pos, key_seg):
    query_at = query_pos[:, :, None]
    query_in = query_seg[:, :, None]
    key_at = key_pos[:, None, :]
    key_in = key_seg[:, None, :]
    earlier = key_at <= query_at
    allowed = (key_in < 0) & ((query_in >= 0) | earlier) | (key_in >= 0) & (
        key_in == query_in
    ) & earlier
    bucket = bucket_of(jnp.maximum(query_at - key_at, 0))
    return (allowed, bucket)


def bias_table(bias_row, bucket):
    full_bias = jnp.zeros((bias_row.shape[0],) + bucket.shape, jnp.float32)
    for number in range(bias_row.shape[1]):
        full_bias = full_bias + jnp.where(
            bucket[None] == number, bias_row[:, number][:, None, None, None], 0.0
        )
    return full_bias


def score_block(query_b, key_every, full_bias, allowed, factor):
    raw = (
        jnp.einsum("grhd,gkhd->hgrk", query_b, key_every, preferred_element_type=jnp.float32)
        * factor
    )
    raw = raw + full_bias
    return jnp.where(allowed[None], raw, -1e30)


def body(
    tokens,
    cotangent,
    w_qkv,
    w_attn,
    attn_gain,
    rel_bias,
    ffn_gain,
    router,
    w_in,
    w_out,
    cont_lengths,
    routes,
    slots,
    drops,
):
    groups, local_rows, model_width = tokens.shape
    head_count = rel_bias.shape[1]
    bucket_count = rel_bias.shape[2]
    head_size = model_width // head_count
    factor = head_size ** (-0.5)
    layer_count = w_qkv.shape[0]
    dp_count = lax.axis_size("dp")
    mp_count = lax.axis_size("mp")
    seq_len = local_rows * mp_count
    local_experts = w_in.shape[1]
    expert_total = local_experts * dp_count
    tok_count = groups * local_rows
    capacity = max(2, 9 * 2 * tok_count // (8 * expert_total))
    slot_total = expert_total * capacity
    rows_here = lax.axis_index("mp") * local_rows + jnp.arange(local_rows, dtype=jnp.int32)
    rows_every = jnp.arange(seq_len, dtype=jnp.int32)
    query_pos, query_seg = geometry(cont_lengths, rows_here)
    key_pos, key_seg = geometry(cont_lengths, rows_every)
    allowed, bucket = visibility(query_pos, query_seg, key_pos, key_seg)
    route_all = routes.reshape(layer_count, tok_count, 2)
    slot_all = slots.reshape(layer_count, tok_count, 2)
    keep_all = (1 - drops.reshape(layer_count, tok_count, 2)).astype(jnp.float32)
    head_shape = (groups, seq_len, head_count, head_size)
    stream = tokens.reshape(tok_count, model_width).astype(jnp.float32)
    stored = []
    for layer_now in range(layer_count):
        normed_b = rms_scale(stream, attn_gain[layer_now]).astype(jnp.bfloat16)
        qkv_all = jnp.dot(normed_b, w_qkv[layer_now], preferred_element_type=jnp.float32).astype(
            jnp.bfloat16
        )
        query_b = qkv_all[:, :model_width].reshape(groups, local_rows, head_count, head_size)
        key_own = qkv_all[:, model_width : 2 * model_width].reshape(groups, local_rows, model_width)
        value_own = qkv_all[:, 2 * model_width :].reshape(groups, local_rows, model_width)
        key_every, value_every = (
            lax.all_gather(key_own, "mp", axis=1, tiled=True),
            lax.all_gather(value_own, "mp", axis=1, tiled=True),
        )
        key_every = key_every.reshape(head_shape)
        value_every = value_every.reshape(head_shape)
        full_bias = bias_table(rel_bias[layer_now], bucket)
        scores = score_block(query_b, key_every, full_bias, allowed, factor)
        top_score = jnp.max(scores, axis=-1, keepdims=True)
        weights = jnp.exp(scores - top_score)
        weight_sum = jnp.sum(weights, axis=-1, keepdims=True)
        log_total = top_score + jnp.log(weight_sum)
        probs_b = (weights / weight_sum).astype(jnp.bfloat16)
        mixed_b = jnp.einsum(
            "hgrk,gkhd->grhd", probs_b, value_every, preferred_element_type=jnp.float32
        )
        mixed_b = mixed_b.reshape(tok_count, model_width).astype(jnp.bfloat16)
        middle = stream + jnp.dot(mixed_b, w_attn[layer_now], preferred_element_type=jnp.float32)
        kept_keys = (key_every, value_every)
        ffn_b = rms_scale(middle, ffn_gain[layer_now]).astype(jnp.bfloat16)
        logits = jnp.dot(ffn_b, router[layer_now], preferred_element_type=jnp.float32)
        chosen = route_all[layer_now]
        keep_pair = keep_all[layer_now]
        gate_pair = jax.nn.softmax(jnp.take_along_axis(logits, chosen, axis=1), axis=-1)
        target = chosen * capacity + slot_all[layer_now]
        sending = jnp.where(
            keep_pair[:, :, None] > 0, ffn_b[:, None, :], jnp.zeros((), jnp.bfloat16)
        )
        send_rows = (
            jnp.zeros((slot_total, model_width), jnp.bfloat16)
            .at[target.reshape(-1)]
            .add(sending.reshape(-1, model_width))
        )
        arrived = lax.all_to_all(
            send_rows.reshape(dp_count, local_experts, capacity, model_width),
            "dp",
            split_axis=0,
            concat_axis=0,
            tiled=True,
        )
        rows_in = lax.all_gather(arrived, "mp", axis=0, tiled=True)
        up_block = w_in[layer_now]
        down_block = w_out[layer_now]
        inner_act = jnp.einsum(
            "secd,edf->secf", rows_in, up_block, preferred_element_type=jnp.float32
        )
        hidden_b = gelu_tanh(inner_act).astype(jnp.bfloat16)
        summed = lax.psum_scatter(
            jnp.einsum(
                "secf,efd->secd", hidden_b, down_block, preferred_element_type=jnp.float32
            ).astype(jnp.bfloat16),
            "mp",
            scatter_dimension=0,
            tiled=True,
        )
        kept_rows = (rows_in, inner_act, hidden_b)
        returned = lax.all_to_all(summed, "dp", split_axis=0, concat_axis=0, tiled=True).reshape(
            slot_total, model_width
        )
        pair_out = returned[target].astype(jnp.float32)
        stored.append(
            (
                stream,
                normed_b,
                query_b,
                key_own,
                value_own,
                kept_keys,
                log_total,
                mixed_b,
                middle,
                ffn_b,
                chosen,
                keep_pair,
                gate_pair,
                target,
                pair_out,
                kept_rows,
                full_bias,
            )
        )
        stream = middle + jnp.sum((gate_pair * keep_pair)[:, :, None] * pair_out, axis=1)
    output = stream.astype(jnp.bfloat16).reshape(groups, local_rows, model_width)
    one_hot = (
        bucket[None] == jnp.arange(bucket_count, dtype=jnp.int32)[:, None, None, None]
    ).astype(jnp.bfloat16)
    expert_ids = jnp.arange(expert_total, dtype=jnp.int32)
    qkv_grads = [None] * layer_count
    attn_grads = [None] * layer_count
    attn_gain_grads = [None] * layer_count
    bias_grads = [None] * layer_count
    ffn_gain_grads = [None] * layer_count
    router_grads = [None] * layer_count
    up_grads = [None] * layer_count
    down_grads = [None] * layer_count
    flowing = cotangent.reshape(tok_count, model_width).astype(jnp.float32)
    for layer_now in reversed(range(layer_count)):
        (
            stream_in,
            normed_b,
            query_b,
            key_own,
            value_own,
            kept_keys,
            log_total,
            mixed_b,
            middle,
            ffn_b,
            chosen,
            keep_pair,
            gate_pair,
            target,
            pair_out,
            kept_rows,
            full_bias,
        ) = stored[layer_now]
        weighted = gate_pair * keep_pair
        pair_grad = weighted[:, :, None] * flowing[:, None, :]
        gate_grad = keep_pair * jnp.sum(flowing[:, None, :] * pair_out, axis=-1)
        picked_grad = gate_pair * (
            gate_grad - jnp.sum(gate_pair * gate_grad, axis=-1, keepdims=True)
        )
        logit_grad = jnp.sum(
            picked_grad[:, :, None] * (chosen[:, :, None] == expert_ids).astype(jnp.float32), axis=1
        )
        back_rows = (
            jnp.zeros((slot_total, model_width), jnp.float32)
            .at[target.reshape(-1)]
            .add(pair_grad.reshape(-1, model_width))
        )
        back_rows = back_rows.astype(jnp.bfloat16).reshape(
            dp_count, local_experts, capacity, model_width
        )
        grad_arrived = lax.all_to_all(back_rows, "dp", split_axis=0, concat_axis=0, tiled=True)
        grad_rows = lax.all_gather(grad_arrived, "mp", axis=0, tiled=True)
        up_block = w_in[layer_now]
        down_block = w_out[layer_now]
        rows_in, inner_act, hidden_b = kept_rows
        down_grad = jnp.einsum(
            "secf,secd->efd", hidden_b, grad_rows, preferred_element_type=jnp.float32
        )
        hidden_grad = jnp.einsum(
            "secd,efd->secf", grad_rows, down_block, preferred_element_type=jnp.float32
        )
        inner_grad = jax.vjp(gelu_tanh, inner_act)[1](hidden_grad)[0].astype(jnp.bfloat16)
        up_grad = jnp.einsum(
            "secd,secf->edf", rows_in, inner_grad, preferred_element_type=jnp.float32
        )
        rows_grad = lax.psum_scatter(
            jnp.einsum(
                "secf,edf->secd", inner_grad, up_block, preferred_element_type=jnp.float32
            ).astype(jnp.bfloat16),
            "mp",
            scatter_dimension=0,
            tiled=True,
        )
        up_grads[layer_now] = up_grad
        down_grads[layer_now] = down_grad
        grad_back = lax.all_to_all(
            rows_grad, "dp", split_axis=0, concat_axis=0, tiled=True
        ).reshape(slot_total, model_width)
        ffn_grad = jnp.sum(keep_pair[:, :, None] * grad_back[target].astype(jnp.float32), axis=1)
        ffn_grad = ffn_grad + jnp.einsum(
            "te,de->td", logit_grad, router[layer_now].astype(jnp.float32), precision=HIGHEST
        )
        router_grads[layer_now] = jnp.einsum(
            "td,te->de", ffn_b.astype(jnp.float32), logit_grad, precision=HIGHEST
        )
        middle_grad, ffn_gain_grads[layer_now] = jax.vjp(rms_scale, middle, ffn_gain[layer_now])[1](
            ffn_grad
        )
        middle_grad = middle_grad + flowing
        branch_grad = middle_grad.astype(jnp.bfloat16)
        attn_grads[layer_now] = jnp.einsum(
            "td,te->de", mixed_b, branch_grad, preferred_element_type=jnp.float32
        )
        mixed_grad = jnp.einsum(
            "te,de->td", branch_grad, w_attn[layer_now], preferred_element_type=jnp.float32
        )
        mixed_grad = mixed_grad.astype(jnp.bfloat16).reshape(
            groups, local_rows, head_count, head_size
        )
        key_every, value_every = kept_keys
        scores = score_block(query_b, key_every, full_bias, allowed, factor)
        probs = jnp.exp(scores - log_total)
        prob_grad = jnp.einsum(
            "grhd,gkhd->hgrk", mixed_grad, value_every, preferred_element_type=jnp.float32
        )
        score_grad = (
            probs * (prob_grad - jnp.sum(probs * prob_grad, axis=-1, keepdims=True))
        ).astype(jnp.bfloat16)
        query_grad = (
            jnp.einsum("hgrk,gkhd->grhd", score_grad, key_every, preferred_element_type=jnp.float32)
            * factor
        )
        key_part = (
            jnp.einsum("hgrk,grhd->gkhd", score_grad, query_b, preferred_element_type=jnp.float32)
            * factor
        )
        value_part = jnp.einsum(
            "hgrk,grhd->gkhd",
            probs.astype(jnp.bfloat16),
            mixed_grad,
            preferred_element_type=jnp.float32,
        )
        key_grad, value_grad = (
            lax.psum_scatter(
                key_part.reshape(groups, seq_len, model_width).astype(jnp.bfloat16),
                "mp",
                scatter_dimension=1,
                tiled=True,
            ).astype(jnp.float32),
            lax.psum_scatter(
                value_part.reshape(groups, seq_len, model_width).astype(jnp.bfloat16),
                "mp",
                scatter_dimension=1,
                tiled=True,
            ).astype(jnp.float32),
        )
        bias_grads[layer_now] = jnp.einsum(
            "hgrk,bgrk->hb", score_grad, one_hot, preferred_element_type=jnp.float32
        )
        qkv_grad = jnp.concatenate(
            [
                query_grad.reshape(tok_count, model_width),
                key_grad.reshape(tok_count, model_width),
                value_grad.reshape(tok_count, model_width),
            ],
            axis=1,
        ).astype(jnp.bfloat16)
        qkv_grads[layer_now] = jnp.einsum(
            "td,te->de", normed_b, qkv_grad, preferred_element_type=jnp.float32
        )
        normed_grad = jnp.einsum(
            "te,de->td", qkv_grad, w_qkv[layer_now], preferred_element_type=jnp.float32
        )
        stream_grad, attn_gain_grads[layer_now] = jax.vjp(
            rms_scale, stream_in, attn_gain[layer_now]
        )[1](normed_grad)
        flowing = middle_grad + stream_grad
    totals = lax.psum(
        (
            jnp.stack(qkv_grads),
            jnp.stack(attn_grads),
            jnp.stack(attn_gain_grads),
            jnp.stack(bias_grads),
            jnp.stack(ffn_gain_grads),
            jnp.stack(router_grads),
        ),
        ("dp", "mp"),
    )
    input_grad = flowing.reshape(groups, local_rows, model_width)
    return (
        output,
        input_grad,
        totals[0],
        totals[1],
        totals[2],
        totals[3],
        totals[4],
        totals[5],
        jnp.stack(up_grads),
        jnp.stack(down_grads),
    )


BF = jnp.bfloat16
F32 = jnp.float32
VMEM = pl.BlockSpec(memory_space=pltpu.VMEM)
SMEM = pl.BlockSpec(memory_space=pltpu.SMEM)
ANY = pl.BlockSpec(memory_space=pl.ANY)
VMEM_BYTES = 61 << 20
MESH = pl.DeviceIdType.MESH
LANES = 128
QB = 256


def nn(a, b):
    return lax.dot_general(a, b, (((1,), (0,)), ((), ())), preferred_element_type=F32)


def nt(a, b):
    return lax.dot_general(a, b, (((1,), (1,)), ((), ())), preferred_element_type=F32)


def tn(a, b):
    return lax.dot_general(a, b, (((0,), (0,)), ((), ())), preferred_element_type=F32)


def layer_spec(array, layer):
    zeros = (0,) * (array.ndim - 1)
    return pl.BlockSpec((None,) + array.shape[1:], lambda i: (layer,) + zeros, pipeline_mode=pl.Buffered(1))


def segments(lens, shape, dim):
    at = lax.broadcasted_iota(jnp.int32, shape, dim)
    segment = jnp.full(shape, -1, jnp.int32)
    begin = jnp.zeros(shape, jnp.int32)
    start = jnp.int32(0)
    for number in range(lens.shape[1]):
        inside = at >= start
        segment = segment + inside.astype(jnp.int32)
        begin = jnp.where(inside, start, begin)
        start = start + lens[0, number]
    return segment, at - begin


def bias_stage(vec, lens, table, cont_bias):
    width = vec.shape[1]
    rows = lax.broadcasted_iota(jnp.int32, (LANES, width), 0)
    skewed = jnp.broadcast_to(vec, (LANES, width))
    for bit in range(7):
        skewed = jnp.where((rows >> bit) % 2 == 1, pltpu.roll(skewed, 1 << bit, 1), skewed)
    table[...] = skewed[:, : width - LANES].T
    cont = cont_bias.shape[1]
    _, offset = segments(lens, (LANES, cont), 1)
    place = (lax.broadcasted_iota(jnp.int32, (LANES, cont), 0) == offset).astype(BF)
    full = table[0:PROMPT, :]
    high = full.astype(BF)
    low = (full - high.astype(F32)).astype(BF)
    cont_bias[...] = nn(jnp.concatenate([high, low], 1), jnp.concatenate([place, place], 0))


def blocks_of(seq):
    out = []
    for start in range(0, PROMPT, QB):
        out.append((start, start + QB, None))
    for start in range(0, seq - PROMPT, QB):
        out.append((PROMPT + start, PROMPT, max(0, start - LANES)))
    return out


def scores_of(keys, query, table, cont_bias, seg_col, seg_row, block, h):
    q0, prompt_keys, cont_from = block
    if cont_from is None:
        left = PROMPT - q0
        bias = jnp.concatenate(
            [table[left : left + prompt_keys, :], table[left - LANES : left - LANES + prompt_keys, :]], 1
        )
        return [(0, prompt_keys, nt(keys[h, 0:prompt_keys, :], query) + bias)]
    at = q0 - PROMPT
    first = nt(keys[h, 0:PROMPT, :], query) + cont_bias[:, at : at + QB]
    k0, k1 = PROMPT + cont_from, q0 + QB
    left = PROMPT + cont_from - at
    bias = jnp.concatenate(
        [table[left : left + k1 - k0, :], table[left - LANES : left - LANES + k1 - k0, :]], 1
    )
    same = seg_col[cont_from : at + QB, :][:, 0:1] == seg_row[:, at : at + QB]
    second = jnp.where(same, nt(keys[h, k0:k1, :], query) + bias, -1e30)
    return [(0, PROMPT, first), (k0, k1, second)]


def diagonals():
    width = PROMPT + 3 * LANES
    at = jnp.arange(width, dtype=jnp.int32)
    distance = jnp.where(at <= PROMPT, PROMPT - at, PROMPT + width - at)
    valid = (at <= PROMPT) | (at > width - LANES)
    return width, distance, valid


def bias_vectors(bias):
    _, distance, valid = diagonals()
    hot = bucket_of(distance)[None, :] == jnp.arange(bias.shape[-1], dtype=jnp.int32)[:, None]
    picked = jnp.sum(jnp.where(hot, bias[..., :, None], 0.0), axis=-2)
    return jnp.where(valid, picked, -1e30)


def scatter_rows(rows, values, send):
    experts, tile, _ = send.shape
    tokens, model = values[0].shape
    half = model // 2
    at = lax.broadcasted_iota(jnp.int32, (experts * tile, tokens), 0)
    place, piece = [], []
    for j in range(2):
        slot = rows[2 + j : 3 + j, :]
        piece.append(jnp.where(rows[4 + j : 5 + j, :] > 0, slot // tile, -1))
        place.append(rows[j : j + 1, :] * tile + slot % tile)

    def pick(number, shift, columns):
        hots = [
            (jnp.where(piece[j] == number, place[j] + shift, -1) == at) for j in range(2)
        ]
        if len(values) == 1:
            return nn((hots[0] | hots[1]).astype(BF), values[0][:, columns])
        return nn(hots[0].astype(BF), values[0][:, columns]) + nn(hots[1].astype(BF), values[1][:, columns])

    for i in range(3):
        send[:, :, i * model : (i + 1) * model] = pick(i, 0, slice(0, model)).astype(BF).reshape(experts, tile, model)
    tail = pick(3, 0, slice(0, half)) + pick(3, 8, slice(half, model))
    send[:, :, 3 * model : 3 * model + half] = tail.astype(BF).reshape(experts, tile, half)


def columns(rows):
    return rows[...].astype(F32).T.astype(jnp.int32)


def scatter_gates(rows, gates, send, start):
    experts, tile, _ = send.shape
    tokens = rows.shape[1]
    at = lax.broadcasted_iota(jnp.int32, (experts * tile, tokens), 0)
    lane = lax.broadcasted_iota(jnp.int32, (tokens, LANES), 1)
    total = 0.0
    for j in range(2):
        slot = rows[2 + j : 3 + j, :]
        piece = jnp.where(rows[4 + j : 5 + j, :] > 0, slot // tile, -1)
        place = rows[j : j + 1, :] * tile + slot % tile
        high = gates[j].astype(BF).astype(F32)
        rest = gates[j] - high
        mid = rest.astype(BF).astype(F32)
        part = jnp.where(lane % 3 == 0, high, jnp.where(lane % 3 == 1, mid, rest - mid))
        for i in range(4):
            hot = (jnp.where(piece == i, place, -1) == at).astype(BF)
            total = total + nn(hot, jnp.where(lane // 3 == i, part, 0.0).astype(BF))
    send[:, :, start:] = total.astype(BF).reshape(experts, tile, LANES)


def gather_rows(cols, j, back):
    experts, tile, wide = back.shape
    half = wide // 7
    model = 2 * half
    tokens = cols.shape[0]
    at = lax.broadcasted_iota(jnp.int32, (tokens, experts * tile), 1)
    slot = cols[:, 2 + j : 3 + j]
    piece = jnp.where(cols[:, 4 + j : 5 + j] > 0, slot // tile, -1)
    place = cols[:, j : j + 1] * tile + slot % tile
    total = 0.0
    for i in range(3):
        hot = (jnp.where(piece == i, place, -1) == at).astype(BF)
        total = total + nn(hot, back[:, :, i * model : (i + 1) * model].reshape(experts * tile, model))
    tail = back[:, :, 3 * model :].reshape(experts * tile, half)
    left = nn((jnp.where(piece == 3, place, -1) == at).astype(BF), tail)
    right = nn((jnp.where(piece == 3, place + 8, -1) == at).astype(BF), tail)
    return total + jnp.concatenate([left, right], 1)


def unfold_tail(block, half):
    wide = block.astype(F32)
    return jnp.concatenate([wide[0:8, :], wide[8:16, :]], 1)


def mp_places():
    me = lax.axis_index("mp")
    core, row = lax.rem(me, 2), me // 2
    return me, core, row * 2 + 1 - core, (1 - row) * 2 + core, (1 - row) * 2 + 1 - core


def signal_to(barrier, **place):
    pl.semaphore_signal(barrier, inc=1, device_id=place, device_id_type=MESH)


def remote(src, dst, send_sem, recv_sem, **place):
    return pltpu.make_async_remote_copy(
        src_ref=src, dst_ref=dst, send_sem=send_sem, recv_sem=recv_sem, device_id=place, device_id_type=MESH
    )


def greet_mp(count, dp_count=1):
    me, core, mate, across, diagonal = mp_places()
    d = lax.axis_index("dp")
    barrier = pltpu.get_barrier_semaphore()
    for to in (mate, across, diagonal)[:count]:
        signal_to(barrier, mp=to)
    for k in range(1, dp_count):
        signal_to(barrier, dp=lax.rem(d + k, dp_count), mp=me)
    pl.semaphore_wait(barrier, count + dp_count - 1)


def share_dp(held, ssem, rsem):
    d, me, count = lax.axis_index("dp"), lax.axis_index("mp"), held.shape[0]
    return [
        remote(held.at[d], held.at[d], ssem.at[k], rsem.at[k], dp=lax.rem(d + k, count), mp=me) for k in range(1, count)
    ]


def scatter_dp(part, come, ssem, rsem):
    d, me, count = lax.axis_index("dp"), lax.axis_index("mp"), part.shape[0]
    copies = []
    for k in range(1, count):
        to = lax.rem(d + k, count)
        copies.append(remote(part.at[to], come.at[d], ssem.at[k], rsem.at[k], dp=to, mp=me))
    return copies


def sum_dp(copies, part, come):
    d, count = lax.axis_index("dp"), part.shape[0]
    total = part[d].astype(F32)
    for k in range(1, count):
        copies[k - 1].wait_recv()
        total = total + come[lax.rem(d + count - k, count)].astype(F32)
    return total


def mean_square_scale(values):
    return lax.rsqrt(jnp.mean(values * values, axis=-1, keepdims=True) + EPSILON)


def norm_grads(values, gain, upstream):
    scale = mean_square_scale(values)
    scaled = upstream * gain
    drift = jnp.mean(values * scaled, axis=-1, keepdims=True)
    return scale * scaled - values * (scale * scale * scale * drift), jnp.sum(
        upstream * values * scale, axis=0, keepdims=True
    )


def pre_kernel(layer, layers, heads, size, *refs):
    refs = list(refs)

    def take(count):
        taken = refs[:count]
        del refs[:count]
        return taken

    first, last = layer == 0, layer == layers - 1
    lens, gain_a, w_qkv_in, vecs, w_attn_in, gain_f, router, rows = take(8)
    if first:
        tokens, cotangent, far_rows = take(3)
    else:
        before, returned, rows_in, gates_in = take(4)
        cols_in = columns(rows_in)
    g_in, g_half = take(2) if last else (None, None)
    (stream_o,) = (None,) if first else take(1)
    normed_o, qkv_o, mixed_o, lse_o, middle_o, ffn_o, gates_o, send_o = take(8)
    (g_o,) = take(1) if first or last else (None,)
    (g_half_o,) = take(1) if first else (None,)
    held, hssem, hrsem = take(3)
    w_qkv, w_attn, qkv_s, iosem = take(4)
    (stream_s,) = (None,) if first else take(1)
    weight, q_s, k_s, vt_s, table, cont_bias, mixt, segc, out_s, mixed_s, mssem, mrsem = take(12)
    if first:
        g_send, g_held, gssem, grsem = take(4)
    if first or last:
        g_over, gfsem, gbsem = take(3)
    me, core, mate, across, diagonal = mp_places()
    d = lax.axis_index("dp")
    dp_count = lax.axis_size("dp")
    seq, own = mixed_o.shape
    local, model = middle_o.shape
    parts = local // LANES
    cols = columns(rows)
    w_qkv_come = pltpu.make_async_copy(w_qkv_in.at[layer], w_qkv, iosem.at[0])
    w_attn_come = pltpu.make_async_copy(w_attn_in.at[layer], w_attn, iosem.at[1])
    normed_go = pltpu.make_async_copy(held, normed_o, iosem.at[2])
    qkv_go = pltpu.make_async_copy(qkv_s, qkv_o, iosem.at[3])
    goes = [normed_go, qkv_go]
    if not first:
        goes.append(pltpu.make_async_copy(stream_s, stream_o, iosem.at[4]))
    w_qkv_come.start()
    w_attn_come.start()

    barrier = pltpu.get_barrier_semaphore()
    for to in (mate, across, diagonal):
        signal_to(barrier, mp=to)
    if first:
        for k in range(2, 2 * dp_count):
            signal_to(barrier, dp=lax.rem(d + k // 2, dp_count), mp=(me // 2) * 2 + lax.rem(core + k % 2, 2))
        count = 3 + 2 * dp_count - 2
    else:
        count = 3
    if first:
        stream = tokens[...].astype(F32)
    else:
        stream = before[...]
        for j in range(2):
            stream = stream + gates_in[:, j : j + 1] * gather_rows(cols_in, j, returned)
        stream_s[...] = stream
        goes[2].start()
    held[me] = (stream * mean_square_scale(stream) * gain_a[layer : layer + 1, :]).astype(BF)
    pl.semaphore_wait(barrier, count)
    over = remote(held.at[me], held.at[me], hssem.at[1], hrsem.at[1], mp=across)
    to_mate = remote(held.at[me], held.at[me], hssem.at[0], hrsem.at[0], mp=mate)
    passed = remote(held.at[across], held.at[across], hssem.at[2], hrsem.at[2], mp=mate)
    over.start()
    to_mate.start()

    index = d * 2 + core

    def far_copy(k):
        dd, cc = lax.rem(d + k // 2, dp_count), lax.rem(core + k % 2, 2)
        if k == 0:
            return pltpu.make_async_copy(g_send.at[index], g_held.at[index], grsem.at[0])
        return remote(g_send.at[dd * 2 + cc], g_held.at[index], gssem.at[k], grsem.at[k], dp=dd, mp=(me // 2) * 2 + cc)

    def far_over(source, n):
        two = pl.ds(lax.rem(d + dp_count - n, dp_count) * 2, 2)
        return remote(source.at[two], g_over.at[two], gfsem.at[n], gbsem.at[n], mp=across)

    def far_wave(n):
        if n < dp_count:
            far_copy(2 * n).start()
            far_copy(2 * n + 1).start()

    def far_arrived(n):
        far_copy(2 * n).wait() if n == 0 else far_copy(2 * n).wait_recv()
        far_copy(2 * n + 1).wait_recv()

    if first:
        scatter_rows(far_rows, [cotangent[...]], g_send)
        for n in range(dp_count):
            far_wave(n)
    elif last:
        for n in range(2, dp_count):
            far_over(g_in, n).start()

    w_qkv_come.wait()
    for m in range(model // own):

        @pl.when(me == m)
        def _():
            for t in range(3):
                weight[:, t * own : (t + 1) * own] = w_qkv[:, t * model + m * own : t * model + (m + 1) * own]

    seg_row, _ = segments(lens, (1, seq - PROMPT), 1)
    segc[...] = segments(lens, (seq - PROMPT, LANES), 0)[0]

    def tables(h, carry):
        bias_stage(vecs[pl.ds(h, 1), :], lens, table.at[h], cont_bias.at[h])
        return carry

    lax.fori_loop(0, heads, tables, 0)

    def project(m):
        at = pl.ds(pl.multiple_of(m * local, LANES), local)
        part = nn(held[m], weight[...]).astype(BF)
        qkv_s[at, :] = part
        for h in range(heads):
            q_s[h, at, :] = part[:, h * size : (h + 1) * size] * BF(0.125)
            k_s[h, at, :] = part[:, own + h * size : own + (h + 1) * size]
            vt_s[h, :, at] = part[:, 2 * own + h * size : 2 * own + (h + 1) * size].astype(F32).T.astype(BF)

    project(me)
    to_mate.wait_recv()
    project(mate)
    over.wait_recv()
    passed.start()
    project(across)
    passed.wait_recv()
    project(diagonal)
    normed_go.start()
    qkv_go.start()

    def handed(n):
        return remote(out_s.at[n], mixed_s.at[me, n % parts], mssem.at[n], mrsem.at[me, n % parts], mp=n // parts)

    early = {1: 0, 3: 1}
    for number, block in enumerate(blocks_of(seq)):
        q0 = block[0]
        if first and number in early:
            far_arrived(early[number])
            far_over(g_held, early[number]).start()

        def head(h, carry):
            query = q_s[h, q0 : q0 + QB, :]
            scored = scores_of(k_s, query, table.at[h], cont_bias.at[h], segc, seg_row, block, h)
            top = functools.reduce(jnp.maximum, [jnp.max(s, axis=0, keepdims=True) for _, _, s in scored])
            total, mixed = 0.0, 0.0
            for k0, k1, s in scored:
                p = jnp.exp(s - top)
                total = total + jnp.sum(p, axis=0, keepdims=True)
                mixed = mixed + nn(vt_s[h, :, k0:k1], p.astype(BF))
            mixt[pl.ds(pl.multiple_of(h * size, size), size), :] = mixed / total
            lse_o[pl.ds(h, 1), q0 : q0 + QB] = top + jnp.log(total)
            return carry

        lax.fori_loop(0, heads, head, 0)
        done = mixt[...].T.astype(BF)
        mixed_o[q0 : q0 + QB, :] = done
        for half in range(QB // LANES):
            n = q0 // LANES + half
            middle_row = half * LANES + LANES // 2
            out_s[n] = jnp.concatenate(
                [done[half * LANES : middle_row, :], done[middle_row : (half + 1) * LANES, :]], 1
            )

            @pl.when(me == n // parts)
            def _():
                pltpu.make_async_copy(out_s.at[n], mixed_s.at[me, n % parts], mrsem.at[me, n % parts]).start()

            @pl.when(me != n // parts)
            def _():
                handed(n).start()

    w_attn_come.wait()
    middle = stream
    for m in range(mixed_s.shape[0]):
        for n in range(parts):
            pltpu.make_async_copy(mixed_s.at[m, n], mixed_s.at[m, n], mrsem.at[m, n]).wait()
        halves = [mixed_s[m, n][:, i * own : (i + 1) * own] for n in range(parts) for i in range(2)]
        middle = middle + nn(jnp.concatenate(halves, 0), w_attn[m * own : (m + 1) * own, :])
    middle_o[...] = middle
    ffn = (middle * mean_square_scale(middle) * gain_f[layer : layer + 1, :]).astype(BF)
    ffn_o[...] = ffn
    logits = nt(ffn, router[...])
    expert = lax.broadcasted_iota(jnp.int32, logits.shape, 1)
    chosen = [
        jnp.sum(jnp.where(expert == cols[:, j : j + 1], logits, 0.0), axis=1, keepdims=True) for j in range(2)
    ]
    top = jnp.maximum(chosen[0], chosen[1])
    powers = [jnp.exp(c - top) for c in chosen]
    gates = [p / (powers[0] + powers[1]) for p in powers]
    gates_o[...] = jnp.concatenate(gates, 1)
    scatter_rows(rows, [ffn], send_o)
    if last:
        scatter_gates(rows, gates, send_o, 7 * model // 2)
    if first:
        for n in range(2, dp_count):
            far_arrived(n)
        g_o[...] = g_held[...]
        for k in range(1, 2 * dp_count):
            far_copy(k).wait_send()
        for n in range(2):
            far_over(g_held, n).wait()
            two = pl.ds(lax.rem(d + dp_count - n, dp_count) * 2, 2)
            g_half_o[two] = g_over[two]
    elif last:
        for n in range(2):
            two = pl.ds(lax.rem(d + dp_count - n, dp_count) * 2, 2)
            g_o[two] = g_half[two]
        for n in range(2, dp_count):
            far_over(g_in, n).wait()
            two = pl.ds(lax.rem(d + dp_count - n, dp_count) * 2, 2)
            g_o[two] = g_over[two]
    for copy in goes:
        copy.wait()
    for copy in (to_mate, over, passed):
        copy.wait_send()
    for n in range(seq // LANES):

        @pl.when(me != n // parts)
        def _():
            handed(n).wait_send()


def pre_call(layer, layers, number, heads, size, lens, normal, mp_count, dp_count, local, model, specials, block):
    first, last = layer == 0, layer == layers - 1
    seq, own = local * mp_count, heads * size
    width = PROMPT + 3 * LANES
    args = list(normal) + list(specials)
    specs = [SMEM] + [layer_spec(*a) if isinstance(a, tuple) else VMEM for a in args]
    specs[2] = specs[4] = ANY
    narrow = block[:2] + (7 * model // 2,)
    send = narrow[:2] + (narrow[2] + LANES,) if last else narrow
    outs = [] if first else [((local, model), F32)]
    outs += [
        ((mp_count, local, model), BF), ((seq, 3 * own), BF), ((seq, own), BF), ((heads, seq), F32),
        ((local, model), F32), ((local, model), BF), ((local, 2), F32), (send, BF),
    ]
    if first or last:
        outs.append((narrow, BF))
    if first:
        outs.append((narrow, BF))
    out_specs = [VMEM] * len(outs)
    for n in (0, 1) if first else (0, 1, 2):
        out_specs[n] = ANY
    scratch = [
        pltpu.VMEM((mp_count, local, model), BF), dma(3), dma(3),
        pltpu.VMEM((model, 3 * model), BF), pltpu.VMEM((model, model), BF), pltpu.VMEM((seq, 3 * own), BF), dma(5),
        *([] if first else [pltpu.VMEM((local, model), F32)]),
        pltpu.VMEM((model, 3 * own), BF),
        pltpu.VMEM((heads, seq, size), BF),
        pltpu.VMEM((heads, seq, size), BF),
        pltpu.VMEM((heads, size, seq), BF),
        pltpu.VMEM((heads, width - LANES, LANES), F32),
        pltpu.VMEM((heads, PROMPT, seq - PROMPT), F32),
        pltpu.VMEM((own, QB), F32),
        pltpu.VMEM((seq - PROMPT, LANES), jnp.int32),
        pltpu.VMEM((seq // LANES, LANES // 2, 2 * own), BF),
        pltpu.VMEM((mp_count, local // LANES, LANES // 2, 2 * own), BF),
        dma(seq // LANES),
        dma(mp_count, local // LANES),
    ]
    if first:
        scratch += [pltpu.VMEM(narrow, BF), pltpu.VMEM(narrow, BF), dma(2 * dp_count), dma(2 * dp_count)]
    if first or last:
        scratch += [pltpu.VMEM(narrow, BF), dma(dp_count), dma(dp_count)]
    return pl.pallas_call(
        functools.partial(pre_kernel, layer, layers, heads, size),
        grid=(1,),
        out_shape=tuple(jax.ShapeDtypeStruct(shape, kind) for shape, kind in outs),
        in_specs=specs,
        out_specs=tuple(out_specs),
        scratch_shapes=scratch,
        compiler_params=pltpu.CompilerParams(
            collective_id=number, has_side_effects=True, vmem_limit_bytes=VMEM_BYTES
        ),
    )(lens, *[a[0] if isinstance(a, tuple) else a for a in args])


def shift_table(flat, width):
    rows = lax.broadcasted_iota(jnp.int32, flat.shape, 0)
    for bit in range(7):
        flat = jnp.where((rows >> bit) % 2 == 1, pltpu.roll(flat, width - (1 << bit), 1), flat)
    return jnp.sum(flat, axis=0, keepdims=True)


def back_kernel(layer, layers, heads, size, buckets, *refs):
    refs = list(refs)

    def take(count):
        taken = refs[:count]
        del refs[:count]
        return taken

    first, last = layer == 0, layer == layers - 1
    lens, vecs, back, returned, flow_in, middle, ffn, gates, rows_own, router, gain_f = take(11)
    normed_in, qkv_in, mixed, lse, w_attn_in, w_qkv_in, stream, gain_a = take(8)
    if first:
        above, small_above = take(2)
    else:
        rows_below, gates_below = take(2)
    (flow_o,) = take(1)
    if first:
        up_out, all_out, small_o = take(3)
    else:
        out_o, send_o, sum_o, small_o = take(4)
    held, hssem, hrsem = take(3)
    normed, qkv, w_attn, w_qkv, insem = take(5)
    normed_t, q_s, k_s, v_s, kt_s, do_s, table, cont_bias, fold, dtable, dk_s, dv_s, dqt, segc, hot, bias_s, gw_a, router_s = take(18)
    dq_s, dq_fold, dq_held, qssem, qrsem, part, come, pssem, prsem = take(9)
    if first:
        small_s, small_come, small_mp, tsem, usem, csem, dsem, vsem, zsem = take(9)
        assem, arsem, ossem, orsem = take(4)
        ussem, ursem, wssem, wrsem = take(4)
        up_o, all_o, outsem = take(3)
    me, core, mate, across, diagonal = mp_places()
    d = lax.axis_index("dp")
    dp_count = part.shape[0]
    local, model = middle.shape
    seq, own = mixed.shape
    cont = seq - PROMPT
    width = vecs.shape[1]
    places = mixed.shape[0] // local
    cols = columns(rows_own)
    sources = (normed_in, qkv_in, w_attn_in.at[layer], w_qkv_in.at[layer])
    come_in = [pltpu.make_async_copy(s, h, insem.at[n]) for n, (s, h) in enumerate(zip(sources, (normed, qkv, w_attn, w_qkv)))]
    for copy in come_in:
        copy.start()

    def dp_share(held_all, ssem, rsem, k):
        return remote(held_all.at[me, d], held_all.at[me, d], ssem.at[k], rsem.at[k], dp=lax.rem(d + k, dp_count), mp=me)

    def mp_share(held_all, ssem, rsem, n, j):
        whose = across if n == 2 else me
        return remote(
            held_all.at[whose, j], held_all.at[whose, j], ssem.at[n, j], rsem.at[n, j], mp=across if n == 1 else mate
        )

    greet_mp(3, dp_count=dp_count)
    if first:
        up_o[me, d] = above[...]
        for k in range(1, dp_count - 2):
            dp_share(up_o, ussem, ursem, k).start()

    flow = flow_in[...].astype(F32)
    outs = [gather_rows(cols, j, returned) for j in range(2)]
    gate = [gates[:, j : j + 1] for j in range(2)]
    keep = [cols[:, 4 + j : 5 + j].astype(F32) for j in range(2)]
    if last:
        out_o[...] = (middle[...] + gate[0] * keep[0] * outs[0] + gate[1] * keep[1] * outs[1]).astype(BF)
    gate_grad = [keep[j] * jnp.sum(flow * outs[j], axis=1, keepdims=True) for j in range(2)]
    shared = gate[0] * gate_grad[0] + gate[1] * gate_grad[1]
    expert = lax.broadcasted_iota(jnp.int32, (local, router.shape[0]), 1)
    logit_grad = 0.0
    for j in range(2):
        logit_grad = logit_grad + jnp.where(expert == cols[:, j : j + 1], gate[j] * (gate_grad[j] - shared), 0.0)
    high = logit_grad.astype(BF)
    low = (logit_grad - high.astype(F32)).astype(BF)
    upstream = gather_rows(cols, 0, back) + gather_rows(cols, 1, back)
    upstream = upstream + nn(high, router[...]) + nn(low, router[...])
    grad, gain_f_grad = norm_grads(middle[...], gain_f[layer : layer + 1, :], upstream)
    grad = grad + flow
    flow_o[...] = grad
    held[me] = grad.astype(BF)
    to_mate = remote(held.at[me], held.at[me], hssem.at[0], hrsem.at[0], mp=mate)
    over = remote(held.at[me], held.at[me], hssem.at[1], hrsem.at[1], mp=across)
    passed = remote(held.at[across], held.at[across], hssem.at[2], hrsem.at[2], mp=mate)
    over.start()
    to_mate.start()

    router_s[...] = tn(jnp.concatenate([high, low], 1), ffn[...])
    for copy in come_in[:3]:
        copy.wait()
    for i in range(seq // local):
        rows = pl.ds(i * local, local)
        normed_t[:, i * local : (i + 1) * local] = normed[i].astype(F32).T.astype(BF)
        piece = qkv[rows, :]
        for h in range(heads):
            q_s[h, rows, :] = piece[:, h * size : (h + 1) * size] * BF(0.125)
            key = piece[:, own + h * size : own + (h + 1) * size]
            k_s[h, rows, :] = key
            kt_s[h, :, i * local : (i + 1) * local] = (key.astype(F32) * 0.125).T.astype(BF)
            v_s[h, rows, :] = piece[:, 2 * own + h * size : 2 * own + (h + 1) * size]
    seg_row, _ = segments(lens, (1, cont), 1)
    segc[...] = segments(lens, (cont, LANES), 0)[0]
    _, offset = segments(lens, (cont, LANES), 0)
    unplace = (lax.broadcasted_iota(jnp.int32, (cont, LANES), 1) == offset).astype(BF)
    at = lax.broadcasted_iota(jnp.int32, (1, width), 1)
    distance = jnp.where(at <= PROMPT, PROMPT - at, PROMPT + width - at)
    bucket = jnp.where((at <= PROMPT) | (at > width - LANES), bucket_of(distance), -1)
    hot[...] = (lax.broadcasted_iota(jnp.int32, (buckets, width), 0) == bucket).astype(F32)
    bias_s[...] = jnp.zeros_like(bias_s)

    def tables(h, carry):
        bias_stage(vecs[pl.ds(h, 1), :], lens, table.at[h], cont_bias.at[h])
        return carry

    lax.fori_loop(0, heads, tables, 0)

    def receive(m):
        dmix = nt(held[m], w_attn[pl.ds(pl.multiple_of(me * own, size), own), :]).astype(BF)
        for h in range(heads):
            do_s[h, pl.ds(pl.multiple_of(m * local, LANES), local), :] = dmix[:, h * size : (h + 1) * size]

    receive(me)
    to_mate.wait_recv()
    receive(mate)
    over.wait_recv()
    passed.start()
    receive(across)
    passed.wait_recv()
    receive(diagonal)
    gw_a[...] = tn(held[...].reshape(seq, model), mixed[...])

    def swap_copy(h, n):
        to = (mate, across, diagonal)[n]
        return remote(dq_fold.at[h, to], dq_held.at[h, me], qssem.at[h, n], qrsem.at[h, me], mp=to)

    def sum_copy(h, k):
        to = lax.rem(d + k, dp_count)
        return remote(part.at[to, h], come.at[d, h], pssem.at[h, k], prsem.at[h, k], dp=to, mp=me)

    def summed(h):
        total = part[d, h].astype(F32)
        for k in range(1, dp_count):
            sum_copy(h, k).wait_recv()
            total = total + come[lax.rem(d + dp_count - k, dp_count), h].astype(F32)
        return total.astype(BF)

    def head_share(h, k):
        place = all_o.at[me, d, h]
        return remote(place, place, assem.at[h, k], arsem.at[h, k], dp=lax.rem(d + k, dp_count), mp=me)

    def head_pass(n, h, j):
        place = all_o.at[across if n == 2 else me, j, h]
        return remote(place, place, ossem.at[n, h, j], orsem.at[n, h, j], mp=across if n == 1 else mate)

    def finish_sum(h):
        all_o[me, d, h] = summed(h)
        for k in range(1, dp_count):
            head_share(h, k).start()

    def hand_on(h):
        for k in range(dp_count):
            j = lax.rem(d + dp_count - k, dp_count)
            if k > 0:
                head_share(h, k).wait_recv()
            head_pass(1, h, j).start()
            head_pass(0, h, j).start()

    def pass_on(h):
        for k in range(dp_count):
            j = lax.rem(d + dp_count - k, dp_count)
            head_pass(1, h, j).wait_recv()
            head_pass(2, h, j).start()

    def head(h, carry):
        dtable[...] = jnp.zeros_like(dtable)
        dk_s[...] = jnp.zeros_like(dk_s)
        dv_s[...] = jnp.zeros_like(dv_s)
        for number, block in enumerate(blocks_of(seq)):
            q0, prompt_keys, cont_from = block
            if first:

                @pl.when(h == 0)
                def _():
                    for k in ((0,), (1,), (2,), (3,), (4, 5), (6, 7))[number]:
                        if k > 0:
                            dp_share(up_o, ussem, ursem, k).wait_recv()
                        if number == 1:
                            for later in range(dp_count - 2, dp_count):
                                dp_share(up_o, ussem, ursem, later).start()
                        j = lax.rem(d + dp_count - k, dp_count)
                        mp_share(up_o, wssem, wrsem, 1, j).start()
                        mp_share(up_o, wssem, wrsem, 0, j).start()

            query = q_s[h, q0 : q0 + QB, :]
            dout = do_s[h, q0 : q0 + QB, :]
            scored = scores_of(k_s, query, table.at[h], cont_bias.at[h], segc, seg_row, block, h)
            lse_row = lse[pl.ds(h, 1), q0 : q0 + QB]
            kept, delta = [], 0.0
            for k0, k1, s in scored:
                p = jnp.exp(s - lse_row)
                dp = nt(v_s[h, k0:k1, :], dout)
                delta = delta + jnp.sum(p * dp, axis=0, keepdims=True)
                dv_s[k0:k1, :] += nn(p.astype(BF), dout)
                kept.append((k0, k1, p, dp))
            dq = 0.0
            for k0, k1, p, dp in kept:
                ds = p * (dp - delta)
                dsb = ds.astype(BF)
                dk_s[k0:k1, :] += nn(dsb, query)
                dq = dq + nn(kt_s[h, :, k0:k1], dsb)
                if cont_from is not None and k0 == 0:
                    fold[:, q0 - PROMPT : q0 - PROMPT + QB] = dsb
                else:
                    left = PROMPT - q0 if cont_from is None else PROMPT + cont_from - (q0 - PROMPT)
                    dtable[left : left + k1 - k0, :] += ds[:, 0:LANES]
                    dtable[left - LANES : left - LANES + k1 - k0, :] += ds[:, LANES:]
            dqt[:, q0 : q0 + QB] = dq
        for m in range(places):
            rows = slice(m * local, (m + 1) * local)
            piece = jnp.concatenate([dqt[:, rows].T.astype(BF), dk_s[rows, :].astype(BF), dv_s[rows, :].astype(BF)], 1)
            dq_s[m] = piece
            dq_fold[h, m] = jnp.concatenate([piece[0 : local // 2, :], piece[local // 2 :, :]], 1)
        for n in (2, 1, 0):
            swap_copy(h, n).start()
        pltpu.make_async_copy(dq_fold.at[h, me], dq_held.at[h, me], qrsem.at[h, me]).start()
        grads = nn(normed_t[...], dq_s[...].reshape(seq, 3 * size))
        for j in range(dp_count):
            rows = slice(j * part.shape[2], (j + 1) * part.shape[2])
            part[j, h, :, 0 : 3 * size] = grads[rows, :].astype(BF)
        for k in range(1, dp_count):
            sum_copy(h, k).start()
        dtable[0:PROMPT, :] += nn(fold[...], unplace)
        flat = jnp.concatenate([dtable[...].T, jnp.zeros((LANES, LANES), F32)], 1)
        found = jnp.sum(hot[...] * shift_table(flat, width), axis=1, keepdims=True)
        lane = lax.broadcasted_iota(jnp.int32, bias_s.shape, 1)
        bias_s[...] += jnp.where(lane == me * heads + h, found, 0.0)
        if first:

            @pl.when(h == heads - 1)
            def _():
                for j in range(dp_count):
                    mp_share(up_o, wssem, wrsem, 1, j).wait_recv()
                    mp_share(up_o, wssem, wrsem, 2, j).start()

            @pl.when(h > 0)
            def _():
                finish_sum(h - 1)

        return carry

    for j in range(dp_count):
        rows = slice(j * part.shape[2], (j + 1) * part.shape[2])
        for h in range(heads):
            part[j, h, :, 3 * size :] = gw_a[rows, h * size : (h + 1) * size].astype(BF)
    lax.fori_loop(0, heads, head, 0, unroll=True)
    if first:
        hand_on(0)
    for h in range(heads):
        for m in range(places):
            pltpu.make_async_copy(dq_held.at[h, m], dq_held.at[h, m], qrsem.at[h, m]).wait()
    come_in[3].wait()
    upstream = 0.0
    for t in range(3):
        halves = []
        for lane in (t * size, own + t * size):
            found = [dq_held[h, m, :, lane : lane + size] for m in range(places) for h in range(heads)]
            halves.append(jnp.concatenate(found, 1))
        piece = jnp.concatenate(halves, 0)
        upstream = upstream + nt(piece, w_qkv[:, t * model : (t + 1) * model])
    inner, gain_a_grad = norm_grads(stream[...].astype(F32), gain_a[layer : layer + 1, :], upstream)
    flow = flow_o[...] + inner
    flow_o[...] = flow
    gains = jnp.concatenate([gain_a_grad, gain_f_grad, jnp.zeros((6, model), F32)], 0)
    tiles = [bias_s[8 * i : 8 * i + 8, :] for i in range(buckets // 8)]
    bias_rows = jnp.concatenate(tiles + [jnp.zeros((8, model - LANES * len(tiles)), F32)], 1)
    router_grad = router_s[0 : router.shape[0], :] + router_s[router.shape[0] :, :]
    small = [gains, bias_rows] + [router_grad[8 * i : 8 * i + 8, :] for i in range(router.shape[0] // 8)]

    if not first:
        cols_below = columns(rows_below)
        scatter_rows(
            rows_below,
            [(gates_below[:, j : j + 1] * cols_below[:, 4 + j : 5 + j].astype(F32) * flow).astype(BF) for j in range(2)],
            send_o,
        )
        for n, block in enumerate(small):
            small_o[n] = block
        for h in range(heads):
            sum_o[h] = summed(h)
    else:
        for n, block in enumerate(small):
            small_s[n] = block
        small_s[len(small) :] = small_above[...]
        small_scattered = scatter_dp(small_s, small_come, tsem, usem)
        for copy in small_scattered:
            copy.start()
        finish_sum(heads - 1)
        for j in range(dp_count):
            mp_share(up_o, wssem, wrsem, 0, j).wait_recv()
            mp_share(up_o, wssem, wrsem, 2, j).wait_recv()
        up_go = pltpu.make_async_copy(up_o, up_out, outsem.at[0])
        all_go = pltpu.make_async_copy(all_o, all_out, outsem.at[1])
        up_go.start()
        hand_on(1)
        small_mp[me] = sum_dp(small_scattered, small_s, small_come)
        small_swaps = [
            remote(small_mp.at[me], small_mp.at[me], csem.at[n], dsem.at[n], mp=to) for n, to in enumerate((mate, across, diagonal))
        ]
        for copy in small_swaps:
            copy.start()
        pass_on(0)
        for copy in small_swaps:
            copy.wait_recv()
        small_o[d] = small_mp[0] + small_mp[1] + small_mp[2] + small_mp[3]
        small_shares = share_dp(small_o, vsem, zsem)
        for copy in small_shares:
            copy.start()
        for h in range(2, heads):
            hand_on(h)
        for h in range(1, heads):
            pass_on(h)
        for copy in small_shares:
            copy.wait_recv()
        for j in range(dp_count):
            for h in range(heads):
                head_pass(0, h, j).wait_recv()
                head_pass(2, h, j).wait_recv()
        all_go.start()
        for j in range(dp_count):
            for n in range(3):
                mp_share(up_o, wssem, wrsem, n, j).wait_send()
                for h in range(heads):
                    head_pass(n, h, j).wait_send()
        for k in range(1, dp_count):
            dp_share(up_o, ussem, ursem, k).wait_send()
            for h in range(heads):
                head_share(h, k).wait_send()
        for copy in small_swaps + small_scattered + small_shares:
            copy.wait_send()
        up_go.wait()
        all_go.wait()
    for copy in (to_mate, over, passed):
        copy.wait_send()
    for h in range(heads):
        for n in range(3):
            swap_copy(h, n).wait_send()
        for k in range(1, dp_count):
            sum_copy(h, k).wait_send()


def back_call(layer, layers, number, heads, size, buckets, lens, normal, mp_count, dp_count, local, model, block, extra):
    first, last = layer == 0, layer == layers - 1
    seq, own = local * mp_count, heads * size
    width = PROMPT + 3 * LANES
    cont = seq - PROMPT
    args = list(normal) + list(extra)
    specs = [SMEM] + [layer_spec(*a) if isinstance(a, tuple) else VMEM for a in args]
    for n in (11, 12, 15, 16):
        specs[n] = ANY
    chunk = (heads, model // dp_count, 4 * size)
    smalls = dp_count // layers
    outs = [((local, model), F32)]
    if first:
        outs += [((mp_count, dp_count) + chunk, BF), ((mp_count, dp_count) + chunk, BF), ((dp_count, 8, model), F32)]
    else:
        outs += [((local, model), BF), (block, BF), (chunk, BF), ((smalls, 8, model), F32)]
    out_specs = [VMEM] * len(outs)
    scratch = [
        pltpu.VMEM((mp_count, local, model), BF), dma(3), dma(3),
        pltpu.VMEM((mp_count, local, model), BF), pltpu.VMEM((seq, 3 * own), BF),
        pltpu.VMEM((model, model), BF), pltpu.VMEM((model, 3 * model), BF), dma(4),
        pltpu.VMEM((model, seq), BF),
        pltpu.VMEM((heads, seq, size), BF),
        pltpu.VMEM((heads, seq, size), BF),
        pltpu.VMEM((heads, seq, size), BF),
        pltpu.VMEM((heads, size, seq), BF),
        pltpu.VMEM((heads, seq, size), BF),
        pltpu.VMEM((heads, width - LANES, LANES), F32),
        pltpu.VMEM((heads, PROMPT, cont), F32),
        pltpu.VMEM((PROMPT, cont), BF),
        pltpu.VMEM((width - LANES, LANES), F32),
        pltpu.VMEM((seq, size), F32),
        pltpu.VMEM((seq, size), F32),
        pltpu.VMEM((size, seq), F32),
        pltpu.VMEM((cont, LANES), jnp.int32),
        pltpu.VMEM((buckets, width), F32),
        pltpu.VMEM((buckets, LANES), F32),
        pltpu.VMEM((model, own), F32),
        pltpu.VMEM((4 * dp_count, model), F32),
        pltpu.VMEM((mp_count, local, 3 * size), BF),
        pltpu.VMEM((heads, mp_count, local // 2, 6 * size), BF),
        pltpu.VMEM((heads, mp_count, local // 2, 6 * size), BF),
        dma(heads, 3),
        dma(heads, mp_count),
        pltpu.VMEM((dp_count,) + chunk, BF),
        pltpu.VMEM((dp_count,) + chunk, BF),
        dma(heads, dp_count),
        dma(heads, dp_count),
    ]
    if first:
        scratch += [
            pltpu.VMEM((dp_count, 8, model), F32),
            pltpu.VMEM((dp_count, 8, model), F32),
            pltpu.VMEM((mp_count, 8, model), F32),
        ]
        scratch += [dma(dp_count)] * 2 + [dma(3)] * 2 + [dma(dp_count)] * 2
        scratch += [dma(heads, dp_count)] * 2 + [dma(3, heads, dp_count)] * 2 + [dma(dp_count)] * 2 + [dma(3, dp_count)] * 2
        scratch += [pltpu.VMEM((mp_count, dp_count) + chunk, BF)] * 2 + [dma(2)]
        out_specs[1] = out_specs[2] = ANY
    return pl.pallas_call(
        functools.partial(back_kernel, layer, layers, heads, size, buckets),
        grid=(1,),
        out_shape=tuple(jax.ShapeDtypeStruct(shape, kind) for shape, kind in outs),
        in_specs=specs,
        out_specs=tuple(out_specs),
        scratch_shapes=scratch,
        compiler_params=pltpu.CompilerParams(
            collective_id=number, has_side_effects=True, vmem_limit_bytes=VMEM_BYTES
        ),
    )(lens, *[a[0] if isinstance(a, tuple) else a for a in args])


def dma(*shape):
    return pltpu.SemaphoreType.DMA(shape) if shape else pltpu.SemaphoreType.DMA


def gelu_grad(values):
    inner = jnp.tanh(SQRT_TWO_PI * (values + 0.044715 * values * values * values))
    slope = SQRT_TWO_PI * (1.0 + 3.0 * 0.044715 * values * values)
    return 0.5 * values * (1.0 + inner), 0.5 * (1.0 + inner) + 0.5 * values * (1.0 - inner * inner) * slope


def expert_kernel(mode, layer, dp_count, *refs):
    forward, backward = mode in ("fwd", "both"), mode in ("both", "bwd")
    refs = list(refs)

    def take(count):
        taken = refs[:count]
        del refs[:count]
        return taken

    (sending,) = take(1)
    far = take(2) if mode == "both" else None
    (x_in,) = take(1) if mode == "bwd" else (None,)
    w_in, w_out = take(2)
    results = take(forward + backward)
    (x_o,) = take(1) if mode == "fwd" else (None,)
    gw_in_o, gw_out_o = take(2) if backward else (None, None)
    w1, w2, wsem, wssem, wrsem = take(5)
    x_all, xsem = take(2)
    recv_a, recv_b, ssem, asem, fsem, bsem = take(6)
    paths = [take(9) for _ in results]
    if backward:
        g_all, hid_all, ig_all, stage, gsem, grsem, glsem = take(7)

    d = lax.axis_index("dp")
    me, core, mate, across, diagonal = mp_places()
    row = me // 2
    index = d * 2 + core
    experts = dp_count * 2
    model = w1.shape[1]
    half = model // 2
    rows_a = x_all.shape[1] // 2
    tile = sending.shape[1]
    ahead = 2

    barrier = pltpu.get_barrier_semaphore()

    def greet(k, carry):
        signal_to(barrier, dp=lax.rem(d + k // 2, dp_count), mp=row * 2 + lax.rem(core + k % 2, 2))
        return carry

    lax.fori_loop(1, experts, greet, 0)
    signal_to(barrier, mp=across)
    pl.semaphore_wait(barrier, experts)

    def send_wave(k):
        dd = lax.rem(d + k, dp_count)
        for cc in range(2):
            to = dd * 2 + cc

            @pl.when(to == index)
            def _():
                pltpu.make_async_copy(sending.at[to], recv_a.at[index], asem.at[index]).start()

            @pl.when(to != index)
            def _():
                remote(sending.at[to], recv_a.at[index], ssem.at[to], asem.at[index], dp=dd, mp=row * 2 + cc).start()

    for k in range(ahead):
        send_wave(k)
    copies = []
    for n, (source, held) in enumerate(((w_in, w1), (w_out, w2))):
        copies.append(remote(source.at[layer, 1 - core], held.at[core], wssem.at[n], wrsem.at[n], mp=mate))
        copies.append(pltpu.make_async_copy(source.at[layer, core], held.at[core], wsem.at[n]))
    if mode == "bwd":
        copies.append(pltpu.make_async_copy(x_in, x_all, xsem))
    for copy in copies:
        copy.start()

    def source_of(g):
        return lax.rem(d + dp_count - g, dp_count)

    def unpack(held, g, side, into, gates):
        base = side * rows_a
        s0 = source_of(g)
        tails = []
        for cc in range(2):
            src = s0 * 2 + cc
            block = held[src]
            factors = None if gates is None else gates[src][:, 7 * half :].astype(F32)

            def factor(i):
                return factors[:, 3 * i : 3 * i + 1] + factors[:, 3 * i + 1 : 3 * i + 2] + factors[:, 3 * i + 2 : 3 * i + 3]

            for i in range(3):
                piece = block[:, i * model : (i + 1) * model]
                if gates is not None:
                    piece = (piece.astype(F32) * factor(i)).astype(BF)
                into[g, base + (2 * i + cc) * tile : base + (2 * i + cc + 1) * tile, :] = piece
            tail = unfold_tail(block[:, 3 * model : 7 * half], half)
            tails.append(tail if gates is None else tail * factor(3)[0:8, :])
        into[g, base + 6 * tile : base + 7 * tile, :] = jnp.concatenate(tails, 0).astype(BF)

    def forward_copy(s0):
        two = pl.ds(s0 * 2, 2)
        return remote(recv_a.at[two], recv_b.at[two], fsem.at[s0], bsem.at[s0], mp=across)

    def partial_copy(path, g):
        kept, part, pssem, prsem, ret_s, ret, rssem, rrsem, psend = path
        return remote(psend.at[g], part.at[g], pssem.at[g], prsem.at[g], mp=across)

    def compute(g):
        x = x_all[g]
        totals = [0.0] * len(results)
        for q in range(2):
            inner = nn(x, w1[q])
            if backward:
                value, slope = gelu_grad(inner)
                hidden = value.astype(BF)
                hid_all[q, g] = hidden
                grad = (nt(g_all[g], w2[q]) * slope).astype(BF)
                ig_all[q, g] = grad
                totals[-1] = totals[-1] + nt(grad, w1[q])
            else:
                hidden = gelu_tanh(inner).astype(BF)
            if forward:
                totals[0] = totals[0] + nn(hidden, w2[q])
        return totals

    def give_back(path, g):
        kept, part, pssem, prsem, ret_s, ret, rssem, rrsem, psend = path
        partial_copy(path, g).wait_recv()
        total = kept[lax.rem(g, 2)] + part[g].astype(F32)
        s0 = source_of(g)
        for cc in range(2):
            src = s0 * 2 + cc
            for i in range(3):
                at = (2 * i + cc) * tile
                ret_s[src, :, i * model : (i + 1) * model] = total[at : at + tile, :].astype(BF)
            at = 6 * tile + 8 * cc
            ret_s[src, :, 3 * model :] = jnp.concatenate(
                [total[at : at + 8, 0:half], total[at : at + 8, half:]], 0
            ).astype(BF)

            @pl.when(src == index)
            def _():
                pltpu.make_async_copy(ret_s.at[src], ret.at[index], rrsem.at[index]).start()

            @pl.when(src != index)
            def _():
                remote(ret_s.at[src], ret.at[index], rssem.at[src], rrsem.at[index], dp=s0, mp=row * 2 + cc).start()

    def products(n, q, part):
        half_groups = pl.ds(part * dp_count // 2, dp_count // 2)
        count = dp_count * rows_a
        if n == 0:
            left, right = x_all[half_groups], ig_all[q, half_groups]
        else:
            left, right = hid_all[q, half_groups], g_all[half_groups]
        return tn(left.reshape(count, model), right.reshape(count, model))

    def arrive(g):
        s0 = source_of(g)
        for cc in range(2):
            src = s0 * 2 + cc
            pltpu.make_async_copy(recv_a.at[src], recv_a.at[src], asem.at[src]).wait()
        forward_copy(s0).start()

    def step(i, carry):
        @pl.when(i < dp_count)
        def _():
            arrive(i)

        @pl.when(i + ahead < dp_count)
        def _():
            send_wave(i + ahead)

        @pl.when((i >= 1) & (i <= dp_count))
        def _():
            g = i - 1
            forward_copy(source_of(g)).wait_recv()
            for side, held in enumerate((recv_a, recv_b)):
                if forward:
                    unpack(held, g, side, x_all, None)
                if mode == "both":
                    unpack(far[side], g, side, g_all, held)
                elif mode == "bwd":
                    unpack(held, g, side, g_all, None)
            for path, total in zip(paths, compute(g)):
                kept, psend = path[0], path[8]
                kept[lax.rem(g, 2)] = total[0:rows_a, :]
                psend[g] = total[rows_a:, :].astype(BF)
                partial_copy(path, g).start()

        @pl.when(i >= 2)
        def _():
            for path in paths:
                give_back(path, i - 2)

        if backward:
            for n in range(2):
                for q in range(2):

                    @pl.when(i == dp_count // 2 + 1 + 2 * n + q)
                    def _():
                        stage[n, q] = products(n, q, 0)

        return carry

    arrive(0)
    send_wave(ahead)
    for copy in copies:
        copy.wait()
    lax.fori_loop(1, dp_count + 2, step, 0)
    if mode == "fwd":
        saved = pltpu.make_async_copy(x_all, x_o, xsem)
        saved.start()
    if backward:
        outs = (gw_in_o, gw_out_o)
        copies = []
        for n in range(2):
            stage[n, 1 - core] += products(n, 1 - core, 1)
            copy = remote(stage.at[n, 1 - core], outs[n].at[core], gsem.at[n], grsem.at[n], mp=mate)
            copy.start()
            copies.append(copy)
        for n in range(2):
            stage[n, core] += products(n, core, 1)
            copy = pltpu.make_async_copy(stage.at[n, core], outs[n].at[core], glsem.at[n])
            copy.start()
            copies.append(copy)
    for path, result in zip(paths, results):
        kept, part, pssem, prsem, ret_s, ret, rssem, rrsem, psend = path

        def end(e, carry):
            pltpu.make_async_copy(ret.at[e], ret.at[e], rrsem.at[e]).wait()

            @pl.when(e != index)
            def _():
                pltpu.make_async_copy(ret_s.at[e], ret_s.at[e], rssem.at[e]).wait()

            return carry

        lax.fori_loop(0, experts, end, 0)

        def end_group(g, carry):
            pltpu.make_async_copy(psend.at[g], psend.at[g], pssem.at[g]).wait()
            return carry

        lax.fori_loop(0, dp_count, end_group, 0)
        result[...] = ret[...]

    def end_send(e, carry):
        @pl.when(e != index)
        def _():
            pltpu.make_async_copy(sending.at[e], sending.at[e], ssem.at[e]).wait()

        return carry

    lax.fori_loop(0, experts, end_send, 0)

    def end_pair(s0, carry):
        two = pl.ds(s0 * 2, 2)
        pltpu.make_async_copy(recv_a.at[two], recv_a.at[two], fsem.at[s0]).wait()
        return carry

    lax.fori_loop(0, dp_count, end_pair, 0)
    if mode == "fwd":
        saved.wait()
    if backward:
        for n in range(2):
            copies[n].wait()
            copies[2 + n].wait()


def expert_call(mode, layer, number, dp_count, send, far, x_in, w_in, w_out):
    forward, backward = mode in ("fwd", "both"), mode in ("both", "bwd")
    experts, tile, _ = send.shape
    model = w_in.shape[2]
    block = (experts, tile, 7 * model // 2)
    rows = 2 * 7 * tile
    args, specs = [send], [VMEM]
    if mode == "both":
        args += far
        specs += [VMEM] * 2
    if mode == "bwd":
        args.append(x_in)
        specs.append(ANY)
    args += [w_in, w_out]
    specs += [ANY, ANY]
    outs, out_specs = [], []

    def out(dims, kind, spec):
        outs.append(jax.ShapeDtypeStruct(dims, kind))
        out_specs.append(spec)

    for _ in range(forward + backward):
        out(block, BF, VMEM)
    if mode == "fwd":
        out((dp_count, rows, model), BF, ANY)
    if backward:
        out((2, model, model), F32, ANY)
        out((2, model, model), F32, ANY)
    scratch = [
        pltpu.VMEM((2, model, model), BF),
        pltpu.VMEM((2, model, model), BF),
        dma(2),
        dma(2),
        dma(2),
        pltpu.VMEM((dp_count, rows, model), BF),
        dma(),
        pltpu.VMEM(send.shape, BF),
        pltpu.VMEM(send.shape, BF),
        dma(experts),
        dma(experts),
        dma(dp_count),
        dma(dp_count),
    ]
    for _ in range(forward + backward):
        scratch += [
            pltpu.VMEM((2, rows // 2, model), F32),
            pltpu.VMEM((dp_count, rows // 2, model), BF),
            dma(dp_count),
            dma(dp_count),
            pltpu.VMEM(block, BF),
            pltpu.VMEM(block, BF),
            dma(experts),
            dma(experts),
            pltpu.VMEM((dp_count, rows // 2, model), BF),
        ]
    if backward:
        scratch += [
            pltpu.VMEM((dp_count, rows, model), BF),
            pltpu.VMEM((2, dp_count, rows, model), BF),
            pltpu.VMEM((2, dp_count, rows, model), BF),
            pltpu.VMEM((2, 2, model, model), F32),
            dma(2),
            dma(2),
            dma(2),
        ]
    return pl.pallas_call(
        functools.partial(expert_kernel, mode, layer, dp_count),
        out_shape=tuple(outs),
        in_specs=specs,
        out_specs=tuple(out_specs),
        scratch_shapes=scratch,
        compiler_params=pltpu.CompilerParams(
            collective_id=number, has_side_effects=True, vmem_limit_bytes=VMEM_BYTES
        ),
    )(*args)


def spread_kernel(size, buckets, count, *refs):
    parts, grads, small = refs[:count], refs[count : 3 * count], refs[3 * count]
    qkv_o, attn_o, in_o, out_o, gain_a_o, bias_o, gain_f_o, router_o, sem = refs[3 * count + 1 :]
    step = pl.program_id(0)
    copies = []
    for n in range(count):
        copies.append(pltpu.make_async_copy(grads[2 * n].at[0], in_o.at[n, step], sem.at[2 * n]))
        copies.append(pltpu.make_async_copy(grads[2 * n + 1].at[0], out_o.at[n, step], sem.at[2 * n + 1]))
    for copy in copies:
        copy.start()
    for n in range(count):
        mp_count, blocks, heads, rows, _ = parts[n].shape
        pieces = [
            parts[n][m, :, h].reshape(blocks * rows, 4 * size).astype(F32) for m in range(mp_count) for h in range(heads)
        ]
        qkv_o[n] = jnp.concatenate([p[:, t * size : (t + 1) * size] for t in range(3) for p in pieces], 1)
        for number, p in enumerate(pieces):
            attn_o[n, number * size : (number + 1) * size, :] = p[:, 3 * size :].T
    lines = small.shape[0] // count
    for n in range(count):
        gain_a_o[n : n + 1, :] = small[n * lines, 0:1, :]
        gain_f_o[n : n + 1, :] = small[n * lines, 1:2, :]
        tiles = [small[n * lines + 1, :, i * LANES : (i + 1) * LANES] for i in range(buckets // 8)]
        bias_o[:, n : n + 1, :] = jnp.concatenate(tiles, 0).T[0 : bias_o.shape[0], :].reshape(bias_o.shape[0], 1, buckets)
        router_o[n] = jnp.concatenate([small[n * lines + i] for i in range(2, lines)], 0)
    for copy in copies:
        copy.wait()


def spread_call(parts, grads, small, size, heads, buckets, experts):
    mp_count, blocks, own_heads, rows, wide = parts[0].shape
    layers, model = len(parts), blocks * rows
    steps = grads[0].shape[0]
    return pl.pallas_call(
        functools.partial(spread_kernel, size, buckets, layers),
        grid=(steps,),
        out_shape=(
            jax.ShapeDtypeStruct((layers, model, 3 * heads * size), F32),
            jax.ShapeDtypeStruct((layers, heads * size, model), F32),
            jax.ShapeDtypeStruct((layers,) + grads[0].shape, F32),
            jax.ShapeDtypeStruct((layers,) + grads[1].shape, F32),
            jax.ShapeDtypeStruct((layers, model), F32),
            jax.ShapeDtypeStruct((heads, layers, buckets), F32),
            jax.ShapeDtypeStruct((layers, model), F32),
            jax.ShapeDtypeStruct((layers, experts, model), F32),
        ),
        in_specs=[pl.BlockSpec((mp_count, blocks // steps, own_heads, rows, wide), lambda i: (0, i, 0, 0, 0))] * layers
        + [pl.BlockSpec((1,) + g.shape[1:], lambda i: (i, 0, 0)) for g in grads]
        + [VMEM],
        out_specs=(
            pl.BlockSpec((layers, model // steps, 3 * heads * size), lambda i: (0, i, 0)),
            pl.BlockSpec((layers, heads * size, model // steps), lambda i: (0, 0, i)),
            ANY,
            ANY,
            VMEM,
            VMEM,
            VMEM,
            VMEM,
        ),
        scratch_shapes=[dma(2 * layers)],
        compiler_params=pltpu.CompilerParams(vmem_limit_bytes=VMEM_BYTES),
    )(*parts, *grads, small)


def fast_body(
    tokens, cotangent, w_qkv, w_attn, attn_gain, rel_bias, ffn_gain, router, w_in, w_out, cont_lengths, routes, slots, drops
):
    _, local, model = tokens.shape
    heads, buckets = rel_bias.shape[1:]
    size = model // heads
    layers = w_qkv.shape[0]
    dp_count, mp_count = lax.axis_size("dp"), lax.axis_size("mp")
    own_heads = heads // mp_count
    experts = dp_count * 2
    me = lax.axis_index("mp")
    block = (experts, 16, 7 * model // 2)
    pairs = jnp.concatenate(
        [routes.reshape(layers, local, 2), slots.reshape(layers, local, 2), 1 - drops.reshape(layers, local, 2)], 2
    )
    rows = jnp.pad(pairs.transpose(0, 2, 1), ((0, 0), (0, 2), (0, 0)))
    router = router.transpose(0, 2, 1)
    vecs = bias_vectors(lax.dynamic_slice_in_dim(rel_bias, me * own_heads, own_heads, 1))

    kept = [None] * layers
    back, far = None, None
    for l in range(layers):
        first, last = l == 0, l == layers - 1
        normal = [attn_gain, w_qkv, vecs[l], w_attn, ffn_gain, (router, l), (rows, l)]
        if first:
            specials = [tokens[0], cotangent[0], (rows, layers - 1)]
        else:
            before = kept[l - 1]
            specials = [before["middle"], before["out"], (rows, l - 1), before["gates"]]
        if last:
            specials += far
        got = pre_call(
            l, layers, l, own_heads, size, cont_lengths, normal, mp_count, dp_count, local, model, specials, block
        )
        got = [tokens[0]] + list(got) if first else list(got)
        names = ("stream", "normed", "qkv", "mixed", "lse", "middle", "ffn", "gates")
        kept[l] = k = dict(zip(names, got))
        if first:
            far = got[9:11]
        if last:
            far = [far[0], got[9]]
            k["out"], back, k["gw_in"], k["gw_out"] = expert_call("both", l, 5, dp_count, got[8], far, None, w_in, w_out)
        else:
            k["out"], k["x_rows"] = expert_call("fwd", l, 4, dp_count, got[8], None, None, w_in, w_out)

    flow = cotangent[0]
    for l in reversed(range(layers)):
        k = kept[l]
        last = l == layers - 1
        normal = [
            vecs[l], back, k["out"], flow, k["middle"], k["ffn"], k["gates"], (rows, l), (router, l), ffn_gain,
            k["normed"], k["qkv"], k["mixed"], k["lse"], w_attn, w_qkv, k["stream"], attn_gain,
        ]
        extra = [(rows, l - 1), kept[l - 1]["gates"]] if last else [heads_sum, small]
        got = back_call(
            l, layers, 6 + last, own_heads, size, buckets, cont_lengths, normal, mp_count, dp_count, local, model, block, extra
        )
        if last:
            flow, output, send, heads_sum, small = got
            b = kept[l - 1]
            back, b["gw_in"], b["gw_out"] = expert_call("bwd", l - 1, 10, dp_count, send, None, b["x_rows"], w_in, w_out)
        else:
            flow, upper, lower, small = got
    grads = [kept[l][name] for l in range(layers) for name in ("gw_in", "gw_out")]
    grad_qkv, grad_attn, grad_in, grad_out, grad_a, grad_bias, grad_f, grad_router = spread_call(
        [lower, upper], grads, small, size, heads, buckets, experts
    )
    return (
        output[None], flow[None], grad_qkv, grad_attn, grad_a, grad_bias.transpose(1, 0, 2), grad_f, grad_router.transpose(0, 2, 1), grad_in, grad_out,
    )


def chosen_body(
    tokens, cotangent, w_qkv, w_attn, attn_gain, rel_bias, ffn_gain, router, w_in, w_out, cont_lengths, routes, slots, drops
):
    groups, local, model = tokens.shape
    heads = rel_bias.shape[1]
    dp_count, mp_count = lax.axis_size("dp"), lax.axis_size("mp")
    capacity = max(2, 9 * 2 * groups * local // (8 * w_in.shape[1] * dp_count))
    seq = local * mp_count
    fits = (
        groups == 1
        and w_qkv.shape[0] == 2
        and mp_count == 4
        and dp_count == 8
        and router.shape[2] == 16
        and rel_bias.shape[2] == 32
        and heads % mp_count == 0
        and model // heads == 64
        and model % 256 == 0
        and local % 128 == 0
        and w_in.shape[1:] == (2, model, model)
        and w_out.shape[1:] == (2, model, model)
        and 48 < capacity <= 56
        and seq > PROMPT
        and (seq - PROMPT) % QB == 0
    )
    plan = fast_body if fits else body
    return plan(
        tokens, cotangent, w_qkv, w_attn, attn_gain, rel_bias, ffn_gain, router, w_in, w_out, cont_lengths, routes, slots, drops
    )


def solution(mesh):
    return jax.shard_map(
        chosen_body,
        mesh=mesh,
        in_specs=(
            P("dp", "mp", None),
            P("dp", "mp", None),
            P(),
            P(),
            P(),
            P(),
            P(),
            P(),
            P(None, "dp", None, "mp"),
            P(None, "dp", "mp", None),
            P("dp", None),
            P(None, "dp", "mp", None),
            P(None, "dp", "mp", None),
            P(None, "dp", "mp", None),
        ),
        out_specs=(
            P("dp", "mp", None),
            P("dp", "mp", None),
            P(),
            P(),
            P(),
            P(),
            P(),
            P(),
            P(None, "dp", None, "mp"),
            P(None, "dp", "mp", None),
        ),
        check_vma=False,
    )
```
